32 devices in a mesh: slab: 8 (over z, y), brick: 4 (over x, core).
Axes of the slice: x: 2, y: 2, z: 4, core: 2. Of those that a mesh axis runs over, the one named last changes fastest.
Arguments:
- positions: float32 [2048, 3, 128], P(('slab', 'brick')), may hold values from -6 to 6
- velocities: float32 [2048, 3, 128], P(('slab', 'brick')), may hold values from -6 to 6
- radii: float32 [2048, 128], P(('slab', 'brick')), may hold values from 0.6 to 1.2
- cell_of: int32 [2048, 128], P(('slab', 'brick')), may hold values from 0 to 65535
- block_route: int32 [2048, 1], P(('slab', 'brick')), may hold values from 0 to 11; in each aligned block of 64 rows (0 to 63, 64 to 127, ...) at most 11 rows name the same one
- ghost_list: int32 [512], P(('slab', 'brick')), may hold values from 0 to 63
- tile_home: int32 [4096], P(('slab', 'brick')), may hold values from 0 to 63
- tile_partner: int32 [4096], P(('slab', 'brick')), may hold values from 0 to 95
- fluid: float32 [3, 32, 128, 512], P(None, 'slab', 'brick'), may hold values from -6 to 6
Outputs:
- velocity_next: float32 [2048, 3, 128], P(('slab', 'brick'))
- fluid_next: float32 [3, 32, 128, 512], P(None, 'slab', 'brick')
The draws below stay inside these ranges and needn't reach their ends.
Inputs may be any that keep to these rules, and one draw needn't show every extreme that they name: `block_route`: within the blocks of one device no code appears more than 11 times, and some device's blocks reach 11 for some code.
All inputs are finite; a program needn't handle non-finite values.
Results may differ from the reference program's by a relative error of at most 0.00013.
Values sent between devices are 32-bit elements; how exact they have to be, the bound alone decides.
No kernel may reach another device: no remote copies, remote signals or barrier semaphores. Data moves between devices by JAX's collectives and lax.ppermute only.
A program may use at most 64 MiB of HBM per device.

```python
import math
import jax
import jax.numpy as jnp
import numpy as np
from jax import lax

BLK = 128
NB = 64
GH = 4
CX = 4
CY = 32
CZ = 512
TILES = 128
CAP = 11
BLOCKS = 2048
CELLS = 65536
NX = 32
NY = 128
N_SLAB = 8
N_BRICK = 4


def set_ends(values, rng, smallest, top_value):
    spot = [jax.random.randint(jax.random.fold_in(rng, axis), (), 0, length) for axis, length in enumerate(values.shape)]
    longest = values.shape.index(max(values.shape))
    next_to = spot[:longest] + [(spot[longest] + 1) % values.shape[longest]] + spot[longest + 1:]
    return values.at[tuple(spot)].set(smallest).at[tuple(next_to)].set(top_value)


def levels(own_key, extent, shards, smallest, top_value):
    def one(position, shards_of):
        steps = jax.random.uniform(jax.random.fold_in(jax.random.fold_in(own_key, 6), position), (shards_of,), jnp.float32, smallest / len(shards), top_value / len(shards))
        return jnp.repeat(jnp.exp(steps), extent[position] // shards_of).reshape((-1,) + (1,) * (len(extent) - position - 1))

    factor_of = one(*shards[0])
    for cut in shards[1:]:
        factor_of = factor_of * one(*cut)
    return factor_of


def assign_block(own_key, own, number, rows, amount, top, bound, skew):
    order = jax.random.permutation(own_key, amount)
    crowded, ordinary = load_shares(amount, rows * top, bound, skew, True), load_shares(amount, rows * top, bound, skew, False)
    places = jnp.arange(amount)

    def named(lengths, rotation):
        used = int((lengths > 0).sum())
        fixed = max(1, used // 4)
        moved = fixed + (places - fixed + rotation * (used - fixed)) % max(1, amount - fixed)
        return jnp.zeros((amount,), jnp.int32).at[order[jnp.where(places < fixed, places, moved)]].set(jnp.asarray(lengths, jnp.int32))

    lengths = jnp.where(number % 4 == 0, named(crowded, number // 4), named(ordinary, number - number // 4 - 1))
    mixed = jax.random.permutation(jax.random.fold_in(own, 3), amount)
    donor, sink = mixed[0:amount // 2 * 2:2], mixed[1:amount // 2 * 2:2]
    room = jnp.minimum(lengths[donor] - 1, bound - lengths[sink]) // 2
    room = jnp.where((donor == order[0]) | (sink == order[0]) | (lengths[sink] == 0), 0, jnp.maximum(room, 0))
    moved = jax.random.randint(jax.random.fold_in(own, 4), (amount // 2,), 0, 1 << 20) % (room + 1)
    lengths = lengths.at[donor].add(-moved).at[sink].add(moved)
    members = jnp.searchsorted(jnp.cumsum(lengths), jnp.arange(rows * top), side="right").astype(jnp.int32)
    grid = members.reshape(top, rows).T
    grid = grid[jax.random.permutation(jax.random.fold_in(own, 1), rows)]
    rotation = jax.random.randint(jax.random.fold_in(own, 2), (rows, 1), 0, top)
    return jnp.take_along_axis(grid, (jnp.arange(top)[None, :] + rotation) % top, axis=1)


def load_shares(amount, total, limit, lean, full):
    weights = [(1 << 20) // math.isqrt(grade ** lean) + 1 for grade in range(1, amount + 1)]
    largest = limit if full else min(limit, max(-(-total // amount), total * weights[0] // sum(weights)))
    least = 1 if total - largest >= amount - 1 else 0
    given, spare = [largest] + [least] * (amount - 1), total - largest - least * (amount - 1)
    while spare > 0:
        movable = [i for i in range(1, amount) if given[i] < largest] or [i for i in range(1, amount) if given[i] < limit]
        pool, remaining = sum([weights[i] for i in movable]), spare
        for i in movable:
            extra = min(limit - given[i], max(1, remaining * weights[i] // pool), spare)
            given[i] = given[i] + extra
            spare = spare - extra
    return np.array(given)


def normal_values(own_key, extent, deviation, limit, shards=(), kind=jnp.bfloat16):
    values = jax.random.normal(own_key, extent, jnp.float32) * deviation
    if len(shards) > 0:
        values = levels(own_key, extent, shards, -0.22, 0.18) * values
    return jnp.clip(values, min=-limit, max=limit).astype(kind)


def setup_inputs(seed: int = 0) -> dict:
    key_of = jax.random.split(jax.random.key(seed), 10)
    positions = normal_values(key_of[0], (BLOCKS, 3, BLK), 1.0, 6.0, ((0, 32),), jnp.float32)
    velocities = normal_values(key_of[1], (BLOCKS, 3, BLK), 1.0, 6.0, ((0, 32),), jnp.float32)
    radii = jnp.clip(0.6 + 0.6 * jax.random.uniform(key_of[2], (BLOCKS, BLK), jnp.float32) ** levels(key_of[2], (BLOCKS, BLK), ((0, 32),), -0.2, 0.2), 0.6, 1.2)
    cell_of = set_ends(jax.random.randint(key_of[3], (BLOCKS, BLK), 0, CELLS), jax.random.fold_in(key_of[3], 1), 0, CELLS - 1).astype(jnp.int32)
    block_route_keys = jax.random.split(jax.random.fold_in(key_of[4], 1), BLOCKS // NB)
    block_route_turns = jax.random.permutation(jax.random.fold_in(key_of[4], 3), BLOCKS // NB)
    block_route = jax.vmap(lambda own, number: assign_block(jax.random.fold_in(key_of[4], 2), own, number, NB, 3 * N_BRICK, 1, CAP, 2))(block_route_keys, block_route_turns).reshape((BLOCKS, 1))
    ghost_list = set_ends(jax.random.randint(key_of[5], (N_SLAB * N_BRICK * 4 * GH,), 0, NB), jax.random.fold_in(key_of[5], 1), 0, NB - 1).astype(jnp.int32)
    tile_home = set_ends(jax.random.randint(key_of[6], (N_SLAB * N_BRICK * TILES,), 0, NB), jax.random.fold_in(key_of[6], 1), 0, NB - 1).astype(jnp.int32)
    tile_partner = set_ends(jax.random.randint(key_of[7], (N_SLAB * N_BRICK * TILES,), 0, NB + 8 * GH), jax.random.fold_in(key_of[7], 1), 0, (NB + 8 * GH) - 1).astype(jnp.int32)
    fluid = normal_values(key_of[8], (3, NX, NY, CZ), 1.0, 6.0, ((1, 8), (2, 4)), jnp.float32)
    return {"positions": positions, "velocities": velocities, "radii": radii, "cell_of": cell_of, "block_route": block_route, "ghost_list": ghost_list, "tile_home": tile_home, "tile_partner": tile_partner, "fluid": fluid}


stiffness = 0.01
damping = 0.005
viscosity = 0.1
coupling = 0.5
relaxation = 0.5


def pack_blocks(positions, velocities, radii):
    return jnp.concatenate([positions, velocities, radii[:, None, :]], axis=1)


def tile_forces(home_block, partner):
    here_pos = home_block[:, 0:3]
    there_pos = partner[:, 0:3]
    here_vel = home_block[:, 3:6]
    there_vel = partner[:, 3:6]
    offsets = here_pos[:, :, :, None] - there_pos[:, :, None, :]
    squared = jnp.sum(offsets * offsets, axis=1)
    contact = home_block[:, 6, :, None] + partner[:, 6, None, :]
    weight = jnp.maximum(contact * contact - squared, 0.0)
    weight_sum = jnp.sum(weight, axis=2)
    spring = jnp.sum(weight[:, None] * offsets, axis=3)
    friction = jnp.einsum("bij,bcj->bci", weight, there_vel, precision=lax.Precision.HIGHEST) - here_vel * weight_sum[:, None]
    return stiffness * spring + damping * friction


def contact_forces(candidates, homes, partners, nblocks):
    width = candidates.shape[2]
    group = math.gcd(homes.shape[0], 16)
    home_groups = homes.reshape(-1, group)
    partner_groups = partners.reshape(-1, group)

    def advance_tiles(accumulated, indices):
        home_ids, partner_ids = indices
        terms = tile_forces(candidates[home_ids], candidates[partner_ids])
        return accumulated.at[home_ids].add(terms), None

    start = jnp.zeros((nblocks, 3, width), jnp.float32)
    result, _ = lax.scan(advance_tiles, start, (home_groups, partner_groups))
    return result


def laplacian_grid(field):
    padded_z = jnp.pad(field, ((0, 0), (0, 0), (0, 0), (1, 1)))
    inner = padded_z[:, :, :, 1:-1]
    total = jnp.roll(field, -1, axis=1) + jnp.roll(field, 1, axis=1)
    total = total + jnp.roll(field, -1, axis=2) + jnp.roll(field, 1, axis=2)
    total = total + padded_z[:, :, :, 2:] + padded_z[:, :, :, :-2]
    return total - 6.0 * inner


def reference(positions, velocities, radii, cell_of, block_route, ghost_list, tile_home, tile_partner, fluid):
    ndev = N_SLAB * N_BRICK
    packed = pack_blocks(positions, velocities, radii).reshape(ndev, NB, 7, BLK)
    ghost_ids = ghost_list.reshape(ndev, 4 * GH)
    ghost_sets = jax.vmap(lambda blocks, ids: blocks[ids])(packed, ghost_ids).reshape(ndev, 2, 2, GH, 7, BLK)
    devices_all = jnp.arange(ndev, dtype=jnp.int32)
    slab_of = devices_all // N_BRICK
    brick_of = devices_all % N_BRICK
    lower_slab = ((slab_of - 1) % N_SLAB) * N_BRICK + brick_of
    upper_slab = ((slab_of + 1) % N_SLAB) * N_BRICK + brick_of
    lower_brick = slab_of * N_BRICK + (brick_of - 1) % N_BRICK
    upper_brick = slab_of * N_BRICK + (brick_of + 1) % N_BRICK
    homes_all = tile_home.reshape(ndev, TILES)
    partners_all = tile_partner.reshape(ndev, TILES)

    def one_device(device):
        candidates = jnp.concatenate([
            packed[device],
            ghost_sets[lower_slab[device]][1].reshape(-1, 7, BLK),
            ghost_sets[upper_slab[device]][0].reshape(-1, 7, BLK),
            ghost_sets[lower_brick[device]][:, 1].reshape(-1, 7, BLK),
            ghost_sets[upper_brick[device]][:, 0].reshape(-1, 7, BLK)], axis=0)
        return contact_forces(candidates, homes_all[device], partners_all[device], NB)

    forces = lax.map(one_device, devices_all).reshape(BLOCKS, 3, BLK)
    masses = radii * radii * radii
    updated = velocities + forces / masses[:, None, :]
    route_code = block_route[:, 0]
    block_slab = jnp.repeat(slab_of, NB)
    destination = ((block_slab + route_code // N_BRICK - 1) % N_SLAB) * N_BRICK + route_code % N_BRICK
    cell_global = (destination[:, None] * CELLS + cell_of).reshape(-1)
    volume = jnp.zeros((ndev * CELLS,), jnp.float32).at[cell_global].add(masses.reshape(-1))
    carried = jnp.moveaxis(masses[:, None, :] * updated, 1, 0).reshape(3, -1)
    momentum = jnp.zeros((3, ndev * CELLS), jnp.float32).at[:, cell_global].add(carried)

    def to_grid(flat):
        chans = flat.shape[0]
        shaped = flat.reshape(chans, N_SLAB, N_BRICK, CX, CY, CZ).transpose(0, 1, 3, 2, 4, 5)
        return shaped.reshape(chans, NX, NY, CZ)

    volume_grid = to_grid(volume[None])
    momentum_grid = to_grid(momentum)
    fluid_next = fluid + viscosity * laplacian_grid(fluid) + coupling * (momentum_grid - volume_grid * fluid)
    back_flat = fluid_next.reshape(3, N_SLAB, CX, N_BRICK, CY, CZ).transpose(0, 1, 3, 2, 4, 5).reshape(3, -1)
    sampled = jnp.moveaxis(back_flat[:, cell_global].reshape(3, BLOCKS, BLK), 0, 1)
    velocity_next = updated + relaxation * (sampled - updated)
    return velocity_next, fluid_next
```

```python
import functools
import math

import jax
import jax.numpy as jnp
from jax import lax
from jax.experimental import pallas as pl
from jax.experimental.pallas import tpu as pltpu
from jax.sharding import PartitionSpec as P

stiffness = 0.01
damping = 0.005
viscosity = 0.1
coupling = 0.5
relaxation = 0.5

f32 = jnp.float32
bf16 = jnp.bfloat16
VMEM = pl.BlockSpec(memory_space=pltpu.VMEM)
SMEM = pl.BlockSpec(memory_space=pltpu.SMEM)
UNROLL = 4
GROUP = 4


def rows_up(count):
    return -(-count // 8) * 8


def call(body, outs, ins, scratch, name, flops=0, nbytes=1 << 20):
    return pl.pallas_call(
        body,
        out_shape=outs,
        in_specs=ins,
        out_specs=[VMEM] * len(outs),
        scratch_shapes=scratch,
        name=name,
        compiler_params=pltpu.CompilerParams(vmem_limit_bytes=40 << 20),
        cost_estimate=pl.CostEstimate(flops=flops, bytes_accessed=nbytes, transcendentals=0),
    )


def rounded(x):
    return x.astype(bf16).astype(f32)


def iota(shape, dim):
    return lax.broadcasted_iota(jnp.int32, shape, dim)


def block_tile(pos_ref, vel_ref, rad_ref, index):
    width = rad_ref.shape[1]
    return jnp.concatenate(
        [
            pos_ref[index],
            rad_ref[pl.ds(index, 1), :],
            vel_ref[index],
            jnp.ones((1, width), f32),
        ],
        axis=0,
    )


def pack_kernel(ghost_ref, pos_ref, vel_ref, rad_ref, fluid_ref, up, down, right, left,
                x_last, x_first, y_last, y_first):
    count = ghost_ref.shape[0] // 4
    for group in range(4):
        i, j = group // 2, group % 2
        for g in range(count):
            tile = block_tile(pos_ref, vel_ref, rad_ref, ghost_ref[group * count + g])
            (up if i else down)[j * count + g] = tile
            (right if j else left)[i * count + g] = tile
    nx, ny = fluid_ref.shape[1:3]
    x_last[...] = fluid_ref[:, nx - 1]
    x_first[...] = fluid_ref[:, 0]
    y_last[...] = fluid_ref[:, :, ny - 1]
    y_first[...] = fluid_ref[:, :, 0]


def split_rows(tile):
    width = tile.shape[1]
    sub = iota((8, width), 0)
    upper = sub < 4
    both = jnp.concatenate([tile[0:4], tile[0:4]], axis=0)
    one = rounded(both)
    rest = both - one
    two = rounded(rest)
    three = rest - two
    square = both * both
    own = square[3:4] - square[0:1] - square[1:2] - square[2:3]
    own_one = rounded(own)
    own_rest = own - own_one
    own_two = rounded(own_rest)
    own_three = own_rest - own_two
    return upper, sub, one, two, three, own_one, own_two, own_three


def own_terms(sub, parts, first):
    a, b, c = parts
    return jnp.where(
        sub == first,
        a,
        jnp.where(
            sub == first + 1,
            b,
            jnp.where(sub == first + 2, c, jnp.where(sub < 6, 1.0, 0.0)),
        ),
    )


def home_rows(tile):
    upper, sub, one, two, three, *own = split_rows(tile)
    return jnp.concatenate(
        [2.0 * one, 2.0 * two, 2.0 * jnp.where(upper, one, three), own_terms(sub, own, 0)], axis=0
    ).astype(bf16)


def partner_columns(tile):
    upper, sub, one, two, three, *own = split_rows(tile)
    crossed = jnp.where(upper, one, two)
    rows = jnp.concatenate(
        [crossed, crossed, jnp.where(upper, three, one), own_terms(sub, own, 3)], axis=0
    )
    return jnp.transpose(rows).astype(bf16)


def value_rows(tile):
    high = rounded(tile)
    both = jnp.concatenate([high, tile - high], axis=0).astype(bf16)
    return jnp.concatenate([both, both], axis=1)


def list_tiles(home_ref, partner_ref, homes, partners, lower, upper, spare):
    def one(t, count):
        partner = partner_ref[t]
        homes[count] = home_ref[t]
        partners[count] = partner - lower
        return count + jnp.where((partner >= lower) & (partner < upper), 1, 0)

    count = lax.fori_loop(0, home_ref.shape[0], one, 0, unroll=4)
    for pad in range(UNROLL):
        homes[count + pad] = spare
        partners[count + pad] = 0
    return count


def add_tiles(count, homes, partners, home_side, partner_side, values, sums):
    def some(step, _):
        for k in range(UNROLL):
            home = homes[step * UNROLL + k]
            partner = partners[step * UNROLL + k]
            weight = jnp.dot(partner_side[partner], home_side[home], preferred_element_type=f32)
            weight = jnp.maximum(weight, 0.0)
            high = weight.astype(bf16)
            low = (weight - high.astype(f32)).astype(bf16)
            sums[home] += jnp.dot(
                values[partner], jnp.concatenate([high, low], axis=0), preferred_element_type=f32
            )
        return 0

    lax.fori_loop(0, (count + UNROLL - 1) // UNROLL, some, 0)


def own_contacts(home_ref, partner_ref, pos_ref, vel_ref, rad_ref, home_side, sums,
                 partner_side, values, homes, partners):
    nblocks = rad_ref.shape[0]

    def prepare(b, _):
        tile = block_tile(pos_ref, vel_ref, rad_ref, b)
        home_side[b] = home_rows(tile)
        partner_side[b] = partner_columns(tile)
        values[b] = value_rows(tile)
        sums[b] = jnp.zeros(sums.shape[1:], f32)
        return 0

    lax.fori_loop(0, nblocks, prepare, 0, unroll=4)
    home_side[nblocks] = jnp.zeros(home_side.shape[1:], bf16)
    sums[nblocks] = jnp.zeros(sums.shape[1:], f32)
    count = list_tiles(home_ref, partner_ref, homes, partners, 0, nblocks, nblocks)
    add_tiles(count, homes, partners, home_side, partner_side, values, sums)


def ghost_contacts(nbrick, cap, home_ref, partner_ref, route_ref, below, above, before, after,
                   home_side, own_sums, pos_ref, vel_ref, rad_ref, cell_ref, updated, outgoing,
                   partner_side, values, sums, homes, partners, taken):
    nblocks, width = rad_ref.shape
    per = below.shape[0]
    for place, ghosts in enumerate((below, above, before, after)):

        def prepare(k, _, place=place, ghosts=ghosts):
            tile = ghosts[k]
            partner_side[place * per + k] = partner_columns(tile)
            values[place * per + k] = value_rows(tile)
            return 0

        lax.fori_loop(0, per, prepare, 0, unroll=4)
    sums[...] = own_sums[...]
    count = list_tiles(home_ref, partner_ref, homes, partners, nblocks, nblocks + 4 * per, nblocks)
    add_tiles(count, homes, partners, home_side, partner_side, values, sums)

    outgoing[...] = jnp.zeros(outgoing.shape, f32)
    chunk = rows_up(5 * cap + 1)
    for code in range(3 * nbrick):
        taken[code] = 0

    def finish(b, _):
        both = sums[b]
        total = both[0:8] + both[8:16]
        here, speed, radius = pos_ref[b], vel_ref[b], rad_ref[pl.ds(b, 1), :]
        weights = total[7:8]
        spring = here * weights - total[0:3]
        friction = total[4:7] - speed * weights
        force = stiffness * spring + damping * friction
        fresh = speed + force / (radius * radius * radius)
        updated[b] = fresh
        code = route_ref[b]
        spot = taken[code]
        taken[code] = spot + 1
        row = ((code % nbrick) * 3 + code // nbrick) * chunk + spot
        outgoing[pl.ds(row, 1), :] = radius
        for c in range(3):
            outgoing[pl.ds(row + (c + 1) * cap, 1), :] = fresh[c : c + 1]
        outgoing[pl.ds(row + 4 * cap, 1), :] = cell_ref[pl.ds(b, 1), :].astype(f32)
        return 0

    lax.fori_loop(0, nblocks, finish, 0, unroll=4)
    for code in range(3 * nbrick):
        row = ((code % nbrick) * 3 + code // nbrick) * chunk + 5 * cap
        outgoing[row : row + 1, :] = jnp.full((1, width), taken[code], jnp.int32).astype(f32)


def list_blocks(arrived, starts, ends, cap, places):
    base, goal = places
    count = 0
    for start, end in zip(starts, ends):
        here = jnp.max(arrived[start + 5 * cap : start + 5 * cap + 1, :]).astype(jnp.int32)
        for spot in range(cap):
            base[count] = start + spot
            goal[count] = end + spot
            count = count + jnp.where(spot < here, 1, 0)
    for pad in range(GROUP):
        base[count + pad] = base[jnp.maximum(count - 1, 0)]
        goal[count + pad] = goal[jnp.maximum(count - 1, 0)]
    return count


def cell_parts(arrived, row, cap, depth):
    cell = arrived[pl.ds(row + 4 * cap, 1), :].astype(jnp.int32)
    shift = depth.bit_length() - 1
    return cell >> shift, cell & (depth - 1)


def level_hot(level, depth):
    width = level.shape[1]
    return jnp.where(iota((depth, width), 0) == level, 1.0, 0.0).astype(bf16)


def deposit(count, arrived, places, cap, total):
    columns, depth = total.shape[0] // 4, total.shape[1]
    width = arrived.shape[1]

    def some(step, _):
        loads_of, levels_of = [], []
        for k in range(GROUP):
            index = step * GROUP + k
            row = places[0][index]
            column, level = cell_parts(arrived, row, cap, depth)
            radius = arrived[pl.ds(row, 1), :]
            mass = radius * radius * radius * jnp.where(index < count, 1.0, 0.0)
            loads = [mass] + [mass * arrived[pl.ds(row + c * cap, 1), :] for c in (1, 2, 3)]
            hit = iota((columns, width), 0) == column
            highs, lows = [], []
            for load in loads:
                high = rounded(load)
                highs.append(jnp.where(hit, high, 0.0).astype(bf16))
                lows.append(jnp.where(hit, load - high, 0.0).astype(bf16))
            hot = level_hot(level, depth)
            loads_of += [jnp.concatenate(highs, axis=0), jnp.concatenate(lows, axis=0)]
            levels_of += [hot, hot]
        total[...] += lax.dot_general(
            jnp.concatenate(loads_of, axis=1),
            jnp.concatenate(levels_of, axis=1),
            (((1,), (1,)), ((), ())),
            preferred_element_type=f32,
        )
        return 0

    lax.fori_loop(0, (count + GROUP - 1) // GROUP, some, 0)


def sample(count, arrived, places, cap, table, answers):
    depth = table.shape[1]
    columns = table.shape[0] // 6
    width = arrived.shape[1]

    def some(step, _):
        hots, hits = [], []
        for k in range(GROUP):
            column, level = cell_parts(arrived, places[0][step * GROUP + k], cap, depth)
            hots.append(level_hot(level, depth))
            hits.append(iota((columns, width), 0) == column)
        along = jnp.dot(table[...], jnp.concatenate(hots, axis=1), preferred_element_type=f32)
        for k in range(GROUP):
            goal = places[1][step * GROUP + k]
            part = along[:, k * width : (k + 1) * width]
            for c in range(3):
                value = part[c * columns : (c + 1) * columns]
                value = value + part[(c + 3) * columns : (c + 4) * columns]
                found = jnp.sum(jnp.where(hits[k], value, 0.0), axis=0, keepdims=True)
                answers[pl.ds(goal + c * cap, 1), :] = found
        return 0

    lax.fori_loop(0, (count + GROUP - 1) // GROUP, some, 0)


def first_deposit(nbrick, cap, crossed, total, base, goal):
    chunk = rows_up(5 * cap + 1)
    total[...] = jnp.zeros(total.shape, f32)
    starts = [(3 * b + 1) * chunk for b in range(nbrick)]
    count = list_blocks(crossed, starts, starts, cap, (base, goal))
    deposit(count, crossed, (base, goal), cap, total)


def advance(nbrick, cap, above, below, start, fluid, x_before, x_after, y_before, y_after,
            fluid_next, table, answers_up, answers_down, arrived, answers, total, base, goal):
    chunk = rows_up(5 * cap + 1)
    back = rows_up(3 * cap)
    rows = nbrick * chunk
    arrived[0:rows, :] = above[...]
    arrived[rows:, :] = below[...]
    starts = [i * chunk for i in range(2 * nbrick)]
    ends = [i * back for i in range(2 * nbrick)]
    total[...] = start[...]
    count = list_blocks(arrived, starts, ends, cap, (base, goal))
    deposit(count, arrived, (base, goal), cap, total)

    nx, ny, nz = fluid.shape[1:]
    columns = nx * ny
    deep = iota((ny, nz), 1)
    for x in range(nx):
        volume = total[x * ny : (x + 1) * ny, :]
        for c in range(3):
            here = fluid[c, x]
            near = (x_before[c] if x == 0 else fluid[c, x - 1]) + (
                x_after[c] if x == nx - 1 else fluid[c, x + 1]
            )
            near = near + jnp.concatenate([y_before[c, x : x + 1], here[:-1]], axis=0)
            near = near + jnp.concatenate([here[1:], y_after[c, x : x + 1]], axis=0)
            near = near + jnp.where(deep == 0, 0.0, pltpu.roll(here, 1, 1))
            near = near + jnp.where(deep == nz - 1, 0.0, pltpu.roll(here, nz - 1, 1))
            at = (c + 1) * columns + x * ny
            moved = total[at : at + ny, :] - volume * here
            fresh = here + viscosity * (near - 6.0 * here) + coupling * moved
            fluid_next[c, x] = fresh
            high = fresh.astype(bf16)
            at = c * columns + x * ny
            table[at : at + ny, :] = high
            table[at + 3 * columns : at + 3 * columns + ny, :] = (
                fresh - high.astype(f32)
            ).astype(bf16)
    sample(count, arrived, (base, goal), cap, table, answers)
    answers_up[...] = answers[0 : nbrick * back, :]
    answers_down[...] = answers[nbrick * back :, :]


def last_sample(nbrick, cap, crossed, table, answers, base, goal):
    chunk = rows_up(5 * cap + 1)
    back = rows_up(3 * cap)
    starts = [(3 * b + 1) * chunk for b in range(nbrick)]
    ends = [b * back for b in range(nbrick)]
    count = list_blocks(crossed, starts, ends, cap, (base, goal))
    sample(count, crossed, (base, goal), cap, table, answers)


def relax(nbrick, cap, route_ref, updated, returned, velocity_next, taken):
    back = rows_up(3 * cap)
    for code in range(3 * nbrick):
        taken[code] = 0

    def one(b, _):
        code = route_ref[b]
        spot = taken[code]
        taken[code] = spot + 1
        row = ((code % nbrick) * 3 + code // nbrick) * back + spot
        picked = jnp.concatenate(
            [returned[pl.ds(row + c * cap, 1), :] for c in range(3)], axis=0
        )
        now = updated[b]
        velocity_next[b] = now + relaxation * (picked - now)
        return 0

    lax.fori_loop(0, updated.shape[0], one, 0, unroll=4)


def on_device(
    positions, velocities, radii, cell_of, block_route, ghost_list, tile_home, tile_partner, fluid
):
    nblocks, _, width = positions.shape
    nslab, nbrick = lax.axis_size("slab"), lax.axis_size("brick")
    _, nx, ny, nz = fluid.shape
    columns = nx * ny
    codes = 3 * nbrick
    cap = max(2, (2 * nblocks + codes - 1) // codes)
    chunk, back = rows_up(5 * cap + 1), rows_up(3 * cap)
    per = ghost_list.shape[0] // 2
    tiles = tile_home.shape[0]
    routes = block_route.reshape(-1)

    def struct(*shape, dtype=f32):
        return jax.ShapeDtypeStruct(shape, dtype)

    def shifted(x, axis, step):
        count = lax.axis_size(axis)
        return lax.ppermute(x, axis, [(i, (i + step) % count) for i in range(count)])

    up, down, right, left, x_last, x_first, y_last, y_first = call(
        pack_kernel,
        [struct(per, 8, width)] * 4 + [struct(3, ny, nz)] * 2 + [struct(3, nx, nz)] * 2,
        [SMEM] + [VMEM] * 4,
        [],
        "pack",
    )(ghost_list, positions, velocities, radii, fluid)
    below = shifted(up, "slab", 1)
    above = shifted(down, "slab", -1)
    before = shifted(right, "brick", 1)
    after = shifted(left, "brick", -1)
    x_before = shifted(x_last, "slab", 1)
    x_after = shifted(x_first, "slab", -1)
    y_before = shifted(y_last, "brick", 1)
    y_after = shifted(y_first, "brick", -1)

    lists = [pltpu.SMEM((tiles + UNROLL,), jnp.int32)] * 2
    contact_flops = tiles * width * width * 200
    home_side, sums = call(
        own_contacts,
        [struct(nblocks + 1, 32, width, dtype=bf16), struct(nblocks + 1, 16, width)],
        [SMEM] * 2 + [VMEM] * 3,
        [pltpu.VMEM((nblocks, width, 32), bf16), pltpu.VMEM((nblocks, 16, 2 * width), bf16)] + lists,
        "own_contacts",
        contact_flops,
    )(tile_home, tile_partner, positions, velocities, radii)
    updated, outgoing = call(
        functools.partial(ghost_contacts, nbrick, cap),
        [struct(nblocks, 3, width), struct(nbrick * 3 * chunk, width)],
        [SMEM] * 3 + [VMEM] * 10,
        [
            pltpu.VMEM((4 * per, width, 32), bf16),
            pltpu.VMEM((4 * per, 16, 2 * width), bf16),
            pltpu.VMEM((nblocks + 1, 16, width), f32),
        ]
        + lists
        + [pltpu.SMEM((codes,), jnp.int32)],
        "ghost_contacts",
        contact_flops // 2,
    )(tile_home, tile_partner, routes, below, above, before, after, home_side, sums,
      positions, velocities, radii, cell_of)

    crossed = lax.all_to_all(
        outgoing.reshape(nbrick, 3 * chunk, width), "brick", split_axis=0, concat_axis=0, tiled=True
    )
    from_above = shifted(crossed[:, 0:chunk], "slab", -1).reshape(nbrick * chunk, width)
    from_below = shifted(crossed[:, 2 * chunk :], "slab", 1).reshape(nbrick * chunk, width)
    crossed = crossed.reshape(nbrick * 3 * chunk, width)

    def places(count):
        return [pltpu.SMEM((count + GROUP,), jnp.int32)] * 2

    block_flops = 16 * columns * nz * width
    (started,) = call(
        functools.partial(first_deposit, nbrick, cap),
        [struct(4 * columns, nz)],
        [VMEM],
        places(nbrick * cap),
        "first_deposit",
        block_flops * nblocks // 3,
    )(crossed)
    fluid_next, table, answers_up, answers_down = call(
        functools.partial(advance, nbrick, cap),
        [
            struct(3, nx, ny, nz),
            struct(6 * columns, nz, dtype=bf16),
            struct(nbrick * back, width),
            struct(nbrick * back, width),
        ],
        [VMEM] * 8,
        [
            pltpu.VMEM((2 * nbrick * chunk, width), f32),
            pltpu.VMEM((2 * nbrick * back, width), f32),
            pltpu.VMEM((4 * columns, nz), f32),
        ]
        + places(2 * nbrick * cap),
        "advance",
        block_flops * nblocks,
    )(from_above, from_below, started, fluid, x_before, x_after, y_before, y_after)
    answers_up = shifted(answers_up.reshape(nbrick, back, width), "slab", 1)
    answers_down = shifted(answers_down.reshape(nbrick, back, width), "slab", -1)
    (answers,) = call(
        functools.partial(last_sample, nbrick, cap),
        [struct(nbrick * back, width)],
        [VMEM] * 2,
        places(nbrick * cap),
        "last_sample",
        block_flops * nblocks // 4,
    )(crossed, table)
    answers = jnp.concatenate(
        [answers_up, answers.reshape(nbrick, back, width), answers_down], axis=1
    )
    returned = lax.all_to_all(answers, "brick", split_axis=0, concat_axis=0, tiled=True)
    (velocity_next,) = call(
        functools.partial(relax, nbrick, cap),
        [struct(nblocks, 3, width)],
        [SMEM] + [VMEM] * 2,
        [pltpu.SMEM((codes,), jnp.int32)],
        "relax",
    )(routes, updated, returned.reshape(nbrick * 3 * back, width))
    return (velocity_next, fluid_next)


def solution(mesh):
    placed = (
        P(("slab", "brick"), None, None),
        P(("slab", "brick"), None, None),
        P(("slab", "brick"), None),
        P(("slab", "brick"), None),
        P(("slab", "brick"), None),
        P(("slab", "brick")),
        P(("slab", "brick")),
        P(("slab", "brick")),
        P(None, "slab", "brick", None),
    )
    return jax.shard_map(
        on_device,
        mesh=mesh,
        in_specs=placed,
        out_specs=(P(("slab", "brick"), None, None), P(None, "slab", "brick", None)),
        check_vma=False,
    )
```

```python
import functools
import math

import jax
import jax.numpy as jnp
from jax import lax
from jax.experimental import pallas as pl
from jax.experimental.pallas import tpu as pltpu
from jax.sharding import PartitionSpec as P

stiffness = 0.01
damping = 0.005
viscosity = 0.1
coupling = 0.5
relaxation = 0.5

f32 = jnp.float32
bf16 = jnp.bfloat16
VMEM = pl.BlockSpec(memory_space=pltpu.VMEM)
SMEM = pl.BlockSpec(memory_space=pltpu.SMEM)
UNROLL = 4
GROUP = 4


def rows_up(count):
    return -(-count // 8) * 8


def call(body, outs, ins, scratch, name, flops=0, nbytes=1 << 20):
    return pl.pallas_call(
        body,
        out_shape=outs,
        in_specs=ins,
        out_specs=[VMEM] * len(outs),
        scratch_shapes=scratch,
        name=name,
        compiler_params=pltpu.CompilerParams(vmem_limit_bytes=40 << 20),
        cost_estimate=pl.CostEstimate(flops=flops, bytes_accessed=nbytes, transcendentals=0),
    )


def rounded(x):
    return x.astype(bf16).astype(f32)


def iota(shape, dim):
    return lax.broadcasted_iota(jnp.int32, shape, dim)


planes = 7


def pack_kernel(ghost_ref, pos, vel, rad, fluid, up, down, right, left, x_last, x_first,
                y_tiles, sems):
    count = ghost_ref.shape[0] // 4
    width = rad.shape[1]
    nx, ny, nz = fluid.shape[1:]
    copies = [
        pltpu.make_async_copy(fluid.at[:, nx - 1], x_last, sems.at[0]),
        pltpu.make_async_copy(fluid.at[:, 0], x_first, sems.at[1]),
        pltpu.make_async_copy(fluid.at[:, :, pl.ds(ny - 8, 8)], y_tiles.at[0], sems.at[2]),
        pltpu.make_async_copy(fluid.at[:, :, pl.ds(0, 8)], y_tiles.at[1], sems.at[3]),
    ]
    for copy in copies:
        copy.start()
    for group in range(4):
        i, j = group // 2, group % 2
        slab_to, brick_to = (up if i else down), (right if j else left)
        for g in range(count):
            block = pl.ds(ghost_ref[group * count + g], 1)
            rows = [pos[c, block, :] for c in range(3)] + [rad[block, :]]
            rows = rows + [vel[c, block, :] for c in range(3)]
            for c, row in enumerate(rows):
                at = c * 2 * count + j * count + g
                slab_to[at : at + 1, :] = row
                at = c * 2 * count + i * count + g
                brick_to[at : at + 1, :] = row
    for copy in copies:
        copy.wait()
    for side, brick_to in enumerate((right, left)):
        row = 0 if side else 7
        for c in range(3):
            for x in range(nx):
                for k in range(nz // width):
                    at = planes * 2 * count + (c * nx + x) * (nz // width) + k
                    brick_to[at : at + 1, :] = y_tiles[
                        side, c, x, row : row + 1, k * width : (k + 1) * width
                    ]


def three_parts(x):
    one = rounded(x)
    rest = x - one
    two = rounded(rest)
    return one, two, rest - two


def put_rows(ref, stride, rows):
    count = rows[0].shape[0]
    for k, row in enumerate(rows):
        ref[pl.ds(k, count, stride=stride), :] = row


def pair_factors(place):
    parts = [three_parts(plane) for plane in place]
    own = three_parts(
        place[3] * place[3] - place[0] * place[0] - place[1] * place[1] - place[2] * place[2]
    )
    return [[part[k] for part in parts] for k in range(3)], list(own)


def home_rows(place):
    (one, two, three), own = pair_factors(place)
    ones, zeros = jnp.ones_like(place[0]), jnp.zeros_like(place[0])
    rows = one + one + two + two + one + three
    return [2.0 * row for row in rows] + own + [ones] * 3 + [zeros] * 2


def partner_rows(place):
    (one, two, three), own = pair_factors(place)
    ones, zeros = jnp.ones_like(place[0]), jnp.zeros_like(place[0])
    return one + two + one + two + three + one + [ones] * 3 + own + [zeros] * 2


def value_rows(values):
    highs = [rounded(plane) for plane in values]
    ones, zeros = jnp.ones_like(values[0]), jnp.zeros_like(values[0])
    lows = [plane - high for plane, high in zip(values, highs)]
    return highs + [ones, zeros] + lows + [zeros, zeros]


def prepare_partners(place, speeds, rows, columns, values):
    count, width = place[0].shape
    put_rows(rows, 32, partner_rows(place))
    put_rows(values, 16, value_rows(place[0:3] + speeds))

    def turn(k, _):
        four = rows[pl.ds(pl.multiple_of(k * 128, 128), 128), :]
        columns[k] = jnp.transpose(four).astype(bf16)
        return 0

    lax.fori_loop(0, count // 4, turn, 0, unroll=2)


def list_tiles(home_ref, partner_ref, homes, partners, lower, upper, spare):
    def one(t, count):
        partner = partner_ref[t]
        homes[count] = home_ref[t]
        partners[count] = partner - lower
        return count + jnp.where((partner >= lower) & (partner < upper), 1, 0)

    count = lax.fori_loop(0, home_ref.shape[0], one, 0, unroll=4)
    for pad in range(UNROLL):
        homes[count + pad] = spare
        partners[count + pad] = 0
    return count


def add_tiles(count, homes, partners, home_side, partner_side, values, sums):
    def some(step, _):
        for k in range(UNROLL):
            home = homes[step * UNROLL + k]
            partner = partners[step * UNROLL + k]
            four, place = partner // 4, partner % 4
            factors = home_side[pl.ds(pl.multiple_of(home * 32, 32), 32), :]
            factors = jnp.concatenate(
                [factors * jnp.where(place == i, 1.0, 0.0) for i in range(4)], axis=0
            ).astype(bf16)
            weight = jnp.dot(partner_side[four], factors, preferred_element_type=f32)
            weight = jnp.maximum(weight, 0.0)
            high = weight.astype(bf16)
            low = (weight - high.astype(f32)).astype(bf16)
            value = values[pl.ds(pl.multiple_of(partner * 16, 16), 16), :].astype(bf16)
            at = pl.ds(pl.multiple_of(home * 16, 16), 16)
            sums[at, :] += jnp.dot(
                jnp.concatenate([value, value], axis=1),
                jnp.concatenate([high, low], axis=0),
                preferred_element_type=f32,
            )
        return 0

    lax.fori_loop(0, (count + UNROLL - 1) // UNROLL, some, 0)


def own_contacts(home_ref, partner_ref, pos, vel, rad, home_side, sums,
                 rows, columns, values, homes, partners):
    nblocks, width = rad.shape
    place = [pos[0], pos[1], pos[2], rad[...]]
    put_rows(home_side, 32, home_rows(place))
    prepare_partners(place, [vel[0], vel[1], vel[2]], rows, columns, values)
    home_side[nblocks * 32 :, :] = jnp.zeros((32, width), f32)
    sums[...] = jnp.zeros(sums.shape, f32)
    count = list_tiles(home_ref, partner_ref, homes, partners, 0, nblocks, nblocks)
    add_tiles(count, homes, partners, home_side, columns, values, sums)


def diffuse(fluid, x_before, x_after, before, after, skip, diffused):
    nx, ny, nz = fluid.shape[1:]
    width = before.shape[1]
    deep = iota((ny, nz), 1)

    def face(ref, c, x):
        at = skip + (c * nx + x) * (nz // width)
        return jnp.concatenate(
            [ref[at + k : at + k + 1, :] for k in range(nz // width)], axis=1
        )

    for x in range(nx):
        for c in range(3):
            here = fluid[c, x]
            near = (x_before[c] if x == 0 else fluid[c, x - 1]) + (
                x_after[c] if x == nx - 1 else fluid[c, x + 1]
            )
            near = near + jnp.concatenate([face(before, c, x), here[:-1]], axis=0)
            near = near + jnp.concatenate([here[1:], face(after, c, x)], axis=0)
            near = near + jnp.where(deep == 0, 0.0, pltpu.roll(here, 1, 1))
            near = near + jnp.where(deep == nz - 1, 0.0, pltpu.roll(here, nz - 1, 1))
            diffused[c, x] = here + viscosity * (near - 6.0 * here)


def ghost_contacts(nbrick, cap, home_ref, partner_ref, route_ref, below, above, before, after,
                   x_before, x_after, home_side, own_sums, pos, vel, rad, cell, fluid,
                   updated, outgoing, diffused,
                   rows, columns, values, sums, homes, partners, taken):
    nblocks, width = rad.shape
    per = below.shape[0] // planes
    stacked = [
        jnp.concatenate(
            [ref[c * per : (c + 1) * per, :] for ref in (below, above, before, after)], axis=0
        )
        for c in range(planes)
    ]
    prepare_partners(stacked[0:4], stacked[4:7], rows, columns, values)
    sums[...] = own_sums[...]
    count = list_tiles(home_ref, partner_ref, homes, partners, nblocks, nblocks + 4 * per, nblocks)
    add_tiles(count, homes, partners, home_side, columns, values, sums)
    diffuse(fluid, x_before, x_after, before, after, planes * per, diffused)

    def total(k):
        high = sums[pl.ds(k, nblocks, stride=16), :]
        return high + sums[pl.ds(k + 8, nblocks, stride=16), :]

    weights = total(6)
    radius = rad[...]
    inverse = 1.0 / (radius * radius * radius)
    for c in range(3):
        spring = pos[c] * weights - total(c)
        friction = total(c + 3) - vel[c] * weights
        updated[c] = vel[c] + (stiffness * spring + damping * friction) * inverse

    chunk = rows_up(5 * cap + 1)
    for code in range(3 * nbrick):
        taken[code] = 0

    def send(b, _):
        code = route_ref[b]
        spot = taken[code]
        taken[code] = spot + 1
        row = ((code % nbrick) * 3 + code // nbrick) * chunk + spot
        outgoing[pl.ds(row, 1), :] = rad[pl.ds(b, 1), :]
        for c in range(3):
            outgoing[pl.ds(row + (c + 1) * cap, 1), :] = updated[c, pl.ds(b, 1), :]
        outgoing[pl.ds(row + 4 * cap, 1), :] = cell[pl.ds(b, 1), :].astype(f32)
        return 0

    lax.fori_loop(0, nblocks, send, 0, unroll=4)
    for code in range(3 * nbrick):
        row = ((code % nbrick) * 3 + code // nbrick) * chunk + 5 * cap
        outgoing[row : row + 1, :] = jnp.full((1, width), taken[code], jnp.int32).astype(f32)


def list_blocks(arrived, starts, ends, cap, places):
    base, goal = places
    count = 0
    for start, end in zip(starts, ends):
        here = jnp.max(arrived[start + 5 * cap : start + 5 * cap + 1, :]).astype(jnp.int32)
        for spot in range(cap):
            base[count] = start + spot
            goal[count] = end + spot
            count = count + jnp.where(spot < here, 1, 0)
    for pad in range(GROUP):
        base[count + pad] = base[jnp.maximum(count - 1, 0)]
        goal[count + pad] = goal[jnp.maximum(count - 1, 0)]
    return count


def cell_parts(arrived, row, cap, depth):
    cell = arrived[pl.ds(row + 4 * cap, 1), :].astype(jnp.int32)
    shift = depth.bit_length() - 1
    return cell >> shift, cell & (depth - 1)


def level_hot(level, depth):
    width = level.shape[1]
    return jnp.where(iota((depth, width), 0) == level, 1.0, 0.0).astype(bf16)


def in_pairs(steps, stage):
    def two(pair, _):
        stage(2 * pair, 0)

        @pl.when(2 * pair + 1 < steps)
        def _():
            stage(2 * pair + 1, 1)

        return 0

    lax.fori_loop(0, (steps + 1) // 2, two, 0)


def deposit(count, arrived, places, cap, total, buffers):
    columns, depth = total.shape[0] // 4, total.shape[1]
    width = arrived.shape[1]
    steps = (count + GROUP - 1) // GROUP

    def build(step, loads_ref, hots_ref):
        for k in range(GROUP):
            index = step * GROUP + k
            row = places[0][jnp.minimum(index, jnp.maximum(count - 1, 0))]
            column, level = cell_parts(arrived, row, cap, depth)
            radius = arrived[pl.ds(row, 1), :]
            mass = radius * radius * radius * jnp.where(index < count, 1.0, 0.0)
            loads = [mass] + [mass * arrived[pl.ds(row + c * cap, 1), :] for c in (1, 2, 3)]
            hit = iota((columns, width), 0) == column
            high_at = slice(k * width, (k + 1) * width)
            low_at = slice((k + GROUP) * width, (k + GROUP + 1) * width)
            for c, load in enumerate(loads):
                high = rounded(load)
                at = slice(c * columns, (c + 1) * columns)
                loads_ref[at, high_at] = jnp.where(hit, high, 0.0).astype(bf16)
                loads_ref[at, low_at] = jnp.where(hit, load - high, 0.0).astype(bf16)
            hots_ref[:, high_at] = level_hot(level, depth)

    def stage(step, even):
        loads_ref, hots_ref = buffers[2 * even : 2 * even + 2]
        hots = hots_ref[...]
        total[...] += lax.dot_general(
            loads_ref[...],
            jnp.concatenate([hots, hots], axis=1),
            (((1,), (1,)), ((), ())),
            preferred_element_type=f32,
        )
        build(step + 1, *buffers[2 - 2 * even : 4 - 2 * even])

    build(0, *buffers[0:2])
    in_pairs(steps, stage)


def deposit_buffers(columns, depth, width):
    one = [
        pltpu.VMEM((4 * columns, 2 * GROUP * width), bf16),
        pltpu.VMEM((depth, GROUP * width), bf16),
    ]
    return one + one


def sample(count, arrived, places, cap, table, answers, buffers):
    depth = table.shape[1]
    columns = table.shape[0] // 6
    width = arrived.shape[1]
    steps = (count + GROUP - 1) // GROUP

    def spot(step, k):
        return jnp.minimum(step * GROUP + k, jnp.maximum(count - 1, 0))

    def build(step, hots_ref):
        for k in range(GROUP):
            _, level = cell_parts(arrived, places[0][spot(step, k)], cap, depth)
            hots_ref[:, k * width : (k + 1) * width] = level_hot(level, depth)

    def gather(step, along_ref):
        for k in range(GROUP):
            column, _ = cell_parts(arrived, places[0][spot(step, k)], cap, depth)
            hit = iota((columns, width), 0) == column
            goal = places[1][spot(step, k)]
            for c in range(3):
                at = slice(k * width, (k + 1) * width)
                value = along_ref[c * columns : (c + 1) * columns, at]
                value = value + along_ref[(c + 3) * columns : (c + 4) * columns, at]
                found = jnp.sum(jnp.where(hit, value, 0.0), axis=0, keepdims=True)
                answers[pl.ds(goal + c * cap, 1), :] = found

    def stage(step, even):
        hots_ref, along_ref = buffers[2 * even : 2 * even + 2]
        next_hots, last_along = buffers[2 - 2 * even : 4 - 2 * even]
        along_ref[...] = jnp.dot(table[...], hots_ref[...], preferred_element_type=f32)
        build(step + 1, next_hots)
        gather(jnp.maximum(step - 1, 0), last_along)

    build(0, buffers[0])
    in_pairs(steps, stage)

    @pl.when((steps > 0) & (steps % 2 == 1))
    def _():
        gather(steps - 1, buffers[1])

    @pl.when((steps > 0) & (steps % 2 == 0))
    def _():
        gather(steps - 1, buffers[3])


def sample_buffers(columns, depth, width):
    one = [
        pltpu.VMEM((depth, GROUP * width), bf16),
        pltpu.VMEM((6 * columns, GROUP * width), f32),
    ]
    return one + one


def first_deposit(nbrick, cap, crossed, total, base, goal, *buffers):
    chunk = rows_up(5 * cap + 1)
    total[...] = jnp.zeros(total.shape, f32)
    starts = [(3 * b + 1) * chunk for b in range(nbrick)]
    count = list_blocks(crossed, starts, starts, cap, (base, goal))
    deposit(count, crossed, (base, goal), cap, total, buffers)


def advance(nbrick, cap, above, below, start, fluid, diffused, fluid_next, table, answers_up,
            answers_down, arrived, answers, total, base, goal, *buffers):
    chunk = rows_up(5 * cap + 1)
    back = rows_up(3 * cap)
    rows = nbrick * chunk
    arrived[0:rows, :] = above[...]
    arrived[rows:, :] = below[...]
    starts = [i * chunk for i in range(2 * nbrick)]
    ends = [i * back for i in range(2 * nbrick)]
    total[...] = start[...]
    count = list_blocks(arrived, starts, ends, cap, (base, goal))
    deposit(count, arrived, (base, goal), cap, total, buffers[0:4])

    nx, ny, nz = fluid.shape[1:]
    columns = nx * ny
    for x in range(nx):
        volume = total[x * ny : (x + 1) * ny, :]
        for c in range(3):
            at = (c + 1) * columns + x * ny
            moved = total[at : at + ny, :] - volume * fluid[c, x]
            fresh = diffused[c, x] + coupling * moved
            fluid_next[c, x] = fresh
            high = fresh.astype(bf16)
            at = c * columns + x * ny
            table[at : at + ny, :] = high
            table[at + 3 * columns : at + 3 * columns + ny, :] = (
                fresh - high.astype(f32)
            ).astype(bf16)
    sample(count, arrived, (base, goal), cap, table, answers, buffers[4:8])
    answers_up[...] = answers[0 : nbrick * back, :]
    answers_down[...] = answers[nbrick * back :, :]


def last_sample(nbrick, cap, crossed, table, answers, base, goal, *buffers):
    chunk = rows_up(5 * cap + 1)
    back = rows_up(3 * cap)
    starts = [(3 * b + 1) * chunk for b in range(nbrick)]
    ends = [b * back for b in range(nbrick)]
    count = list_blocks(crossed, starts, ends, cap, (base, goal))
    sample(count, crossed, (base, goal), cap, table, answers, buffers)


def relax(nbrick, cap, route_ref, updated, returned, velocity_next, picked, taken):
    back = rows_up(3 * cap)
    for code in range(3 * nbrick):
        taken[code] = 0

    def one(b, _):
        code = route_ref[b]
        spot = taken[code]
        taken[code] = spot + 1
        row = ((code % nbrick) * 3 + code // nbrick) * back + spot
        for c in range(3):
            picked[c, pl.ds(b, 1), :] = returned[pl.ds(row + c * cap, 1), :]
        return 0

    lax.fori_loop(0, updated.shape[1], one, 0, unroll=4)
    now = updated[...]
    velocity_next[...] = now + relaxation * (picked[...] - now)


def on_device(
    positions, velocities, radii, cell_of, block_route, ghost_list, tile_home, tile_partner, fluid
):
    nblocks, _, width = positions.shape
    nbrick = lax.axis_size("brick")
    _, nx, ny, nz = fluid.shape
    columns = nx * ny
    codes = 3 * nbrick
    cap = max(2, (2 * nblocks + codes - 1) // codes)
    chunk, back = rows_up(5 * cap + 1), rows_up(3 * cap)
    per = ghost_list.shape[0] // 2
    tiles = tile_home.shape[0]
    routes = block_route.reshape(-1)
    positions = jnp.transpose(positions, (1, 0, 2))
    velocities = jnp.transpose(velocities, (1, 0, 2))

    def struct(*shape, dtype=f32):
        return jax.ShapeDtypeStruct(shape, dtype)

    def shifted(x, axis, step):
        count = lax.axis_size(axis)
        return lax.ppermute(x, axis, [(i, (i + step) % count) for i in range(count)])

    face_rows = 3 * nx * (nz // width)
    up, down, right, left, x_last, x_first = call(
        pack_kernel,
        [struct(planes * per, width)] * 2
        + [struct(planes * per + face_rows, width)] * 2
        + [struct(3, ny, nz)] * 2,
        [SMEM] + [VMEM] * 3 + [pl.BlockSpec(memory_space=pl.ANY)],
        [pltpu.VMEM((2, 3, nx, 8, nz), f32), pltpu.SemaphoreType.DMA((4,))],
        "pack",
    )(ghost_list, positions, velocities, radii, fluid)
    below = shifted(up, "slab", 1)
    above = shifted(down, "slab", -1)
    before = shifted(right, "brick", 1)
    after = shifted(left, "brick", -1)
    x_before = shifted(x_last, "slab", 1)
    x_after = shifted(x_first, "slab", -1)

    def sides(count):
        return [
            pltpu.VMEM((count * 32, width), f32),
            pltpu.VMEM((count // 4, width, 128), bf16),
            pltpu.VMEM((count * 16, width), f32),
        ]

    lists = [pltpu.SMEM((tiles + UNROLL,), jnp.int32)] * 2
    contact_flops = tiles * width * width * 200
    home_side, sums = call(
        own_contacts,
        [struct((nblocks + 1) * 32, width), struct((nblocks + 1) * 16, width)],
        [SMEM] * 2 + [VMEM] * 3,
        sides(nblocks) + lists,
        "own_contacts",
        contact_flops,
    )(tile_home, tile_partner, positions, velocities, radii)
    updated, outgoing, diffused = call(
        functools.partial(ghost_contacts, nbrick, cap),
        [struct(3, nblocks, width), struct(nbrick * 3 * chunk, width), struct(3, nx, ny, nz)],
        [SMEM] * 3 + [VMEM] * 13,
        sides(4 * per)
        + [pltpu.VMEM(((nblocks + 1) * 16, width), f32)]
        + lists
        + [pltpu.SMEM((codes,), jnp.int32)],
        "ghost_contacts",
        contact_flops // 2,
    )(tile_home, tile_partner, routes, below, above, before, after, x_before, x_after,
      home_side, sums, positions, velocities, radii, cell_of, fluid)

    crossed = lax.all_to_all(
        outgoing.reshape(nbrick, 3 * chunk, width), "brick", split_axis=0, concat_axis=0, tiled=True
    )
    from_above = shifted(crossed[:, 0:chunk], "slab", -1).reshape(nbrick * chunk, width)
    from_below = shifted(crossed[:, 2 * chunk :], "slab", 1).reshape(nbrick * chunk, width)
    crossed = crossed.reshape(nbrick * 3 * chunk, width)

    def places(count):
        return [pltpu.SMEM((count + GROUP,), jnp.int32)] * 2

    block_flops = 16 * columns * nz * width
    (started,) = call(
        functools.partial(first_deposit, nbrick, cap),
        [struct(4 * columns, nz)],
        [VMEM],
        places(nbrick * cap) + deposit_buffers(columns, nz, width),
        "first_deposit",
        block_flops * nblocks // 3,
    )(crossed)
    fluid_next, table, answers_up, answers_down = call(
        functools.partial(advance, nbrick, cap),
        [
            struct(3, nx, ny, nz),
            struct(6 * columns, nz, dtype=bf16),
            struct(nbrick * back, width),
            struct(nbrick * back, width),
        ],
        [VMEM] * 5,
        [
            pltpu.VMEM((2 * nbrick * chunk, width), f32),
            pltpu.VMEM((2 * nbrick * back, width), f32),
            pltpu.VMEM((4 * columns, nz), f32),
        ]
        + places(2 * nbrick * cap)
        + deposit_buffers(columns, nz, width)
        + sample_buffers(columns, nz, width),
        "advance",
        block_flops * nblocks,
    )(from_above, from_below, started, fluid, diffused)
    answers_up = shifted(answers_up.reshape(nbrick, back, width), "slab", 1)
    answers_down = shifted(answers_down.reshape(nbrick, back, width), "slab", -1)
    (answers,) = call(
        functools.partial(last_sample, nbrick, cap),
        [struct(nbrick * back, width)],
        [VMEM] * 2,
        places(nbrick * cap) + sample_buffers(columns, nz, width),
        "last_sample",
        block_flops * nblocks // 4,
    )(crossed, table)
    answers = jnp.concatenate(
        [answers_up, answers.reshape(nbrick, back, width), answers_down], axis=1
    )
    returned = lax.all_to_all(answers, "brick", split_axis=0, concat_axis=0, tiled=True)
    (velocity_next,) = call(
        functools.partial(relax, nbrick, cap),
        [struct(3, nblocks, width)],
        [SMEM] + [VMEM] * 2,
        [pltpu.VMEM((3, nblocks, width), f32), pltpu.SMEM((codes,), jnp.int32)],
        "relax",
    )(routes, updated, returned.reshape(nbrick * 3 * back, width))
    return (jnp.transpose(velocity_next, (1, 0, 2)), fluid_next)


def solution(mesh):
    placed = (
        P(("slab", "brick"), None, None),
        P(("slab", "brick"), None, None),
        P(("slab", "brick"), None),
        P(("slab", "brick"), None),
        P(("slab", "brick"), None),
        P(("slab", "brick")),
        P(("slab", "brick")),
        P(("slab", "brick")),
        P(None, "slab", "brick", None),
    )
    return jax.shard_map(
        on_device,
        mesh=mesh,
        in_specs=placed,
        out_specs=(P(("slab", "brick"), None, None), P(None, "slab", "brick", None)),
        check_vma=False,
    )
```

```python
import functools
import math

import jax
import jax.numpy as jnp
from jax import lax
from jax.experimental import pallas as pl
from jax.experimental.pallas import tpu as pltpu
from jax.sharding import PartitionSpec as P

stiffness = 0.01
damping = 0.005
viscosity = 0.1
coupling = 0.5
relaxation = 0.5

f32 = jnp.float32
bf16 = jnp.bfloat16
VMEM = pl.BlockSpec(memory_space=pltpu.VMEM)
HBM = pl.BlockSpec(memory_space=pltpu.HBM)
UNROLL = 8
GROUP = 4


def rows_up(count):
    return -(-count // 8) * 8


def call(body, outs, ins, scratch, name, flops=0, nbytes=1 << 20, places=None):
    return pl.pallas_call(
        body,
        out_shape=outs,
        in_specs=ins,
        out_specs=places or [VMEM] * len(outs),
        scratch_shapes=scratch,
        name=name,
        compiler_params=pltpu.CompilerParams(vmem_limit_bytes=40 << 20),
        cost_estimate=pl.CostEstimate(flops=flops, bytes_accessed=nbytes, transcendentals=0),
    )


def rounded(x):
    return x.astype(bf16).astype(f32)


def iota(shape, dim):
    return lax.broadcasted_iota(jnp.int32, shape, dim)


planes = 7


def copy_all(pairs, sems):
    copies = [pltpu.make_async_copy(*pair, sems.at[i]) for i, pair in enumerate(pairs)]
    for copy in copies:
        copy.start()
    return copies


def wait_all(copies):
    for copy in copies:
        copy.wait()


def pack_kernel(ghost_list, pos, vel, rad, cell, fluid, up, down, right, left, x_last, x_first,
                state, ghost_ref, cells, y_tiles, sems):
    count = ghost_ref.shape[0] // 4
    width = rad.shape[1]
    nx, ny, nz = fluid.shape[1:]
    particles = copy_all(
        [
            (ghost_list, ghost_ref),
            (pos, state.at[0:3]),
            (rad, state.at[3]),
            (vel, state.at[4:7]),
            (cell, cells),
        ],
        sems,
    )
    faces = copy_all(
        [
            (fluid.at[:, :, pl.ds(ny - 8, 8)], y_tiles.at[0]),
            (fluid.at[:, :, pl.ds(0, 8)], y_tiles.at[1]),
            (fluid.at[:, nx - 1], x_last),
            (fluid.at[:, 0], x_first),
        ],
        sems.at[5:9],
    )
    wait_all(particles)
    state[planes] = cells[...].astype(f32)
    for group in range(4):
        i, j = group // 2, group % 2
        slab_to, brick_to = (up if i else down), (right if j else left)
        for g in range(count):
            block = pl.ds(ghost_ref[group * count + g], 1)
            for c in range(planes):
                row = state[c, block, :]
                at = c * 2 * count + j * count + g
                slab_to[at : at + 1, :] = row
                at = c * 2 * count + i * count + g
                brick_to[at : at + 1, :] = row
    wait_all(faces)
    for side, brick_to in enumerate((right, left)):
        row = 0 if side else 7
        for c in range(3):
            for x in range(nx):
                for k in range(nz // width):
                    at = planes * 2 * count + (c * nx + x) * (nz // width) + k
                    brick_to[at : at + 1, :] = y_tiles[
                        side, c, x, row : row + 1, k * width : (k + 1) * width
                    ]


def three_parts(x):
    one = rounded(x)
    rest = x - one
    two = rounded(rest)
    return one, two, rest - two


def put_rows(ref, stride, rows):
    count = rows[0].shape[0]
    for k, row in enumerate(rows):
        ref[pl.ds(k, count, stride=stride), :] = row


def pair_factors(place):
    parts = [three_parts(plane) for plane in place]
    own = three_parts(
        place[3] * place[3] - place[0] * place[0] - place[1] * place[1] - place[2] * place[2]
    )
    return [[part[k] for part in parts] for k in range(3)], list(own)


def home_rows(place):
    (one, two, three), own = pair_factors(place)
    ones, zeros = jnp.ones_like(place[0]), jnp.zeros_like(place[0])
    rows = one + one + two + two + one + three
    return [2.0 * row for row in rows] + own + [ones] * 3 + [zeros] * 2


def partner_rows(place):
    (one, two, three), own = pair_factors(place)
    ones, zeros = jnp.ones_like(place[0]), jnp.zeros_like(place[0])
    return one + two + one + two + three + one + [ones] * 3 + own + [zeros] * 2


def value_rows(values):
    highs = [rounded(plane) for plane in values]
    ones, zeros = jnp.ones_like(values[0]), jnp.zeros_like(values[0])
    lows = [plane - high for plane, high in zip(values, highs)]
    return highs + [ones, zeros] + lows + [zeros, zeros]


def prepare_partners(place, speeds, rows, columns, values):
    count, width = place[0].shape
    put_rows(rows, 32, partner_rows(place))
    put_rows(values, 16, value_rows(place[0:3] + speeds))

    def turn(b, _):
        block = rows[pl.ds(pl.multiple_of(b * 32, 32), 32), :]
        columns[b] = jnp.transpose(block).astype(bf16)
        return 0

    lax.fori_loop(0, count, turn, 0, unroll=4)


def list_tiles(home_ref, partner_ref, homes, partners, lower, upper, spare):
    def one(t, count):
        partner = partner_ref[t]
        homes[count] = home_ref[t]
        partners[count] = partner - lower
        return count + jnp.where((partner >= lower) & (partner < upper), 1, 0)

    count = lax.fori_loop(0, home_ref.shape[0], one, 0, unroll=4)
    for pad in range(UNROLL):
        homes[count + pad] = spare
        partners[count + pad] = 0
    return count


def add_tiles(count, homes, partners, home_side, partner_side, values, sums):
    def some(step, _):
        for k in range(UNROLL):
            home = homes[step * UNROLL + k]
            partner = partners[step * UNROLL + k]
            factors = home_side[pl.ds(pl.multiple_of(home * 32, 32), 32), :].astype(bf16)
            weight = jnp.dot(partner_side[partner], factors, preferred_element_type=f32)
            weight = jnp.maximum(weight, 0.0)
            high = weight.astype(bf16)
            low = (weight - high.astype(f32)).astype(bf16)
            value = values[pl.ds(pl.multiple_of(partner * 16, 16), 16), :].astype(bf16)
            at = pl.ds(pl.multiple_of(home * 16, 16), 16)
            sums[at, :] += jnp.dot(
                jnp.concatenate([value, value], axis=1),
                jnp.concatenate([high, low], axis=0),
                preferred_element_type=f32,
            )
        return 0

    lax.fori_loop(0, (count + UNROLL - 1) // UNROLL, some, 0)


def own_contacts(home_list, partner_list, state, home_side, sums,
                 rows, columns, values, homes, partners, home_ref, partner_ref, sems):
    nblocks, width = state.shape[1:]
    copies = copy_all([(home_list, home_ref), (partner_list, partner_ref)], sems)
    place = [state[c] for c in range(4)]
    put_rows(home_side, 32, home_rows(place))
    prepare_partners(place, [state[c] for c in (4, 5, 6)], rows, columns, values)
    home_side[nblocks * 32 :, :] = jnp.zeros((32, width), f32)
    sums[...] = jnp.zeros(sums.shape, f32)
    wait_all(copies)
    count = list_tiles(home_ref, partner_ref, homes, partners, 0, nblocks, nblocks)
    add_tiles(count, homes, partners, home_side, columns, values, sums)


def diffuse(fluid, x_before, x_after, before, after, skip, diffused):
    nx, ny, nz = fluid.shape[1:]
    width = before.shape[1]
    deep = iota((ny, nz), 1)

    def face(ref, c, x):
        at = skip + (c * nx + x) * (nz // width)
        return jnp.concatenate(
            [ref[at + k : at + k + 1, :] for k in range(nz // width)], axis=1
        )

    for x in range(nx):
        for c in range(3):
            here = fluid[c, x]
            near = (x_before[c] if x == 0 else fluid[c, x - 1]) + (
                x_after[c] if x == nx - 1 else fluid[c, x + 1]
            )
            near = near + jnp.concatenate([face(before, c, x), here[:-1]], axis=0)
            near = near + jnp.concatenate([here[1:], face(after, c, x)], axis=0)
            near = near + jnp.where(deep == 0, 0.0, pltpu.roll(here, 1, 1))
            near = near + jnp.where(deep == nz - 1, 0.0, pltpu.roll(here, nz - 1, 1))
            diffused[c, x] = here + viscosity * (near - 6.0 * here)


def ghost_contacts(nbrick, cap, home_list, partner_list, routes, below, above, before, after,
                   x_before, x_after, home_side, own_sums, state, fluid,
                   updated, outgoing, diffused,
                   rows, columns, values, sums, homes, partners, taken,
                   home_ref, partner_ref, route_ref, flow, sems):
    nblocks, width = state.shape[1:]
    per = below.shape[0] // planes
    copies = copy_all(
        [
            (home_list, home_ref),
            (partner_list, partner_ref),
            (routes, route_ref),
            (fluid, flow),
        ],
        sems,
    )
    stacked = [
        jnp.concatenate(
            [ref[c * per : (c + 1) * per, :] for ref in (below, above, before, after)], axis=0
        )
        for c in range(planes)
    ]
    prepare_partners(stacked[0:4], stacked[4:7], rows, columns, values)
    sums[...] = own_sums[...]
    wait_all(copies)
    count = list_tiles(home_ref, partner_ref, homes, partners, nblocks, nblocks + 4 * per, nblocks)
    add_tiles(count, homes, partners, home_side, columns, values, sums)
    diffuse(flow, x_before, x_after, before, after, planes * per, diffused)

    def total(k):
        high = sums[pl.ds(k, nblocks, stride=16), :]
        return high + sums[pl.ds(k + 8, nblocks, stride=16), :]

    weights = total(6)
    radius = state[3]
    inverse = 1.0 / (radius * radius * radius)
    for c in range(3):
        speed = state[c + 4]
        spring = state[c] * weights - total(c)
        friction = total(c + 3) - speed * weights
        updated[c] = speed + (stiffness * spring + damping * friction) * inverse

    chunk = rows_up(5 * cap + 1)
    for code in range(3 * nbrick):
        taken[code] = 0

    def send(b, _):
        code = route_ref[b]
        spot = taken[code]
        taken[code] = spot + 1
        row = ((code % nbrick) * 3 + code // nbrick) * chunk + spot
        outgoing[pl.ds(row, 1), :] = state[3, pl.ds(b, 1), :]
        for c in range(3):
            outgoing[pl.ds(row + (c + 1) * cap, 1), :] = updated[c, pl.ds(b, 1), :]
        outgoing[pl.ds(row + 4 * cap, 1), :] = state[planes, pl.ds(b, 1), :]
        return 0

    lax.fori_loop(0, nblocks, send, 0, unroll=4)
    for code in range(3 * nbrick):
        row = ((code % nbrick) * 3 + code // nbrick) * chunk + 5 * cap
        outgoing[row : row + 1, :] = jnp.full((1, width), taken[code], jnp.int32).astype(f32)


def list_blocks(arrived, starts, ends, cap, places):
    base, goal = places
    count = 0
    for start, end in zip(starts, ends):
        here = jnp.max(arrived[start + 5 * cap : start + 5 * cap + 1, :]).astype(jnp.int32)
        for spot in range(cap):
            base[count] = start + spot
            goal[count] = end + spot
            count = count + jnp.where(spot < here, 1, 0)
    for pad in range(GROUP):
        base[count + pad] = base[jnp.maximum(count - 1, 0)]
        goal[count + pad] = goal[jnp.maximum(count - 1, 0)]
    return count


def cell_parts(arrived, row, cap, depth):
    cell = arrived[pl.ds(row + 4 * cap, 1), :].astype(jnp.int32)
    shift = depth.bit_length() - 1
    return cell >> shift, cell & (depth - 1)


def level_hot(level, depth):
    width = level.shape[1]
    return jnp.where(iota((depth, width), 0) == level, 1.0, 0.0).astype(bf16)


def deposit(count, arrived, places, cap, total):
    columns, depth = total.shape[0] // 4, total.shape[1]
    width = arrived.shape[1]

    def some(step, _):
        loads_of, levels_of = [], []
        for k in range(GROUP):
            index = step * GROUP + k
            row = places[0][index]
            column, level = cell_parts(arrived, row, cap, depth)
            radius = arrived[pl.ds(row, 1), :]
            mass = radius * radius * radius * jnp.where(index < count, 1.0, 0.0)
            loads = [mass] + [mass * arrived[pl.ds(row + c * cap, 1), :] for c in (1, 2, 3)]
            hit = iota((columns, width), 0) == column
            highs, lows = [], []
            for load in loads:
                high = rounded(load)
                highs.append(jnp.where(hit, high, 0.0).astype(bf16))
                lows.append(jnp.where(hit, load - high, 0.0).astype(bf16))
            hot = level_hot(level, depth)
            loads_of += [jnp.concatenate(highs, axis=0), jnp.concatenate(lows, axis=0)]
            levels_of += [hot, hot]
        total[...] += lax.dot_general(
            jnp.concatenate(loads_of, axis=1),
            jnp.concatenate(levels_of, axis=1),
            (((1,), (1,)), ((), ())),
            preferred_element_type=f32,
        )
        return 0

    lax.fori_loop(0, (count + GROUP - 1) // GROUP, some, 0)


def sample(count, arrived, places, cap, table, answers):
    depth = table.shape[1]
    columns = table.shape[0] // 6
    width = arrived.shape[1]

    def some(step, _):
        hots, hits = [], []
        for k in range(GROUP):
            column, level = cell_parts(arrived, places[0][step * GROUP + k], cap, depth)
            hots.append(level_hot(level, depth))
            hits.append(iota((columns, width), 0) == column)
        along = jnp.dot(table[...], jnp.concatenate(hots, axis=1), preferred_element_type=f32)
        for k in range(GROUP):
            goal = places[1][step * GROUP + k]
            part = along[:, k * width : (k + 1) * width]
            for c in range(3):
                value = part[c * columns : (c + 1) * columns]
                value = value + part[(c + 3) * columns : (c + 4) * columns]
                found = jnp.sum(jnp.where(hits[k], value, 0.0), axis=0, keepdims=True)
                answers[pl.ds(goal + c * cap, 1), :] = found
        return 0

    lax.fori_loop(0, (count + GROUP - 1) // GROUP, some, 0)


def first_deposit(nbrick, cap, crossed, total, base, goal):
    chunk = rows_up(5 * cap + 1)
    total[...] = jnp.zeros(total.shape, f32)
    starts = [(3 * b + 1) * chunk for b in range(nbrick)]
    count = list_blocks(crossed, starts, starts, cap, (base, goal))
    deposit(count, crossed, (base, goal), cap, total)


def advance(nbrick, cap, above, below, start, fluid, diffused, fluid_next, table, answers_up,
            answers_down, arrived, answers, total, flow, fresh_flow, base, goal, sems):
    reading = pltpu.make_async_copy(fluid, flow, sems.at[0])
    reading.start()
    chunk = rows_up(5 * cap + 1)
    back = rows_up(3 * cap)
    rows = nbrick * chunk
    arrived[0:rows, :] = above[...]
    arrived[rows:, :] = below[...]
    starts = [i * chunk for i in range(2 * nbrick)]
    ends = [i * back for i in range(2 * nbrick)]
    total[...] = start[...]
    count = list_blocks(arrived, starts, ends, cap, (base, goal))
    deposit(count, arrived, (base, goal), cap, total)
    reading.wait()

    nx, ny, nz = flow.shape[1:]
    columns = nx * ny
    for x in range(nx):
        volume = total[x * ny : (x + 1) * ny, :]
        for c in range(3):
            at = (c + 1) * columns + x * ny
            moved = total[at : at + ny, :] - volume * flow[c, x]
            fresh = diffused[c, x] + coupling * moved
            fresh_flow[c, x] = fresh
            high = fresh.astype(bf16)
            at = c * columns + x * ny
            table[at : at + ny, :] = high
            table[at + 3 * columns : at + 3 * columns + ny, :] = (
                fresh - high.astype(f32)
            ).astype(bf16)
    writing = pltpu.make_async_copy(fresh_flow, fluid_next, sems.at[1])
    writing.start()
    sample(count, arrived, (base, goal), cap, table, answers)
    answers_up[...] = answers[0 : nbrick * back, :]
    answers_down[...] = answers[nbrick * back :, :]
    writing.wait()


def last_sample(nbrick, cap, crossed, table, answers, base, goal):
    chunk = rows_up(5 * cap + 1)
    back = rows_up(3 * cap)
    starts = [(3 * b + 1) * chunk for b in range(nbrick)]
    ends = [b * back for b in range(nbrick)]
    count = list_blocks(crossed, starts, ends, cap, (base, goal))
    sample(count, crossed, (base, goal), cap, table, answers)


def relax(nbrick, cap, routes, updated, returned, velocity_next, picked, taken, route_ref, sems):
    wait_all(copy_all([(routes, route_ref)], sems))
    back = rows_up(3 * cap)
    for code in range(3 * nbrick):
        taken[code] = 0

    def one(b, _):
        code = route_ref[b]
        spot = taken[code]
        taken[code] = spot + 1
        row = ((code % nbrick) * 3 + code // nbrick) * back + spot
        for c in range(3):
            picked[c, pl.ds(b, 1), :] = returned[pl.ds(row + c * cap, 1), :]
        return 0

    lax.fori_loop(0, updated.shape[1], one, 0, unroll=4)
    now = updated[...]
    velocity_next[...] = now + relaxation * (picked[...] - now)


def on_device(
    positions, velocities, radii, cell_of, block_route, ghost_list, tile_home, tile_partner, fluid
):
    nblocks, _, width = positions.shape
    nbrick = lax.axis_size("brick")
    _, nx, ny, nz = fluid.shape
    columns = nx * ny
    codes = 3 * nbrick
    cap = max(2, (2 * nblocks + codes - 1) // codes)
    chunk, back = rows_up(5 * cap + 1), rows_up(3 * cap)
    per = ghost_list.shape[0] // 2
    tiles = tile_home.shape[0]
    routes = block_route.reshape(-1)
    positions = jnp.transpose(positions, (1, 0, 2))
    velocities = jnp.transpose(velocities, (1, 0, 2))

    def struct(*shape, dtype=f32):
        return jax.ShapeDtypeStruct(shape, dtype)

    def shifted(x, axis, step):
        count = lax.axis_size(axis)
        return lax.ppermute(x, axis, [(i, (i + step) % count) for i in range(count)])

    def ints(count):
        return pltpu.SMEM((count,), jnp.int32)

    face_rows = 3 * nx * (nz // width)
    up, down, right, left, x_last, x_first, state = call(
        pack_kernel,
        [struct(planes * per, width)] * 2
        + [struct(planes * per + face_rows, width)] * 2
        + [struct(3, ny, nz)] * 2
        + [struct(planes + 1, nblocks, width)],
        [HBM] * 6,
        [
            ints(2 * per),
            pltpu.VMEM((nblocks, width), jnp.int32),
            pltpu.VMEM((2, 3, nx, 8, nz), f32),
            pltpu.SemaphoreType.DMA((9,)),
        ],
        "pack",
    )(ghost_list, positions, velocities, radii, cell_of, fluid)
    below = shifted(up, "slab", 1)
    above = shifted(down, "slab", -1)
    before = shifted(right, "brick", 1)
    after = shifted(left, "brick", -1)
    x_before = shifted(x_last, "slab", 1)
    x_after = shifted(x_first, "slab", -1)

    def sides(count):
        return [
            pltpu.VMEM((count * 32, width), f32),
            pltpu.VMEM((count, width, 32), bf16),
            pltpu.VMEM((count * 16, width), f32),
        ]

    lists = [ints(tiles + UNROLL)] * 2
    contact_flops = tiles * width * width * 200
    home_side, sums = call(
        own_contacts,
        [struct((nblocks + 1) * 32, width), struct((nblocks + 1) * 16, width)],
        [HBM] * 2 + [VMEM],
        sides(nblocks) + lists + [ints(tiles)] * 2 + [pltpu.SemaphoreType.DMA((2,))],
        "own_contacts",
        contact_flops,
    )(tile_home, tile_partner, state)
    updated, outgoing, diffused = call(
        functools.partial(ghost_contacts, nbrick, cap),
        [struct(3, nblocks, width), struct(nbrick * 3 * chunk, width), struct(3, nx, ny, nz)],
        [HBM] * 3 + [VMEM] * 9 + [HBM],
        sides(4 * per)
        + [pltpu.VMEM(((nblocks + 1) * 16, width), f32)]
        + lists
        + [ints(codes), ints(tiles), ints(tiles), ints(nblocks)]
        + [pltpu.VMEM((3, nx, ny, nz), f32), pltpu.SemaphoreType.DMA((4,))],
        "ghost_contacts",
        contact_flops // 2,
    )(tile_home, tile_partner, routes, below, above, before, after, x_before, x_after,
      home_side, sums, state, fluid)

    crossed = lax.all_to_all(
        outgoing.reshape(nbrick, 3 * chunk, width), "brick", split_axis=0, concat_axis=0, tiled=True
    )
    from_above = shifted(crossed[:, 0:chunk], "slab", -1).reshape(nbrick * chunk, width)
    from_below = shifted(crossed[:, 2 * chunk :], "slab", 1).reshape(nbrick * chunk, width)
    crossed = crossed.reshape(nbrick * 3 * chunk, width)

    def places(count):
        return [ints(count + GROUP)] * 2

    block_flops = 16 * columns * nz * width
    (started,) = call(
        functools.partial(first_deposit, nbrick, cap),
        [struct(4 * columns, nz)],
        [VMEM],
        places(nbrick * cap),
        "first_deposit",
        block_flops * nblocks // 3,
    )(crossed)
    fluid_next, table, answers_up, answers_down = call(
        functools.partial(advance, nbrick, cap),
        [
            struct(3, nx, ny, nz),
            struct(6 * columns, nz, dtype=bf16),
            struct(nbrick * back, width),
            struct(nbrick * back, width),
        ],
        [VMEM] * 3 + [HBM, VMEM],
        [
            pltpu.VMEM((2 * nbrick * chunk, width), f32),
            pltpu.VMEM((2 * nbrick * back, width), f32),
            pltpu.VMEM((4 * columns, nz), f32),
        ]
        + [pltpu.VMEM((3, nx, ny, nz), f32)] * 2
        + places(2 * nbrick * cap)
        + [pltpu.SemaphoreType.DMA((2,))],
        "advance",
        block_flops * nblocks,
        places=[HBM] + [VMEM] * 3,
    )(from_above, from_below, started, fluid, diffused)
    answers_up = shifted(answers_up.reshape(nbrick, back, width), "slab", 1)
    answers_down = shifted(answers_down.reshape(nbrick, back, width), "slab", -1)
    (answers,) = call(
        functools.partial(last_sample, nbrick, cap),
        [struct(nbrick * back, width)],
        [VMEM] * 2,
        places(nbrick * cap),
        "last_sample",
        block_flops * nblocks // 4,
    )(crossed, table)
    answers = jnp.concatenate(
        [answers_up, answers.reshape(nbrick, back, width), answers_down], axis=1
    )
    returned = lax.all_to_all(answers, "brick", split_axis=0, concat_axis=0, tiled=True)
    (velocity_next,) = call(
        functools.partial(relax, nbrick, cap),
        [struct(3, nblocks, width)],
        [HBM] + [VMEM] * 2,
        [pltpu.VMEM((3, nblocks, width), f32), ints(codes), ints(nblocks)]
        + [pltpu.SemaphoreType.DMA((1,))],
        "relax",
    )(routes, updated, returned.reshape(nbrick * 3 * back, width))
    return (jnp.transpose(velocity_next, (1, 0, 2)), fluid_next)


def solution(mesh):
    placed = (
        P(("slab", "brick"), None, None),
        P(("slab", "brick"), None, None),
        P(("slab", "brick"), None),
        P(("slab", "brick"), None),
        P(("slab", "brick"), None),
        P(("slab", "brick")),
        P(("slab", "brick")),
        P(("slab", "brick")),
        P(None, "slab", "brick", None),
    )
    return jax.shard_map(
        on_device,
        mesh=mesh,
        in_specs=placed,
        out_specs=(P(("slab", "brick"), None, None), P(None, "slab", "brick", None)),
        check_vma=False,
    )
```

```python
import functools
import math

import jax
import jax.numpy as jnp
from jax import lax
from jax.experimental import pallas as pl
from jax.experimental.pallas import tpu as pltpu
from jax.sharding import PartitionSpec as P

stiffness = 0.01
damping = 0.005
viscosity = 0.1
coupling = 0.5
relaxation = 0.5

f32 = jnp.float32
bf16 = jnp.bfloat16
VMEM = pl.BlockSpec(memory_space=pltpu.VMEM)
SMEM = pl.BlockSpec(memory_space=pltpu.SMEM)
HBM = pl.BlockSpec(memory_space=pltpu.HBM)
UNROLL = 8
GROUP = 4


def rows_up(count):
    return -(-count // 8) * 8


def call(body, outs, ins, scratch, name, flops=0, nbytes=1 << 20, places=None):
    return pl.pallas_call(
        body,
        out_shape=outs,
        in_specs=ins,
        out_specs=places or [VMEM] * len(outs),
        scratch_shapes=scratch,
        name=name,
        compiler_params=pltpu.CompilerParams(vmem_limit_bytes=40 << 20),
        cost_estimate=pl.CostEstimate(flops=flops, bytes_accessed=nbytes, transcendentals=0),
    )


def rounded(x):
    return x.astype(bf16).astype(f32)


def iota(shape, dim):
    return lax.broadcasted_iota(jnp.int32, shape, dim)


planes = 7


def copy_all(pairs, sems):
    copies = [pltpu.make_async_copy(*pair, sems.at[i]) for i, pair in enumerate(pairs)]
    for copy in copies:
        copy.start()
    return copies


def wait_all(copies):
    for copy in copies:
        copy.wait()


def pack_kernel(ghost_ref, state, fluid, up, down, right, left):
    count = ghost_ref.shape[0] // 4
    width = state.shape[2]
    nx, ny, nz = fluid.shape[1:]
    for group in range(4):
        i, j = group // 2, group % 2
        slab_to, brick_to = (up if i else down), (right if j else left)
        for g in range(count):
            block = pl.ds(ghost_ref[group * count + g], 1)
            for c in range(planes):
                row = state[c, block, :]
                at = c * 2 * count + j * count + g
                slab_to[at : at + 1, :] = row
                at = c * 2 * count + i * count + g
                brick_to[at : at + 1, :] = row
    for slab_to, x in ((up, nx - 1), (down, 0)):
        for c in range(3):
            for k in range(nz // width):
                at = planes * 2 * count + (c * (nz // width) + k) * ny
                slab_to[at : at + ny, :] = fluid[c, x, :, k * width : (k + 1) * width]
    for brick_to, y in ((right, ny - 1), (left, 0)):
        for c in range(3):
            for x in range(nx):
                for k in range(nz // width):
                    at = planes * 2 * count + (c * nx + x) * (nz // width) + k
                    brick_to[at : at + 1, :] = fluid[
                        c, x, y : y + 1, k * width : (k + 1) * width
                    ]


def three_parts(x):
    one = rounded(x)
    rest = x - one
    two = rounded(rest)
    return one, two, rest - two


def put_rows(ref, stride, rows):
    count = rows[0].shape[0]
    for k, row in enumerate(rows):
        ref[pl.ds(k, count, stride=stride), :] = row


def pair_factors(place):
    parts = [three_parts(plane) for plane in place]
    own = three_parts(
        place[3] * place[3] - place[0] * place[0] - place[1] * place[1] - place[2] * place[2]
    )
    return [[part[k] for part in parts] for k in range(3)], list(own)


def home_rows(place):
    (one, two, three), own = pair_factors(place)
    ones, zeros = jnp.ones_like(place[0]), jnp.zeros_like(place[0])
    rows = one + one + two + two + one + three
    return [2.0 * row for row in rows] + own + [ones] * 3 + [zeros] * 2


def partner_rows(place):
    (one, two, three), own = pair_factors(place)
    ones, zeros = jnp.ones_like(place[0]), jnp.zeros_like(place[0])
    return one + two + one + two + three + one + [ones] * 3 + own + [zeros] * 2


def value_rows(values):
    highs = [rounded(plane) for plane in values]
    ones, zeros = jnp.ones_like(values[0]), jnp.zeros_like(values[0])
    lows = [plane - high for plane, high in zip(values, highs)]
    return highs + [ones, zeros] + lows + [zeros, zeros]


def prepare_partners(place, speeds, rows, columns, values):
    count, width = place[0].shape
    put_rows(rows, 32, partner_rows(place))
    put_rows(values, 16, value_rows(place[0:3] + speeds))

    def turn(b, _):
        block = rows[pl.ds(pl.multiple_of(b * 32, 32), 32), :]
        columns[b] = jnp.transpose(block).astype(bf16)
        return 0

    lax.fori_loop(0, count, turn, 0, unroll=4)


def list_tiles(home_ref, partner_ref, homes, partners, lower, upper, spare):
    def one(t, count):
        partner = partner_ref[t]
        homes[count] = home_ref[t]
        partners[count] = partner - lower
        return count + jnp.where((partner >= lower) & (partner < upper), 1, 0)

    count = lax.fori_loop(0, home_ref.shape[0], one, 0, unroll=4)
    for pad in range(UNROLL):
        homes[count + pad] = spare
        partners[count + pad] = 0
    return count


def add_tiles(count, homes, partners, home_side, partner_side, values, sums):
    def some(step, _):
        for k in range(UNROLL):
            home = homes[step * UNROLL + k]
            partner = partners[step * UNROLL + k]
            factors = home_side[pl.ds(pl.multiple_of(home * 32, 32), 32), :].astype(bf16)
            weight = jnp.dot(partner_side[partner], factors, preferred_element_type=f32)
            weight = jnp.maximum(weight, 0.0)
            high = weight.astype(bf16)
            low = (weight - high.astype(f32)).astype(bf16)
            value = values[pl.ds(pl.multiple_of(partner * 16, 16), 16), :].astype(bf16)
            at = pl.ds(pl.multiple_of(home * 16, 16), 16)
            sums[at, :] += jnp.dot(
                jnp.concatenate([value, value], axis=1),
                jnp.concatenate([high, low], axis=0),
                preferred_element_type=f32,
            )
        return 0

    lax.fori_loop(0, (count + UNROLL - 1) // UNROLL, some, 0)


def own_contacts(home_list, partner_list, state, home_side, sums,
                 rows, columns, values, homes, partners, home_ref, partner_ref, sems):
    nblocks, width = state.shape[1:]
    copies = copy_all([(home_list, home_ref), (partner_list, partner_ref)], sems)
    place = [state[c] for c in range(4)]
    put_rows(home_side, 32, home_rows(place))
    prepare_partners(place, [state[c] for c in (4, 5, 6)], rows, columns, values)
    home_side[nblocks * 32 :, :] = jnp.zeros((32, width), f32)
    sums[...] = jnp.zeros(sums.shape, f32)
    wait_all(copies)
    count = list_tiles(home_ref, partner_ref, homes, partners, 0, nblocks, nblocks)
    add_tiles(count, homes, partners, home_side, columns, values, sums)


def diffuse(fluid, below, above, before, after, skip, diffused):
    nx, ny, nz = fluid.shape[1:]
    width = before.shape[1]
    deep = iota((ny, nz), 1)

    def face(ref, c, x):
        at = skip + (c * nx + x) * (nz // width)
        return jnp.concatenate(
            [ref[at + k : at + k + 1, :] for k in range(nz // width)], axis=1
        )

    def layer(ref, c):
        at = [skip + (c * (nz // width) + k) * ny for k in range(nz // width)]
        return jnp.concatenate([ref[start : start + ny, :] for start in at], axis=1)

    for x in range(nx):
        for c in range(3):
            here = fluid[c, x]
            near = (layer(below, c) if x == 0 else fluid[c, x - 1]) + (
                layer(above, c) if x == nx - 1 else fluid[c, x + 1]
            )
            near = near + jnp.concatenate([face(before, c, x), here[:-1]], axis=0)
            near = near + jnp.concatenate([here[1:], face(after, c, x)], axis=0)
            near = near + jnp.where(deep == 0, 0.0, pltpu.roll(here, 1, 1))
            near = near + jnp.where(deep == nz - 1, 0.0, pltpu.roll(here, nz - 1, 1))
            diffused[c, x] = here + viscosity * (near - 6.0 * here)


def ghost_contacts(nbrick, cap, partner_blocks, home_list, partner_list, routes, below, above, before, after,
                   home_side, own_sums, state, fluid,
                   updated, outgoing, diffused,
                   rows, columns, values, sums, homes, partners, taken,
                   home_ref, partner_ref, route_ref, flow, sems):
    nblocks, width = state.shape[1:]
    per = partner_blocks // 4
    copies = copy_all(
        [
            (home_list, home_ref),
            (partner_list, partner_ref),
            (routes, route_ref),
            (fluid, flow),
        ],
        sems,
    )
    stacked = [
        jnp.concatenate(
            [ref[c * per : (c + 1) * per, :] for ref in (below, above, before, after)], axis=0
        )
        for c in range(planes)
    ]
    prepare_partners(stacked[0:4], stacked[4:7], rows, columns, values)
    sums[...] = own_sums[...]
    wait_all(copies)
    count = list_tiles(home_ref, partner_ref, homes, partners, nblocks, nblocks + 4 * per, nblocks)
    add_tiles(count, homes, partners, home_side, columns, values, sums)
    diffuse(flow, below, above, before, after, planes * per, diffused)

    def total(k):
        high = sums[pl.ds(k, nblocks, stride=16), :]
        return high + sums[pl.ds(k + 8, nblocks, stride=16), :]

    weights = total(6)
    radius = state[3]
    inverse = 1.0 / (radius * radius * radius)
    for c in range(3):
        speed = state[c + 4]
        spring = state[c] * weights - total(c)
        friction = total(c + 3) - speed * weights
        updated[c] = speed + (stiffness * spring + damping * friction) * inverse

    chunk = rows_up(5 * cap + 1)
    for code in range(3 * nbrick):
        taken[code] = 0

    def send(b, _):
        code = route_ref[b]
        spot = taken[code]
        taken[code] = spot + 1
        row = ((code % nbrick) * 3 + code // nbrick) * chunk + spot
        outgoing[pl.ds(row, 1), :] = state[3, pl.ds(b, 1), :]
        for c in range(3):
            outgoing[pl.ds(row + (c + 1) * cap, 1), :] = updated[c, pl.ds(b, 1), :]
        outgoing[pl.ds(row + 4 * cap, 1), :] = state[planes, pl.ds(b, 1), :]
        return 0

    lax.fori_loop(0, nblocks, send, 0, unroll=4)
    for code in range(3 * nbrick):
        row = ((code % nbrick) * 3 + code // nbrick) * chunk + 5 * cap
        outgoing[row : row + 1, :] = jnp.full((1, width), taken[code], jnp.int32).astype(f32)


def list_blocks(arrived, starts, ends, cap, places):
    base, goal = places
    count = 0
    for start, end in zip(starts, ends):
        here = jnp.max(arrived[start + 5 * cap : start + 5 * cap + 1, :]).astype(jnp.int32)
        for spot in range(cap):
            base[count] = start + spot
            goal[count] = end + spot
            count = count + jnp.where(spot < here, 1, 0)
    for pad in range(GROUP):
        base[count + pad] = base[jnp.maximum(count - 1, 0)]
        goal[count + pad] = goal[jnp.maximum(count - 1, 0)]
    return count


def cell_parts(arrived, row, cap, depth):
    cell = arrived[pl.ds(row + 4 * cap, 1), :].astype(jnp.int32)
    shift = depth.bit_length() - 1
    return cell >> shift, cell & (depth - 1)


def level_hot(level, depth):
    width = level.shape[1]
    return jnp.where(iota((depth, width), 0) == level, 1.0, 0.0).astype(bf16)


def deposit(count, arrived, places, cap, total):
    columns, depth = total.shape[0] // 4, total.shape[1]
    width = arrived.shape[1]

    def some(step, _):
        loads_of, levels_of = [], []
        for k in range(GROUP):
            index = step * GROUP + k
            row = places[0][index]
            column, level = cell_parts(arrived, row, cap, depth)
            radius = arrived[pl.ds(row, 1), :]
            mass = radius * radius * radius * jnp.where(index < count, 1.0, 0.0)
            loads = [mass] + [mass * arrived[pl.ds(row + c * cap, 1), :] for c in (1, 2, 3)]
            hit = iota((columns, width), 0) == column
            highs, lows = [], []
            for load in loads:
                high = rounded(load)
                highs.append(jnp.where(hit, high, 0.0).astype(bf16))
                lows.append(jnp.where(hit, load - high, 0.0).astype(bf16))
            hot = level_hot(level, depth)
            loads_of += [jnp.concatenate(highs, axis=0), jnp.concatenate(lows, axis=0)]
            levels_of += [hot, hot]
        total[...] += lax.dot_general(
            jnp.concatenate(loads_of, axis=1),
            jnp.concatenate(levels_of, axis=1),
            (((1,), (1,)), ((), ())),
            preferred_element_type=f32,
        )
        return 0

    lax.fori_loop(0, (count + GROUP - 1) // GROUP, some, 0)


def sample(count, arrived, places, cap, table, answers):
    depth = table.shape[1]
    columns = table.shape[0] // 6
    width = arrived.shape[1]

    def some(step, _):
        hots, hits = [], []
        for k in range(GROUP):
            column, level = cell_parts(arrived, places[0][step * GROUP + k], cap, depth)
            hots.append(level_hot(level, depth))
            hits.append(iota((columns, width), 0) == column)
        along = jnp.dot(table[...], jnp.concatenate(hots, axis=1), preferred_element_type=f32)
        for k in range(GROUP):
            goal = places[1][step * GROUP + k]
            part = along[:, k * width : (k + 1) * width]
            for c in range(3):
                value = part[c * columns : (c + 1) * columns]
                value = value + part[(c + 3) * columns : (c + 4) * columns]
                found = jnp.sum(jnp.where(hits[k], value, 0.0), axis=0, keepdims=True)
                answers[pl.ds(goal + c * cap, 1), :] = found
        return 0

    lax.fori_loop(0, (count + GROUP - 1) // GROUP, some, 0)


def first_deposit(nbrick, cap, crossed, total, base, goal):
    chunk = rows_up(5 * cap + 1)
    total[...] = jnp.zeros(total.shape, f32)
    starts = [(3 * b + 1) * chunk for b in range(nbrick)]
    count = list_blocks(crossed, starts, starts, cap, (base, goal))
    deposit(count, crossed, (base, goal), cap, total)


def advance(nbrick, cap, above, below, start, fluid, diffused, fluid_next, table, answers_up,
            answers_down, arrived, answers, total, flow, fresh_flow, base, goal, sems):
    reading = pltpu.make_async_copy(fluid, flow, sems.at[0])
    reading.start()
    chunk = rows_up(5 * cap + 1)
    back = rows_up(3 * cap)
    rows = nbrick * chunk
    arrived[0:rows, :] = above[...]
    arrived[rows:, :] = below[...]
    starts = [i * chunk for i in range(2 * nbrick)]
    ends = [i * back for i in range(2 * nbrick)]
    total[...] = start[...]
    count = list_blocks(arrived, starts, ends, cap, (base, goal))
    deposit(count, arrived, (base, goal), cap, total)
    reading.wait()

    nx, ny, nz = flow.shape[1:]
    columns = nx * ny
    for x in range(nx):
        volume = total[x * ny : (x + 1) * ny, :]
        for c in range(3):
            at = (c + 1) * columns + x * ny
            moved = total[at : at + ny, :] - volume * flow[c, x]
            fresh = diffused[c, x] + coupling * moved
            fresh_flow[c, x] = fresh
            high = fresh.astype(bf16)
            at = c * columns + x * ny
            table[at : at + ny, :] = high
            table[at + 3 * columns : at + 3 * columns + ny, :] = (
                fresh - high.astype(f32)
            ).astype(bf16)
    writing = pltpu.make_async_copy(fresh_flow, fluid_next, sems.at[1])
    writing.start()
    sample(count, arrived, (base, goal), cap, table, answers)
    answers_up[...] = answers[0 : nbrick * back, :]
    answers_down[...] = answers[nbrick * back :, :]
    writing.wait()


def last_sample(nbrick, cap, crossed, table, answers, base, goal):
    chunk = rows_up(5 * cap + 1)
    back = rows_up(3 * cap)
    starts = [(3 * b + 1) * chunk for b in range(nbrick)]
    ends = [b * back for b in range(nbrick)]
    count = list_blocks(crossed, starts, ends, cap, (base, goal))
    sample(count, crossed, (base, goal), cap, table, answers)


def relax(nbrick, cap, route_ref, updated, returned, velocity_next, picked, taken):
    back = rows_up(3 * cap)
    for code in range(3 * nbrick):
        taken[code] = 0

    def one(b, _):
        code = route_ref[b]
        spot = taken[code]
        taken[code] = spot + 1
        row = ((code % nbrick) * 3 + code // nbrick) * back + spot
        for c in range(3):
            picked[c, pl.ds(b, 1), :] = returned[pl.ds(row + c * cap, 1), :]
        return 0

    lax.fori_loop(0, updated.shape[1], one, 0, unroll=4)
    now = updated[...]
    velocity_next[...] = now + relaxation * (picked[...] - now)


def on_device(
    positions, velocities, radii, cell_of, block_route, ghost_list, tile_home, tile_partner, fluid
):
    nblocks, _, width = positions.shape
    nbrick = lax.axis_size("brick")
    _, nx, ny, nz = fluid.shape
    columns = nx * ny
    codes = 3 * nbrick
    cap = max(2, (2 * nblocks + codes - 1) // codes)
    chunk, back = rows_up(5 * cap + 1), rows_up(3 * cap)
    per = ghost_list.shape[0] // 2
    tiles = tile_home.shape[0]
    routes = block_route.reshape(-1)
    positions = jnp.transpose(positions, (1, 0, 2))
    velocities = jnp.transpose(velocities, (1, 0, 2))

    def struct(*shape, dtype=f32):
        return jax.ShapeDtypeStruct(shape, dtype)

    def shifted(x, axis, step):
        count = lax.axis_size(axis)
        return lax.ppermute(x, axis, [(i, (i + step) % count) for i in range(count)])

    def ints(count):
        return pltpu.SMEM((count,), jnp.int32)

    state = jnp.concatenate(
        [positions, radii[None], velocities, cell_of.astype(f32)[None]], axis=0
    )
    ghost_rows, chunks = planes * per, 3 * (nz // width)
    up, down, right, left = call(
        pack_kernel,
        [struct(ghost_rows + chunks * ny, width)] * 2 + [struct(ghost_rows + chunks * nx, width)] * 2,
        [SMEM] + [VMEM] * 2,
        [],
        "pack",
    )(ghost_list, state, fluid)
    below = shifted(up, "slab", 1)
    above = shifted(down, "slab", -1)
    before = shifted(right, "brick", 1)
    after = shifted(left, "brick", -1)

    def sides(count):
        return [
            pltpu.VMEM((count * 32, width), f32),
            pltpu.VMEM((count, width, 32), bf16),
            pltpu.VMEM((count * 16, width), f32),
        ]

    lists = [ints(tiles + UNROLL)] * 2
    contact_flops = tiles * width * width * 200
    home_side, sums = call(
        own_contacts,
        [struct((nblocks + 1) * 32, width), struct((nblocks + 1) * 16, width)],
        [HBM] * 2 + [VMEM],
        sides(nblocks) + lists + [ints(tiles)] * 2 + [pltpu.SemaphoreType.DMA((2,))],
        "own_contacts",
        contact_flops,
    )(tile_home, tile_partner, state)
    updated, outgoing, diffused = call(
        functools.partial(ghost_contacts, nbrick, cap, 4 * per),
        [struct(3, nblocks, width), struct(nbrick * 3 * chunk, width), struct(3, nx, ny, nz)],
        [HBM] * 3 + [VMEM] * 7 + [HBM],
        sides(4 * per)
        + [pltpu.VMEM(((nblocks + 1) * 16, width), f32)]
        + lists
        + [ints(codes), ints(tiles), ints(tiles), ints(nblocks)]
        + [pltpu.VMEM((3, nx, ny, nz), f32), pltpu.SemaphoreType.DMA((4,))],
        "ghost_contacts",
        contact_flops // 2,
    )(tile_home, tile_partner, routes, below, above, before, after,
      home_side, sums, state, fluid)

    crossed = lax.all_to_all(
        outgoing.reshape(nbrick, 3 * chunk, width), "brick", split_axis=0, concat_axis=0, tiled=True
    )
    from_above = shifted(crossed[:, 0:chunk], "slab", -1).reshape(nbrick * chunk, width)
    from_below = shifted(crossed[:, 2 * chunk :], "slab", 1).reshape(nbrick * chunk, width)
    crossed = crossed.reshape(nbrick * 3 * chunk, width)

    def places(count):
        return [ints(count + GROUP)] * 2

    block_flops = 16 * columns * nz * width
    (started,) = call(
        functools.partial(first_deposit, nbrick, cap),
        [struct(4 * columns, nz)],
        [VMEM],
        places(nbrick * cap),
        "first_deposit",
        block_flops * nblocks // 3,
    )(crossed)
    fluid_next, table, answers_up, answers_down = call(
        functools.partial(advance, nbrick, cap),
        [
            struct(3, nx, ny, nz),
            struct(6 * columns, nz, dtype=bf16),
            struct(nbrick * back, width),
            struct(nbrick * back, width),
        ],
        [VMEM] * 3 + [HBM, VMEM],
        [
            pltpu.VMEM((2 * nbrick * chunk, width), f32),
            pltpu.VMEM((2 * nbrick * back, width), f32),
            pltpu.VMEM((4 * columns, nz), f32),
        ]
        + [pltpu.VMEM((3, nx, ny, nz), f32)] * 2
        + places(2 * nbrick * cap)
        + [pltpu.SemaphoreType.DMA((2,))],
        "advance",
        block_flops * nblocks,
        places=[HBM] + [VMEM] * 3,
    )(from_above, from_below, started, fluid, diffused)
    answers_up = shifted(answers_up.reshape(nbrick, back, width), "slab", 1)
    answers_down = shifted(answers_down.reshape(nbrick, back, width), "slab", -1)
    (answers,) = call(
        functools.partial(last_sample, nbrick, cap),
        [struct(nbrick * back, width)],
        [VMEM] * 2,
        places(nbrick * cap),
        "last_sample",
        block_flops * nblocks // 4,
    )(crossed, table)
    answers = jnp.concatenate(
        [answers_up, answers.reshape(nbrick, back, width), answers_down], axis=1
    )
    returned = lax.all_to_all(answers, "brick", split_axis=0, concat_axis=0, tiled=True)
    (velocity_next,) = call(
        functools.partial(relax, nbrick, cap),
        [struct(3, nblocks, width)],
        [SMEM] + [VMEM] * 2,
        [pltpu.VMEM((3, nblocks, width), f32), ints(codes)],
        "relax",
    )(routes, updated, returned.reshape(nbrick * 3 * back, width))
    return (jnp.transpose(velocity_next, (1, 0, 2)), fluid_next)


def solution(mesh):
    placed = (
        P(("slab", "brick"), None, None),
        P(("slab", "brick"), None, None),
        P(("slab", "brick"), None),
        P(("slab", "brick"), None),
        P(("slab", "brick"), None),
        P(("slab", "brick")),
        P(("slab", "brick")),
        P(("slab", "brick")),
        P(None, "slab", "brick", None),
    )
    return jax.shard_map(
        on_device,
        mesh=mesh,
        in_specs=placed,
        out_specs=(P(("slab", "brick"), None, None), P(None, "slab", "brick", None)),
        check_vma=False,
    )
```

```python
import functools
import math

import jax
import jax.numpy as jnp
from jax import lax
from jax.experimental import pallas as pl
from jax.experimental.pallas import tpu as pltpu
from jax.sharding import PartitionSpec as P

stiffness = 0.01
damping = 0.005
viscosity = 0.1
coupling = 0.5
relaxation = 0.5

f32 = jnp.float32
bf16 = jnp.bfloat16
VMEM = pl.BlockSpec(memory_space=pltpu.VMEM)
SMEM = pl.BlockSpec(memory_space=pltpu.SMEM)
HBM = pl.BlockSpec(memory_space=pltpu.HBM)
UNROLL = 8
GROUP = 4
PART = 2


def rows_up(count):
    return -(-count // 8) * 8


def call(body, outs, ins, scratch, name, flops=0, nbytes=1 << 20, places=None):
    return pl.pallas_call(
        body,
        out_shape=outs,
        in_specs=ins,
        out_specs=places or [VMEM] * len(outs),
        scratch_shapes=scratch,
        name=name,
        compiler_params=pltpu.CompilerParams(vmem_limit_bytes=40 << 20),
        cost_estimate=pl.CostEstimate(flops=flops, bytes_accessed=nbytes, transcendentals=0),
    )


def rounded(x):
    return x.astype(bf16).astype(f32)


def iota(shape, dim):
    return lax.broadcasted_iota(jnp.int32, shape, dim)


planes = 7


def copy_all(pairs, sems):
    copies = [pltpu.make_async_copy(*pair, sems.at[i]) for i, pair in enumerate(pairs)]
    for copy in copies:
        copy.start()
    return copies


def wait_all(copies):
    for copy in copies:
        copy.wait()


def pack_kernel(ghost_ref, state, fluid, up, down, right, left):
    count = ghost_ref.shape[0] // 4
    width = state.shape[2]
    nx, ny, nz = fluid.shape[1:]
    for group in range(4):
        i, j = group // 2, group % 2
        slab_to, brick_to = (up if i else down), (right if j else left)
        for g in range(count):
            block = pl.ds(ghost_ref[group * count + g], 1)
            for c in range(planes):
                row = state[c, block, :]
                at = c * 2 * count + j * count + g
                slab_to[at : at + 1, :] = row
                at = c * 2 * count + i * count + g
                brick_to[at : at + 1, :] = row
    for slab_to, x in ((up, nx - 1), (down, 0)):
        for c in range(3):
            for k in range(nz // width):
                at = planes * 2 * count + (c * (nz // width) + k) * ny
                slab_to[at : at + ny, :] = fluid[c, x, :, k * width : (k + 1) * width]
    for brick_to, y in ((right, ny - 1), (left, 0)):
        for c in range(3):
            for x in range(nx):
                for k in range(nz // width):
                    at = planes * 2 * count + (c * nx + x) * (nz // width) + k
                    brick_to[at : at + 1, :] = fluid[
                        c, x, y : y + 1, k * width : (k + 1) * width
                    ]


def three_parts(x):
    one = rounded(x)
    rest = x - one
    two = rounded(rest)
    return one, two, rest - two


def put_rows(ref, stride, rows):
    count = rows[0].shape[0]
    for k, row in enumerate(rows):
        ref[pl.ds(k, count, stride=stride), :] = row


def pair_factors(place):
    parts = [three_parts(plane) for plane in place]
    own = three_parts(
        place[3] * place[3] - place[0] * place[0] - place[1] * place[1] - place[2] * place[2]
    )
    return [[part[k] for part in parts] for k in range(3)], list(own)


def home_rows(place):
    (one, two, three), own = pair_factors(place)
    ones, zeros = jnp.ones_like(place[0]), jnp.zeros_like(place[0])
    rows = one + one + two + two + one + three
    return [2.0 * row for row in rows] + own + [ones] * 3 + [zeros] * 2


def partner_rows(place):
    (one, two, three), own = pair_factors(place)
    ones, zeros = jnp.ones_like(place[0]), jnp.zeros_like(place[0])
    return one + two + one + two + three + one + [ones] * 3 + own + [zeros] * 2


def value_rows(values):
    highs = [rounded(plane) for plane in values]
    ones, zeros = jnp.ones_like(values[0]), jnp.zeros_like(values[0])
    lows = [plane - high for plane, high in zip(values, highs)]
    return highs + [ones, zeros] + lows + [zeros, zeros]


def prepare_partners(place, speeds, partner_side, values):
    put_rows(partner_side, 32, partner_rows(place))
    put_rows(values, 16, value_rows(place[0:3] + speeds))


def prepare_homes(place, rows, home_side):
    put_rows(rows, 32, home_rows(place))

    def turn(b, _):
        block = rows[pl.ds(pl.multiple_of(b * 32, 32), 32), :]
        home_side[b] = jnp.transpose(block).astype(bf16)
        return 0

    lax.fori_loop(0, place[0].shape[0], turn, 0, unroll=4)


def list_tiles(home_ref, partner_ref, homes, partners, lower, upper, spare):
    def one(t, count):
        partner = partner_ref[t]
        homes[count] = home_ref[t]
        partners[count] = partner - lower
        return count + jnp.where((partner >= lower) & (partner < upper), 1, 0)

    count = lax.fori_loop(0, home_ref.shape[0], one, 0, unroll=4)
    for pad in range(UNROLL):
        homes[count + pad] = spare
        partners[count + pad] = 0
    return count


def add_tiles(count, homes, partners, home_side, partner_side, values, sums):
    def some(step, _):
        for k in range(UNROLL):
            home = homes[step * UNROLL + k]
            partner = partners[step * UNROLL + k]
            factors = partner_side[pl.ds(pl.multiple_of(partner * 32, 32), 32), :].astype(bf16)
            weight = jnp.dot(home_side[home], factors, preferred_element_type=f32)
            weight = jnp.maximum(weight, 0.0)
            high = weight.astype(bf16)
            low = (weight - high.astype(f32)).astype(bf16)
            value = values[pl.ds(pl.multiple_of(partner * 16, 16), 16), :].astype(bf16)
            at = pl.ds(pl.multiple_of(home * 16, 16), 16)
            sums[at, :] += lax.dot_general(
                jnp.concatenate([value, value], axis=1),
                jnp.concatenate([high, low], axis=1),
                (((1,), (1,)), ((), ())),
                preferred_element_type=f32,
            )
        return 0

    lax.fori_loop(0, (count + UNROLL - 1) // UNROLL, some, 0)


def own_contacts(home_list, partner_list, state, home_side, sums,
                 rows, partner_side, values, homes, partners, home_ref, partner_ref, sems):
    nblocks, width = state.shape[1:]
    copies = copy_all([(home_list, home_ref), (partner_list, partner_ref)], sems)
    place = [state[c] for c in range(4)]
    prepare_homes(place, rows, home_side)
    prepare_partners(place, [state[c] for c in (4, 5, 6)], partner_side, values)
    home_side[nblocks] = jnp.zeros(home_side.shape[1:], bf16)
    sums[...] = jnp.zeros(sums.shape, f32)
    wait_all(copies)
    count = list_tiles(home_ref, partner_ref, homes, partners, 0, nblocks, nblocks)
    add_tiles(count, homes, partners, home_side, partner_side, values, sums)


def diffuse(fluid, below, above, before, after, skip, diffused):
    nx, ny, nz = fluid.shape[1:]
    width = before.shape[1]
    deep = iota((ny, nz), 1)

    def face(ref, c, x):
        at = skip + (c * nx + x) * (nz // width)
        return jnp.concatenate(
            [ref[at + k : at + k + 1, :] for k in range(nz // width)], axis=1
        )

    def layer(ref, c):
        at = [skip + (c * (nz // width) + k) * ny for k in range(nz // width)]
        return jnp.concatenate([ref[start : start + ny, :] for start in at], axis=1)

    for x in range(nx):
        for c in range(3):
            here = fluid[c, x]
            near = (layer(below, c) if x == 0 else fluid[c, x - 1]) + (
                layer(above, c) if x == nx - 1 else fluid[c, x + 1]
            )
            near = near + jnp.concatenate([face(before, c, x), here[:-1]], axis=0)
            near = near + jnp.concatenate([here[1:], face(after, c, x)], axis=0)
            near = near + jnp.where(deep == 0, 0.0, pltpu.roll(here, 1, 1))
            near = near + jnp.where(deep == nz - 1, 0.0, pltpu.roll(here, nz - 1, 1))
            diffused[c, x] = here + viscosity * (near - 6.0 * here)


def ghost_contacts(nbrick, cap, partner_blocks, home_list, partner_list, routes, below, above, before, after,
                   home_side, own_sums, state, cell, fluid,
                   updated, outgoing, diffused, goals,
                   partner_side, values, sums, homes, partners, taken,
                   home_ref, partner_ref, route_ref, flow, sems):
    nblocks, width = state.shape[1:]
    per = partner_blocks // 4
    copies = copy_all(
        [
            (home_list, home_ref),
            (partner_list, partner_ref),
            (routes, route_ref),
            (fluid, flow),
        ],
        sems,
    )
    stacked = [
        jnp.concatenate(
            [ref[c * per : (c + 1) * per, :] for ref in (below, above, before, after)], axis=0
        )
        for c in range(planes)
    ]
    prepare_partners(stacked[0:4], stacked[4:7], partner_side, values)
    sums[...] = own_sums[...]
    wait_all(copies)
    count = list_tiles(home_ref, partner_ref, homes, partners, nblocks, nblocks + 4 * per, nblocks)
    add_tiles(count, homes, partners, home_side, partner_side, values, sums)
    diffuse(flow, below, above, before, after, planes * per, diffused)

    def total(k):
        high = sums[pl.ds(k, nblocks, stride=16), :]
        return high + sums[pl.ds(k + 8, nblocks, stride=16), :]

    weights = total(6)
    radius = state[3]
    inverse = 1.0 / (radius * radius * radius)
    for c in range(3):
        speed = state[c + 4]
        spring = state[c] * weights - total(c)
        friction = total(c + 3) - speed * weights
        updated[c] = speed + (stiffness * spring + damping * friction) * inverse

    chunk, back = rows_up(5 * cap + 1), rows_up(3 * cap)
    for code in range(3 * nbrick):
        taken[code] = 0

    def send(b, _):
        code = route_ref[b]
        spot = taken[code]
        taken[code] = spot + 1
        place = (code % nbrick) * 3 + code // nbrick
        row = place * chunk + spot
        goals[b] = place * back + spot
        outgoing[pl.ds(row, 1), :] = state[3, pl.ds(b, 1), :]
        for c in range(3):
            outgoing[pl.ds(row + (c + 1) * cap, 1), :] = updated[c, pl.ds(b, 1), :]
        outgoing[pl.ds(row + 4 * cap, 1), :] = cell[pl.ds(b, 1), :].astype(f32)
        return 0

    lax.fori_loop(0, nblocks, send, 0, unroll=4)
    for code in range(3 * nbrick):
        row = ((code % nbrick) * 3 + code // nbrick) * chunk + 5 * cap
        outgoing[row : row + 1, :] = jnp.full((1, width), taken[code], jnp.int32).astype(f32)


def list_blocks(arrived, starts, ends, cap, places):
    base, goal = places
    count = 0
    for start, end in zip(starts, ends):
        here = jnp.max(arrived[start + 5 * cap : start + 5 * cap + 1, :]).astype(jnp.int32)
        for spot in range(cap):
            base[count] = start + spot
            goal[count] = end + spot
            count = count + jnp.where(spot < here, 1, 0)
    for pad in range(GROUP):
        base[count + pad] = base[jnp.maximum(count - 1, 0)]
        goal[count + pad] = goal[jnp.maximum(count - 1, 0)]
    return count


def cell_parts(arrived, row, cap, depth):
    cell = arrived[pl.ds(row + 4 * cap, 1), :].astype(jnp.int32)
    shift = depth.bit_length() - 1
    return cell >> shift, (cell & (depth - 1)) - depth // 2


def all_levels(depth, width):
    return (iota((depth, width), 0) - depth // 2).astype(f32).astype(bf16)


def level_hot(level, levels):
    hit = levels == jnp.broadcast_to(level.astype(f32).astype(bf16), levels.shape)
    return jnp.where(hit, jnp.ones((), bf16), jnp.zeros((), bf16))


def deposit(count, arrived, places, cap, total):
    columns, depth = total.shape[0] // 4, total.shape[1]
    width = arrived.shape[1]
    numbers = iota((columns, width), 0).astype(f32).astype(bf16)
    levels = all_levels(depth, width)

    def some(step, _):
        for start in range(0, GROUP, PART):
            loads_of, levels_of = [], []
            for k in range(start, start + PART):
                index = step * GROUP + k
                row = places[0][index]
                column, level = cell_parts(arrived, row, cap, depth)
                radius = arrived[pl.ds(row, 1), :]
                mass = radius * radius * radius * jnp.where(index < count, 1.0, 0.0)
                loads = [mass] + [mass * arrived[pl.ds(row + c * cap, 1), :] for c in (1, 2, 3)]
                column = jnp.broadcast_to(column.astype(f32).astype(bf16), (columns, width))
                hit = numbers == column
                highs, lows = [], []
                for load in loads:
                    high = load.astype(bf16)
                    low = (load - high.astype(f32)).astype(bf16)
                    for parts, part in ((highs, high), (lows, low)):
                        part = jnp.broadcast_to(part, (columns, width))
                        parts.append(jnp.where(hit, part, jnp.zeros((), bf16)))
                hot = level_hot(level, levels)
                loads_of += [jnp.concatenate(highs, axis=0), jnp.concatenate(lows, axis=0)]
                levels_of += [hot, hot]
            total[...] += lax.dot_general(
                jnp.concatenate(loads_of, axis=1),
                jnp.concatenate(levels_of, axis=1),
                (((1,), (1,)), ((), ())),
                preferred_element_type=f32,
            )
        return 0

    lax.fori_loop(0, (count + GROUP - 1) // GROUP, some, 0)


def sample(count, arrived, places, cap, table, answers):
    depth = table.shape[1]
    columns = table.shape[0] // 6
    width = arrived.shape[1]
    levels = all_levels(depth, width)

    def some(step, _):
        hots, hits = [], []
        for k in range(GROUP):
            column, level = cell_parts(arrived, places[0][step * GROUP + k], cap, depth)
            hots.append(level_hot(level, levels))
            hits.append(iota((columns, width), 0) == column)
        along = jnp.dot(table[...], jnp.concatenate(hots, axis=1), preferred_element_type=f32)
        for k in range(GROUP):
            goal = places[1][step * GROUP + k]
            part = along[:, k * width : (k + 1) * width]
            for c in range(3):
                value = part[c * columns : (c + 1) * columns]
                value = value + part[(c + 3) * columns : (c + 4) * columns]
                found = jnp.sum(jnp.where(hits[k], value, 0.0), axis=0, keepdims=True)
                answers[pl.ds(goal + c * cap, 1), :] = found
        return 0

    lax.fori_loop(0, (count + GROUP - 1) // GROUP, some, 0)


def first_deposit(nbrick, cap, crossed, total, base, goal):
    chunk = rows_up(5 * cap + 1)
    total[...] = jnp.zeros(total.shape, f32)
    starts = [(3 * b + 1) * chunk for b in range(nbrick)]
    count = list_blocks(crossed, starts, starts, cap, (base, goal))
    deposit(count, crossed, (base, goal), cap, total)


def advance(nbrick, cap, above, below, start, fluid, diffused, fluid_next, table, answers_up,
            answers_down, arrived, answers, total, flow, fresh_flow, base, goal, sems):
    reading = pltpu.make_async_copy(fluid, flow, sems.at[0])
    reading.start()
    chunk = rows_up(5 * cap + 1)
    back = rows_up(3 * cap)
    rows = nbrick * chunk
    arrived[0:rows, :] = above[...]
    arrived[rows:, :] = below[...]
    starts = [i * chunk for i in range(2 * nbrick)]
    ends = [i * back for i in range(2 * nbrick)]
    total[...] = start[...]
    count = list_blocks(arrived, starts, ends, cap, (base, goal))
    deposit(count, arrived, (base, goal), cap, total)
    reading.wait()

    nx, ny, nz = flow.shape[1:]
    columns = nx * ny
    for x in range(nx):
        volume = total[x * ny : (x + 1) * ny, :]
        for c in range(3):
            at = (c + 1) * columns + x * ny
            moved = total[at : at + ny, :] - volume * flow[c, x]
            fresh = diffused[c, x] + coupling * moved
            fresh_flow[c, x] = fresh
            high = fresh.astype(bf16)
            at = c * columns + x * ny
            table[at : at + ny, :] = high
            table[at + 3 * columns : at + 3 * columns + ny, :] = (
                fresh - high.astype(f32)
            ).astype(bf16)
    writing = pltpu.make_async_copy(fresh_flow, fluid_next, sems.at[1])
    writing.start()
    sample(count, arrived, (base, goal), cap, table, answers)
    answers_up[...] = answers[0 : nbrick * back, :]
    answers_down[...] = answers[nbrick * back :, :]
    writing.wait()


def last_sample(nbrick, cap, crossed, table, answers, base, goal):
    chunk = rows_up(5 * cap + 1)
    back = rows_up(3 * cap)
    starts = [(3 * b + 1) * chunk for b in range(nbrick)]
    ends = [b * back for b in range(nbrick)]
    count = list_blocks(crossed, starts, ends, cap, (base, goal))
    sample(count, crossed, (base, goal), cap, table, answers)


def relax(cap, goals, updated, returned, velocity_next, picked):
    def one(b, _):
        row = goals[b]
        for c in range(3):
            picked[c, pl.ds(b, 1), :] = returned[pl.ds(row + c * cap, 1), :]
        return 0

    lax.fori_loop(0, updated.shape[1], one, 0, unroll=8)
    now = updated[...]
    velocity_next[...] = now + relaxation * (picked[...] - now)


def on_device(
    positions, velocities, radii, cell_of, block_route, ghost_list, tile_home, tile_partner, fluid
):
    nblocks, _, width = positions.shape
    nbrick = lax.axis_size("brick")
    _, nx, ny, nz = fluid.shape
    columns = nx * ny
    codes = 3 * nbrick
    cap = max(2, (2 * nblocks + codes - 1) // codes)
    chunk, back = rows_up(5 * cap + 1), rows_up(3 * cap)
    per = ghost_list.shape[0] // 2
    tiles = tile_home.shape[0]
    routes = block_route.reshape(-1)
    positions = jnp.transpose(positions, (1, 0, 2))
    velocities = jnp.transpose(velocities, (1, 0, 2))

    def struct(*shape, dtype=f32):
        return jax.ShapeDtypeStruct(shape, dtype)

    def shifted(x, axis, step):
        count = lax.axis_size(axis)
        return lax.ppermute(x, axis, [(i, (i + step) % count) for i in range(count)])

    def ints(count):
        return pltpu.SMEM((count,), jnp.int32)

    state = jnp.concatenate([positions, radii[None], velocities], axis=0)
    ghost_rows, chunks = planes * per, 3 * (nz // width)
    up, down, right, left = call(
        pack_kernel,
        [struct(ghost_rows + chunks * ny, width)] * 2 + [struct(ghost_rows + chunks * nx, width)] * 2,
        [SMEM] + [VMEM] * 2,
        [],
        "pack",
    )(ghost_list, state, fluid)
    below = shifted(up, "slab", 1)
    above = shifted(down, "slab", -1)
    before = shifted(right, "brick", 1)
    after = shifted(left, "brick", -1)

    def sides(count):
        return [pltpu.VMEM((count * 32, width), f32), pltpu.VMEM((count * 16, width), f32)]

    lists = [ints(tiles + UNROLL)] * 2
    contact_flops = tiles * width * width * 200
    home_side, sums = call(
        own_contacts,
        [struct(nblocks + 1, width, 32, dtype=bf16), struct((nblocks + 1) * 16, width)],
        [HBM] * 2 + [VMEM],
        [pltpu.VMEM((nblocks * 32, width), f32)]
        + sides(nblocks)
        + lists
        + [ints(tiles)] * 2 + [pltpu.SemaphoreType.DMA((2,))],
        "own_contacts",
        contact_flops,
    )(tile_home, tile_partner, state)
    updated, outgoing, diffused, goals = call(
        functools.partial(ghost_contacts, nbrick, cap, 4 * per),
        [struct(3, nblocks, width), struct(nbrick * 3 * chunk, width), struct(3, nx, ny, nz)]
        + [struct(nblocks, dtype=jnp.int32)],
        [HBM] * 3 + [VMEM] * 8 + [HBM],
        sides(4 * per)
        + [pltpu.VMEM(((nblocks + 1) * 16, width), f32)]
        + lists
        + [ints(codes), ints(tiles), ints(tiles), ints(nblocks)]
        + [pltpu.VMEM((3, nx, ny, nz), f32), pltpu.SemaphoreType.DMA((4,))],
        "ghost_contacts",
        contact_flops // 2,
        places=[VMEM] * 3 + [SMEM],
    )(tile_home, tile_partner, routes, below, above, before, after,
      home_side, sums, state, cell_of, fluid)

    crossed = lax.all_to_all(
        outgoing.reshape(nbrick, 3 * chunk, width), "brick", split_axis=0, concat_axis=0, tiled=True
    )
    from_above = shifted(crossed[:, 0:chunk], "slab", -1).reshape(nbrick * chunk, width)
    from_below = shifted(crossed[:, 2 * chunk :], "slab", 1).reshape(nbrick * chunk, width)
    crossed = crossed.reshape(nbrick * 3 * chunk, width)

    def places(count):
        return [ints(count + GROUP)] * 2

    block_flops = 16 * columns * nz * width
    (started,) = call(
        functools.partial(first_deposit, nbrick, cap),
        [struct(4 * columns, nz)],
        [VMEM],
        places(nbrick * cap),
        "first_deposit",
        block_flops * nblocks // 3,
    )(crossed)
    fluid_next, table, answers_up, answers_down = call(
        functools.partial(advance, nbrick, cap),
        [
            struct(3, nx, ny, nz),
            struct(6 * columns, nz, dtype=bf16),
            struct(nbrick * back, width),
            struct(nbrick * back, width),
        ],
        [VMEM] * 3 + [HBM, VMEM],
        [
            pltpu.VMEM((2 * nbrick * chunk, width), f32),
            pltpu.VMEM((2 * nbrick * back, width), f32),
            pltpu.VMEM((4 * columns, nz), f32),
        ]
        + [pltpu.VMEM((3, nx, ny, nz), f32)] * 2
        + places(2 * nbrick * cap)
        + [pltpu.SemaphoreType.DMA((2,))],
        "advance",
        block_flops * nblocks,
        places=[HBM] + [VMEM] * 3,
    )(from_above, from_below, started, fluid, diffused)
    answers_up = shifted(answers_up.reshape(nbrick, back, width), "slab", 1)
    answers_down = shifted(answers_down.reshape(nbrick, back, width), "slab", -1)
    (answers,) = call(
        functools.partial(last_sample, nbrick, cap),
        [struct(nbrick * back, width)],
        [VMEM] * 2,
        places(nbrick * cap),
        "last_sample",
        block_flops * nblocks // 4,
    )(crossed, table)
    answers = jnp.concatenate(
        [answers_up, answers.reshape(nbrick, back, width), answers_down], axis=1
    )
    returned = lax.all_to_all(answers, "brick", split_axis=0, concat_axis=0, tiled=True)
    (velocity_next,) = call(
        functools.partial(relax, cap),
        [struct(3, nblocks, width)],
        [SMEM] + [VMEM] * 2,
        [pltpu.VMEM((3, nblocks, width), f32)],
        "relax",
    )(goals, updated, returned.reshape(nbrick * 3 * back, width))
    return (jnp.transpose(velocity_next, (1, 0, 2)), fluid_next)


def solution(mesh):
    placed = (
        P(("slab", "brick"), None, None),
        P(("slab", "brick"), None, None),
        P(("slab", "brick"), None),
        P(("slab", "brick"), None),
        P(("slab", "brick"), None),
        P(("slab", "brick")),
        P(("slab", "brick")),
        P(("slab", "brick")),
        P(None, "slab", "brick", None),
    )
    return jax.shard_map(
        on_device,
        mesh=mesh,
        in_specs=placed,
        out_specs=(P(("slab", "brick"), None, None), P(None, "slab", "brick", None)),
        check_vma=False,
    )
```

```python
import functools
import math

import jax
import jax.numpy as jnp
from jax import lax
from jax.experimental import pallas as pl
from jax.experimental.pallas import tpu as pltpu
from jax.sharding import PartitionSpec as P

stiffness = 0.01
damping = 0.005
viscosity = 0.1
coupling = 0.5
relaxation = 0.5

f32 = jnp.float32
bf16 = jnp.bfloat16
VMEM = pl.BlockSpec(memory_space=pltpu.VMEM)
SMEM = pl.BlockSpec(memory_space=pltpu.SMEM)
HBM = pl.BlockSpec(memory_space=pltpu.HBM)
UNROLL = 8
GROUP = 4


def rows_up(count):
    return -(-count // 8) * 8


def call(body, outs, ins, scratch, name, flops=0, nbytes=1 << 20, places=None):
    return pl.pallas_call(
        body,
        out_shape=outs,
        in_specs=ins,
        out_specs=places or [VMEM] * len(outs),
        scratch_shapes=scratch,
        name=name,
        compiler_params=pltpu.CompilerParams(vmem_limit_bytes=40 << 20),
        cost_estimate=pl.CostEstimate(flops=flops, bytes_accessed=nbytes, transcendentals=0),
    )


def rounded(x):
    return x.astype(bf16).astype(f32)


def iota(shape, dim):
    return lax.broadcasted_iota(jnp.int32, shape, dim)


planes = 7


def copy_all(pairs, sems):
    copies = [pltpu.make_async_copy(*pair, sems.at[i]) for i, pair in enumerate(pairs)]
    for copy in copies:
        copy.start()
    return copies


def wait_all(copies):
    for copy in copies:
        copy.wait()


def pack_kernel(ghost_ref, state, fluid, up, down, right, left):
    count = ghost_ref.shape[0] // 4
    width = state.shape[2]
    nx, ny, nz = fluid.shape[1:]
    for group in range(4):
        i, j = group // 2, group % 2
        slab_to, brick_to = (up if i else down), (right if j else left)
        for g in range(count):
            block = pl.ds(ghost_ref[group * count + g], 1)
            for c in range(planes):
                row = state[c, block, :]
                at = c * 2 * count + j * count + g
                slab_to[at : at + 1, :] = row
                at = c * 2 * count + i * count + g
                brick_to[at : at + 1, :] = row
    for slab_to, x in ((up, nx - 1), (down, 0)):
        for c in range(3):
            for k in range(nz // width):
                at = planes * 2 * count + (c * (nz // width) + k) * ny
                slab_to[at : at + ny, :] = fluid[c, x, :, k * width : (k + 1) * width]
    for brick_to, y in ((right, ny - 1), (left, 0)):
        for c in range(3):
            for x in range(nx):
                for k in range(nz // width):
                    at = planes * 2 * count + (c * nx + x) * (nz // width) + k
                    brick_to[at : at + 1, :] = fluid[
                        c, x, y : y + 1, k * width : (k + 1) * width
                    ]


def three_parts(x):
    one = rounded(x)
    rest = x - one
    two = rounded(rest)
    return one, two, rest - two


def put_rows(ref, stride, rows):
    count = rows[0].shape[0]
    for k, row in enumerate(rows):
        ref[pl.ds(k, count, stride=stride), :] = row


def pair_factors(place):
    parts = [three_parts(plane) for plane in place]
    own = three_parts(
        place[3] * place[3] - place[0] * place[0] - place[1] * place[1] - place[2] * place[2]
    )
    return [[part[k] for part in parts] for k in range(3)], list(own)


def home_rows(place):
    (one, two, three), own = pair_factors(place)
    ones, zeros = jnp.ones_like(place[0]), jnp.zeros_like(place[0])
    rows = one + one + two + two + one + three
    return [2.0 * row for row in rows] + own + [ones] * 3 + [zeros] * 2


def partner_rows(place):
    (one, two, three), own = pair_factors(place)
    ones, zeros = jnp.ones_like(place[0]), jnp.zeros_like(place[0])
    return one + two + one + two + three + one + [ones] * 3 + own + [zeros] * 2


def value_rows(values):
    highs = [rounded(plane) for plane in values]
    ones, zeros = jnp.ones_like(values[0]), jnp.zeros_like(values[0])
    lows = [plane - high for plane, high in zip(values, highs)]
    return highs + [ones, zeros] + lows + [zeros, zeros]


def prepare_partners(place, speeds, rows, columns, values):
    count, width = place[0].shape
    put_rows(rows, 32, partner_rows(place))
    put_rows(values, 16, value_rows(place[0:3] + speeds))

    def turn(b, _):
        block = rows[pl.ds(pl.multiple_of(b * 32, 32), 32), :]
        columns[b] = jnp.transpose(block).astype(bf16)
        return 0

    lax.fori_loop(0, count, turn, 0, unroll=4)


def list_tiles(home_ref, partner_ref, homes, partners, lower, upper, spare):
    def one(t, count):
        partner = partner_ref[t]
        homes[count] = home_ref[t]
        partners[count] = partner - lower
        return count + jnp.where((partner >= lower) & (partner < upper), 1, 0)

    count = lax.fori_loop(0, home_ref.shape[0], one, 0, unroll=4)
    for pad in range(UNROLL):
        homes[count + pad] = spare
        partners[count + pad] = 0
    return count


def add_tiles(count, homes, partners, home_side, partner_side, values, sums):
    def some(step, _):
        for k in range(UNROLL):
            home = homes[step * UNROLL + k]
            partner = partners[step * UNROLL + k]
            factors = home_side[pl.ds(pl.multiple_of(home * 32, 32), 32), :].astype(bf16)
            weight = jnp.dot(partner_side[partner], factors, preferred_element_type=f32)
            weight = jnp.maximum(weight, 0.0)
            high = weight.astype(bf16)
            low = (weight - high.astype(f32)).astype(bf16)
            value = values[pl.ds(pl.multiple_of(partner * 16, 16), 16), :].astype(bf16)
            at = pl.ds(pl.multiple_of(home * 16, 16), 16)
            sums[at, :] += jnp.dot(
                jnp.concatenate([value, value], axis=1),
                jnp.concatenate([high, low], axis=0),
                preferred_element_type=f32,
            )
        return 0

    lax.fori_loop(0, (count + UNROLL - 1) // UNROLL, some, 0)


def own_contacts(home_list, partner_list, state, home_side, sums,
                 rows, columns, values, homes, partners, home_ref, partner_ref, sems):
    nblocks, width = state.shape[1:]
    copies = copy_all([(home_list, home_ref), (partner_list, partner_ref)], sems)
    place = [state[c] for c in range(4)]
    put_rows(home_side, 32, home_rows(place))
    prepare_partners(place, [state[c] for c in (4, 5, 6)], rows, columns, values)
    home_side[nblocks * 32 :, :] = jnp.zeros((32, width), f32)
    sums[...] = jnp.zeros(sums.shape, f32)
    wait_all(copies)
    count = list_tiles(home_ref, partner_ref, homes, partners, 0, nblocks, nblocks)
    add_tiles(count, homes, partners, home_side, columns, values, sums)


def diffuse(fluid, below, above, before, after, skip, diffused):
    nx, ny, nz = fluid.shape[1:]
    width = before.shape[1]
    deep = iota((ny, nz), 1)

    def face(ref, c, x):
        at = skip + (c * nx + x) * (nz // width)
        return jnp.concatenate(
            [ref[at + k : at + k + 1, :] for k in range(nz // width)], axis=1
        )

    def layer(ref, c):
        at = [skip + (c * (nz // width) + k) * ny for k in range(nz // width)]
        return jnp.concatenate([ref[start : start + ny, :] for start in at], axis=1)

    for x in range(nx):
        for c in range(3):
            here = fluid[c, x]
            near = (layer(below, c) if x == 0 else fluid[c, x - 1]) + (
                layer(above, c) if x == nx - 1 else fluid[c, x + 1]
            )
            near = near + jnp.concatenate([face(before, c, x), here[:-1]], axis=0)
            near = near + jnp.concatenate([here[1:], face(after, c, x)], axis=0)
            near = near + jnp.where(deep == 0, 0.0, pltpu.roll(here, 1, 1))
            near = near + jnp.where(deep == nz - 1, 0.0, pltpu.roll(here, nz - 1, 1))
            diffused[c, x] = here + viscosity * (near - 6.0 * here)


def ghost_contacts(nbrick, cap, partner_blocks, home_list, partner_list, routes, below, above, before, after,
                   home_side, own_sums, state, cell, fluid,
                   updated, outgoing, diffused, goals,
                   rows, columns, values, sums, homes, partners, taken,
                   home_ref, partner_ref, route_ref, flow, sems):
    nblocks, width = state.shape[1:]
    per = partner_blocks // 4
    copies = copy_all(
        [
            (home_list, home_ref),
            (partner_list, partner_ref),
            (routes, route_ref),
            (fluid, flow),
        ],
        sems,
    )
    stacked = [
        jnp.concatenate(
            [ref[c * per : (c + 1) * per, :] for ref in (below, above, before, after)], axis=0
        )
        for c in range(planes)
    ]
    prepare_partners(stacked[0:4], stacked[4:7], rows, columns, values)
    sums[...] = own_sums[...]
    wait_all(copies)
    count = list_tiles(home_ref, partner_ref, homes, partners, nblocks, nblocks + 4 * per, nblocks)
    add_tiles(count, homes, partners, home_side, columns, values, sums)
    diffuse(flow, below, above, before, after, planes * per, diffused)

    def total(k):
        high = sums[pl.ds(k, nblocks, stride=16), :]
        return high + sums[pl.ds(k + 8, nblocks, stride=16), :]

    weights = total(6)
    radius = state[3]
    inverse = 1.0 / (radius * radius * radius)
    for c in range(3):
        speed = state[c + 4]
        spring = state[c] * weights - total(c)
        friction = total(c + 3) - speed * weights
        updated[c] = speed + (stiffness * spring + damping * friction) * inverse

    chunk, back = rows_up(5 * cap + 1), rows_up(3 * cap)
    for code in range(3 * nbrick):
        taken[code] = 0

    def send(b, _):
        code = route_ref[b]
        spot = taken[code]
        taken[code] = spot + 1
        place = (code % nbrick) * 3 + code // nbrick
        row = place * chunk + spot
        goals[b] = place * back + spot
        outgoing[pl.ds(row, 1), :] = state[3, pl.ds(b, 1), :]
        for c in range(3):
            outgoing[pl.ds(row + (c + 1) * cap, 1), :] = updated[c, pl.ds(b, 1), :]
        outgoing[pl.ds(row + 4 * cap, 1), :] = cell[pl.ds(b, 1), :].astype(f32)
        return 0

    lax.fori_loop(0, nblocks, send, 0, unroll=4)
    for code in range(3 * nbrick):
        row = ((code % nbrick) * 3 + code // nbrick) * chunk + 5 * cap
        outgoing[row : row + 1, :] = jnp.full((1, width), taken[code], jnp.int32).astype(f32)


def list_blocks(arrived, starts, ends, cap, places):
    base, goal = places
    count = 0
    for start, end in zip(starts, ends):
        here = jnp.max(arrived[start + 5 * cap : start + 5 * cap + 1, :]).astype(jnp.int32)
        for spot in range(cap):
            base[count] = start + spot
            goal[count] = end + spot
            count = count + jnp.where(spot < here, 1, 0)
    for pad in range(GROUP):
        base[count + pad] = base[jnp.maximum(count - 1, 0)]
        goal[count + pad] = goal[jnp.maximum(count - 1, 0)]
    return count


def cell_parts(arrived, row, cap, depth):
    cell = arrived[pl.ds(row + 4 * cap, 1), :].astype(jnp.int32)
    shift = depth.bit_length() - 1
    return cell >> shift, (cell & (depth - 1)) - depth // 2


def all_levels(depth, width):
    return (iota((depth, width), 0) - depth // 2).astype(f32).astype(bf16)


def level_hot(level, levels):
    hit = levels == jnp.broadcast_to(level.astype(f32).astype(bf16), levels.shape)
    return jnp.where(hit, jnp.ones((), bf16), jnp.zeros((), bf16))


def deposit(count, arrived, places, cap, total):
    columns, depth = total.shape[0] // 4, total.shape[1]
    width = arrived.shape[1]
    numbers = iota((columns, width), 0).astype(f32).astype(bf16)
    levels = iota((width, depth), 1) - depth // 2

    def some(step, _):
        high_of, low_of, level_of = [], [], []
        for k in range(GROUP):
            index = step * GROUP + k
            row = places[0][index]
            column, level = cell_parts(arrived, row, cap, depth)
            radius = arrived[pl.ds(row, 1), :]
            mass = radius * radius * radius * jnp.where(index < count, 1.0, 0.0)
            loads = [mass] + [mass * arrived[pl.ds(row + c * cap, 1), :] for c in (1, 2, 3)]
            column = jnp.broadcast_to(column.astype(f32).astype(bf16), (columns, width))
            hit = numbers == column
            highs, lows = [], []
            for load in loads:
                high = load.astype(bf16)
                low = (load - high.astype(f32)).astype(bf16)
                for parts, part in ((highs, high), (lows, low)):
                    part = jnp.broadcast_to(part, (columns, width))
                    parts.append(jnp.where(hit, part, jnp.zeros((), bf16)))
            high_of.append(jnp.concatenate(highs, axis=0))
            low_of.append(jnp.concatenate(lows, axis=0))
            level_of.append(level.astype(f32))
        turned = jnp.transpose(jnp.concatenate(level_of * (8 // GROUP), axis=0)).astype(jnp.int32)
        hots = [
            jnp.where(levels == turned[:, k : k + 1], 1.0, 0.0).astype(bf16)
            for k in range(GROUP)
        ]
        total[...] += jnp.dot(
            jnp.concatenate(high_of + low_of, axis=1),
            jnp.concatenate(hots + hots, axis=0),
            preferred_element_type=f32,
        )
        return 0

    lax.fori_loop(0, (count + GROUP - 1) // GROUP, some, 0)


def sample(count, arrived, places, cap, table, answers):
    depth = table.shape[1] // 2
    columns = table.shape[0] // 3
    width = arrived.shape[1]
    levels = all_levels(depth, width)

    def some(step, _):
        hots, hits = [], []
        for k in range(GROUP):
            column, level = cell_parts(arrived, places[0][step * GROUP + k], cap, depth)
            hots.append(level_hot(level, levels))
            hits.append(iota((columns, width), 0) == column)
        hot = jnp.concatenate(hots, axis=1)
        along = jnp.dot(
            table[...], jnp.concatenate([hot, hot], axis=0), preferred_element_type=f32
        )
        for k in range(GROUP):
            goal = places[1][step * GROUP + k]
            for c in range(3):
                value = along[c * columns : (c + 1) * columns, k * width : (k + 1) * width]
                found = jnp.sum(jnp.where(hits[k], value, 0.0), axis=0, keepdims=True)
                answers[pl.ds(goal + c * cap, 1), :] = found
        return 0

    lax.fori_loop(0, (count + GROUP - 1) // GROUP, some, 0)


def first_deposit(nbrick, cap, crossed, total, base, goal):
    chunk = rows_up(5 * cap + 1)
    total[...] = jnp.zeros(total.shape, f32)
    starts = [(3 * b + 1) * chunk for b in range(nbrick)]
    count = list_blocks(crossed, starts, starts, cap, (base, goal))
    deposit(count, crossed, (base, goal), cap, total)


def advance(nbrick, cap, above, below, start, fluid, diffused, fluid_next, table, answers_up,
            answers_down, arrived, answers, total, flow, fresh_flow, base, goal, sems):
    reading = pltpu.make_async_copy(fluid, flow, sems.at[0])
    reading.start()
    chunk = rows_up(5 * cap + 1)
    back = rows_up(3 * cap)
    rows = nbrick * chunk
    arrived[0:rows, :] = above[...]
    arrived[rows:, :] = below[...]
    starts = [i * chunk for i in range(2 * nbrick)]
    ends = [i * back for i in range(2 * nbrick)]
    total[...] = start[...]
    count = list_blocks(arrived, starts, ends, cap, (base, goal))
    deposit(count, arrived, (base, goal), cap, total)
    reading.wait()

    nx, ny, nz = flow.shape[1:]
    columns = nx * ny
    for x in range(nx):
        volume = total[x * ny : (x + 1) * ny, :]
        for c in range(3):
            at = (c + 1) * columns + x * ny
            moved = total[at : at + ny, :] - volume * flow[c, x]
            fresh = diffused[c, x] + coupling * moved
            fresh_flow[c, x] = fresh
            high = fresh.astype(bf16)
            at = c * columns + x * ny
            table[at : at + ny, 0:nz] = high
            table[at : at + ny, nz:] = (fresh - high.astype(f32)).astype(bf16)
    writing = pltpu.make_async_copy(fresh_flow, fluid_next, sems.at[1])
    writing.start()
    sample(count, arrived, (base, goal), cap, table, answers)
    answers_up[...] = answers[0 : nbrick * back, :]
    answers_down[...] = answers[nbrick * back :, :]
    writing.wait()


def last_sample(nbrick, cap, crossed, table, answers, base, goal):
    chunk = rows_up(5 * cap + 1)
    back = rows_up(3 * cap)
    starts = [(3 * b + 1) * chunk for b in range(nbrick)]
    ends = [b * back for b in range(nbrick)]
    count = list_blocks(crossed, starts, ends, cap, (base, goal))
    sample(count, crossed, (base, goal), cap, table, answers)


def relax(cap, goals, updated, returned, velocity_next, picked):
    def one(b, _):
        row = goals[b]
        for c in range(3):
            picked[c, pl.ds(b, 1), :] = returned[pl.ds(row + c * cap, 1), :]
        return 0

    lax.fori_loop(0, updated.shape[1], one, 0, unroll=8)
    now = updated[...]
    velocity_next[...] = now + relaxation * (picked[...] - now)


def on_device(
    positions, velocities, radii, cell_of, block_route, ghost_list, tile_home, tile_partner, fluid
):
    nblocks, _, width = positions.shape
    nbrick = lax.axis_size("brick")
    _, nx, ny, nz = fluid.shape
    columns = nx * ny
    codes = 3 * nbrick
    cap = max(2, (2 * nblocks + codes - 1) // codes)
    chunk, back = rows_up(5 * cap + 1), rows_up(3 * cap)
    per = ghost_list.shape[0] // 2
    tiles = tile_home.shape[0]
    routes = block_route.reshape(-1)
    positions = jnp.transpose(positions, (1, 0, 2))
    velocities = jnp.transpose(velocities, (1, 0, 2))

    def struct(*shape, dtype=f32):
        return jax.ShapeDtypeStruct(shape, dtype)

    def shifted(x, axis, step):
        count = lax.axis_size(axis)
        return lax.ppermute(x, axis, [(i, (i + step) % count) for i in range(count)])

    def ints(count):
        return pltpu.SMEM((count,), jnp.int32)

    state = jnp.concatenate([positions, radii[None], velocities], axis=0)
    ghost_rows, chunks = planes * per, 3 * (nz // width)
    up, down, right, left = call(
        pack_kernel,
        [struct(ghost_rows + chunks * ny, width)] * 2 + [struct(ghost_rows + chunks * nx, width)] * 2,
        [SMEM] + [VMEM] * 2,
        [],
        "pack",
    )(ghost_list, state, fluid)
    below = shifted(up, "slab", 1)
    above = shifted(down, "slab", -1)
    before = shifted(right, "brick", 1)
    after = shifted(left, "brick", -1)

    def sides(count):
        return [
            pltpu.VMEM((count * 32, width), f32),
            pltpu.VMEM((count, width, 32), bf16),
            pltpu.VMEM((count * 16, width), f32),
        ]

    lists = [ints(tiles + UNROLL)] * 2
    contact_flops = tiles * width * width * 200
    home_side, sums = call(
        own_contacts,
        [struct((nblocks + 1) * 32, width), struct((nblocks + 1) * 16, width)],
        [HBM] * 2 + [VMEM],
        sides(nblocks) + lists + [ints(tiles)] * 2 + [pltpu.SemaphoreType.DMA((2,))],
        "own_contacts",
        contact_flops,
    )(tile_home, tile_partner, state)
    updated, outgoing, diffused, goals = call(
        functools.partial(ghost_contacts, nbrick, cap, 4 * per),
        [struct(3, nblocks, width), struct(nbrick * 3 * chunk, width), struct(3, nx, ny, nz)]
        + [struct(nblocks, dtype=jnp.int32)],
        [HBM] * 3 + [VMEM] * 8 + [HBM],
        sides(4 * per)
        + [pltpu.VMEM(((nblocks + 1) * 16, width), f32)]
        + lists
        + [ints(codes), ints(tiles), ints(tiles), ints(nblocks)]
        + [pltpu.VMEM((3, nx, ny, nz), f32), pltpu.SemaphoreType.DMA((4,))],
        "ghost_contacts",
        contact_flops // 2,
        places=[VMEM] * 3 + [SMEM],
    )(tile_home, tile_partner, routes, below, above, before, after,
      home_side, sums, state, cell_of, fluid)

    crossed = lax.all_to_all(
        outgoing.reshape(nbrick, 3 * chunk, width), "brick", split_axis=0, concat_axis=0, tiled=True
    )
    from_above = shifted(crossed[:, 0:chunk], "slab", -1).reshape(nbrick * chunk, width)
    from_below = shifted(crossed[:, 2 * chunk :], "slab", 1).reshape(nbrick * chunk, width)
    crossed = crossed.reshape(nbrick * 3 * chunk, width)

    def places(count):
        return [ints(count + GROUP)] * 2

    block_flops = 16 * columns * nz * width
    (started,) = call(
        functools.partial(first_deposit, nbrick, cap),
        [struct(4 * columns, nz)],
        [VMEM],
        places(nbrick * cap),
        "first_deposit",
        block_flops * nblocks // 3,
    )(crossed)
    fluid_next, table, answers_up, answers_down = call(
        functools.partial(advance, nbrick, cap),
        [
            struct(3, nx, ny, nz),
            struct(3 * columns, 2 * nz, dtype=bf16),
            struct(nbrick * back, width),
            struct(nbrick * back, width),
        ],
        [VMEM] * 3 + [HBM, VMEM],
        [
            pltpu.VMEM((2 * nbrick * chunk, width), f32),
            pltpu.VMEM((2 * nbrick * back, width), f32),
            pltpu.VMEM((4 * columns, nz), f32),
        ]
        + [pltpu.VMEM((3, nx, ny, nz), f32)] * 2
        + places(2 * nbrick * cap)
        + [pltpu.SemaphoreType.DMA((2,))],
        "advance",
        block_flops * nblocks,
        places=[HBM] + [VMEM] * 3,
    )(from_above, from_below, started, fluid, diffused)
    answers_up = shifted(answers_up.reshape(nbrick, back, width), "slab", 1)
    answers_down = shifted(answers_down.reshape(nbrick, back, width), "slab", -1)
    (answers,) = call(
        functools.partial(last_sample, nbrick, cap),
        [struct(nbrick * back, width)],
        [VMEM] * 2,
        places(nbrick * cap),
        "last_sample",
        block_flops * nblocks // 4,
    )(crossed, table)
    answers = jnp.concatenate(
        [answers_up, answers.reshape(nbrick, back, width), answers_down], axis=1
    )
    returned = lax.all_to_all(answers, "brick", split_axis=0, concat_axis=0, tiled=True)
    (velocity_next,) = call(
        functools.partial(relax, cap),
        [struct(3, nblocks, width)],
        [SMEM] + [VMEM] * 2,
        [pltpu.VMEM((3, nblocks, width), f32)],
        "relax",
    )(goals, updated, returned.reshape(nbrick * 3 * back, width))
    return (jnp.transpose(velocity_next, (1, 0, 2)), fluid_next)


def solution(mesh):
    placed = (
        P(("slab", "brick"), None, None),
        P(("slab", "brick"), None, None),
        P(("slab", "brick"), None),
        P(("slab", "brick"), None),
        P(("slab", "brick"), None),
        P(("slab", "brick")),
        P(("slab", "brick")),
        P(("slab", "brick")),
        P(None, "slab", "brick", None),
    )
    return jax.shard_map(
        on_device,
        mesh=mesh,
        in_specs=placed,
        out_specs=(P(("slab", "brick"), None, None), P(None, "slab", "brick", None)),
        check_vma=False,
    )
```

```python
import functools
import math

import jax
import jax.numpy as jnp
from jax import lax
from jax.experimental import pallas as pl
from jax.experimental.pallas import tpu as pltpu
from jax.sharding import PartitionSpec as P

stiffness = 0.01
damping = 0.005
viscosity = 0.1
coupling = 0.5
relaxation = 0.5

f32 = jnp.float32
bf16 = jnp.bfloat16
VMEM = pl.BlockSpec(memory_space=pltpu.VMEM)
SMEM = pl.BlockSpec(memory_space=pltpu.SMEM)
ANY = pl.BlockSpec(memory_space=pl.ANY)
HBM = pl.BlockSpec(memory_space=pltpu.HBM)
UNROLL = 8
GROUP = 4


def rows_up(count):
    return -(-count // 8) * 8


def call(body, outs, ins, scratch, name, flops=0, nbytes=1 << 20, places=None):
    return pl.pallas_call(
        body,
        out_shape=outs,
        in_specs=ins,
        out_specs=places or [VMEM] * len(outs),
        scratch_shapes=scratch,
        name=name,
        compiler_params=pltpu.CompilerParams(vmem_limit_bytes=40 << 20),
        cost_estimate=pl.CostEstimate(flops=flops, bytes_accessed=nbytes, transcendentals=0),
    )


def rounded(x):
    return x.astype(bf16).astype(f32)


def iota(shape, dim):
    return lax.broadcasted_iota(jnp.int32, shape, dim)


planes = 7


def copy_all(pairs, sems):
    copies = [pltpu.make_async_copy(*pair, sems.at[i]) for i, pair in enumerate(pairs)]
    for copy in copies:
        copy.start()
    return copies


def wait_all(copies):
    for copy in copies:
        copy.wait()


def pack_kernel(ghost_ref, state, fluid, up, down, right, left):
    count = ghost_ref.shape[0] // 4
    width = state.shape[2]
    nx, ny, nz = fluid.shape[1:]
    for group in range(4):
        i, j = group // 2, group % 2
        slab_to, brick_to = (up if i else down), (right if j else left)
        for g in range(count):
            block = pl.ds(ghost_ref[group * count + g], 1)
            for c in range(planes):
                row = state[c, block, :]
                at = c * 2 * count + j * count + g
                slab_to[at : at + 1, :] = row
                at = c * 2 * count + i * count + g
                brick_to[at : at + 1, :] = row
    for slab_to, x in ((up, nx - 1), (down, 0)):
        for c in range(3):
            for k in range(nz // width):
                at = planes * 2 * count + (c * (nz // width) + k) * ny
                slab_to[at : at + ny, :] = fluid[c, x, :, k * width : (k + 1) * width]
    for brick_to, y in ((right, ny - 1), (left, 0)):
        for c in range(3):
            for x in range(nx):
                for k in range(nz // width):
                    at = planes * 2 * count + (c * nx + x) * (nz // width) + k
                    brick_to[at : at + 1, :] = fluid[
                        c, x, y : y + 1, k * width : (k + 1) * width
                    ]


def three_parts(x):
    one = rounded(x)
    rest = x - one
    two = rounded(rest)
    return one, two, rest - two


def put_rows(ref, stride, rows):
    count = rows[0].shape[0]
    for k, row in enumerate(rows):
        ref[pl.ds(k, count, stride=stride), :] = row


def pair_factors(place):
    parts = [three_parts(plane) for plane in place]
    own = three_parts(
        place[3] * place[3] - place[0] * place[0] - place[1] * place[1] - place[2] * place[2]
    )
    return [[part[k] for part in parts] for k in range(3)], list(own)


def home_rows(place):
    (one, two, three), own = pair_factors(place)
    ones, zeros = jnp.ones_like(place[0]), jnp.zeros_like(place[0])
    rows = one + one + two + two + one + three
    return [2.0 * row for row in rows] + own + [ones] * 3 + [zeros] * 2


def partner_rows(place):
    (one, two, three), own = pair_factors(place)
    ones, zeros = jnp.ones_like(place[0]), jnp.zeros_like(place[0])
    return one + two + one + two + three + one + [ones] * 3 + own + [zeros] * 2


def value_rows(values):
    highs = [rounded(plane) for plane in values]
    ones, zeros = jnp.ones_like(values[0]), jnp.zeros_like(values[0])
    lows = [plane - high for plane, high in zip(values, highs)]
    return highs + [ones, zeros] + lows + [zeros, zeros]


def prepare_partners(place, speeds, rows, columns, values):
    count, width = place[0].shape
    put_rows(rows, 32, partner_rows(place))
    put_rows(values, 16, value_rows(place[0:3] + speeds))

    def turn(b, _):
        block = rows[pl.ds(pl.multiple_of(b * 32, 32), 32), :]
        columns[b] = jnp.transpose(block).astype(bf16)
        return 0

    lax.fori_loop(0, count, turn, 0, unroll=4)


def list_tiles(home_ref, partner_ref, homes, partners, lower, upper, spare):
    def one(t, count):
        partner = partner_ref[t]
        homes[count] = home_ref[t]
        partners[count] = partner - lower
        return count + jnp.where((partner >= lower) & (partner < upper), 1, 0)

    count = lax.fori_loop(0, home_ref.shape[0], one, 0, unroll=4)
    for pad in range(UNROLL):
        homes[count + pad] = spare
        partners[count + pad] = 0
    return count


def add_tiles(count, homes, partners, home_side, partner_side, values, sums):
    def some(step, _):
        for k in range(UNROLL):
            home = homes[step * UNROLL + k]
            partner = partners[step * UNROLL + k]
            factors = home_side[pl.ds(pl.multiple_of(home * 32, 32), 32), :].astype(bf16)
            weight = jnp.dot(partner_side[partner], factors, preferred_element_type=f32)
            weight = jnp.maximum(weight, 0.0)
            high = weight.astype(bf16)
            low = (weight - high.astype(f32)).astype(bf16)
            value = values[pl.ds(pl.multiple_of(partner * 16, 16), 16), :].astype(bf16)
            at = pl.ds(pl.multiple_of(home * 16, 16), 16)
            sums[at, :] += jnp.dot(
                jnp.concatenate([value, value], axis=1),
                jnp.concatenate([high, low], axis=0),
                preferred_element_type=f32,
            )
        return 0

    lax.fori_loop(0, (count + UNROLL - 1) // UNROLL, some, 0)


def dot(left, right):
    return jnp.dot(left.astype(bf16), right.astype(bf16), preferred_element_type=f32)


def plan_sort(codes, cell, route, columns, depth, spots, plan, bounds):
    nblocks, width = cell.shape
    shift = depth.bit_length() - 1
    number = cell[...]
    right = (number >> shift) >= columns // 2
    deep = (number & (depth - 1)) >= depth // 2
    kind = jnp.where(right, 2, 0) + jnp.where(deep, 1, 0)
    members = [jnp.where(kind == j, 1.0, 0.0) for j in range(4)]
    before = jnp.where(iota((width, width), 0) < iota((width, width), 1), 1.0, 0.0)
    stacked = jnp.concatenate(members, axis=0)
    ranks = dot(stacked, before)
    lengths = dot(stacked, jnp.ones((width, width), f32))
    ranks = [ranks[j * nblocks : (j + 1) * nblocks] for j in range(4)]
    lengths = [lengths[j * nblocks : (j + 1) * nblocks] for j in range(4)]

    across = jnp.broadcast_to(route[...].astype(f32), (nblocks, nblocks))
    same = across == jnp.transpose(across)
    earlier = iota((nblocks, nblocks), 1) < iota((nblocks, nblocks), 0)
    side_by_side = jnp.concatenate(lengths, axis=1)
    ahead = dot(jnp.where(same & earlier, 1.0, 0.0), side_by_side)
    whole = dot(jnp.where(same, 1.0, 0.0), side_by_side)
    rows = bounds.shape[0]
    of_code = jnp.broadcast_to(route[...], (rows, nblocks)) == iota((rows, nblocks), 0)
    totals = dot(jnp.where(of_code, 1.0, 0.0), side_by_side)

    lane = iota((nblocks, width), 1)
    bound_lane = iota((rows, width), 1)
    spot = jnp.zeros((nblocks, width), f32)
    first, chunk_first = jnp.zeros((nblocks, width), f32), jnp.zeros((nblocks, width), f32)
    bound, line = jnp.zeros((rows, width), f32), jnp.zeros((rows, width), f32)
    table = jnp.zeros((nblocks, width), f32)
    for j in range(4):
        at = slice(j * width, (j + 1) * width)
        spot = spot + members[j] * (first + ranks[j])
        table = jnp.where(lane == j, chunk_first + ahead[:, at], table)
        table = jnp.where(lane == 4 + j, first, table)
        table = jnp.where(lane == 8 + j, lengths[j], table)
        first = first + lengths[j]
        chunk_first = chunk_first + whole[:, at]
        bound = bound + totals[:, at]
        line = jnp.where(bound_lane == j, bound, line)
    spots[...] = spot
    plan[...] = table.astype(jnp.int32)
    bounds[...] = line


def place_of(plan, b, j, width):
    at = plan[b, j]
    return at // width, at % width, plan[b, 4 + j], plan[b, 8 + j]


def block_order(spots, b):
    width = spots.shape[1]
    row = jnp.broadcast_to(spots[pl.ds(b, 1), :], (width, width))
    return jnp.where(iota((width, width), 0).astype(f32) == row, 1.0, 0.0).astype(bf16)


def sort_blocks(route_ref, plan, spots, data, tiles, cap):
    nblocks, width = spots.shape
    lane = iota((8, width), 1)

    def one(b, _):
        rows = data[pl.ds(pl.multiple_of(b * 16, 16), 16), :].astype(bf16)
        both = lax.dot_general(
            rows, block_order(spots, b), (((1,), (1,)), ((), ())), preferred_element_type=f32
        )
        block = both[0:8] + both[8:16]
        chunk = route_ref[b] * (cap + 2)
        for j in range(4):
            tile, at, first, length = place_of(plan, b, j, width)
            moved = pltpu.roll(block, (at - first + width) % width, 1)
            now, later = chunk + tile, chunk + tile + 1
            tiles[now] = jnp.where((lane >= at) & (lane < at + length), moved, tiles[now])
            tiles[later] = jnp.where(lane < at + length - width, moved, tiles[later])
        return 0

    lax.fori_loop(0, nblocks, one, 0, unroll=4)


def own_contacts(codes, columns, depth, home_list, partner_list, state, cell, route,
                 home_side, sums, spots, plan, bounds,
                 rows, partner_side, values, homes, partners, home_ref, partner_ref, sems):
    nblocks, width = state.shape[1:]
    copies = copy_all([(home_list, home_ref), (partner_list, partner_ref)], sems)
    plan_sort(codes, cell, route, columns, depth, spots, plan, bounds)
    place = [state[c] for c in range(4)]
    put_rows(home_side, 32, home_rows(place))
    prepare_partners(place, [state[c] for c in (4, 5, 6)], rows, partner_side, values)
    home_side[nblocks * 32 :, :] = jnp.zeros((32, width), f32)
    sums[...] = jnp.zeros(sums.shape, f32)
    wait_all(copies)
    count = list_tiles(home_ref, partner_ref, homes, partners, 0, nblocks, nblocks)
    add_tiles(count, homes, partners, home_side, partner_side, values, sums)


def diffuse(fluid, below, above, before, after, skip, diffused):
    nx, ny, nz = fluid.shape[1:]
    width = before.shape[1]
    deep = iota((ny, nz), 1)

    def face(ref, c, x):
        at = skip + (c * nx + x) * (nz // width)
        return jnp.concatenate(
            [ref[at + k : at + k + 1, :] for k in range(nz // width)], axis=1
        )

    def layer(ref, c):
        at = [skip + (c * (nz // width) + k) * ny for k in range(nz // width)]
        return jnp.concatenate([ref[start : start + ny, :] for start in at], axis=1)

    for x in range(nx):
        for c in range(3):
            here = fluid[c, x]
            near = (layer(below, c) if x == 0 else fluid[c, x - 1]) + (
                layer(above, c) if x == nx - 1 else fluid[c, x + 1]
            )
            near = near + jnp.concatenate([face(before, c, x), here[:-1]], axis=0)
            near = near + jnp.concatenate([here[1:], face(after, c, x)], axis=0)
            near = near + jnp.where(deep == 0, 0.0, pltpu.roll(here, 1, 1))
            near = near + jnp.where(deep == nz - 1, 0.0, pltpu.roll(here, nz - 1, 1))
            diffused[c, x] = here + viscosity * (near - 6.0 * here)


def ghost_contacts(nbrick, cap, partner_blocks, home_list, partner_list, routes, plan, below,
                   above, before, after, home_side, own_sums, state, cell, spots, bounds, fluid,
                   updated, outgoing, diffused,
                   rows, columns, values, sums, data, tiles, homes, partners,
                   home_ref, partner_ref, route_ref, plan_ref, flow, sems):
    nblocks, width = state.shape[1:]
    per = partner_blocks // 4
    copies = copy_all(
        [
            (home_list, home_ref),
            (partner_list, partner_ref),
            (routes, route_ref),
            (plan, plan_ref),
            (fluid, flow),
        ],
        sems,
    )
    stacked = [
        jnp.concatenate(
            [ref[c * per : (c + 1) * per, :] for ref in (below, above, before, after)], axis=0
        )
        for c in range(planes)
    ]
    prepare_partners(stacked[0:4], stacked[4:7], rows, columns, values)
    sums[...] = own_sums[...]
    wait_all(copies)
    count = list_tiles(home_ref, partner_ref, homes, partners, nblocks, nblocks + 4 * per, nblocks)
    add_tiles(count, homes, partners, home_side, columns, values, sums)
    diffuse(flow, below, above, before, after, planes * per, diffused)

    def total(k):
        high = sums[pl.ds(k, nblocks, stride=16), :]
        return high + sums[pl.ds(k + 8, nblocks, stride=16), :]

    weights = total(6)
    radius = state[3]
    inverse = 1.0 / (radius * radius * radius)
    fresh = []
    for c in range(3):
        speed = state[c + 4]
        spring = state[c] * weights - total(c)
        friction = total(c + 3) - speed * weights
        fresh.append(speed + (stiffness * spring + damping * friction) * inverse)
        updated[c] = fresh[c]

    number = cell[...]
    zeros = jnp.zeros_like(radius)
    highs = [rounded(plane) for plane in [radius] + fresh]
    lows = [plane - high for plane, high in zip([radius] + fresh, highs)]
    highs.append(((number >> 8) * 256).astype(f32))
    lows.append((number & 255).astype(f32))
    put_rows(data, 16, highs + [zeros] * 3 + lows + [zeros] * 3)
    sort_blocks(route_ref, plan_ref, spots, data, tiles, cap)

    chunk = rows_up(5 * cap + 1)
    flat = tiles.reshape(tiles.shape[0] * 8, width)
    for code in range(3 * nbrick):
        row = ((code % nbrick) * 3 + code // nbrick) * chunk
        for c in range(5):
            outgoing[row + c * cap : row + (c + 1) * cap, :] = flat[
                pl.ds(code * (cap + 2) * 8 + c, cap, stride=8), :
            ]
        outgoing[row + 5 * cap : row + 5 * cap + 1, :] = bounds[code : code + 1, :]


def list_stride(segments, cap):
    return (segments + 1) * cap + GROUP


def list_arrived(arrived, starts, ends, cap, places, counts):
    base, goal = places
    width = arrived.shape[1]
    stride = list_stride(len(starts), cap)
    lane = iota((1, width), 1)
    filled = [jnp.int32(0)] * 4
    for start, end in zip(starts, ends):
        row = arrived[start + 5 * cap : start + 5 * cap + 1, :]
        edge = jnp.int32(0)
        for j in range(4):
            next_edge = jnp.sum(jnp.where(lane == j, row, 0.0)).astype(jnp.int32)
            first = edge // width
            last = jnp.where(next_edge > edge, (next_edge + width - 1) // width, first)
            for i in range(cap):
                base[j * stride + filled[j] + i] = start + first + i
                goal[j * stride + filled[j] + i] = end + first + i
            filled[j] = filled[j] + last - first
            edge = next_edge
    for j in range(4):
        counts[j] = filled[j]
        last = j * stride + jnp.maximum(filled[j] - 1, 0)
        for pad in range(GROUP):
            base[j * stride + filled[j] + pad] = base[last]
            goal[j * stride + filled[j] + pad] = goal[last]


def cell_parts(arrived, row, cap, columns, depth, bucket):
    cell = arrived[pl.ds(row + 4 * cap, 1), :].astype(jnp.int32)
    shift = (2 * depth).bit_length() - 1
    column = (cell >> shift) - (bucket // 2) * columns
    level = (cell & (2 * depth - 1)) - (bucket % 2) * depth - depth // 2
    return column.astype(f32), level.astype(f32)


def all_levels(depth, width):
    return (iota((depth, width), 0) - depth // 2).astype(f32).astype(bf16)


def level_hot(level, levels):
    hit = levels == jnp.broadcast_to(level.astype(bf16), levels.shape)
    return jnp.where(hit, jnp.ones((), bf16), jnp.zeros((), bf16))


def deposit(segments, counts, arrived, base, cap, total):
    columns, depth = total.shape[0] // 16, total.shape[1]
    width = arrived.shape[1]
    stride = list_stride(segments, cap)
    numbers = iota((columns, width), 0).astype(f32).astype(bf16)
    levels = all_levels(depth, width)

    def one(bucket, _):
        count = counts[bucket]

        def some(step, _):
            high_of, low_of, level_of = [], [], []
            for k in range(GROUP):
                index = step * GROUP + k
                row = base[bucket * stride + index]
                column, level = cell_parts(arrived, row, cap, columns, depth, bucket)
                radius = arrived[pl.ds(row, 1), :]
                mass = radius * radius * radius * jnp.where(index < count, 1.0, 0.0)
                loads = [mass] + [mass * arrived[pl.ds(row + c * cap, 1), :] for c in (1, 2, 3)]
                hit = numbers == jnp.broadcast_to(column.astype(bf16), (columns, width))
                highs, lows = [], []
                for load in loads:
                    high = load.astype(bf16)
                    low = (load - high.astype(f32)).astype(bf16)
                    for parts, part in ((highs, high), (lows, low)):
                        part = jnp.broadcast_to(part, (columns, width))
                        parts.append(jnp.where(hit, part, jnp.zeros((), bf16)))
                high_of.append(jnp.concatenate(highs, axis=0))
                low_of.append(jnp.concatenate(lows, axis=0))
                level_of.append(level_hot(level, levels))
            both = lax.dot_general(
                jnp.concatenate(
                    [jnp.concatenate(high_of, axis=1), jnp.concatenate(low_of, axis=1)], axis=0
                ),
                jnp.concatenate(level_of, axis=1),
                (((1,), (1,)), ((), ())),
                preferred_element_type=f32,
            )
            at = pl.ds(pl.multiple_of(bucket * 4 * columns, 4 * columns), 4 * columns)
            total[at, :] += both[0 : 4 * columns] + both[4 * columns :]
            return 0

        lax.fori_loop(0, (count + GROUP - 1) // GROUP, some, 0)
        return 0

    lax.fori_loop(0, 4, one, 0)


def sample(segments, counts, arrived, places, cap, table, answers):
    columns, depth = table.shape[0] // 24, table.shape[1]
    width = arrived.shape[1]
    stride = list_stride(segments, cap)
    levels = all_levels(depth, width)
    numbers = iota((columns, width), 0).astype(f32)
    answers[...] = jnp.zeros(answers.shape, f32)

    def one(bucket, _):
        count = counts[bucket]

        def some(step, _):
            hots, hits = [], []
            for k in range(GROUP):
                row = places[0][bucket * stride + step * GROUP + k]
                column, level = cell_parts(arrived, row, cap, columns, depth, bucket)
                hots.append(level_hot(level, levels))
                hits.append(numbers == column)
            at = pl.ds(pl.multiple_of(bucket * 6 * columns, 6 * columns), 6 * columns)
            along = jnp.dot(
                table[at, :], jnp.concatenate(hots, axis=1), preferred_element_type=f32
            )
            for k in range(GROUP):
                index = step * GROUP + k
                goal = places[1][bucket * stride + index]
                real = jnp.where(index < count, 1.0, 0.0)
                part = along[:, k * width : (k + 1) * width]
                for c in range(3):
                    value = part[c * columns : (c + 1) * columns]
                    value = value + part[(c + 3) * columns : (c + 4) * columns]
                    found = jnp.sum(jnp.where(hits[k], value, 0.0), axis=0, keepdims=True)
                    answers[pl.ds(goal + c * cap, 1), :] += found * real
            return 0

        lax.fori_loop(0, (count + GROUP - 1) // GROUP, some, 0)
        return 0

    lax.fori_loop(0, 4, one, 0)


def first_deposit(nbrick, cap, crossed, total, base, goal, counts):
    chunk = rows_up(5 * cap + 1)
    total[...] = jnp.zeros(total.shape, f32)
    starts = [(3 * b + 1) * chunk for b in range(nbrick)]
    list_arrived(crossed, starts, starts, cap, (base, goal), counts)
    deposit(nbrick, counts, crossed, base, cap, total)


def advance(nbrick, cap, above, below, start, fluid, diffused, fluid_next, table, answers_up,
            answers_down, arrived, answers, total, flow, fresh_flow, base, goal, counts, sems):
    reading = pltpu.make_async_copy(fluid, flow, sems.at[0])
    reading.start()
    chunk = rows_up(5 * cap + 1)
    back = rows_up(3 * cap)
    rows = nbrick * chunk
    arrived[0:rows, :] = above[...]
    arrived[rows:, :] = below[...]
    starts = [i * chunk for i in range(2 * nbrick)]
    ends = [i * back for i in range(2 * nbrick)]
    total[...] = start[...]
    list_arrived(arrived, starts, ends, cap, (base, goal), counts)
    deposit(2 * nbrick, counts, arrived, base, cap, total)
    reading.wait()

    nx, ny, nz = flow.shape[1:]
    columns, depth = nx * ny // 2, nz // 2
    for x in range(nx):
        buckets = [2 * (x * ny // columns) + deep for deep in range(2)]
        at = x * ny % columns

        def load(c):
            spots = [4 * columns * bucket + c * columns + at for bucket in buckets]
            return jnp.concatenate([total[spot : spot + ny, :] for spot in spots], axis=1)

        volume = load(0)
        for c in range(3):
            moved = load(c + 1) - volume * flow[c, x]
            fresh = diffused[c, x] + coupling * moved
            fresh_flow[c, x] = fresh
            high = fresh.astype(bf16)
            low = (fresh - high.astype(f32)).astype(bf16)
            for deep, bucket in enumerate(buckets):
                spot = 6 * columns * bucket + c * columns + at
                half = slice(deep * depth, (deep + 1) * depth)
                table[spot : spot + ny, :] = high[:, half]
                table[spot + 3 * columns : spot + 3 * columns + ny, :] = low[:, half]
    writing = pltpu.make_async_copy(fresh_flow, fluid_next, sems.at[1])
    writing.start()
    sample(2 * nbrick, counts, arrived, (base, goal), cap, table, answers)
    answers_up[...] = answers[0 : nbrick * back, :]
    answers_down[...] = answers[nbrick * back :, :]
    writing.wait()


def last_sample(nbrick, cap, crossed, table, answers, base, goal, counts):
    chunk = rows_up(5 * cap + 1)
    back = rows_up(3 * cap)
    starts = [(3 * b + 1) * chunk for b in range(nbrick)]
    ends = [b * back for b in range(nbrick)]
    list_arrived(crossed, starts, ends, cap, (base, goal), counts)
    sample(nbrick, counts, crossed, (base, goal), cap, table, answers)


def relax(nbrick, cap, route_ref, plan, updated, returned, spots, velocity_next, picked, tiles,
          plan_ref, sems):
    copies = copy_all([(plan, plan_ref)], sems)
    nblocks, width = spots.shape
    back = rows_up(3 * cap)
    flat = tiles.reshape(tiles.shape[0] * 8, width)
    for code in range(3 * nbrick):
        row = ((code % nbrick) * 3 + code // nbrick) * back
        for c in range(3):
            flat[pl.ds(code * (cap + 2) * 8 + c, cap, stride=8), :] = returned[
                row + c * cap : row + (c + 1) * cap, :
            ]
    lane = iota((8, width), 1)
    wait_all(copies)

    def one(b, _):
        chunk = route_ref[b] * (cap + 2)
        block = jnp.zeros((8, width), f32)
        for j in range(4):
            tile, at, first, length = place_of(plan_ref, b, j, width)
            run = jnp.where(lane >= at, tiles[chunk + tile], tiles[chunk + tile + 1])
            run = pltpu.roll(run, (first - at + width) % width, 1)
            block = jnp.where((lane >= first) & (lane < first + length), run, block)
        high = rounded(block)
        both = jnp.dot(
            jnp.concatenate([high, block - high], axis=0).astype(bf16),
            block_order(spots, b),
            preferred_element_type=f32,
        )
        block = both[0:8] + both[8:16]
        for c in range(3):
            picked[c, pl.ds(b, 1), :] = block[c : c + 1]
        return 0

    lax.fori_loop(0, nblocks, one, 0, unroll=4)
    now = updated[...]
    velocity_next[...] = now + relaxation * (picked[...] - now)


def on_device(
    positions, velocities, radii, cell_of, block_route, ghost_list, tile_home, tile_partner, fluid
):
    nblocks, _, width = positions.shape
    nbrick = lax.axis_size("brick")
    _, nx, ny, nz = fluid.shape
    columns = nx * ny
    codes = 3 * nbrick
    cap = max(2, (2 * nblocks + codes - 1) // codes)
    chunk, back = rows_up(5 * cap + 1), rows_up(3 * cap)
    per = ghost_list.shape[0] // 2
    tiles = tile_home.shape[0]
    routes = block_route.reshape(-1)
    positions = jnp.transpose(positions, (1, 0, 2))
    velocities = jnp.transpose(velocities, (1, 0, 2))

    def struct(*shape, dtype=f32):
        return jax.ShapeDtypeStruct(shape, dtype)

    def shifted(x, axis, step):
        count = lax.axis_size(axis)
        return lax.ppermute(x, axis, [(i, (i + step) % count) for i in range(count)])

    def ints(count):
        return pltpu.SMEM((count,), jnp.int32)

    state = jnp.concatenate([positions, radii[None], velocities], axis=0)
    ghost_rows, chunks = planes * per, 3 * (nz // width)
    up, down, right, left = call(
        pack_kernel,
        [struct(ghost_rows + chunks * ny, width)] * 2 + [struct(ghost_rows + chunks * nx, width)] * 2,
        [SMEM] + [VMEM] * 2,
        [],
        "pack",
    )(ghost_list, state, fluid)
    below = shifted(up, "slab", 1)
    above = shifted(down, "slab", -1)
    before = shifted(right, "brick", 1)
    after = shifted(left, "brick", -1)

    def sides(count):
        return [
            pltpu.VMEM((count * 32, width), f32),
            pltpu.VMEM((count, width, 32), bf16),
            pltpu.VMEM((count * 16, width), f32),
        ]

    lists = [ints(tiles + UNROLL)] * 2
    contact_flops = tiles * width * width * 200
    chunk_tiles = pltpu.VMEM((codes * (cap + 2), 8, width), f32)
    plan_copy = pltpu.SMEM((nblocks, width), jnp.int32)
    home_side, sums, spots, plan, bounds = call(
        functools.partial(own_contacts, codes, columns, nz),
        [
            struct((nblocks + 1) * 32, width),
            struct((nblocks + 1) * 16, width),
            struct(nblocks, width),
            struct(nblocks, width, dtype=jnp.int32),
            struct(rows_up(codes), width),
        ],
        [HBM] * 2 + [VMEM] * 3,
        sides(nblocks) + lists + [ints(tiles)] * 2 + [pltpu.SemaphoreType.DMA((2,))],
        "own_contacts",
        contact_flops,
    )(tile_home, tile_partner, state, cell_of, routes.reshape(1, nblocks))
    updated, outgoing, diffused = call(
        functools.partial(ghost_contacts, nbrick, cap, 4 * per),
        [struct(3, nblocks, width), struct(nbrick * 3 * chunk, width), struct(3, nx, ny, nz)],
        [HBM] * 3 + [ANY] + [VMEM] * 10 + [HBM],
        sides(4 * per)
        + [pltpu.VMEM(((nblocks + 1) * 16, width), f32)]
        + [pltpu.VMEM((nblocks * 16, width), f32), chunk_tiles]
        + lists
        + [ints(tiles), ints(tiles), ints(nblocks), plan_copy]
        + [pltpu.VMEM((3, nx, ny, nz), f32), pltpu.SemaphoreType.DMA((5,))],
        "ghost_contacts",
        contact_flops // 2,
    )(tile_home, tile_partner, routes, plan, below, above, before, after,
      home_side, sums, state, cell_of, spots, bounds, fluid)

    crossed = lax.all_to_all(
        outgoing.reshape(nbrick, 3 * chunk, width), "brick", split_axis=0, concat_axis=0, tiled=True
    )
    from_above = shifted(crossed[:, 0:chunk], "slab", -1).reshape(nbrick * chunk, width)
    from_below = shifted(crossed[:, 2 * chunk :], "slab", 1).reshape(nbrick * chunk, width)
    crossed = crossed.reshape(nbrick * 3 * chunk, width)

    def places(count):
        return [ints(4 * list_stride(count, cap))] * 2 + [ints(4)]

    block_flops = 8 * columns * nz * width
    (started,) = call(
        functools.partial(first_deposit, nbrick, cap),
        [struct(8 * columns, nz // 2)],
        [VMEM],
        places(nbrick),
        "first_deposit",
        block_flops * nblocks // 3,
    )(crossed)
    fluid_next, table, answers_up, answers_down = call(
        functools.partial(advance, nbrick, cap),
        [
            struct(3, nx, ny, nz),
            struct(12 * columns, nz // 2, dtype=bf16),
            struct(nbrick * back, width),
            struct(nbrick * back, width),
        ],
        [VMEM] * 3 + [HBM, VMEM],
        [
            pltpu.VMEM((2 * nbrick * chunk, width), f32),
            pltpu.VMEM((2 * nbrick * back, width), f32),
            pltpu.VMEM((8 * columns, nz // 2), f32),
        ]
        + [pltpu.VMEM((3, nx, ny, nz), f32)] * 2
        + places(2 * nbrick)
        + [pltpu.SemaphoreType.DMA((2,))],
        "advance",
        block_flops * nblocks,
        places=[HBM] + [VMEM] * 3,
    )(from_above, from_below, started, fluid, diffused)
    answers_up = shifted(answers_up.reshape(nbrick, back, width), "slab", 1)
    answers_down = shifted(answers_down.reshape(nbrick, back, width), "slab", -1)
    (answers,) = call(
        functools.partial(last_sample, nbrick, cap),
        [struct(nbrick * back, width)],
        [VMEM] * 2,
        places(nbrick),
        "last_sample",
        block_flops * nblocks // 4,
    )(crossed, table)
    answers = jnp.concatenate(
        [answers_up, answers.reshape(nbrick, back, width), answers_down], axis=1
    )
    returned = lax.all_to_all(answers, "brick", split_axis=0, concat_axis=0, tiled=True)
    (velocity_next,) = call(
        functools.partial(relax, nbrick, cap),
        [struct(3, nblocks, width)],
        [SMEM, ANY] + [VMEM] * 3,
        [pltpu.VMEM((3, nblocks, width), f32), chunk_tiles, plan_copy]
        + [pltpu.SemaphoreType.DMA((1,))],
        "relax",
    )(routes, plan, updated, returned.reshape(nbrick * 3 * back, width), spots)
    return (jnp.transpose(velocity_next, (1, 0, 2)), fluid_next)


def solution(mesh):
    placed = (
        P(("slab", "brick"), None, None),
        P(("slab", "brick"), None, None),
        P(("slab", "brick"), None),
        P(("slab", "brick"), None),
        P(("slab", "brick"), None),
        P(("slab", "brick")),
        P(("slab", "brick")),
        P(("slab", "brick")),
        P(None, "slab", "brick", None),
    )
    return jax.shard_map(
        on_device,
        mesh=mesh,
        in_specs=placed,
        out_specs=(P(("slab", "brick"), None, None), P(None, "slab", "brick", None)),
        check_vma=False,
    )
```

```python
import functools
import math

import jax
import jax.numpy as jnp
from jax import lax
from jax.experimental import pallas as pl
from jax.experimental.pallas import tpu as pltpu
from jax.sharding import PartitionSpec as P

stiffness = 0.01
damping = 0.005
viscosity = 0.1
coupling = 0.5
relaxation = 0.5

f32 = jnp.float32
bf16 = jnp.bfloat16
VMEM = pl.BlockSpec(memory_space=pltpu.VMEM)
SMEM = pl.BlockSpec(memory_space=pltpu.SMEM)
ANY = pl.BlockSpec(memory_space=pl.ANY)
HBM = pl.BlockSpec(memory_space=pltpu.HBM)
UNROLL = 8
GROUP = 2


def rows_up(count):
    return -(-count // 8) * 8


def call(body, outs, ins, scratch, name, flops=0, nbytes=1 << 20, places=None):
    return pl.pallas_call(
        body,
        out_shape=outs,
        in_specs=ins,
        out_specs=places or [VMEM] * len(outs),
        scratch_shapes=scratch,
        name=name,
        compiler_params=pltpu.CompilerParams(vmem_limit_bytes=40 << 20),
        cost_estimate=pl.CostEstimate(flops=flops, bytes_accessed=nbytes, transcendentals=0),
    )


def rounded(x):
    return x.astype(bf16).astype(f32)


def iota(shape, dim):
    return lax.broadcasted_iota(jnp.int32, shape, dim)


planes = 7


def copy_all(pairs, sems):
    copies = [pltpu.make_async_copy(*pair, sems.at[i]) for i, pair in enumerate(pairs)]
    for copy in copies:
        copy.start()
    return copies


def wait_all(copies):
    for copy in copies:
        copy.wait()


def pack_kernel(ghost_ref, state, fluid, up, down, right, left):
    count = ghost_ref.shape[0] // 4
    width = state.shape[2]
    nx, ny, nz = fluid.shape[1:]
    for group in range(4):
        i, j = group // 2, group % 2
        slab_to, brick_to = (up if i else down), (right if j else left)
        for g in range(count):
            block = pl.ds(ghost_ref[group * count + g], 1)
            for c in range(planes):
                row = state[c, block, :]
                at = c * 2 * count + j * count + g
                slab_to[at : at + 1, :] = row
                at = c * 2 * count + i * count + g
                brick_to[at : at + 1, :] = row
    for slab_to, x in ((up, nx - 1), (down, 0)):
        for c in range(3):
            for k in range(nz // width):
                at = planes * 2 * count + (c * (nz // width) + k) * ny
                slab_to[at : at + ny, :] = fluid[c, x, :, k * width : (k + 1) * width]
    for brick_to, y in ((right, ny - 1), (left, 0)):
        for c in range(3):
            for x in range(nx):
                for k in range(nz // width):
                    at = planes * 2 * count + (c * nx + x) * (nz // width) + k
                    brick_to[at : at + 1, :] = fluid[
                        c, x, y : y + 1, k * width : (k + 1) * width
                    ]


def three_parts(x):
    one = rounded(x)
    rest = x - one
    two = rounded(rest)
    return one, two, rest - two


def put_rows(ref, stride, rows):
    count = rows[0].shape[0]
    for k, row in enumerate(rows):
        ref[pl.ds(k, count, stride=stride), :] = row


def pair_factors(place):
    parts = [three_parts(plane) for plane in place]
    own = three_parts(
        place[3] * place[3] - place[0] * place[0] - place[1] * place[1] - place[2] * place[2]
    )
    return [[part[k] for part in parts] for k in range(3)], list(own)


def home_rows(place):
    (one, two, three), own = pair_factors(place)
    ones, zeros = jnp.ones_like(place[0]), jnp.zeros_like(place[0])
    rows = one + one + two + two + one + three
    return [2.0 * row for row in rows] + own + [ones] * 3 + [zeros] * 2


def partner_rows(place):
    (one, two, three), own = pair_factors(place)
    ones, zeros = jnp.ones_like(place[0]), jnp.zeros_like(place[0])
    return one + two + one + two + three + one + [ones] * 3 + own + [zeros] * 2


def value_rows(values):
    highs = [rounded(plane) for plane in values]
    ones, zeros = jnp.ones_like(values[0]), jnp.zeros_like(values[0])
    lows = [plane - high for plane, high in zip(values, highs)]
    return highs + [ones, zeros] + lows + [zeros, zeros]


def prepare_partners(place, speeds, rows, columns, values):
    count, width = place[0].shape
    put_rows(rows, 32, partner_rows(place))
    put_rows(values, 16, value_rows(place[0:3] + speeds))

    def turn(b, _):
        block = rows[pl.ds(pl.multiple_of(b * 32, 32), 32), :]
        columns[b] = jnp.transpose(block).astype(bf16)
        return 0

    lax.fori_loop(0, count, turn, 0, unroll=4)


def list_tiles(home_ref, partner_ref, homes, partners, lower, upper, spare):
    def one(t, count):
        partner = partner_ref[t]
        homes[count] = home_ref[t]
        partners[count] = partner - lower
        return count + jnp.where((partner >= lower) & (partner < upper), 1, 0)

    count = lax.fori_loop(0, home_ref.shape[0], one, 0, unroll=4)
    for pad in range(UNROLL):
        homes[count + pad] = spare
        partners[count + pad] = 0
    return count


def add_tiles(count, homes, partners, home_side, partner_side, values, sums):
    def some(step, _):
        for k in range(UNROLL):
            home = homes[step * UNROLL + k]
            partner = partners[step * UNROLL + k]
            factors = home_side[pl.ds(pl.multiple_of(home * 32, 32), 32), :].astype(bf16)
            weight = jnp.dot(partner_side[partner], factors, preferred_element_type=f32)
            weight = jnp.maximum(weight, 0.0)
            high = weight.astype(bf16)
            low = (weight - high.astype(f32)).astype(bf16)
            value = values[pl.ds(pl.multiple_of(partner * 16, 16), 16), :].astype(bf16)
            at = pl.ds(pl.multiple_of(home * 16, 16), 16)
            sums[at, :] += jnp.dot(
                jnp.concatenate([value, value], axis=1),
                jnp.concatenate([high, low], axis=0),
                preferred_element_type=f32,
            )
        return 0

    lax.fori_loop(0, (count + UNROLL - 1) // UNROLL, some, 0)


def dot(left, right):
    return jnp.dot(left.astype(bf16), right.astype(bf16), preferred_element_type=f32)


def plan_sort(codes, cell, route, columns, depth, spots, plan, bounds):
    nblocks, width = cell.shape
    shift = depth.bit_length() - 1
    number = cell[...]
    right = (number >> shift) >= columns // 2
    deep = (number & (depth - 1)) >= depth // 2
    kind = jnp.where(right, 2, 0) + jnp.where(deep, 1, 0)
    members = [jnp.where(kind == j, 1.0, 0.0) for j in range(4)]
    before = jnp.where(iota((width, width), 0) < iota((width, width), 1), 1.0, 0.0)
    stacked = jnp.concatenate(members, axis=0)
    ranks = dot(stacked, before)
    lengths = dot(stacked, jnp.ones((width, width), f32))
    ranks = [ranks[j * nblocks : (j + 1) * nblocks] for j in range(4)]
    lengths = [lengths[j * nblocks : (j + 1) * nblocks] for j in range(4)]

    across = jnp.broadcast_to(route[...].astype(f32), (nblocks, nblocks))
    same = across == jnp.transpose(across)
    earlier = iota((nblocks, nblocks), 1) < iota((nblocks, nblocks), 0)
    side_by_side = jnp.concatenate(lengths, axis=1)
    ahead = dot(jnp.where(same & earlier, 1.0, 0.0), side_by_side)
    whole = dot(jnp.where(same, 1.0, 0.0), side_by_side)
    rows = bounds.shape[0]
    of_code = jnp.broadcast_to(route[...], (rows, nblocks)) == iota((rows, nblocks), 0)
    totals = dot(jnp.where(of_code, 1.0, 0.0), side_by_side)

    lane = iota((nblocks, width), 1)
    bound_lane = iota((rows, width), 1)
    spot = jnp.zeros((nblocks, width), f32)
    first, chunk_first = jnp.zeros((nblocks, width), f32), jnp.zeros((nblocks, width), f32)
    bound, line = jnp.zeros((rows, width), f32), jnp.zeros((rows, width), f32)
    table = jnp.zeros((nblocks, width), f32)
    for j in range(4):
        at = slice(j * width, (j + 1) * width)
        spot = spot + members[j] * (first + ranks[j])
        table = jnp.where(lane == j, chunk_first + ahead[:, at], table)
        table = jnp.where(lane == 4 + j, first, table)
        table = jnp.where(lane == 8 + j, lengths[j], table)
        first = first + lengths[j]
        chunk_first = chunk_first + whole[:, at]
        bound = bound + totals[:, at]
        line = jnp.where(bound_lane == j, bound, line)
    spots[...] = spot
    plan[...] = table.astype(jnp.int32)
    bounds[...] = line


def place_of(plan, b, j, width):
    at = plan[b, j]
    return at // width, at % width, plan[b, 4 + j], plan[b, 8 + j]


def block_order(spots, b):
    width = spots.shape[1]
    row = jnp.broadcast_to(spots[pl.ds(b, 1), :], (width, width))
    return jnp.where(iota((width, width), 0).astype(f32) == row, 1.0, 0.0).astype(bf16)


def sort_blocks(route_ref, plan, spots, data, sorted_rows, tiles, cap):
    nblocks, width = spots.shape
    lane = iota((8, width), 1)

    def order(b, _):
        rows = data[pl.ds(pl.multiple_of(b * 16, 16), 16), :].astype(bf16)
        both = lax.dot_general(
            rows, block_order(spots, b), (((1,), (1,)), ((), ())), preferred_element_type=f32
        )
        sorted_rows[b] = both[0:8] + both[8:16]
        return 0

    def spread(b, _):
        block = sorted_rows[b]
        chunk = route_ref[b] * (cap + 2)
        for j in range(4):
            tile, at, first, length = place_of(plan, b, j, width)
            moved = pltpu.roll(block, (at - first + width) % width, 1)
            here = (lane >= at) & (lane < at + length)
            pltpu.store(tiles.at[chunk + tile], moved, mask=here)
            pltpu.store(tiles.at[chunk + tile + 1], moved, mask=lane < at + length - width)
        return 0

    lax.fori_loop(0, nblocks, order, 0, unroll=8)
    lax.fori_loop(0, nblocks, spread, 0, unroll=8)


def own_contacts(codes, columns, depth, home_list, partner_list, state, cell, route,
                 home_side, sums, spots, plan, bounds,
                 rows, partner_side, values, homes, partners, home_ref, partner_ref, sems):
    nblocks, width = state.shape[1:]
    copies = copy_all([(home_list, home_ref), (partner_list, partner_ref)], sems)
    plan_sort(codes, cell, route, columns, depth, spots, plan, bounds)
    place = [state[c] for c in range(4)]
    put_rows(home_side, 32, home_rows(place))
    prepare_partners(place, [state[c] for c in (4, 5, 6)], rows, partner_side, values)
    home_side[nblocks * 32 :, :] = jnp.zeros((32, width), f32)
    sums[...] = jnp.zeros(sums.shape, f32)
    wait_all(copies)
    count = list_tiles(home_ref, partner_ref, homes, partners, 0, nblocks, nblocks)
    add_tiles(count, homes, partners, home_side, partner_side, values, sums)


def diffuse(fluid, below, above, before, after, skip, diffused):
    nx, ny, nz = fluid.shape[1:]
    width = before.shape[1]
    deep = iota((ny, nz), 1)

    def face(ref, c, x):
        at = skip + (c * nx + x) * (nz // width)
        return jnp.concatenate(
            [ref[at + k : at + k + 1, :] for k in range(nz // width)], axis=1
        )

    def layer(ref, c):
        at = [skip + (c * (nz // width) + k) * ny for k in range(nz // width)]
        return jnp.concatenate([ref[start : start + ny, :] for start in at], axis=1)

    for x in range(nx):
        for c in range(3):
            here = fluid[c, x]
            near = (layer(below, c) if x == 0 else fluid[c, x - 1]) + (
                layer(above, c) if x == nx - 1 else fluid[c, x + 1]
            )
            near = near + jnp.concatenate([face(before, c, x), here[:-1]], axis=0)
            near = near + jnp.concatenate([here[1:], face(after, c, x)], axis=0)
            near = near + jnp.where(deep == 0, 0.0, pltpu.roll(here, 1, 1))
            near = near + jnp.where(deep == nz - 1, 0.0, pltpu.roll(here, nz - 1, 1))
            diffused[c, x] = here + viscosity * (near - 6.0 * here)


def ghost_contacts(nbrick, cap, partner_blocks, home_list, partner_list, routes, plan, below,
                   above, before, after, home_side, own_sums, state, cell, spots, bounds, fluid,
                   updated, outgoing, diffused,
                   rows, columns, values, sums, data, sorted_rows, tiles, homes, partners,
                   home_ref, partner_ref, route_ref, plan_ref, flow, sems):
    nblocks, width = state.shape[1:]
    per = partner_blocks // 4
    copies = copy_all(
        [
            (home_list, home_ref),
            (partner_list, partner_ref),
            (routes, route_ref),
            (plan, plan_ref),
            (fluid, flow),
        ],
        sems,
    )
    stacked = [
        jnp.concatenate(
            [ref[c * per : (c + 1) * per, :] for ref in (below, above, before, after)], axis=0
        )
        for c in range(planes)
    ]
    prepare_partners(stacked[0:4], stacked[4:7], rows, columns, values)
    sums[...] = own_sums[...]
    wait_all(copies)
    count = list_tiles(home_ref, partner_ref, homes, partners, nblocks, nblocks + 4 * per, nblocks)
    add_tiles(count, homes, partners, home_side, columns, values, sums)
    diffuse(flow, below, above, before, after, planes * per, diffused)

    def total(k):
        high = sums[pl.ds(k, nblocks, stride=16), :]
        return high + sums[pl.ds(k + 8, nblocks, stride=16), :]

    weights = total(6)
    radius = state[3]
    inverse = 1.0 / (radius * radius * radius)
    fresh = []
    for c in range(3):
        speed = state[c + 4]
        spring = state[c] * weights - total(c)
        friction = total(c + 3) - speed * weights
        fresh.append(speed + (stiffness * spring + damping * friction) * inverse)
        updated[c] = fresh[c]

    number = cell[...]
    zeros = jnp.zeros_like(radius)
    highs = [rounded(plane) for plane in [radius] + fresh]
    lows = [plane - high for plane, high in zip([radius] + fresh, highs)]
    highs.append(((number >> 8) * 256).astype(f32))
    lows.append((number & 255).astype(f32))
    put_rows(data, 16, highs + [zeros] * 3 + lows + [zeros] * 3)
    sort_blocks(route_ref, plan_ref, spots, data, sorted_rows, tiles, cap)

    chunk = rows_up(5 * cap + 1)
    flat = tiles.reshape(tiles.shape[0] * 8, width)
    for code in range(3 * nbrick):
        row = ((code % nbrick) * 3 + code // nbrick) * chunk
        for c in range(5):
            outgoing[row + c * cap : row + (c + 1) * cap, :] = flat[
                pl.ds(code * (cap + 2) * 8 + c, cap, stride=8), :
            ]
        outgoing[row + 5 * cap : row + 5 * cap + 1, :] = bounds[code : code + 1, :]


def list_stride(segments, cap):
    return (segments + 1) * cap


def list_arrived(arrived, starts, ends, cap, places, counts):
    base, goal = places
    width = arrived.shape[1]
    stride = list_stride(len(starts), cap)
    lane = iota((1, width), 1)
    filled = [jnp.int32(0)] * 4
    for start, end in zip(starts, ends):
        row = arrived[start + 5 * cap : start + 5 * cap + 1, :]
        edge = jnp.int32(0)
        for j in range(4):
            next_edge = jnp.sum(jnp.where(lane == j, row, 0.0)).astype(jnp.int32)
            first = edge // width
            last = jnp.where(next_edge > edge, (next_edge + width - 1) // width, first)
            for i in range(cap):
                base[j * stride + filled[j] + i] = start + first + i
                goal[j * stride + filled[j] + i] = end + first + i
            filled[j] = filled[j] + last - first
            edge = next_edge
    for j in range(4):
        counts[j] = filled[j]


def cell_parts(arrived, row, cap, columns, depth, bucket):
    cell = arrived[pl.ds(row + 4 * cap, 1), :].astype(jnp.int32)
    shift = (2 * depth).bit_length() - 1
    column = (cell >> shift) - (bucket // 2) * columns
    level = (cell & (2 * depth - 1)) - (bucket % 2) * depth - depth // 2
    return column.astype(f32), level.astype(f32)


def all_levels(depth, width):
    return (iota((depth, width), 0) - depth // 2).astype(f32).astype(bf16)


def level_hot(level, levels):
    hit = levels == jnp.broadcast_to(level.astype(bf16), levels.shape)
    return jnp.where(hit, jnp.ones((), bf16), jnp.zeros((), bf16))


def steps_of(counts):
    longest = jnp.maximum(
        jnp.maximum(counts[0], counts[1]), jnp.maximum(counts[2], counts[3])
    )
    return (longest + GROUP - 1) // GROUP


def tile_of(counts, bucket, index, width):
    count = counts[bucket]
    real = jnp.full((1, width), jnp.where(index < count, 1, 0), jnp.int32) > 0
    return jnp.minimum(index, jnp.maximum(count - 1, 0)), real


def deposit(segments, counts, arrived, base, cap, total):
    columns, depth = total.shape[0] // 16, total.shape[1]
    width = arrived.shape[1]
    stride = list_stride(segments, cap)
    numbers = iota((columns, width), 0).astype(f32).astype(bf16)
    levels = all_levels(depth, width)

    def some(step, _):
        sums = []
        for bucket in range(4):
            high_of, low_of, level_of = [], [], []
            for k in range(GROUP):
                index, real = tile_of(counts, bucket, step * GROUP + k, width)
                row = base[bucket * stride + index]
                column, level = cell_parts(arrived, row, cap, columns, depth, bucket)
                radius = arrived[pl.ds(row, 1), :]
                mass = radius * radius * radius
                loads = [mass] + [mass * arrived[pl.ds(row + c * cap, 1), :] for c in (1, 2, 3)]
                hit = numbers == jnp.broadcast_to(column.astype(bf16), (columns, width))
                highs, lows = [], []
                for load in loads:
                    load = jnp.where(real, load, 0.0)
                    high = load.astype(bf16)
                    low = (load - high.astype(f32)).astype(bf16)
                    for parts, part in ((highs, high), (lows, low)):
                        part = jnp.broadcast_to(part, (columns, width))
                        parts.append(jnp.where(hit, part, jnp.zeros((), bf16)))
                high_of.append(jnp.concatenate(highs, axis=0))
                low_of.append(jnp.concatenate(lows, axis=0))
                level_of.append(level_hot(level, levels))
            both = lax.dot_general(
                jnp.concatenate(
                    [jnp.concatenate(high_of, axis=1), jnp.concatenate(low_of, axis=1)], axis=0
                ),
                jnp.concatenate(level_of, axis=1),
                (((1,), (1,)), ((), ())),
                preferred_element_type=f32,
            )
            sums.append(both[0 : 4 * columns] + both[4 * columns :])
        for bucket in range(4):
            total[bucket * 4 * columns : (bucket + 1) * 4 * columns, :] += sums[bucket]
        return 0

    lax.fori_loop(0, steps_of(counts), some, 0)


def sample(segments, counts, arrived, places, cap, table, answers):
    columns, depth = table.shape[0] // 24, table.shape[1]
    width = arrived.shape[1]
    stride = list_stride(segments, cap)
    levels = all_levels(depth, width)
    numbers = iota((columns, width), 0).astype(f32)
    answers[...] = jnp.zeros(answers.shape, f32)

    def some(step, _):
        found = []
        for bucket in range(4):
            hots, hits = [], []
            for k in range(GROUP):
                index, real = tile_of(counts, bucket, step * GROUP + k, width)
                row = places[0][bucket * stride + index]
                column, level = cell_parts(arrived, row, cap, columns, depth, bucket)
                hots.append(level_hot(level, levels))
                hits.append((numbers == column, real, places[1][bucket * stride + index]))
            along = jnp.dot(
                table[bucket * 6 * columns : (bucket + 1) * 6 * columns, :],
                jnp.concatenate(hots, axis=1),
                preferred_element_type=f32,
            )
            for k, (hit, real, goal) in enumerate(hits):
                part = along[:, k * width : (k + 1) * width]
                for c in range(3):
                    value = part[c * columns : (c + 1) * columns]
                    value = value + part[(c + 3) * columns : (c + 4) * columns]
                    value = jnp.sum(jnp.where(hit, value, 0.0), axis=0, keepdims=True)
                    found.append((goal + c * cap, jnp.where(real, value, 0.0)))
        for goal, value in found:
            answers[pl.ds(goal, 1), :] += value
        return 0

    lax.fori_loop(0, steps_of(counts), some, 0)


def first_deposit(nbrick, cap, crossed, total, base, goal, counts):
    chunk = rows_up(5 * cap + 1)
    total[...] = jnp.zeros(total.shape, f32)
    starts = [(3 * b + 1) * chunk for b in range(nbrick)]
    list_arrived(crossed, starts, starts, cap, (base, goal), counts)
    deposit(nbrick, counts, crossed, base, cap, total)


def advance(nbrick, cap, above, below, start, fluid, diffused, fluid_next, table, answers_up,
            answers_down, arrived, answers, total, flow, fresh_flow, base, goal, counts, sems):
    reading = pltpu.make_async_copy(fluid, flow, sems.at[0])
    reading.start()
    chunk = rows_up(5 * cap + 1)
    back = rows_up(3 * cap)
    rows = nbrick * chunk
    arrived[0:rows, :] = above[...]
    arrived[rows:, :] = below[...]
    starts = [i * chunk for i in range(2 * nbrick)]
    ends = [i * back for i in range(2 * nbrick)]
    total[...] = start[...]
    list_arrived(arrived, starts, ends, cap, (base, goal), counts)
    deposit(2 * nbrick, counts, arrived, base, cap, total)
    reading.wait()

    nx, ny, nz = flow.shape[1:]
    columns, depth = nx * ny // 2, nz // 2
    for x in range(nx):
        buckets = [2 * (x * ny // columns) + deep for deep in range(2)]
        at = x * ny % columns

        def load(c):
            spots = [4 * columns * bucket + c * columns + at for bucket in buckets]
            return jnp.concatenate([total[spot : spot + ny, :] for spot in spots], axis=1)

        volume = load(0)
        for c in range(3):
            moved = load(c + 1) - volume * flow[c, x]
            fresh = diffused[c, x] + coupling * moved
            fresh_flow[c, x] = fresh
            high = fresh.astype(bf16)
            low = (fresh - high.astype(f32)).astype(bf16)
            for deep, bucket in enumerate(buckets):
                spot = 6 * columns * bucket + c * columns + at
                half = slice(deep * depth, (deep + 1) * depth)
                table[spot : spot + ny, :] = high[:, half]
                table[spot + 3 * columns : spot + 3 * columns + ny, :] = low[:, half]
    writing = pltpu.make_async_copy(fresh_flow, fluid_next, sems.at[1])
    writing.start()
    sample(2 * nbrick, counts, arrived, (base, goal), cap, table, answers)
    answers_up[...] = answers[0 : nbrick * back, :]
    answers_down[...] = answers[nbrick * back :, :]
    writing.wait()


def last_sample(nbrick, cap, crossed, table, answers, base, goal, counts):
    chunk = rows_up(5 * cap + 1)
    back = rows_up(3 * cap)
    starts = [(3 * b + 1) * chunk for b in range(nbrick)]
    ends = [b * back for b in range(nbrick)]
    list_arrived(crossed, starts, ends, cap, (base, goal), counts)
    sample(nbrick, counts, crossed, (base, goal), cap, table, answers)


def relax(nbrick, cap, route_ref, plan, updated, returned, spots, velocity_next, picked,
          sorted_rows, tiles, plan_ref, sems):
    copies = copy_all([(plan, plan_ref)], sems)
    nblocks, width = spots.shape
    back = rows_up(3 * cap)
    flat = tiles.reshape(tiles.shape[0] * 8, width)
    for code in range(3 * nbrick):
        row = ((code % nbrick) * 3 + code // nbrick) * back
        for c in range(3):
            flat[pl.ds(code * (cap + 2) * 8 + c, cap, stride=8), :] = returned[
                row + c * cap : row + (c + 1) * cap, :
            ]
    lane = iota((8, width), 1)
    wait_all(copies)

    def gather(b, _):
        chunk = route_ref[b] * (cap + 2)
        block = jnp.zeros((8, width), f32)
        for j in range(4):
            tile, at, first, length = place_of(plan_ref, b, j, width)
            run = jnp.where(lane >= at, tiles[chunk + tile], tiles[chunk + tile + 1])
            run = pltpu.roll(run, (first - at + width) % width, 1)
            block = jnp.where((lane >= first) & (lane < first + length), run, block)
        sorted_rows[b] = block
        return 0

    def order(b, _):
        block = sorted_rows[b]
        high = rounded(block)
        both = jnp.dot(
            jnp.concatenate([high, block - high], axis=0).astype(bf16),
            block_order(spots, b),
            preferred_element_type=f32,
        )
        picked[b] = both[0:8] + both[8:16]
        return 0

    lax.fori_loop(0, nblocks, gather, 0, unroll=8)
    lax.fori_loop(0, nblocks, order, 0, unroll=8)
    flat = picked.reshape(nblocks * 8, width)
    for c in range(3):
        now = updated[c]
        velocity_next[c] = now + relaxation * (flat[pl.ds(c, nblocks, stride=8), :] - now)


def on_device(
    positions, velocities, radii, cell_of, block_route, ghost_list, tile_home, tile_partner, fluid
):
    nblocks, _, width = positions.shape
    nbrick = lax.axis_size("brick")
    _, nx, ny, nz = fluid.shape
    columns = nx * ny
    codes = 3 * nbrick
    cap = max(2, (2 * nblocks + codes - 1) // codes)
    chunk, back = rows_up(5 * cap + 1), rows_up(3 * cap)
    per = ghost_list.shape[0] // 2
    tiles = tile_home.shape[0]
    routes = block_route.reshape(-1)
    positions = jnp.transpose(positions, (1, 0, 2))
    velocities = jnp.transpose(velocities, (1, 0, 2))

    def struct(*shape, dtype=f32):
        return jax.ShapeDtypeStruct(shape, dtype)

    def shifted(x, axis, step):
        count = lax.axis_size(axis)
        return lax.ppermute(x, axis, [(i, (i + step) % count) for i in range(count)])

    def ints(count):
        return pltpu.SMEM((count,), jnp.int32)

    state = jnp.concatenate([positions, radii[None], velocities], axis=0)
    ghost_rows, chunks = planes * per, 3 * (nz // width)
    up, down, right, left = call(
        pack_kernel,
        [struct(ghost_rows + chunks * ny, width)] * 2 + [struct(ghost_rows + chunks * nx, width)] * 2,
        [SMEM] + [VMEM] * 2,
        [],
        "pack",
    )(ghost_list, state, fluid)
    below = shifted(up, "slab", 1)
    above = shifted(down, "slab", -1)
    before = shifted(right, "brick", 1)
    after = shifted(left, "brick", -1)

    def sides(count):
        return [
            pltpu.VMEM((count * 32, width), f32),
            pltpu.VMEM((count, width, 32), bf16),
            pltpu.VMEM((count * 16, width), f32),
        ]

    lists = [ints(tiles + UNROLL)] * 2
    contact_flops = tiles * width * width * 200
    chunk_tiles = pltpu.VMEM((codes * (cap + 2), 8, width), f32)
    block_tiles = pltpu.VMEM((nblocks, 8, width), f32)
    plan_copy = pltpu.SMEM((nblocks, width), jnp.int32)
    home_side, sums, spots, plan, bounds = call(
        functools.partial(own_contacts, codes, columns, nz),
        [
            struct((nblocks + 1) * 32, width),
            struct((nblocks + 1) * 16, width),
            struct(nblocks, width),
            struct(nblocks, width, dtype=jnp.int32),
            struct(rows_up(codes), width),
        ],
        [HBM] * 2 + [VMEM] * 3,
        sides(nblocks) + lists + [ints(tiles)] * 2 + [pltpu.SemaphoreType.DMA((2,))],
        "own_contacts",
        contact_flops,
    )(tile_home, tile_partner, state, cell_of, routes.reshape(1, nblocks))
    updated, outgoing, diffused = call(
        functools.partial(ghost_contacts, nbrick, cap, 4 * per),
        [struct(3, nblocks, width), struct(nbrick * 3 * chunk, width), struct(3, nx, ny, nz)],
        [HBM] * 3 + [ANY] + [VMEM] * 10 + [HBM],
        sides(4 * per)
        + [pltpu.VMEM(((nblocks + 1) * 16, width), f32)]
        + [pltpu.VMEM((nblocks * 16, width), f32), block_tiles, chunk_tiles]
        + lists
        + [ints(tiles), ints(tiles), ints(nblocks), plan_copy]
        + [pltpu.VMEM((3, nx, ny, nz), f32), pltpu.SemaphoreType.DMA((5,))],
        "ghost_contacts",
        contact_flops // 2,
    )(tile_home, tile_partner, routes, plan, below, above, before, after,
      home_side, sums, state, cell_of, spots, bounds, fluid)

    crossed = lax.all_to_all(
        outgoing.reshape(nbrick, 3 * chunk, width), "brick", split_axis=0, concat_axis=0, tiled=True
    )
    from_above = shifted(crossed[:, 0:chunk], "slab", -1).reshape(nbrick * chunk, width)
    from_below = shifted(crossed[:, 2 * chunk :], "slab", 1).reshape(nbrick * chunk, width)
    crossed = crossed.reshape(nbrick * 3 * chunk, width)

    def places(count):
        return [ints(4 * list_stride(count, cap))] * 2 + [ints(4)]

    block_flops = 8 * columns * nz * width
    (started,) = call(
        functools.partial(first_deposit, nbrick, cap),
        [struct(8 * columns, nz // 2)],
        [VMEM],
        places(nbrick),
        "first_deposit",
        block_flops * nblocks // 3,
    )(crossed)
    fluid_next, table, answers_up, answers_down = call(
        functools.partial(advance, nbrick, cap),
        [
            struct(3, nx, ny, nz),
            struct(12 * columns, nz // 2, dtype=bf16),
            struct(nbrick * back, width),
            struct(nbrick * back, width),
        ],
        [VMEM] * 3 + [HBM, VMEM],
        [
            pltpu.VMEM((2 * nbrick * chunk, width), f32),
            pltpu.VMEM((2 * nbrick * back, width), f32),
            pltpu.VMEM((8 * columns, nz // 2), f32),
        ]
        + [pltpu.VMEM((3, nx, ny, nz), f32)] * 2
        + places(2 * nbrick)
        + [pltpu.SemaphoreType.DMA((2,))],
        "advance",
        block_flops * nblocks,
        places=[HBM] + [VMEM] * 3,
    )(from_above, from_below, started, fluid, diffused)
    answers_up = shifted(answers_up.reshape(nbrick, back, width), "slab", 1)
    answers_down = shifted(answers_down.reshape(nbrick, back, width), "slab", -1)
    (answers,) = call(
        functools.partial(last_sample, nbrick, cap),
        [struct(nbrick * back, width)],
        [VMEM] * 2,
        places(nbrick),
        "last_sample",
        block_flops * nblocks // 4,
    )(crossed, table)
    answers = jnp.concatenate(
        [answers_up, answers.reshape(nbrick, back, width), answers_down], axis=1
    )
    returned = lax.all_to_all(answers, "brick", split_axis=0, concat_axis=0, tiled=True)
    (velocity_next,) = call(
        functools.partial(relax, nbrick, cap),
        [struct(3, nblocks, width)],
        [SMEM, ANY] + [VMEM] * 3,
        [block_tiles, block_tiles, chunk_tiles, plan_copy]
        + [pltpu.SemaphoreType.DMA((1,))],
        "relax",
    )(routes, plan, updated, returned.reshape(nbrick * 3 * back, width), spots)
    return (jnp.transpose(velocity_next, (1, 0, 2)), fluid_next)


def solution(mesh):
    placed = (
        P(("slab", "brick"), None, None),
        P(("slab", "brick"), None, None),
        P(("slab", "brick"), None),
        P(("slab", "brick"), None),
        P(("slab", "brick"), None),
        P(("slab", "brick")),
        P(("slab", "brick")),
        P(("slab", "brick")),
        P(None, "slab", "brick", None),
    )
    return jax.shard_map(
        on_device,
        mesh=mesh,
        in_specs=placed,
        out_specs=(P(("slab", "brick"), None, None), P(None, "slab", "brick", None)),
        check_vma=False,
    )
```

```python
import functools
import math

import jax
import jax.numpy as jnp
from jax import lax
from jax.experimental import pallas as pl
from jax.experimental.pallas import tpu as pltpu
from jax.sharding import PartitionSpec as P

stiffness = 0.01
damping = 0.005
viscosity = 0.1
coupling = 0.5
relaxation = 0.5

f32 = jnp.float32
bf16 = jnp.bfloat16
VMEM = pl.BlockSpec(memory_space=pltpu.VMEM)
SMEM = pl.BlockSpec(memory_space=pltpu.SMEM)
ANY = pl.BlockSpec(memory_space=pl.ANY)
HBM = pl.BlockSpec(memory_space=pltpu.HBM)
UNROLL = 8
GROUP = 2


def rows_up(count):
    return -(-count // 8) * 8


def call(body, outs, ins, scratch, name, flops=0, nbytes=1 << 20, places=None):
    return pl.pallas_call(
        body,
        out_shape=outs,
        in_specs=ins,
        out_specs=places or [VMEM] * len(outs),
        scratch_shapes=scratch,
        name=name,
        compiler_params=pltpu.CompilerParams(vmem_limit_bytes=40 << 20),
        cost_estimate=pl.CostEstimate(flops=flops, bytes_accessed=nbytes, transcendentals=0),
    )


def rounded(x):
    return x.astype(bf16).astype(f32)


def iota(shape, dim):
    return lax.broadcasted_iota(jnp.int32, shape, dim)


planes = 7


def copy_all(pairs, sems):
    copies = [pltpu.make_async_copy(*pair, sems.at[i]) for i, pair in enumerate(pairs)]
    for copy in copies:
        copy.start()
    return copies


def wait_all(copies):
    for copy in copies:
        copy.wait()


def pack_kernel(ghost_ref, state, fluid, up, down, right, left):
    count = ghost_ref.shape[0] // 4
    width = state.shape[2]
    nx, ny, nz = fluid.shape[1:]
    for group in range(4):
        i, j = group // 2, group % 2
        slab_to, brick_to = (up if i else down), (right if j else left)
        for g in range(count):
            block = pl.ds(ghost_ref[group * count + g], 1)
            for c in range(planes):
                row = state[c, block, :]
                at = c * 2 * count + j * count + g
                slab_to[at : at + 1, :] = row
                at = c * 2 * count + i * count + g
                brick_to[at : at + 1, :] = row
    for slab_to, x in ((up, nx - 1), (down, 0)):
        for c in range(3):
            for k in range(nz // width):
                at = planes * 2 * count + (c * (nz // width) + k) * ny
                slab_to[at : at + ny, :] = fluid[c, x, :, k * width : (k + 1) * width]
    for brick_to, y in ((right, ny - 1), (left, 0)):
        for c in range(3):
            for x in range(nx):
                for k in range(nz // width):
                    at = planes * 2 * count + (c * nx + x) * (nz // width) + k
                    brick_to[at : at + 1, :] = fluid[
                        c, x, y : y + 1, k * width : (k + 1) * width
                    ]


def three_parts(x):
    one = rounded(x)
    rest = x - one
    two = rounded(rest)
    return one, two, rest - two


def put_rows(ref, stride, rows):
    count = rows[0].shape[0]
    for k, row in enumerate(rows):
        ref[pl.ds(k, count, stride=stride), :] = row


def pair_factors(place):
    parts = [three_parts(plane) for plane in place]
    own = three_parts(
        place[3] * place[3] - place[0] * place[0] - place[1] * place[1] - place[2] * place[2]
    )
    return [[part[k] for part in parts] for k in range(3)], list(own)


def home_rows(place):
    (one, two, three), own = pair_factors(place)
    ones, zeros = jnp.ones_like(place[0]), jnp.zeros_like(place[0])
    rows = one + one + two + two + one + three
    return [2.0 * row for row in rows] + own + [ones] * 3 + [zeros] * 2


def partner_rows(place):
    (one, two, three), own = pair_factors(place)
    ones, zeros = jnp.ones_like(place[0]), jnp.zeros_like(place[0])
    return one + two + one + two + three + one + [ones] * 3 + own + [zeros] * 2


def value_rows(values):
    highs = [rounded(plane) for plane in values]
    ones, zeros = jnp.ones_like(values[0]), jnp.zeros_like(values[0])
    lows = [plane - high for plane, high in zip(values, highs)]
    return highs + [ones, zeros] + lows + [zeros, zeros]


def prepare_partners(place, speeds, rows, columns, values):
    count, width = place[0].shape
    put_rows(rows, 32, partner_rows(place))
    put_rows(values, 16, value_rows(place[0:3] + speeds))

    def turn(b, _):
        block = rows[pl.ds(pl.multiple_of(b * 32, 32), 32), :]
        columns[b] = jnp.transpose(block).astype(bf16)
        return 0

    lax.fori_loop(0, count, turn, 0, unroll=4)


def list_tiles(home_ref, partner_ref, homes, partners, lower, upper, spare):
    def one(t, count):
        partner = partner_ref[t]
        homes[count] = home_ref[t]
        partners[count] = partner - lower
        return count + jnp.where((partner >= lower) & (partner < upper), 1, 0)

    count = lax.fori_loop(0, home_ref.shape[0], one, 0, unroll=4)
    for pad in range(UNROLL):
        homes[count + pad] = spare
        partners[count + pad] = 0
    return count


def add_tiles(count, homes, partners, home_side, partner_side, values, sums):
    def some(step, _):
        for k in range(UNROLL):
            home = homes[step * UNROLL + k]
            partner = partners[step * UNROLL + k]
            factors = home_side[pl.ds(pl.multiple_of(home * 32, 32), 32), :].astype(bf16)
            weight = jnp.dot(partner_side[partner], factors, preferred_element_type=f32)
            weight = jnp.maximum(weight, 0.0)
            high = weight.astype(bf16)
            low = (weight - high.astype(f32)).astype(bf16)
            value = values[pl.ds(pl.multiple_of(partner * 16, 16), 16), :].astype(bf16)
            at = pl.ds(pl.multiple_of(home * 16, 16), 16)
            sums[at, :] += jnp.dot(
                jnp.concatenate([value, value], axis=1),
                jnp.concatenate([high, low], axis=0),
                preferred_element_type=f32,
            )
        return 0

    lax.fori_loop(0, (count + UNROLL - 1) // UNROLL, some, 0)


def dot(left, right):
    return jnp.dot(left.astype(bf16), right.astype(bf16), preferred_element_type=f32)


def plan_sort(cap, cell, route, columns, depth, spots, plan, bounds):
    nblocks, width = cell.shape
    shift = depth.bit_length() - 1
    number = cell[...]
    right = (number >> shift) >= columns // 2
    deep = (number & (depth - 1)) >= depth // 2
    kind = jnp.where(right, 2, 0) + jnp.where(deep, 1, 0)
    members = [jnp.where(kind == j, 1.0, 0.0) for j in range(4)]
    before = jnp.where(iota((width, width), 0) < iota((width, width), 1), 1.0, 0.0)
    stacked = jnp.concatenate(members, axis=0)
    ranks = dot(stacked, before)
    lengths = dot(stacked, jnp.ones((width, width), f32))
    ranks = [ranks[j * nblocks : (j + 1) * nblocks] for j in range(4)]
    lengths = [lengths[j * nblocks : (j + 1) * nblocks] for j in range(4)]

    across = jnp.broadcast_to(route[...].astype(f32), (nblocks, nblocks))
    same = across == jnp.transpose(across)
    earlier = iota((nblocks, nblocks), 1) < iota((nblocks, nblocks), 0)
    side_by_side = jnp.concatenate(lengths, axis=1)
    ahead = dot(jnp.where(same & earlier, 1.0, 0.0), side_by_side)
    whole = dot(jnp.where(same, 1.0, 0.0), side_by_side)
    rows = bounds.shape[0]
    of_code = jnp.broadcast_to(route[...], (rows, nblocks)) == iota((rows, nblocks), 0)
    totals = dot(jnp.where(of_code, 1.0, 0.0), side_by_side)

    lane = iota((nblocks, width), 1)
    bound_lane = iota((rows, width), 1)
    spot = jnp.zeros((nblocks, width), f32)
    first, chunk_first = jnp.zeros((nblocks, width), f32), jnp.zeros((nblocks, width), f32)
    bound, line = jnp.zeros((rows, width), f32), jnp.zeros((rows, width), f32)
    table = jnp.zeros((nblocks, width), jnp.int32)
    own_code = jnp.transpose(across).astype(jnp.int32)
    own_code = jnp.concatenate([own_code] * (width // nblocks), axis=1)
    for j in range(4):
        at = slice(j * width, (j + 1) * width)
        spot = spot + members[j] * (first + ranks[j])
        where = (chunk_first + ahead[:, at]).astype(jnp.int32)
        start, there = first.astype(jnp.int32), where & (width - 1)
        parts = [
            own_code * (cap + 2) + (where >> (width.bit_length() - 1)),
            there,
            start,
            lengths[j].astype(jnp.int32),
            (there - start) & (width - 1),
            (start - there) & (width - 1),
        ]
        for k, part in enumerate(parts):
            table = jnp.where(lane == 4 * k + j, part, table)
        first = first + lengths[j]
        chunk_first = chunk_first + whole[:, at]
        bound = bound + totals[:, at]
        line = jnp.where(bound_lane == j, bound, line)
    spots[...] = spot
    plan[...] = table
    bounds[...] = line


def block_order(spots, b):
    width = spots.shape[1]
    row = jnp.broadcast_to(spots[pl.ds(b, 1), :].astype(bf16), (width, width))
    hit = iota((width, width), 0).astype(f32).astype(bf16) == row
    return jnp.where(hit, jnp.ones((), bf16), jnp.zeros((), bf16))


def sort_blocks(plan, spots, data, sorted_rows, tiles):
    nblocks, width = spots.shape
    lane = iota((8, width), 1)

    def order(b, _):
        rows = data[pl.ds(pl.multiple_of(b * 16, 16), 16), :].astype(bf16)
        both = lax.dot_general(
            rows, block_order(spots, b), (((1,), (1,)), ((), ())), preferred_element_type=f32
        )
        sorted_rows[b] = both[0:8] + both[8:16]
        return 0

    def spread(b, _):
        block = sorted_rows[b]
        for j in range(4):
            tile, at, length = plan[b, j], plan[b, 4 + j], plan[b, 12 + j]
            moved = pltpu.roll(block, plan[b, 16 + j], 1)
            here = (lane >= at) & (lane < at + length)
            pltpu.store(tiles.at[tile], moved, mask=here)
            pltpu.store(tiles.at[tile + 1], moved, mask=lane < at + length - width)
        return 0

    lax.fori_loop(0, nblocks, order, 0, unroll=8)
    lax.fori_loop(0, nblocks, spread, 0, unroll=8)


def own_contacts(cap, columns, depth, home_list, partner_list, state, cell, route,
                 home_side, sums, spots, plan, bounds,
                 rows, partner_side, values, homes, partners, home_ref, partner_ref, sems):
    nblocks, width = state.shape[1:]
    copies = copy_all([(home_list, home_ref), (partner_list, partner_ref)], sems)
    plan_sort(cap, cell, route, columns, depth, spots, plan, bounds)
    place = [state[c] for c in range(4)]
    put_rows(home_side, 32, home_rows(place))
    prepare_partners(place, [state[c] for c in (4, 5, 6)], rows, partner_side, values)
    home_side[nblocks * 32 :, :] = jnp.zeros((32, width), f32)
    sums[...] = jnp.zeros(sums.shape, f32)
    wait_all(copies)
    count = list_tiles(home_ref, partner_ref, homes, partners, 0, nblocks, nblocks)
    add_tiles(count, homes, partners, home_side, partner_side, values, sums)


def diffuse(fluid, below, above, before, after, skip, diffused):
    nx, ny, nz = fluid.shape[1:]
    width = before.shape[1]
    deep = iota((ny, nz), 1)

    def face(ref, c, x):
        at = skip + (c * nx + x) * (nz // width)
        return jnp.concatenate(
            [ref[at + k : at + k + 1, :] for k in range(nz // width)], axis=1
        )

    def layer(ref, c):
        at = [skip + (c * (nz // width) + k) * ny for k in range(nz // width)]
        return jnp.concatenate([ref[start : start + ny, :] for start in at], axis=1)

    for x in range(nx):
        for c in range(3):
            here = fluid[c, x]
            near = (layer(below, c) if x == 0 else fluid[c, x - 1]) + (
                layer(above, c) if x == nx - 1 else fluid[c, x + 1]
            )
            near = near + jnp.concatenate([face(before, c, x), here[:-1]], axis=0)
            near = near + jnp.concatenate([here[1:], face(after, c, x)], axis=0)
            near = near + jnp.where(deep == 0, 0.0, pltpu.roll(here, 1, 1))
            near = near + jnp.where(deep == nz - 1, 0.0, pltpu.roll(here, nz - 1, 1))
            diffused[c, x] = here + viscosity * (near - 6.0 * here)


def ghost_contacts(nbrick, cap, partner_blocks, home_list, partner_list, plan, below,
                   above, before, after, home_side, own_sums, state, cell, spots, bounds, fluid,
                   updated, outgoing, diffused,
                   rows, columns, values, sums, data, sorted_rows, tiles, homes, partners,
                   home_ref, partner_ref, plan_ref, flow, sems):
    nblocks, width = state.shape[1:]
    per = partner_blocks // 4
    copies = copy_all(
        [
            (home_list, home_ref),
            (partner_list, partner_ref),
            (plan, plan_ref),
            (fluid, flow),
        ],
        sems,
    )
    stacked = [
        jnp.concatenate(
            [ref[c * per : (c + 1) * per, :] for ref in (below, above, before, after)], axis=0
        )
        for c in range(planes)
    ]
    prepare_partners(stacked[0:4], stacked[4:7], rows, columns, values)
    sums[...] = own_sums[...]
    wait_all(copies)
    count = list_tiles(home_ref, partner_ref, homes, partners, nblocks, nblocks + 4 * per, nblocks)
    add_tiles(count, homes, partners, home_side, columns, values, sums)
    diffuse(flow, below, above, before, after, planes * per, diffused)

    def total(k):
        high = sums[pl.ds(k, nblocks, stride=16), :]
        return high + sums[pl.ds(k + 8, nblocks, stride=16), :]

    weights = total(6)
    radius = state[3]
    inverse = 1.0 / (radius * radius * radius)
    fresh = []
    for c in range(3):
        speed = state[c + 4]
        spring = state[c] * weights - total(c)
        friction = total(c + 3) - speed * weights
        fresh.append(speed + (stiffness * spring + damping * friction) * inverse)
        updated[c] = fresh[c]

    number = cell[...]
    zeros = jnp.zeros_like(radius)
    highs = [rounded(plane) for plane in [radius] + fresh]
    lows = [plane - high for plane, high in zip([radius] + fresh, highs)]
    highs.append(((number >> 8) * 256).astype(f32))
    lows.append((number & 255).astype(f32))
    put_rows(data, 16, highs + [zeros] * 3 + lows + [zeros] * 3)
    sort_blocks(plan_ref, spots, data, sorted_rows, tiles)

    chunk = rows_up(5 * cap + 1)
    flat = tiles.reshape(tiles.shape[0] * 8, width)
    for code in range(3 * nbrick):
        row = ((code % nbrick) * 3 + code // nbrick) * chunk
        for c in range(5):
            outgoing[row + c * cap : row + (c + 1) * cap, :] = flat[
                pl.ds(code * (cap + 2) * 8 + c, cap, stride=8), :
            ]
        outgoing[row + 5 * cap : row + 5 * cap + 1, :] = bounds[code : code + 1, :]


def list_stride(segments, cap):
    return (segments + 1) * cap


def list_arrived(arrived, starts, ends, cap, places, counts):
    base, goal = places
    width = arrived.shape[1]
    stride = list_stride(len(starts), cap)
    shift = width.bit_length() - 1
    lane = iota((1, width), 1)
    filled = [jnp.int32(0)] * 4
    for start, end in zip(starts, ends):
        row = arrived[start + 5 * cap : start + 5 * cap + 1, :]
        edge = jnp.int32(0)
        for j in range(4):
            next_edge = jnp.sum(jnp.where(lane == j, row, 0.0)).astype(jnp.int32)
            first = edge >> shift
            last = jnp.where(next_edge > edge, (next_edge + width - 1) >> shift, first)
            for i in range(cap):
                base[j * stride + filled[j] + i] = start + first + i
                goal[j * stride + filled[j] + i] = end + first + i
            filled[j] = filled[j] + last - first
            edge = next_edge
    for j in range(4):
        counts[j] = filled[j]


def cell_parts(arrived, row, cap, columns, depth, bucket):
    cell = arrived[pl.ds(row + 4 * cap, 1), :].astype(jnp.int32)
    shift = (2 * depth).bit_length() - 1
    column = (cell >> shift) - (bucket // 2) * columns
    level = (cell & (2 * depth - 1)) - (bucket % 2) * depth - depth // 2
    return column.astype(f32), level.astype(f32)


def all_levels(depth, width):
    return (iota((depth, width), 0) - depth // 2).astype(f32).astype(bf16)


def level_hot(level, levels):
    hit = levels == jnp.broadcast_to(level.astype(bf16), levels.shape)
    return jnp.where(hit, jnp.ones((), bf16), jnp.zeros((), bf16))


def steps_of(counts):
    longest = jnp.maximum(
        jnp.maximum(counts[0], counts[1]), jnp.maximum(counts[2], counts[3])
    )
    return lax.shift_right_logical(longest + GROUP - 1, GROUP.bit_length() - 1)


def tile_of(counts, bucket, index, width):
    count = counts[bucket]
    real = jnp.full((1, width), jnp.where(index < count, 1, 0), jnp.int32) > 0
    return jnp.minimum(index, jnp.maximum(count - 1, 0)), real


def deposit(segments, counts, arrived, base, cap, total):
    columns, depth = total.shape[0] // 16, total.shape[1]
    width = arrived.shape[1]
    stride = list_stride(segments, cap)
    numbers = iota((columns, width), 0).astype(f32).astype(bf16)
    levels = all_levels(depth, width)

    def some(step, _):
        sums = []
        for bucket in range(4):
            high_of, low_of, level_of = [], [], []
            for k in range(GROUP):
                index, real = tile_of(counts, bucket, step * GROUP + k, width)
                row = base[bucket * stride + index]
                column, level = cell_parts(arrived, row, cap, columns, depth, bucket)
                radius = arrived[pl.ds(row, 1), :]
                mass = radius * radius * radius
                loads = [mass] + [mass * arrived[pl.ds(row + c * cap, 1), :] for c in (1, 2, 3)]
                hit = numbers == jnp.broadcast_to(column.astype(bf16), (columns, width))
                highs, lows = [], []
                for load in loads:
                    load = jnp.where(real, load, 0.0)
                    high = load.astype(bf16)
                    low = (load - high.astype(f32)).astype(bf16)
                    for parts, part in ((highs, high), (lows, low)):
                        part = jnp.broadcast_to(part, (columns, width))
                        parts.append(jnp.where(hit, part, jnp.zeros((), bf16)))
                high_of.append(jnp.concatenate(highs, axis=0))
                low_of.append(jnp.concatenate(lows, axis=0))
                level_of.append(level_hot(level, levels))
            both = lax.dot_general(
                jnp.concatenate(
                    [jnp.concatenate(high_of, axis=1), jnp.concatenate(low_of, axis=1)], axis=0
                ),
                jnp.concatenate(level_of, axis=1),
                (((1,), (1,)), ((), ())),
                preferred_element_type=f32,
            )
            sums.append(both[0 : 4 * columns] + both[4 * columns :])
        for bucket in range(4):
            total[bucket * 4 * columns : (bucket + 1) * 4 * columns, :] += sums[bucket]
        return 0

    lax.fori_loop(0, steps_of(counts), some, 0)


def sample(segments, counts, arrived, places, cap, table, answers):
    columns, depth = table.shape[0] // 24, table.shape[1]
    width = arrived.shape[1]
    stride = list_stride(segments, cap)
    levels = all_levels(depth, width)
    numbers = iota((columns, width), 0).astype(f32)
    answers[...] = jnp.zeros(answers.shape, f32)

    def some(step, _):
        found = []
        for bucket in range(4):
            hots, hits = [], []
            for k in range(GROUP):
                index, real = tile_of(counts, bucket, step * GROUP + k, width)
                row = places[0][bucket * stride + index]
                column, level = cell_parts(arrived, row, cap, columns, depth, bucket)
                hots.append(level_hot(level, levels))
                hits.append((numbers == column, real, places[1][bucket * stride + index]))
            along = jnp.dot(
                table[bucket * 6 * columns : (bucket + 1) * 6 * columns, :],
                jnp.concatenate(hots, axis=1),
                preferred_element_type=f32,
            )
            for k, (hit, real, goal) in enumerate(hits):
                part = along[:, k * width : (k + 1) * width]
                for c in range(3):
                    value = part[c * columns : (c + 1) * columns]
                    value = value + part[(c + 3) * columns : (c + 4) * columns]
                    value = jnp.sum(jnp.where(hit, value, 0.0), axis=0, keepdims=True)
                    found.append((goal + c * cap, jnp.where(real, value, 0.0)))
        for goal, value in found:
            answers[pl.ds(goal, 1), :] += value
        return 0

    lax.fori_loop(0, steps_of(counts), some, 0)


def first_deposit(nbrick, cap, crossed, total, base, goal, counts):
    chunk = rows_up(5 * cap + 1)
    total[...] = jnp.zeros(total.shape, f32)
    starts = [(3 * b + 1) * chunk for b in range(nbrick)]
    list_arrived(crossed, starts, starts, cap, (base, goal), counts)
    deposit(nbrick, counts, crossed, base, cap, total)


def advance(nbrick, cap, above, below, start, fluid, diffused, fluid_next, table, answers_up,
            answers_down, arrived, answers, total, flow, fresh_flow, base, goal, counts, sems):
    reading = pltpu.make_async_copy(fluid, flow, sems.at[0])
    reading.start()
    chunk = rows_up(5 * cap + 1)
    back = rows_up(3 * cap)
    rows = nbrick * chunk
    arrived[0:rows, :] = above[...]
    arrived[rows:, :] = below[...]
    starts = [i * chunk for i in range(2 * nbrick)]
    ends = [i * back for i in range(2 * nbrick)]
    total[...] = start[...]
    list_arrived(arrived, starts, ends, cap, (base, goal), counts)
    deposit(2 * nbrick, counts, arrived, base, cap, total)
    reading.wait()

    nx, ny, nz = flow.shape[1:]
    columns, depth = nx * ny // 2, nz // 2
    for x in range(nx):
        buckets = [2 * (x * ny // columns) + deep for deep in range(2)]
        at = x * ny % columns

        def load(c):
            spots = [4 * columns * bucket + c * columns + at for bucket in buckets]
            return jnp.concatenate([total[spot : spot + ny, :] for spot in spots], axis=1)

        volume = load(0)
        for c in range(3):
            moved = load(c + 1) - volume * flow[c, x]
            fresh = diffused[c, x] + coupling * moved
            fresh_flow[c, x] = fresh
            high = fresh.astype(bf16)
            low = (fresh - high.astype(f32)).astype(bf16)
            for deep, bucket in enumerate(buckets):
                spot = 6 * columns * bucket + c * columns + at
                half = slice(deep * depth, (deep + 1) * depth)
                table[spot : spot + ny, :] = high[:, half]
                table[spot + 3 * columns : spot + 3 * columns + ny, :] = low[:, half]
    writing = pltpu.make_async_copy(fresh_flow, fluid_next, sems.at[1])
    writing.start()
    sample(2 * nbrick, counts, arrived, (base, goal), cap, table, answers)
    answers_up[...] = answers[0 : nbrick * back, :]
    answers_down[...] = answers[nbrick * back :, :]
    writing.wait()


def last_sample(nbrick, cap, crossed, table, answers, base, goal, counts):
    chunk = rows_up(5 * cap + 1)
    back = rows_up(3 * cap)
    starts = [(3 * b + 1) * chunk for b in range(nbrick)]
    ends = [b * back for b in range(nbrick)]
    list_arrived(crossed, starts, ends, cap, (base, goal), counts)
    sample(nbrick, counts, crossed, (base, goal), cap, table, answers)


def relax(nbrick, cap, plan, updated, returned, spots, velocity_next, picked,
          sorted_rows, tiles, plan_ref, sems):
    copies = copy_all([(plan, plan_ref)], sems)
    nblocks, width = spots.shape
    back = rows_up(3 * cap)
    flat = tiles.reshape(tiles.shape[0] * 8, width)
    for code in range(3 * nbrick):
        row = ((code % nbrick) * 3 + code // nbrick) * back
        for c in range(3):
            flat[pl.ds(code * (cap + 2) * 8 + c, cap, stride=8), :] = returned[
                row + c * cap : row + (c + 1) * cap, :
            ]
    lane = iota((8, width), 1)
    wait_all(copies)

    def gather(b, _):
        block = jnp.zeros((8, width), f32)
        for j in range(4):
            tile, at = plan_ref[b, j], plan_ref[b, 4 + j]
            first, length = plan_ref[b, 8 + j], plan_ref[b, 12 + j]
            run = jnp.where(lane >= at, tiles[tile], tiles[tile + 1])
            run = pltpu.roll(run, plan_ref[b, 20 + j], 1)
            block = jnp.where((lane >= first) & (lane < first + length), run, block)
        sorted_rows[b] = block
        return 0

    def order(b, _):
        block = sorted_rows[b]
        high = rounded(block)
        both = jnp.dot(
            jnp.concatenate([high, block - high], axis=0).astype(bf16),
            block_order(spots, b),
            preferred_element_type=f32,
        )
        picked[b] = both[0:8] + both[8:16]
        return 0

    lax.fori_loop(0, nblocks, gather, 0, unroll=8)
    lax.fori_loop(0, nblocks, order, 0, unroll=8)
    flat = picked.reshape(nblocks * 8, width)
    for c in range(3):
        now = updated[c]
        velocity_next[c] = now + relaxation * (flat[pl.ds(c, nblocks, stride=8), :] - now)


def on_device(
    positions, velocities, radii, cell_of, block_route, ghost_list, tile_home, tile_partner, fluid
):
    nblocks, _, width = positions.shape
    nbrick = lax.axis_size("brick")
    _, nx, ny, nz = fluid.shape
    columns = nx * ny
    codes = 3 * nbrick
    cap = max(2, (2 * nblocks + codes - 1) // codes)
    chunk, back = rows_up(5 * cap + 1), rows_up(3 * cap)
    per = ghost_list.shape[0] // 2
    tiles = tile_home.shape[0]
    routes = block_route.reshape(-1)
    positions = jnp.transpose(positions, (1, 0, 2))
    velocities = jnp.transpose(velocities, (1, 0, 2))

    def struct(*shape, dtype=f32):
        return jax.ShapeDtypeStruct(shape, dtype)

    def shifted(x, axis, step):
        count = lax.axis_size(axis)
        return lax.ppermute(x, axis, [(i, (i + step) % count) for i in range(count)])

    def ints(count):
        return pltpu.SMEM((count,), jnp.int32)

    state = jnp.concatenate([positions, radii[None], velocities], axis=0)
    ghost_rows, chunks = planes * per, 3 * (nz // width)
    up, down, right, left = call(
        pack_kernel,
        [struct(ghost_rows + chunks * ny, width)] * 2 + [struct(ghost_rows + chunks * nx, width)] * 2,
        [SMEM] + [VMEM] * 2,
        [],
        "pack",
    )(ghost_list, state, fluid)
    below = shifted(up, "slab", 1)
    above = shifted(down, "slab", -1)
    before = shifted(right, "brick", 1)
    after = shifted(left, "brick", -1)

    def sides(count):
        return [
            pltpu.VMEM((count * 32, width), f32),
            pltpu.VMEM((count, width, 32), bf16),
            pltpu.VMEM((count * 16, width), f32),
        ]

    lists = [ints(tiles + UNROLL)] * 2
    contact_flops = tiles * width * width * 200
    chunk_tiles = pltpu.VMEM((codes * (cap + 2), 8, width), f32)
    block_tiles = pltpu.VMEM((nblocks, 8, width), f32)
    plan_copy = pltpu.SMEM((nblocks, width), jnp.int32)
    home_side, sums, spots, plan, bounds = call(
        functools.partial(own_contacts, cap, columns, nz),
        [
            struct((nblocks + 1) * 32, width),
            struct((nblocks + 1) * 16, width),
            struct(nblocks, width),
            struct(nblocks, width, dtype=jnp.int32),
            struct(rows_up(codes), width),
        ],
        [HBM] * 2 + [VMEM] * 3,
        sides(nblocks) + lists + [ints(tiles)] * 2 + [pltpu.SemaphoreType.DMA((2,))],
        "own_contacts",
        contact_flops,
    )(tile_home, tile_partner, state, cell_of, routes.reshape(1, nblocks))
    updated, outgoing, diffused = call(
        functools.partial(ghost_contacts, nbrick, cap, 4 * per),
        [struct(3, nblocks, width), struct(nbrick * 3 * chunk, width), struct(3, nx, ny, nz)],
        [HBM] * 2 + [ANY] + [VMEM] * 10 + [HBM],
        sides(4 * per)
        + [pltpu.VMEM(((nblocks + 1) * 16, width), f32)]
        + [pltpu.VMEM((nblocks * 16, width), f32), block_tiles, chunk_tiles]
        + lists
        + [ints(tiles), ints(tiles), plan_copy]
        + [pltpu.VMEM((3, nx, ny, nz), f32), pltpu.SemaphoreType.DMA((4,))],
        "ghost_contacts",
        contact_flops // 2,
    )(tile_home, tile_partner, plan, below, above, before, after,
      home_side, sums, state, cell_of, spots, bounds, fluid)

    crossed = lax.all_to_all(
        outgoing.reshape(nbrick, 3 * chunk, width), "brick", split_axis=0, concat_axis=0, tiled=True
    )
    from_above = shifted(crossed[:, 0:chunk], "slab", -1).reshape(nbrick * chunk, width)
    from_below = shifted(crossed[:, 2 * chunk :], "slab", 1).reshape(nbrick * chunk, width)
    crossed = crossed.reshape(nbrick * 3 * chunk, width)

    def places(count):
        return [ints(4 * list_stride(count, cap))] * 2 + [ints(4)]

    block_flops = 8 * columns * nz * width
    (started,) = call(
        functools.partial(first_deposit, nbrick, cap),
        [struct(8 * columns, nz // 2)],
        [VMEM],
        places(nbrick),
        "first_deposit",
        block_flops * nblocks // 3,
    )(crossed)
    fluid_next, table, answers_up, answers_down = call(
        functools.partial(advance, nbrick, cap),
        [
            struct(3, nx, ny, nz),
            struct(12 * columns, nz // 2, dtype=bf16),
            struct(nbrick * back, width),
            struct(nbrick * back, width),
        ],
        [VMEM] * 3 + [HBM, VMEM],
        [
            pltpu.VMEM((2 * nbrick * chunk, width), f32),
            pltpu.VMEM((2 * nbrick * back, width), f32),
            pltpu.VMEM((8 * columns, nz // 2), f32),
        ]
        + [pltpu.VMEM((3, nx, ny, nz), f32)] * 2
        + places(2 * nbrick)
        + [pltpu.SemaphoreType.DMA((2,))],
        "advance",
        block_flops * nblocks,
        places=[HBM] + [VMEM] * 3,
    )(from_above, from_below, started, fluid, diffused)
    answers_up = shifted(answers_up.reshape(nbrick, back, width), "slab", 1)
    answers_down = shifted(answers_down.reshape(nbrick, back, width), "slab", -1)
    (answers,) = call(
        functools.partial(last_sample, nbrick, cap),
        [struct(nbrick * back, width)],
        [VMEM] * 2,
        places(nbrick),
        "last_sample",
        block_flops * nblocks // 4,
    )(crossed, table)
    answers = jnp.concatenate(
        [answers_up, answers.reshape(nbrick, back, width), answers_down], axis=1
    )
    returned = lax.all_to_all(answers, "brick", split_axis=0, concat_axis=0, tiled=True)
    (velocity_next,) = call(
        functools.partial(relax, nbrick, cap),
        [struct(3, nblocks, width)],
        [ANY] + [VMEM] * 3,
        [block_tiles, block_tiles, chunk_tiles, plan_copy]
        + [pltpu.SemaphoreType.DMA((1,))],
        "relax",
    )(plan, updated, returned.reshape(nbrick * 3 * back, width), spots)
    return (jnp.transpose(velocity_next, (1, 0, 2)), fluid_next)


def solution(mesh):
    placed = (
        P(("slab", "brick"), None, None),
        P(("slab", "brick"), None, None),
        P(("slab", "brick"), None),
        P(("slab", "brick"), None),
        P(("slab", "brick"), None),
        P(("slab", "brick")),
        P(("slab", "brick")),
        P(("slab", "brick")),
        P(None, "slab", "brick", None),
    )
    return jax.shard_map(
        on_device,
        mesh=mesh,
        in_specs=placed,
        out_specs=(P(("slab", "brick"), None, None), P(None, "slab", "brick", None)),
        check_vma=False,
    )
```

```python
import functools
import math

import jax
import jax.numpy as jnp
from jax import lax
from jax.experimental import pallas as pl
from jax.experimental.pallas import tpu as pltpu
from jax.sharding import PartitionSpec as P

stiffness = 0.01
damping = 0.005
viscosity = 0.1
coupling = 0.5
relaxation = 0.5

f32 = jnp.float32
bf16 = jnp.bfloat16
VMEM = pl.BlockSpec(memory_space=pltpu.VMEM)
SMEM = pl.BlockSpec(memory_space=pltpu.SMEM)
ANY = pl.BlockSpec(memory_space=pl.ANY)
HBM = pl.BlockSpec(memory_space=pltpu.HBM)
UNROLL = 8
GROUP = 2


def rows_up(count):
    return -(-count // 8) * 8


def call(body, outs, ins, scratch, name, flops=0, nbytes=1 << 20, places=None):
    return pl.pallas_call(
        body,
        out_shape=outs,
        in_specs=ins,
        out_specs=places or [VMEM] * len(outs),
        scratch_shapes=scratch,
        name=name,
        compiler_params=pltpu.CompilerParams(vmem_limit_bytes=40 << 20),
        cost_estimate=pl.CostEstimate(flops=flops, bytes_accessed=nbytes, transcendentals=0),
    )


def rounded(x):
    return x.astype(bf16).astype(f32)


def iota(shape, dim):
    return lax.broadcasted_iota(jnp.int32, shape, dim)


planes = 7


def copy_all(pairs, sems):
    copies = [pltpu.make_async_copy(*pair, sems.at[i]) for i, pair in enumerate(pairs)]
    for copy in copies:
        copy.start()
    return copies


def wait_all(copies):
    for copy in copies:
        copy.wait()


def pack_kernel(ghost_ref, state, fluid, up, down, right, left):
    count = ghost_ref.shape[0] // 4
    width = state.shape[2]
    nx, ny, nz = fluid.shape[1:]
    for group in range(4):
        i, j = group // 2, group % 2
        slab_to, brick_to = (up if i else down), (right if j else left)
        for g in range(count):
            block = pl.ds(ghost_ref[group * count + g], 1)
            for c in range(planes):
                row = state[c, block, :]
                at = c * 2 * count + j * count + g
                slab_to[at : at + 1, :] = row
                at = c * 2 * count + i * count + g
                brick_to[at : at + 1, :] = row
    for slab_to, x in ((up, nx - 1), (down, 0)):
        for c in range(3):
            for k in range(nz // width):
                at = planes * 2 * count + (c * (nz // width) + k) * ny
                slab_to[at : at + ny, :] = fluid[c, x, :, k * width : (k + 1) * width]
    for brick_to, y in ((right, ny - 1), (left, 0)):
        for c in range(3):
            for x in range(nx):
                for k in range(nz // width):
                    at = planes * 2 * count + (c * nx + x) * (nz // width) + k
                    brick_to[at : at + 1, :] = fluid[
                        c, x, y : y + 1, k * width : (k + 1) * width
                    ]


def three_parts(x):
    one = rounded(x)
    rest = x - one
    two = rounded(rest)
    return one, two, rest - two


def put_rows(ref, stride, rows):
    count = rows[0].shape[0]
    for k, row in enumerate(rows):
        ref[pl.ds(k, count, stride=stride), :] = row


def pair_factors(place):
    parts = [three_parts(plane) for plane in place]
    own = three_parts(
        place[3] * place[3] - place[0] * place[0] - place[1] * place[1] - place[2] * place[2]
    )
    return [[part[k] for part in parts] for k in range(3)], list(own)


def home_rows(place):
    (one, two, three), own = pair_factors(place)
    ones, zeros = jnp.ones_like(place[0]), jnp.zeros_like(place[0])
    rows = one + one + two + two + one + three
    return [2.0 * row for row in rows] + own + [ones] * 3 + [zeros] * 2


def partner_rows(place):
    (one, two, three), own = pair_factors(place)
    ones, zeros = jnp.ones_like(place[0]), jnp.zeros_like(place[0])
    return one + two + one + two + three + one + [ones] * 3 + own + [zeros] * 2


def value_rows(values):
    highs = [rounded(plane) for plane in values]
    ones, zeros = jnp.ones_like(values[0]), jnp.zeros_like(values[0])
    lows = [plane - high for plane, high in zip(values, highs)]
    return highs + [ones, zeros] + lows + [zeros, zeros]


def prepare_partners(place, speeds, rows, columns, values):
    count, width = place[0].shape
    put_rows(rows, 32, partner_rows(place))
    put_rows(values, 16, value_rows(place[0:3] + speeds))

    def turn(b, _):
        block = rows[pl.ds(pl.multiple_of(b * 32, 32), 32), :]
        columns[b] = jnp.transpose(block).astype(bf16)
        return 0

    lax.fori_loop(0, count, turn, 0, unroll=4)


def list_tiles(home_ref, partner_ref, homes, partners, lower, upper, spare):
    def one(t, count):
        partner = partner_ref[t]
        homes[count] = home_ref[t]
        partners[count] = partner - lower
        return count + jnp.where((partner >= lower) & (partner < upper), 1, 0)

    count = lax.fori_loop(0, home_ref.shape[0], one, 0, unroll=4)
    for pad in range(UNROLL):
        homes[count + pad] = spare
        partners[count + pad] = 0
    return count


def add_tiles(count, homes, partners, home_side, partner_side, values, sums):
    def some(step, _):
        for k in range(UNROLL):
            home = homes[step * UNROLL + k]
            partner = partners[step * UNROLL + k]
            factors = home_side[pl.ds(pl.multiple_of(home * 32, 32), 32), :].astype(bf16)
            weight = jnp.dot(partner_side[partner], factors, preferred_element_type=f32)
            weight = jnp.maximum(weight, 0.0)
            high = weight.astype(bf16)
            low = (weight - high.astype(f32)).astype(bf16)
            value = values[pl.ds(pl.multiple_of(partner * 16, 16), 16), :].astype(bf16)
            at = pl.ds(pl.multiple_of(home * 16, 16), 16)
            sums[at, :] += jnp.dot(
                jnp.concatenate([value, value], axis=1),
                jnp.concatenate([high, low], axis=0),
                preferred_element_type=f32,
            )
        return 0

    lax.fori_loop(0, (count + UNROLL - 1) // UNROLL, some, 0)


def dot(left, right):
    return jnp.dot(left.astype(bf16), right.astype(bf16), preferred_element_type=f32)


def plan_sort(cap, cell, route, columns, depth, spots, plan, bounds):
    nblocks, width = cell.shape
    shift = depth.bit_length() - 1
    number = cell[...]
    right = (number >> shift) >= columns // 2
    deep = (number & (depth - 1)) >= depth // 2
    kind = jnp.where(right, 2, 0) + jnp.where(deep, 1, 0)
    members = [jnp.where(kind == j, 1.0, 0.0) for j in range(4)]
    before = jnp.where(iota((width, width), 0) < iota((width, width), 1), 1.0, 0.0)
    stacked = jnp.concatenate(members, axis=0)
    ranks = dot(stacked, before)
    lengths = dot(stacked, jnp.ones((width, width), f32))
    ranks = [ranks[j * nblocks : (j + 1) * nblocks] for j in range(4)]
    lengths = [lengths[j * nblocks : (j + 1) * nblocks] for j in range(4)]

    across = jnp.broadcast_to(route[...].astype(f32), (nblocks, nblocks))
    same = across == jnp.transpose(across)
    earlier = iota((nblocks, nblocks), 1) < iota((nblocks, nblocks), 0)
    side_by_side = jnp.concatenate(lengths, axis=1)
    ahead = dot(jnp.where(same & earlier, 1.0, 0.0), side_by_side)
    whole = dot(jnp.where(same, 1.0, 0.0), side_by_side)
    rows = bounds.shape[0]
    of_code = jnp.broadcast_to(route[...], (rows, nblocks)) == iota((rows, nblocks), 0)
    totals = dot(jnp.where(of_code, 1.0, 0.0), side_by_side)

    lane = iota((nblocks, width), 1)
    bound_lane = iota((rows, width), 1)
    spot = jnp.zeros((nblocks, width), f32)
    first, chunk_first = jnp.zeros((nblocks, width), f32), jnp.zeros((nblocks, width), f32)
    bound, line = jnp.zeros((rows, width), f32), jnp.zeros((rows, width), f32)
    table = jnp.zeros((nblocks, width), jnp.int32)
    own_code = jnp.transpose(across).astype(jnp.int32)
    own_code = jnp.concatenate([own_code] * (width // nblocks), axis=1)
    for j in range(4):
        at = slice(j * width, (j + 1) * width)
        spot = spot + members[j] * (first + ranks[j])
        where = (chunk_first + ahead[:, at]).astype(jnp.int32)
        start, there = first.astype(jnp.int32), where & (width - 1)
        parts = [
            own_code * (cap + 2) + (where >> (width.bit_length() - 1)),
            there,
            start,
            lengths[j].astype(jnp.int32),
            (there - start) & (width - 1),
            (start - there) & (width - 1),
        ]
        for k, part in enumerate(parts):
            table = jnp.where(lane == 4 * k + j, part, table)
        first = first + lengths[j]
        chunk_first = chunk_first + whole[:, at]
        bound = bound + totals[:, at]
        line = jnp.where(bound_lane == j, bound, line)
    spots[...] = spot
    plan[...] = table
    bounds[...] = line


def block_order(spots, b):
    width = spots.shape[1]
    row = jnp.broadcast_to(spots[pl.ds(b, 1), :].astype(bf16), (width, width))
    hit = iota((width, width), 0).astype(f32).astype(bf16) == row
    return jnp.where(hit, jnp.ones((), bf16), jnp.zeros((), bf16))


def sort_blocks(plan, spots, data, sorted_rows, tiles):
    nblocks, width = spots.shape
    lane = iota((8, width), 1)

    def order(b, _):
        rows = data[pl.ds(pl.multiple_of(b * 16, 16), 16), :].astype(bf16)
        both = lax.dot_general(
            rows, block_order(spots, b), (((1,), (1,)), ((), ())), preferred_element_type=f32
        )
        sorted_rows[b] = both[0:8] + both[8:16]
        return 0

    def spread(b, _):
        block = sorted_rows[b]
        for j in range(4):
            tile, at, length = plan[b, j], plan[b, 4 + j], plan[b, 12 + j]
            moved = pltpu.roll(block, plan[b, 16 + j], 1)
            here = (lane >= at) & (lane < at + length)
            pltpu.store(tiles.at[tile], moved, mask=here)
            pltpu.store(tiles.at[tile + 1], moved, mask=lane < at + length - width)
        return 0

    lax.fori_loop(0, nblocks, order, 0, unroll=8)
    lax.fori_loop(0, nblocks, spread, 0, unroll=8)


def own_contacts(cap, columns, depth, home_list, partner_list, state, cell, route,
                 home_side, sums, spots, plan, bounds,
                 rows, partner_side, values, homes, partners, home_ref, partner_ref, sems):
    nblocks, width = state.shape[1:]
    copies = copy_all([(home_list, home_ref), (partner_list, partner_ref)], sems)
    plan_sort(cap, cell, route, columns, depth, spots, plan, bounds)
    place = [state[c] for c in range(4)]
    put_rows(home_side, 32, home_rows(place))
    prepare_partners(place, [state[c] for c in (4, 5, 6)], rows, partner_side, values)
    home_side[nblocks * 32 :, :] = jnp.zeros((32, width), f32)
    sums[...] = jnp.zeros(sums.shape, f32)
    wait_all(copies)
    count = list_tiles(home_ref, partner_ref, homes, partners, 0, nblocks, nblocks)
    add_tiles(count, homes, partners, home_side, partner_side, values, sums)


def diffuse(fluid, below, above, before, after, skip, diffused):
    nx, ny, nz = fluid.shape[1:]
    width = before.shape[1]
    deep = iota((ny, nz), 1)

    def face(ref, c, x):
        at = skip + (c * nx + x) * (nz // width)
        return jnp.concatenate(
            [ref[at + k : at + k + 1, :] for k in range(nz // width)], axis=1
        )

    def layer(ref, c):
        at = [skip + (c * (nz // width) + k) * ny for k in range(nz // width)]
        return jnp.concatenate([ref[start : start + ny, :] for start in at], axis=1)

    for x in range(nx):
        for c in range(3):
            here = fluid[c, x]
            near = (layer(below, c) if x == 0 else fluid[c, x - 1]) + (
                layer(above, c) if x == nx - 1 else fluid[c, x + 1]
            )
            near = near + jnp.concatenate([face(before, c, x), here[:-1]], axis=0)
            near = near + jnp.concatenate([here[1:], face(after, c, x)], axis=0)
            near = near + jnp.where(deep == 0, 0.0, pltpu.roll(here, 1, 1))
            near = near + jnp.where(deep == nz - 1, 0.0, pltpu.roll(here, nz - 1, 1))
            diffused[c, x] = here + viscosity * (near - 6.0 * here)


def brick_ahead(ahead, nbrick):
    return lax.rem(lax.axis_index("brick") + ahead, nbrick)


def ghost_contacts(nbrick, cap, partner_blocks, home_list, partner_list, plan, below,
                   above, before, after, home_side, own_sums, state, cell, spots, bounds, fluid,
                   updated, diffused, *rest):
    outgoings = rest[:nbrick]
    (rows, columns, values, sums, data, sorted_rows, tiles, homes, partners,
     home_ref, partner_ref, plan_ref, flow, sems) = rest[nbrick:]
    nblocks, width = state.shape[1:]
    per = partner_blocks // 4
    copies = copy_all(
        [
            (home_list, home_ref),
            (partner_list, partner_ref),
            (plan, plan_ref),
            (fluid, flow),
        ],
        sems,
    )
    stacked = [
        jnp.concatenate(
            [ref[c * per : (c + 1) * per, :] for ref in (below, above, before, after)], axis=0
        )
        for c in range(planes)
    ]
    prepare_partners(stacked[0:4], stacked[4:7], rows, columns, values)
    sums[...] = own_sums[...]
    wait_all(copies)
    count = list_tiles(home_ref, partner_ref, homes, partners, nblocks, nblocks + 4 * per, nblocks)
    add_tiles(count, homes, partners, home_side, columns, values, sums)
    diffuse(flow, below, above, before, after, planes * per, diffused)

    def total(k):
        high = sums[pl.ds(k, nblocks, stride=16), :]
        return high + sums[pl.ds(k + 8, nblocks, stride=16), :]

    weights = total(6)
    radius = state[3]
    inverse = 1.0 / (radius * radius * radius)
    fresh = []
    for c in range(3):
        speed = state[c + 4]
        spring = state[c] * weights - total(c)
        friction = total(c + 3) - speed * weights
        fresh.append(speed + (stiffness * spring + damping * friction) * inverse)
        updated[c] = fresh[c]

    number = cell[...]
    zeros = jnp.zeros_like(radius)
    highs = [rounded(plane) for plane in [radius] + fresh]
    lows = [plane - high for plane, high in zip([radius] + fresh, highs)]
    highs.append(((number >> 8) * 256).astype(f32))
    lows.append((number & 255).astype(f32))
    put_rows(data, 16, highs + [zeros] * 3 + lows + [zeros] * 3)
    sort_blocks(plan_ref, spots, data, sorted_rows, tiles)

    chunk = rows_up(5 * cap + 1)
    flat = tiles.reshape(tiles.shape[0] * 8, width)
    for ahead, outgoing in enumerate(outgoings):
        target = brick_ahead(ahead, nbrick)
        for side in range(3):
            code, row = side * nbrick + target, side * chunk
            for c in range(5):
                outgoing[row + c * cap : row + (c + 1) * cap, :] = flat[
                    pl.ds(code * (cap + 2) * 8 + c, cap, stride=8), :
                ]
            outgoing[row + 5 * cap : row + 5 * cap + 1, :] = bounds[pl.ds(code, 1), :]


def list_stride(segments, cap):
    return (segments + 1) * cap


def list_arrived(arrived, starts, ends, cap, places, counts):
    base, goal = places
    width = arrived.shape[1]
    stride = list_stride(len(starts), cap)
    shift = width.bit_length() - 1
    lane = iota((1, width), 1)
    filled = [jnp.int32(0)] * 4
    for start, end in zip(starts, ends):
        row = arrived[start + 5 * cap : start + 5 * cap + 1, :]
        edge = jnp.int32(0)
        for j in range(4):
            next_edge = jnp.sum(jnp.where(lane == j, row, 0.0)).astype(jnp.int32)
            first = edge >> shift
            last = jnp.where(next_edge > edge, (next_edge + width - 1) >> shift, first)
            for i in range(cap):
                base[j * stride + filled[j] + i] = start + first + i
                goal[j * stride + filled[j] + i] = end + first + i
            filled[j] = filled[j] + last - first
            edge = next_edge
    for j in range(4):
        counts[j] = filled[j]


def cell_parts(arrived, row, cap, columns, depth, bucket):
    cell = arrived[pl.ds(row + 4 * cap, 1), :].astype(jnp.int32)
    shift = (2 * depth).bit_length() - 1
    column = (cell >> shift) - (bucket // 2) * columns
    level = (cell & (2 * depth - 1)) - (bucket % 2) * depth - depth // 2
    return column.astype(f32), level.astype(f32)


def all_levels(depth, width):
    return (iota((depth, width), 0) - depth // 2).astype(f32).astype(bf16)


def level_hot(level, levels):
    hit = levels == jnp.broadcast_to(level.astype(bf16), levels.shape)
    return jnp.where(hit, jnp.ones((), bf16), jnp.zeros((), bf16))


def steps_of(counts):
    longest = jnp.maximum(
        jnp.maximum(counts[0], counts[1]), jnp.maximum(counts[2], counts[3])
    )
    return lax.shift_right_logical(longest + GROUP - 1, GROUP.bit_length() - 1)


def tile_of(counts, bucket, index, width):
    count = counts[bucket]
    real = jnp.full((1, width), jnp.where(index < count, 1, 0), jnp.int32) > 0
    return jnp.minimum(index, jnp.maximum(count - 1, 0)), real


def deposit(segments, counts, arrived, base, cap, total):
    columns, depth = total.shape[0] // 16, total.shape[1]
    width = arrived.shape[1]
    stride = list_stride(segments, cap)
    numbers = iota((columns, width), 0).astype(f32).astype(bf16)
    levels = all_levels(depth, width)

    def some(step, _):
        sums = []
        for bucket in range(4):
            high_of, low_of, level_of = [], [], []
            for k in range(GROUP):
                index, real = tile_of(counts, bucket, step * GROUP + k, width)
                row = base[bucket * stride + index]
                column, level = cell_parts(arrived, row, cap, columns, depth, bucket)
                radius = arrived[pl.ds(row, 1), :]
                mass = radius * radius * radius
                loads = [mass] + [mass * arrived[pl.ds(row + c * cap, 1), :] for c in (1, 2, 3)]
                hit = numbers == jnp.broadcast_to(column.astype(bf16), (columns, width))
                highs, lows = [], []
                for load in loads:
                    load = jnp.where(real, load, 0.0)
                    high = load.astype(bf16)
                    low = (load - high.astype(f32)).astype(bf16)
                    for parts, part in ((highs, high), (lows, low)):
                        part = jnp.broadcast_to(part, (columns, width))
                        parts.append(jnp.where(hit, part, jnp.zeros((), bf16)))
                high_of.append(jnp.concatenate(highs, axis=0))
                low_of.append(jnp.concatenate(lows, axis=0))
                level_of.append(level_hot(level, levels))
            both = lax.dot_general(
                jnp.concatenate(
                    [jnp.concatenate(high_of, axis=1), jnp.concatenate(low_of, axis=1)], axis=0
                ),
                jnp.concatenate(level_of, axis=1),
                (((1,), (1,)), ((), ())),
                preferred_element_type=f32,
            )
            sums.append(both[0 : 4 * columns] + both[4 * columns :])
        for bucket in range(4):
            total[bucket * 4 * columns : (bucket + 1) * 4 * columns, :] += sums[bucket]
        return 0

    lax.fori_loop(0, steps_of(counts), some, 0)


def sample(segments, counts, arrived, places, cap, table, answers):
    columns, depth = table.shape[0] // 24, table.shape[1]
    width = arrived.shape[1]
    stride = list_stride(segments, cap)
    levels = all_levels(depth, width)
    numbers = iota((columns, width), 0).astype(f32)
    answers[...] = jnp.zeros(answers.shape, f32)

    def some(step, _):
        found = []
        for bucket in range(4):
            hots, hits = [], []
            for k in range(GROUP):
                index, real = tile_of(counts, bucket, step * GROUP + k, width)
                row = places[0][bucket * stride + index]
                column, level = cell_parts(arrived, row, cap, columns, depth, bucket)
                hots.append(level_hot(level, levels))
                hits.append((numbers == column, real, places[1][bucket * stride + index]))
            along = jnp.dot(
                table[bucket * 6 * columns : (bucket + 1) * 6 * columns, :],
                jnp.concatenate(hots, axis=1),
                preferred_element_type=f32,
            )
            for k, (hit, real, goal) in enumerate(hits):
                part = along[:, k * width : (k + 1) * width]
                for c in range(3):
                    value = part[c * columns : (c + 1) * columns]
                    value = value + part[(c + 3) * columns : (c + 4) * columns]
                    value = jnp.sum(jnp.where(hit, value, 0.0), axis=0, keepdims=True)
                    found.append((goal + c * cap, jnp.where(real, value, 0.0)))
        for goal, value in found:
            answers[pl.ds(goal, 1), :] += value
        return 0

    lax.fori_loop(0, steps_of(counts), some, 0)


def first_deposit(nbrick, cap, crossed, total, base, goal, counts):
    chunk = rows_up(5 * cap + 1)
    total[...] = jnp.zeros(total.shape, f32)
    starts = [b * chunk for b in range(nbrick)]
    list_arrived(crossed, starts, starts, cap, (base, goal), counts)
    deposit(nbrick, counts, crossed, base, cap, total)


def advance(nbrick, cap, above, below, start, fluid, diffused, fluid_next, table, answers_up,
            answers_down, arrived, answers, total, flow, fresh_flow, base, goal, counts, sems):
    reading = pltpu.make_async_copy(fluid, flow, sems.at[0])
    reading.start()
    chunk = rows_up(5 * cap + 1)
    back = rows_up(3 * cap)
    rows = nbrick * chunk
    arrived[0:rows, :] = above[...]
    arrived[rows:, :] = below[...]
    starts = [i * chunk for i in range(2 * nbrick)]
    ends = [i * back for i in range(2 * nbrick)]
    total[...] = start[...]
    list_arrived(arrived, starts, ends, cap, (base, goal), counts)
    deposit(2 * nbrick, counts, arrived, base, cap, total)
    reading.wait()

    nx, ny, nz = flow.shape[1:]
    columns, depth = nx * ny // 2, nz // 2
    for x in range(nx):
        buckets = [2 * (x * ny // columns) + deep for deep in range(2)]
        at = x * ny % columns

        def load(c):
            spots = [4 * columns * bucket + c * columns + at for bucket in buckets]
            return jnp.concatenate([total[spot : spot + ny, :] for spot in spots], axis=1)

        volume = load(0)
        for c in range(3):
            moved = load(c + 1) - volume * flow[c, x]
            fresh = diffused[c, x] + coupling * moved
            fresh_flow[c, x] = fresh
            high = fresh.astype(bf16)
            low = (fresh - high.astype(f32)).astype(bf16)
            for deep, bucket in enumerate(buckets):
                spot = 6 * columns * bucket + c * columns + at
                half = slice(deep * depth, (deep + 1) * depth)
                table[spot : spot + ny, :] = high[:, half]
                table[spot + 3 * columns : spot + 3 * columns + ny, :] = low[:, half]
    writing = pltpu.make_async_copy(fresh_flow, fluid_next, sems.at[1])
    writing.start()
    sample(2 * nbrick, counts, arrived, (base, goal), cap, table, answers)
    answers_up[...] = answers[0 : nbrick * back, :]
    answers_down[...] = answers[nbrick * back :, :]
    writing.wait()


def last_sample(nbrick, cap, crossed, table, answers, base, goal, counts):
    chunk = rows_up(5 * cap + 1)
    back = rows_up(3 * cap)
    starts = [b * chunk for b in range(nbrick)]
    ends = [b * back for b in range(nbrick)]
    list_arrived(crossed, starts, ends, cap, (base, goal), counts)
    sample(nbrick, counts, crossed, (base, goal), cap, table, answers)


def relax(nbrick, cap, plan, updated, spots, *rest):
    returneds = rest[:nbrick]
    velocity_next, picked, sorted_rows, tiles, plan_ref, sems = rest[nbrick:]
    copies = copy_all([(plan, plan_ref)], sems)
    nblocks, width = spots.shape
    back = rows_up(3 * cap)
    flat = tiles.reshape(tiles.shape[0] * 8, width)
    for ahead, returned in enumerate(returneds):
        target = brick_ahead(ahead, nbrick)
        for side in range(3):
            code, row = side * nbrick + target, side * back
            for c in range(3):
                flat[pl.ds(code * (cap + 2) * 8 + c, cap, stride=8), :] = returned[
                    row + c * cap : row + (c + 1) * cap, :
                ]
    lane = iota((8, width), 1)
    wait_all(copies)

    def gather(b, _):
        block = jnp.zeros((8, width), f32)
        for j in range(4):
            tile, at = plan_ref[b, j], plan_ref[b, 4 + j]
            first, length = plan_ref[b, 8 + j], plan_ref[b, 12 + j]
            run = jnp.where(lane >= at, tiles[tile], tiles[tile + 1])
            run = pltpu.roll(run, plan_ref[b, 20 + j], 1)
            block = jnp.where((lane >= first) & (lane < first + length), run, block)
        sorted_rows[b] = block
        return 0

    def order(b, _):
        block = sorted_rows[b]
        high = rounded(block)
        both = jnp.dot(
            jnp.concatenate([high, block - high], axis=0).astype(bf16),
            block_order(spots, b),
            preferred_element_type=f32,
        )
        picked[b] = both[0:8] + both[8:16]
        return 0

    lax.fori_loop(0, nblocks, gather, 0, unroll=8)
    lax.fori_loop(0, nblocks, order, 0, unroll=8)
    flat = picked.reshape(nblocks * 8, width)
    for c in range(3):
        now = updated[c]
        velocity_next[c] = now + relaxation * (flat[pl.ds(c, nblocks, stride=8), :] - now)


def on_device(
    positions, velocities, radii, cell_of, block_route, ghost_list, tile_home, tile_partner, fluid
):
    nblocks, _, width = positions.shape
    nbrick = lax.axis_size("brick")
    _, nx, ny, nz = fluid.shape
    columns = nx * ny
    codes = 3 * nbrick
    cap = max(2, (2 * nblocks + codes - 1) // codes)
    chunk, back = rows_up(5 * cap + 1), rows_up(3 * cap)
    per = ghost_list.shape[0] // 2
    tiles = tile_home.shape[0]
    routes = block_route.reshape(-1)
    positions = jnp.transpose(positions, (1, 0, 2))
    velocities = jnp.transpose(velocities, (1, 0, 2))

    def struct(*shape, dtype=f32):
        return jax.ShapeDtypeStruct(shape, dtype)

    def shifted(x, axis, step):
        if step == 0:
            return x
        count = lax.axis_size(axis)
        return lax.ppermute(x, axis, [(i, (i + step) % count) for i in range(count)])

    def ints(count):
        return pltpu.SMEM((count,), jnp.int32)

    state = jnp.concatenate([positions, radii[None], velocities], axis=0)
    ghost_rows, chunks = planes * per, 3 * (nz // width)
    up, down, right, left = call(
        pack_kernel,
        [struct(ghost_rows + chunks * ny, width)] * 2 + [struct(ghost_rows + chunks * nx, width)] * 2,
        [SMEM] + [VMEM] * 2,
        [],
        "pack",
    )(ghost_list, state, fluid)
    below = shifted(up, "slab", 1)
    above = shifted(down, "slab", -1)
    before = shifted(right, "brick", 1)
    after = shifted(left, "brick", -1)

    def sides(count):
        return [
            pltpu.VMEM((count * 32, width), f32),
            pltpu.VMEM((count, width, 32), bf16),
            pltpu.VMEM((count * 16, width), f32),
        ]

    lists = [ints(tiles + UNROLL)] * 2
    contact_flops = tiles * width * width * 200
    chunk_tiles = pltpu.VMEM((codes * (cap + 2), 8, width), f32)
    block_tiles = pltpu.VMEM((nblocks, 8, width), f32)
    plan_copy = pltpu.SMEM((nblocks, width), jnp.int32)
    home_side, sums, spots, plan, bounds = call(
        functools.partial(own_contacts, cap, columns, nz),
        [
            struct((nblocks + 1) * 32, width),
            struct((nblocks + 1) * 16, width),
            struct(nblocks, width),
            struct(nblocks, width, dtype=jnp.int32),
            struct(rows_up(codes), width),
        ],
        [HBM] * 2 + [VMEM] * 3,
        sides(nblocks) + lists + [ints(tiles)] * 2 + [pltpu.SemaphoreType.DMA((2,))],
        "own_contacts",
        contact_flops,
    )(tile_home, tile_partner, state, cell_of, routes.reshape(1, nblocks))
    updated, diffused, *outgoing = call(
        functools.partial(ghost_contacts, nbrick, cap, 4 * per),
        [struct(3, nblocks, width), struct(3, nx, ny, nz)] + [struct(3 * chunk, width)] * nbrick,
        [HBM] * 2 + [ANY] + [VMEM] * 10 + [HBM],
        sides(4 * per)
        + [pltpu.VMEM(((nblocks + 1) * 16, width), f32)]
        + [pltpu.VMEM((nblocks * 16, width), f32), block_tiles, chunk_tiles]
        + lists
        + [ints(tiles), ints(tiles), plan_copy]
        + [pltpu.VMEM((3, nx, ny, nz), f32), pltpu.SemaphoreType.DMA((4,))],
        "ghost_contacts",
        contact_flops // 2,
    )(tile_home, tile_partner, plan, below, above, before, after,
      home_side, sums, state, cell_of, spots, bounds, fluid)

    crossed = [shifted(part, "brick", ahead) for ahead, part in enumerate(outgoing)]

    def side(k):
        return jnp.concatenate([part[k * chunk : (k + 1) * chunk] for part in crossed], axis=0)

    from_above = shifted(side(0), "slab", -1)
    from_below = shifted(side(2), "slab", 1)
    crossed = side(1)

    def places(count):
        return [ints(4 * list_stride(count, cap))] * 2 + [ints(4)]

    block_flops = 8 * columns * nz * width
    (started,) = call(
        functools.partial(first_deposit, nbrick, cap),
        [struct(8 * columns, nz // 2)],
        [VMEM],
        places(nbrick),
        "first_deposit",
        block_flops * nblocks // 3,
    )(crossed)
    fluid_next, table, answers_up, answers_down = call(
        functools.partial(advance, nbrick, cap),
        [
            struct(3, nx, ny, nz),
            struct(12 * columns, nz // 2, dtype=bf16),
            struct(nbrick * back, width),
            struct(nbrick * back, width),
        ],
        [VMEM] * 3 + [HBM, VMEM],
        [
            pltpu.VMEM((2 * nbrick * chunk, width), f32),
            pltpu.VMEM((2 * nbrick * back, width), f32),
            pltpu.VMEM((8 * columns, nz // 2), f32),
        ]
        + [pltpu.VMEM((3, nx, ny, nz), f32)] * 2
        + places(2 * nbrick)
        + [pltpu.SemaphoreType.DMA((2,))],
        "advance",
        block_flops * nblocks,
        places=[HBM] + [VMEM] * 3,
    )(from_above, from_below, started, fluid, diffused)
    answers_up = shifted(answers_up, "slab", 1)
    answers_down = shifted(answers_down, "slab", -1)
    (answers,) = call(
        functools.partial(last_sample, nbrick, cap),
        [struct(nbrick * back, width)],
        [VMEM] * 2,
        places(nbrick),
        "last_sample",
        block_flops * nblocks // 4,
    )(crossed, table)
    returned = []
    for behind in range(nbrick):
        at = slice(behind * back, (behind + 1) * back)
        part = jnp.concatenate([answers_up[at], answers[at], answers_down[at]], axis=0)
        returned.append(shifted(part, "brick", -behind))
    (velocity_next,) = call(
        functools.partial(relax, nbrick, cap),
        [struct(3, nblocks, width)],
        [ANY] + [VMEM] * (2 + nbrick),
        [block_tiles, block_tiles, chunk_tiles, plan_copy]
        + [pltpu.SemaphoreType.DMA((1,))],
        "relax",
    )(plan, updated, spots, *returned)
    return (jnp.transpose(velocity_next, (1, 0, 2)), fluid_next)


def solution(mesh):
    placed = (
        P(("slab", "brick"), None, None),
        P(("slab", "brick"), None, None),
        P(("slab", "brick"), None),
        P(("slab", "brick"), None),
        P(("slab", "brick"), None),
        P(("slab", "brick")),
        P(("slab", "brick")),
        P(("slab", "brick")),
        P(None, "slab", "brick", None),
    )
    return jax.shard_map(
        on_device,
        mesh=mesh,
        in_specs=placed,
        out_specs=(P(("slab", "brick"), None, None), P(None, "slab", "brick", None)),
        check_vma=False,
    )
```

```python
import functools
import math

import jax
import jax.numpy as jnp
from jax import lax
from jax.experimental import pallas as pl
from jax.experimental.pallas import tpu as pltpu
from jax.sharding import PartitionSpec as P

stiffness = 0.01
damping = 0.005
viscosity = 0.1
coupling = 0.5
relaxation = 0.5

f32 = jnp.float32
bf16 = jnp.bfloat16
VMEM = pl.BlockSpec(memory_space=pltpu.VMEM)
SMEM = pl.BlockSpec(memory_space=pltpu.SMEM)
ANY = pl.BlockSpec(memory_space=pl.ANY)
HBM = pl.BlockSpec(memory_space=pltpu.HBM)
UNROLL = 8
GROUP = 2


def rows_up(count):
    return -(-count // 8) * 8


def call(body, outs, ins, scratch, name, flops=0, nbytes=1 << 20, places=None, vmem=40 << 20):
    return pl.pallas_call(
        body,
        out_shape=outs,
        in_specs=ins,
        out_specs=places or [VMEM] * len(outs),
        scratch_shapes=scratch,
        name=name,
        compiler_params=pltpu.CompilerParams(vmem_limit_bytes=vmem),
        cost_estimate=pl.CostEstimate(flops=flops, bytes_accessed=nbytes, transcendentals=0),
    )


def rounded(x):
    return x.astype(bf16).astype(f32)


def iota(shape, dim):
    return lax.broadcasted_iota(jnp.int32, shape, dim)


planes = 7


def copy_all(pairs, sems):
    copies = [pltpu.make_async_copy(*pair, sems.at[i]) for i, pair in enumerate(pairs)]
    for copy in copies:
        copy.start()
    return copies


def wait_all(copies):
    for copy in copies:
        copy.wait()


def pack_kernel(ghost_ref, state, fluid, up, down, right, left):
    count = ghost_ref.shape[0] // 4
    width = state.shape[2]
    nx, ny, nz = fluid.shape[1:]
    for group in range(4):
        i, j = group // 2, group % 2
        slab_to, brick_to = (up if i else down), (right if j else left)
        for g in range(count):
            block = pl.ds(ghost_ref[group * count + g], 1)
            for c in range(planes):
                row = state[c, block, :]
                at = c * 2 * count + j * count + g
                slab_to[at : at + 1, :] = row
                at = c * 2 * count + i * count + g
                brick_to[at : at + 1, :] = row
    for slab_to, x in ((up, nx - 1), (down, 0)):
        for c in range(3):
            for k in range(nz // width):
                at = planes * 2 * count + (c * (nz // width) + k) * ny
                slab_to[at : at + ny, :] = fluid[c, x, :, k * width : (k + 1) * width]
    for brick_to, y in ((right, ny - 1), (left, 0)):
        for c in range(3):
            for x in range(nx):
                for k in range(nz // width):
                    at = planes * 2 * count + (c * nx + x) * (nz // width) + k
                    brick_to[at : at + 1, :] = fluid[
                        c, x, y : y + 1, k * width : (k + 1) * width
                    ]


def three_parts(x):
    one = rounded(x)
    rest = x - one
    two = rounded(rest)
    return one, two, rest - two


def put_rows(ref, stride, rows):
    count = rows[0].shape[0]
    for k, row in enumerate(rows):
        ref[pl.ds(k, count, stride=stride), :] = row


def pair_factors(place):
    parts = [three_parts(plane) for plane in place]
    own = three_parts(
        place[3] * place[3] - place[0] * place[0] - place[1] * place[1] - place[2] * place[2]
    )
    return [[part[k] for part in parts] for k in range(3)], list(own)


def home_rows(place):
    (one, two, three), own = pair_factors(place)
    ones, zeros = jnp.ones_like(place[0]), jnp.zeros_like(place[0])
    rows = one + one + two + two + one + three
    return [2.0 * row for row in rows] + own + [ones] * 3 + [zeros] * 2


def partner_rows(place):
    (one, two, three), own = pair_factors(place)
    ones, zeros = jnp.ones_like(place[0]), jnp.zeros_like(place[0])
    return one + two + one + two + three + one + [ones] * 3 + own + [zeros] * 2


def value_rows(values):
    highs = [rounded(plane) for plane in values]
    ones, zeros = jnp.ones_like(values[0]), jnp.zeros_like(values[0])
    lows = [plane - high for plane, high in zip(values, highs)]
    return highs + [ones, zeros] + lows + [zeros, zeros]


def prepare_partners(place, speeds, rows, columns, values):
    count, width = place[0].shape
    put_rows(rows, 32, partner_rows(place))
    put_rows(values, 16, value_rows(place[0:3] + speeds))

    def turn(b, _):
        block = rows[pl.ds(pl.multiple_of(b * 32, 32), 32), :]
        columns[b] = jnp.transpose(block).astype(bf16)
        return 0

    lax.fori_loop(0, count, turn, 0, unroll=4)


def list_tiles(home_ref, partner_ref, homes, partners, lower, upper, spare):
    def one(t, count):
        partner = partner_ref[t]
        homes[count] = home_ref[t]
        partners[count] = partner - lower
        return count + jnp.where((partner >= lower) & (partner < upper), 1, 0)

    count = lax.fori_loop(0, home_ref.shape[0], one, 0, unroll=4)
    for pad in range(UNROLL):
        homes[count + pad] = spare
        partners[count + pad] = 0
    return count


def add_tiles(count, homes, partners, home_side, partner_side, values, sums):
    def some(step, _):
        for k in range(UNROLL):
            home = homes[step * UNROLL + k]
            partner = partners[step * UNROLL + k]
            factors = home_side[pl.ds(pl.multiple_of(home * 32, 32), 32), :].astype(bf16)
            weight = jnp.dot(partner_side[partner], factors, preferred_element_type=f32)
            weight = jnp.maximum(weight, 0.0)
            high = weight.astype(bf16)
            low = (weight - high.astype(f32)).astype(bf16)
            value = values[pl.ds(pl.multiple_of(partner * 16, 16), 16), :].astype(bf16)
            at = pl.ds(pl.multiple_of(home * 16, 16), 16)
            sums[at, :] += jnp.dot(
                jnp.concatenate([value, value], axis=1),
                jnp.concatenate([high, low], axis=0),
                preferred_element_type=f32,
            )
        return 0

    lax.fori_loop(0, (count + UNROLL - 1) // UNROLL, some, 0)


def dot(left, right):
    return jnp.dot(left.astype(bf16), right.astype(bf16), preferred_element_type=f32)


def plan_sort(cap, cell, route, columns, depth, spots, plan, bounds):
    nblocks, width = cell.shape
    shift = depth.bit_length() - 1
    number = cell[...]
    right = (number >> shift) >= columns // 2
    deep = (number & (depth - 1)) >= depth // 2
    kind = jnp.where(right, 2, 0) + jnp.where(deep, 1, 0)
    members = [jnp.where(kind == j, 1.0, 0.0) for j in range(4)]
    before = jnp.where(iota((width, width), 0) < iota((width, width), 1), 1.0, 0.0)
    stacked = jnp.concatenate(members, axis=0)
    ranks = dot(stacked, before)
    lengths = dot(stacked, jnp.ones((width, width), f32))
    ranks = [ranks[j * nblocks : (j + 1) * nblocks] for j in range(4)]
    lengths = [lengths[j * nblocks : (j + 1) * nblocks] for j in range(4)]

    across = jnp.broadcast_to(route[...].astype(f32), (nblocks, nblocks))
    same = across == jnp.transpose(across)
    earlier = iota((nblocks, nblocks), 1) < iota((nblocks, nblocks), 0)
    side_by_side = jnp.concatenate(lengths, axis=1)
    ahead = dot(jnp.where(same & earlier, 1.0, 0.0), side_by_side)
    whole = dot(jnp.where(same, 1.0, 0.0), side_by_side)
    rows = bounds.shape[0]
    of_code = jnp.broadcast_to(route[...], (rows, nblocks)) == iota((rows, nblocks), 0)
    totals = dot(jnp.where(of_code, 1.0, 0.0), side_by_side)

    lane = iota((nblocks, width), 1)
    bound_lane = iota((rows, width), 1)
    spot = jnp.zeros((nblocks, width), f32)
    first, chunk_first = jnp.zeros((nblocks, width), f32), jnp.zeros((nblocks, width), f32)
    bound, line = jnp.zeros((rows, width), f32), jnp.zeros((rows, width), f32)
    table = jnp.zeros((nblocks, width), jnp.int32)
    own_code = jnp.transpose(across).astype(jnp.int32)
    own_code = jnp.concatenate([own_code] * (width // nblocks), axis=1)
    for j in range(4):
        at = slice(j * width, (j + 1) * width)
        spot = spot + members[j] * (first + ranks[j])
        where = (chunk_first + ahead[:, at]).astype(jnp.int32)
        start, there = first.astype(jnp.int32), where & (width - 1)
        parts = [
            own_code * (cap + 2) + (where >> (width.bit_length() - 1)),
            there,
            start,
            lengths[j].astype(jnp.int32),
            (there - start) & (width - 1),
            (start - there) & (width - 1),
        ]
        for k, part in enumerate(parts):
            table = jnp.where(lane == 4 * k + j, part, table)
        first = first + lengths[j]
        chunk_first = chunk_first + whole[:, at]
        bound = bound + totals[:, at]
        line = jnp.where(bound_lane == j, bound, line)
    spots[...] = spot
    plan[...] = table
    bounds[...] = line


def block_order(spots, b):
    width = spots.shape[1]
    row = jnp.broadcast_to(spots[pl.ds(b, 1), :].astype(bf16), (width, width))
    hit = iota((width, width), 0).astype(f32).astype(bf16) == row
    return jnp.where(hit, jnp.ones((), bf16), jnp.zeros((), bf16))


def sort_blocks(plan, spots, data, sorted_rows, tiles):
    nblocks, width = spots.shape
    lane = iota((8, width), 1)

    def order(b, _):
        rows = data[pl.ds(pl.multiple_of(b * 16, 16), 16), :].astype(bf16)
        both = lax.dot_general(
            rows, block_order(spots, b), (((1,), (1,)), ((), ())), preferred_element_type=f32
        )
        sorted_rows[b] = both[0:8] + both[8:16]
        return 0

    def spread(b, _):
        block = sorted_rows[b]
        for j in range(4):
            tile, at, length = plan[b, j], plan[b, 4 + j], plan[b, 12 + j]
            moved = pltpu.roll(block, plan[b, 16 + j], 1)
            here = (lane >= at) & (lane < at + length)
            pltpu.store(tiles.at[tile], moved, mask=here)
            pltpu.store(tiles.at[tile + 1], moved, mask=lane < at + length - width)
        return 0

    lax.fori_loop(0, nblocks, order, 0, unroll=8)
    lax.fori_loop(0, nblocks, spread, 0, unroll=8)


def own_contacts(cap, columns, depth, home_list, partner_list, state, cell, route,
                 home_side, sums, spots, plan, bounds,
                 rows, partner_side, values, homes, partners, home_ref, partner_ref, sems):
    nblocks, width = state.shape[1:]
    copies = copy_all([(home_list, home_ref), (partner_list, partner_ref)], sems)
    plan_sort(cap, cell, route, columns, depth, spots, plan, bounds)
    place = [state[c] for c in range(4)]
    put_rows(home_side, 32, home_rows(place))
    prepare_partners(place, [state[c] for c in (4, 5, 6)], rows, partner_side, values)
    home_side[nblocks * 32 :, :] = jnp.zeros((32, width), f32)
    sums[...] = jnp.zeros(sums.shape, f32)
    wait_all(copies)
    count = list_tiles(home_ref, partner_ref, homes, partners, 0, nblocks, nblocks)
    add_tiles(count, homes, partners, home_side, partner_side, values, sums)


def diffuse(fluid, below, above, before, after, skip, diffused):
    nx, ny, nz = fluid.shape[1:]
    width = before.shape[1]
    deep = iota((ny, nz), 1)

    def face(ref, c, x):
        at = skip + (c * nx + x) * (nz // width)
        return jnp.concatenate(
            [ref[at + k : at + k + 1, :] for k in range(nz // width)], axis=1
        )

    def layer(ref, c):
        at = [skip + (c * (nz // width) + k) * ny for k in range(nz // width)]
        return jnp.concatenate([ref[start : start + ny, :] for start in at], axis=1)

    for x in range(nx):
        for c in range(3):
            here = fluid[c, x]
            near = (layer(below, c) if x == 0 else fluid[c, x - 1]) + (
                layer(above, c) if x == nx - 1 else fluid[c, x + 1]
            )
            near = near + jnp.concatenate([face(before, c, x), here[:-1]], axis=0)
            near = near + jnp.concatenate([here[1:], face(after, c, x)], axis=0)
            near = near + jnp.where(deep == 0, 0.0, pltpu.roll(here, 1, 1))
            near = near + jnp.where(deep == nz - 1, 0.0, pltpu.roll(here, nz - 1, 1))
            diffused[c, x] = here + viscosity * (near - 6.0 * here)


def brick_ahead(ahead, nbrick):
    return lax.rem(lax.axis_index("brick") + ahead, nbrick)


def ghost_contacts(nbrick, cap, partner_blocks, home_list, partner_list, plan, below,
                   above, before, after, home_side, own_sums, state, cell, spots, bounds,
                   updated, *rest):
    outgoings = rest[:nbrick]
    (rows, columns, values, sums, data, sorted_rows, tiles, homes, partners,
     home_ref, partner_ref, plan_ref, sems) = rest[nbrick:]
    nblocks, width = state.shape[1:]
    per = partner_blocks // 4
    copies = copy_all(
        [
            (home_list, home_ref),
            (partner_list, partner_ref),
            (plan, plan_ref),
        ],
        sems,
    )
    stacked = [
        jnp.concatenate(
            [ref[c * per : (c + 1) * per, :] for ref in (below, above, before, after)], axis=0
        )
        for c in range(planes)
    ]
    prepare_partners(stacked[0:4], stacked[4:7], rows, columns, values)
    sums[...] = own_sums[...]
    wait_all(copies)
    count = list_tiles(home_ref, partner_ref, homes, partners, nblocks, nblocks + 4 * per, nblocks)
    add_tiles(count, homes, partners, home_side, columns, values, sums)

    def total(k):
        high = sums[pl.ds(k, nblocks, stride=16), :]
        return high + sums[pl.ds(k + 8, nblocks, stride=16), :]

    weights = total(6)
    radius = state[3]
    inverse = 1.0 / (radius * radius * radius)
    fresh = []
    for c in range(3):
        speed = state[c + 4]
        spring = state[c] * weights - total(c)
        friction = total(c + 3) - speed * weights
        fresh.append(speed + (stiffness * spring + damping * friction) * inverse)
        updated[c] = fresh[c]

    number = cell[...]
    zeros = jnp.zeros_like(radius)
    highs = [rounded(plane) for plane in [radius] + fresh]
    lows = [plane - high for plane, high in zip([radius] + fresh, highs)]
    highs.append(((number >> 8) * 256).astype(f32))
    lows.append((number & 255).astype(f32))
    put_rows(data, 16, highs + [zeros] * 3 + lows + [zeros] * 3)
    sort_blocks(plan_ref, spots, data, sorted_rows, tiles)

    chunk = rows_up(5 * cap + 1)
    flat = tiles.reshape(tiles.shape[0] * 8, width)
    for ahead, outgoing in enumerate(outgoings):
        target = brick_ahead(ahead, nbrick)
        for side in range(3):
            code, row = side * nbrick + target, side * chunk
            for c in range(5):
                outgoing[row + c * cap : row + (c + 1) * cap, :] = flat[
                    pl.ds(code * (cap + 2) * 8 + c, cap, stride=8), :
                ]
            outgoing[row + 5 * cap : row + 5 * cap + 1, :] = bounds[pl.ds(code, 1), :]


def list_stride(segments, cap):
    return (segments + 1) * cap


def list_arrived(arrived, starts, ends, cap, places, counts):
    base, goal = places
    width = arrived.shape[1]
    stride = list_stride(len(starts), cap)
    shift = width.bit_length() - 1
    lane = iota((1, width), 1)
    filled = [jnp.int32(0)] * 4
    for start, end in zip(starts, ends):
        row = arrived[start + 5 * cap : start + 5 * cap + 1, :]
        edge = jnp.int32(0)
        for j in range(4):
            next_edge = jnp.sum(jnp.where(lane == j, row, 0.0)).astype(jnp.int32)
            first = edge >> shift
            last = jnp.where(next_edge > edge, (next_edge + width - 1) >> shift, first)
            for i in range(cap):
                base[j * stride + filled[j] + i] = start + first + i
                goal[j * stride + filled[j] + i] = end + first + i
            filled[j] = filled[j] + last - first
            edge = next_edge
    for j in range(4):
        counts[j] = filled[j]


def cell_parts(arrived, row, cap, columns, depth, bucket):
    cell = arrived[pl.ds(row + 4 * cap, 1), :].astype(jnp.int32)
    shift = (2 * depth).bit_length() - 1
    column = (cell >> shift) - (bucket // 2) * columns
    level = (cell & (2 * depth - 1)) - (bucket % 2) * depth - depth // 2
    return column.astype(f32), level.astype(f32)


def all_levels(depth, width):
    return (iota((depth, width), 0) - depth // 2).astype(f32).astype(bf16)


def level_hot(level, levels):
    hit = levels == jnp.broadcast_to(level.astype(bf16), levels.shape)
    return jnp.where(hit, jnp.ones((), bf16), jnp.zeros((), bf16))


def steps_of(counts):
    longest = jnp.maximum(
        jnp.maximum(counts[0], counts[1]), jnp.maximum(counts[2], counts[3])
    )
    return lax.shift_right_logical(longest + GROUP - 1, GROUP.bit_length() - 1)


def tile_of(counts, bucket, index, width):
    count = counts[bucket]
    real = jnp.full((1, width), jnp.where(index < count, 1, 0), jnp.int32) > 0
    return jnp.minimum(index, jnp.maximum(count - 1, 0)), real


def deposit(segments, counts, arrived, base, cap, total):
    columns, depth = total.shape[0] // 16, total.shape[1]
    width = arrived.shape[1]
    stride = list_stride(segments, cap)
    numbers = iota((columns, width), 0).astype(f32).astype(bf16)
    levels = all_levels(depth, width)

    def some(step, _):
        sums = []
        for bucket in range(4):
            high_of, low_of, level_of = [], [], []
            for k in range(GROUP):
                index, real = tile_of(counts, bucket, step * GROUP + k, width)
                row = base[bucket * stride + index]
                column, level = cell_parts(arrived, row, cap, columns, depth, bucket)
                radius = arrived[pl.ds(row, 1), :]
                mass = radius * radius * radius
                loads = [mass] + [mass * arrived[pl.ds(row + c * cap, 1), :] for c in (1, 2, 3)]
                hit = numbers == jnp.broadcast_to(column.astype(bf16), (columns, width))
                highs, lows = [], []
                for load in loads:
                    load = jnp.where(real, load, 0.0)
                    high = load.astype(bf16)
                    low = (load - high.astype(f32)).astype(bf16)
                    for parts, part in ((highs, high), (lows, low)):
                        part = jnp.broadcast_to(part, (columns, width))
                        parts.append(jnp.where(hit, part, jnp.zeros((), bf16)))
                high_of.append(jnp.concatenate(highs, axis=0))
                low_of.append(jnp.concatenate(lows, axis=0))
                level_of.append(level_hot(level, levels))
            both = lax.dot_general(
                jnp.concatenate(
                    [jnp.concatenate(high_of, axis=1), jnp.concatenate(low_of, axis=1)], axis=0
                ),
                jnp.concatenate(level_of, axis=1),
                (((1,), (1,)), ((), ())),
                preferred_element_type=f32,
            )
            sums.append(both[0 : 4 * columns] + both[4 * columns :])
        for bucket in range(4):
            total[bucket * 4 * columns : (bucket + 1) * 4 * columns, :] += sums[bucket]
        return 0

    lax.fori_loop(0, steps_of(counts), some, 0)


def sample(segments, counts, arrived, places, cap, table, answers):
    columns, depth = table.shape[0] // 24, table.shape[1]
    width = arrived.shape[1]
    stride = list_stride(segments, cap)
    levels = all_levels(depth, width)
    numbers = iota((columns, width), 0).astype(f32)
    answers[...] = jnp.zeros(answers.shape, f32)

    def some(step, _):
        found = []
        for bucket in range(4):
            hots, hits = [], []
            for k in range(GROUP):
                index, real = tile_of(counts, bucket, step * GROUP + k, width)
                row = places[0][bucket * stride + index]
                column, level = cell_parts(arrived, row, cap, columns, depth, bucket)
                hots.append(level_hot(level, levels))
                hits.append((numbers == column, real, places[1][bucket * stride + index]))
            along = jnp.dot(
                table[bucket * 6 * columns : (bucket + 1) * 6 * columns, :],
                jnp.concatenate(hots, axis=1),
                preferred_element_type=f32,
            )
            for k, (hit, real, goal) in enumerate(hits):
                part = along[:, k * width : (k + 1) * width]
                for c in range(3):
                    value = part[c * columns : (c + 1) * columns]
                    value = value + part[(c + 3) * columns : (c + 4) * columns]
                    value = jnp.sum(jnp.where(hit, value, 0.0), axis=0, keepdims=True)
                    found.append((goal + c * cap, jnp.where(real, value, 0.0)))
        for goal, value in found:
            answers[pl.ds(goal, 1), :] += value
        return 0

    lax.fori_loop(0, steps_of(counts), some, 0)


def first_deposit(nbrick, cap, skip, crossed, below, above, before, after, fluid, total, diffused,
                  flow, base, goal, counts, sems):
    reading = copy_all([(fluid, flow)], sems)
    chunk = rows_up(5 * cap + 1)
    total[...] = jnp.zeros(total.shape, f32)
    starts = [b * chunk for b in range(nbrick)]
    list_arrived(crossed, starts, starts, cap, (base, goal), counts)
    deposit(nbrick, counts, crossed, base, cap, total)
    wait_all(reading)
    diffuse(flow, below, above, before, after, skip, diffused)


def advance(nbrick, cap, above, below, start, fluid, diffused, fluid_next, table, answers_up,
            answers_down, arrived, answers, total, flow, fresh_flow, base, goal, counts, sems):
    reading = pltpu.make_async_copy(fluid, flow, sems.at[0])
    reading.start()
    chunk = rows_up(5 * cap + 1)
    back = rows_up(3 * cap)
    rows = nbrick * chunk
    arrived[0:rows, :] = above[...]
    arrived[rows:, :] = below[...]
    starts = [i * chunk for i in range(2 * nbrick)]
    ends = [i * back for i in range(2 * nbrick)]
    total[...] = start[...]
    list_arrived(arrived, starts, ends, cap, (base, goal), counts)
    deposit(2 * nbrick, counts, arrived, base, cap, total)
    reading.wait()

    nx, ny, nz = flow.shape[1:]
    columns, depth = nx * ny // 2, nz // 2
    for x in range(nx):
        buckets = [2 * (x * ny // columns) + deep for deep in range(2)]
        at = x * ny % columns

        def load(c):
            spots = [4 * columns * bucket + c * columns + at for bucket in buckets]
            return jnp.concatenate([total[spot : spot + ny, :] for spot in spots], axis=1)

        volume = load(0)
        for c in range(3):
            moved = load(c + 1) - volume * flow[c, x]
            fresh = diffused[c, x] + coupling * moved
            fresh_flow[c, x] = fresh
            high = fresh.astype(bf16)
            low = (fresh - high.astype(f32)).astype(bf16)
            for deep, bucket in enumerate(buckets):
                spot = 6 * columns * bucket + c * columns + at
                half = slice(deep * depth, (deep + 1) * depth)
                table[spot : spot + ny, :] = high[:, half]
                table[spot + 3 * columns : spot + 3 * columns + ny, :] = low[:, half]
    writing = pltpu.make_async_copy(fresh_flow, fluid_next, sems.at[1])
    writing.start()
    sample(2 * nbrick, counts, arrived, (base, goal), cap, table, answers)
    answers_up[...] = answers[0 : nbrick * back, :]
    answers_down[...] = answers[nbrick * back :, :]
    writing.wait()


def last_sample(nbrick, cap, crossed, table, *rest):
    answers, base, goal, counts = rest[nbrick:]
    chunk = rows_up(5 * cap + 1)
    back = rows_up(3 * cap)
    starts = [b * chunk for b in range(nbrick)]
    ends = [b * back for b in range(nbrick)]
    list_arrived(crossed, starts, ends, cap, (base, goal), counts)
    sample(nbrick, counts, crossed, (base, goal), cap, table, answers)
    for b, part in enumerate(rest[:nbrick]):
        part[...] = answers[b * back : (b + 1) * back, :]


def relax(nbrick, cap, plan, updated, spots, *rest):
    returneds = rest[:nbrick]
    velocity_next, picked, sorted_rows, tiles, plan_ref, sems = rest[nbrick:]
    copies = copy_all([(plan, plan_ref)], sems)
    nblocks, width = spots.shape
    back = rows_up(3 * cap)
    flat = tiles.reshape(tiles.shape[0] * 8, width)
    for ahead, returned in enumerate(returneds):
        target = brick_ahead(ahead, nbrick)
        for side in range(3):
            code, row = side * nbrick + target, side * back
            for c in range(3):
                flat[pl.ds(code * (cap + 2) * 8 + c, cap, stride=8), :] = returned[
                    row + c * cap : row + (c + 1) * cap, :
                ]
    lane = iota((8, width), 1)
    wait_all(copies)

    def gather(b, _):
        block = jnp.zeros((8, width), f32)
        for j in range(4):
            tile, at = plan_ref[b, j], plan_ref[b, 4 + j]
            first, length = plan_ref[b, 8 + j], plan_ref[b, 12 + j]
            run = jnp.where(lane >= at, tiles[tile], tiles[tile + 1])
            run = pltpu.roll(run, plan_ref[b, 20 + j], 1)
            block = jnp.where((lane >= first) & (lane < first + length), run, block)
        sorted_rows[b] = block
        return 0

    def order(b, _):
        block = sorted_rows[b]
        high = rounded(block)
        both = jnp.dot(
            jnp.concatenate([high, block - high], axis=0).astype(bf16),
            block_order(spots, b),
            preferred_element_type=f32,
        )
        picked[b] = both[0:8] + both[8:16]
        return 0

    lax.fori_loop(0, nblocks, gather, 0, unroll=8)
    lax.fori_loop(0, nblocks, order, 0, unroll=8)
    flat = picked.reshape(nblocks * 8, width)
    for c in range(3):
        now = updated[c]
        velocity_next[c] = now + relaxation * (flat[pl.ds(c, nblocks, stride=8), :] - now)


def on_device(
    positions, velocities, radii, cell_of, block_route, ghost_list, tile_home, tile_partner, fluid
):
    nblocks, _, width = positions.shape
    nbrick = lax.axis_size("brick")
    _, nx, ny, nz = fluid.shape
    columns = nx * ny
    codes = 3 * nbrick
    cap = max(2, (2 * nblocks + codes - 1) // codes)
    chunk, back = rows_up(5 * cap + 1), rows_up(3 * cap)
    per = ghost_list.shape[0] // 2
    tiles = tile_home.shape[0]
    routes = block_route.reshape(-1)
    positions = jnp.transpose(positions, (1, 0, 2))
    velocities = jnp.transpose(velocities, (1, 0, 2))

    def struct(*shape, dtype=f32):
        return jax.ShapeDtypeStruct(shape, dtype)

    def shifted(x, axis, step):
        if step == 0:
            return x
        count = lax.axis_size(axis)
        return lax.ppermute(x, axis, [(i, (i + step) % count) for i in range(count)])

    def ints(count):
        return pltpu.SMEM((count,), jnp.int32)

    state = jnp.concatenate([positions, radii[None], velocities], axis=0)
    ghost_rows, chunks = planes * per, 3 * (nz // width)
    up, down, right, left = call(
        pack_kernel,
        [struct(ghost_rows + chunks * ny, width)] * 2 + [struct(ghost_rows + chunks * nx, width)] * 2,
        [SMEM] + [VMEM] * 2,
        [],
        "pack",
    )(ghost_list, state, fluid)
    below = shifted(up, "slab", 1)
    above = shifted(down, "slab", -1)
    before = shifted(right, "brick", 1)
    after = shifted(left, "brick", -1)

    def sides(count):
        return [
            pltpu.VMEM((count * 32, width), f32),
            pltpu.VMEM((count, width, 32), bf16),
            pltpu.VMEM((count * 16, width), f32),
        ]

    lists = [ints(tiles + UNROLL)] * 2
    contact_flops = tiles * width * width * 200
    chunk_tiles = pltpu.VMEM((codes * (cap + 2), 8, width), f32)
    block_tiles = pltpu.VMEM((nblocks, 8, width), f32)
    plan_copy = pltpu.SMEM((nblocks, width), jnp.int32)
    home_side, sums, spots, plan, bounds = call(
        functools.partial(own_contacts, cap, columns, nz),
        [
            struct((nblocks + 1) * 32, width),
            struct((nblocks + 1) * 16, width),
            struct(nblocks, width),
            struct(nblocks, width, dtype=jnp.int32),
            struct(rows_up(codes), width),
        ],
        [HBM] * 2 + [VMEM] * 3,
        sides(nblocks) + lists + [ints(tiles)] * 2 + [pltpu.SemaphoreType.DMA((2,))],
        "own_contacts",
        contact_flops,
    )(tile_home, tile_partner, state, cell_of, routes.reshape(1, nblocks))
    updated, *outgoing = call(
        functools.partial(ghost_contacts, nbrick, cap, 4 * per),
        [struct(3, nblocks, width)] + [struct(3 * chunk, width)] * nbrick,
        [HBM] * 2 + [ANY] + [VMEM] * 10,
        sides(4 * per)
        + [pltpu.VMEM(((nblocks + 1) * 16, width), f32)]
        + [pltpu.VMEM((nblocks * 16, width), f32), block_tiles, chunk_tiles]
        + lists
        + [ints(tiles), ints(tiles), plan_copy, pltpu.SemaphoreType.DMA((3,))],
        "ghost_contacts",
        contact_flops // 2,
    )(tile_home, tile_partner, plan, below, above, before, after,
      home_side, sums, state, cell_of, spots, bounds)

    crossed = [shifted(part, "brick", ahead) for ahead, part in enumerate(outgoing)]

    def side(k):
        return jnp.concatenate([part[k * chunk : (k + 1) * chunk] for part in crossed], axis=0)

    from_above = shifted(side(0), "slab", -1)
    from_below = shifted(side(2), "slab", 1)
    crossed = side(1)

    def places(count):
        return [ints(4 * list_stride(count, cap))] * 2 + [ints(4)]

    block_flops = 8 * columns * nz * width
    started, diffused = call(
        functools.partial(first_deposit, nbrick, cap, ghost_rows),
        [struct(8 * columns, nz // 2), struct(3, nx, ny, nz)],
        [VMEM] * 5 + [HBM],
        [pltpu.VMEM((3, nx, ny, nz), f32)]
        + places(nbrick)
        + [pltpu.SemaphoreType.DMA((1,))],
        "first_deposit",
        block_flops * nblocks // 3,
    )(crossed, below, above, before, after, fluid)
    fluid_next, table, answers_up, answers_down = call(
        functools.partial(advance, nbrick, cap),
        [
            struct(3, nx, ny, nz),
            struct(12 * columns, nz // 2, dtype=bf16),
            struct(nbrick * back, width),
            struct(nbrick * back, width),
        ],
        [VMEM] * 3 + [HBM, VMEM],
        [
            pltpu.VMEM((2 * nbrick * chunk, width), f32),
            pltpu.VMEM((2 * nbrick * back, width), f32),
            pltpu.VMEM((8 * columns, nz // 2), f32),
        ]
        + [pltpu.VMEM((3, nx, ny, nz), f32)] * 2
        + places(2 * nbrick)
        + [pltpu.SemaphoreType.DMA((2,))],
        "advance",
        block_flops * nblocks,
        places=[HBM] + [VMEM] * 3,
    )(from_above, from_below, started, fluid, diffused)
    answers_up = shifted(answers_up, "slab", 1)
    answers_down = shifted(answers_down, "slab", -1)
    answers = call(
        functools.partial(last_sample, nbrick, cap),
        [struct(back, width)] * nbrick,
        [VMEM] * 2,
        [pltpu.VMEM((nbrick * back, width), f32)] + places(nbrick),
        "last_sample",
        block_flops * nblocks // 4,
    )(crossed, table)
    returned = []
    for behind in range(nbrick):
        at = slice(behind * back, (behind + 1) * back)
        part = jnp.concatenate([answers_up[at], answers[behind], answers_down[at]], axis=0)
        returned.append(shifted(part, "brick", -behind))
    (velocity_next,) = call(
        functools.partial(relax, nbrick, cap),
        [struct(3, nblocks, width)],
        [ANY] + [VMEM] * (2 + nbrick),
        [block_tiles, block_tiles, chunk_tiles, plan_copy]
        + [pltpu.SemaphoreType.DMA((1,))],
        "relax",
    )(plan, updated, spots, *returned)
    return (jnp.transpose(velocity_next, (1, 0, 2)), fluid_next)


def solution(mesh):
    placed = (
        P(("slab", "brick"), None, None),
        P(("slab", "brick"), None, None),
        P(("slab", "brick"), None),
        P(("slab", "brick"), None),
        P(("slab", "brick"), None),
        P(("slab", "brick")),
        P(("slab", "brick")),
        P(("slab", "brick")),
        P(None, "slab", "brick", None),
    )
    return jax.shard_map(
        on_device,
        mesh=mesh,
        in_specs=placed,
        out_specs=(P(("slab", "brick"), None, None), P(None, "slab", "brick", None)),
        check_vma=False,
    )
```

```python
import functools
import math

import jax
import jax.numpy as jnp
from jax import lax
from jax.experimental import pallas as pl
from jax.experimental.pallas import tpu as pltpu
from jax.sharding import PartitionSpec as P

stiffness = 0.01
damping = 0.005
viscosity = 0.1
coupling = 0.5
relaxation = 0.5

f32 = jnp.float32
bf16 = jnp.bfloat16
VMEM = pl.BlockSpec(memory_space=pltpu.VMEM)
SMEM = pl.BlockSpec(memory_space=pltpu.SMEM)
ANY = pl.BlockSpec(memory_space=pl.ANY)
HBM = pl.BlockSpec(memory_space=pltpu.HBM)
UNROLL = 8
GROUP = 2


def rows_up(count):
    return -(-count // 8) * 8


def call(body, outs, ins, scratch, name, flops=0, nbytes=1 << 20, places=None, vmem=40 << 20):
    return pl.pallas_call(
        body,
        out_shape=outs,
        in_specs=ins,
        out_specs=places or [VMEM] * len(outs),
        scratch_shapes=scratch,
        name=name,
        compiler_params=pltpu.CompilerParams(vmem_limit_bytes=vmem),
        cost_estimate=pl.CostEstimate(flops=flops, bytes_accessed=nbytes, transcendentals=0),
    )


def rounded(x):
    return x.astype(bf16).astype(f32)


def iota(shape, dim):
    return lax.broadcasted_iota(jnp.int32, shape, dim)


planes = 7


def copy_all(pairs, sems):
    copies = [pltpu.make_async_copy(*pair, sems.at[i]) for i, pair in enumerate(pairs)]
    for copy in copies:
        copy.start()
    return copies


def wait_all(copies):
    for copy in copies:
        copy.wait()


def pack_kernel(ghost_ref, state, fluid, up, down, right, left):
    count = ghost_ref.shape[0] // 4
    width = state.shape[2]
    nx, ny, nz = fluid.shape[1:]
    for group in range(4):
        i, j = group // 2, group % 2
        slab_to, brick_to = (up if i else down), (right if j else left)
        for g in range(count):
            block = pl.ds(ghost_ref[group * count + g], 1)
            for c in range(planes):
                row = state[c, block, :]
                at = c * 2 * count + j * count + g
                slab_to[at : at + 1, :] = row
                at = c * 2 * count + i * count + g
                brick_to[at : at + 1, :] = row
    for slab_to, x in ((up, nx - 1), (down, 0)):
        for c in range(3):
            for k in range(nz // width):
                at = planes * 2 * count + (c * (nz // width) + k) * ny
                slab_to[at : at + ny, :] = fluid[c, x, :, k * width : (k + 1) * width]
    for brick_to, y in ((right, ny - 1), (left, 0)):
        for c in range(3):
            for x in range(nx):
                for k in range(nz // width):
                    at = planes * 2 * count + (c * nx + x) * (nz // width) + k
                    brick_to[at : at + 1, :] = fluid[
                        c, x, y : y + 1, k * width : (k + 1) * width
                    ]


def three_parts(x):
    one = rounded(x)
    rest = x - one
    two = rounded(rest)
    return one, two, rest - two


def put_rows(ref, stride, rows):
    count = rows[0].shape[0]
    for k, row in enumerate(rows):
        ref[pl.ds(k, count, stride=stride), :] = row


def pair_factors(place):
    parts = [three_parts(plane) for plane in place]
    own = three_parts(
        place[3] * place[3] - place[0] * place[0] - place[1] * place[1] - place[2] * place[2]
    )
    return [[part[k] for part in parts] for k in range(3)], list(own)


def home_rows(place):
    (one, two, three), own = pair_factors(place)
    ones, zeros = jnp.ones_like(place[0]), jnp.zeros_like(place[0])
    rows = one + one + two + two + one + three
    return [2.0 * row for row in rows] + own + [ones] * 3 + [zeros] * 2


def partner_rows(place):
    (one, two, three), own = pair_factors(place)
    ones, zeros = jnp.ones_like(place[0]), jnp.zeros_like(place[0])
    return one + two + one + two + three + one + [ones] * 3 + own + [zeros] * 2


def value_rows(values):
    highs = [rounded(plane) for plane in values]
    ones, zeros = jnp.ones_like(values[0]), jnp.zeros_like(values[0])
    lows = [plane - high for plane, high in zip(values, highs)]
    return highs + [ones, zeros] + lows + [zeros, zeros]


def prepare_partners(place, speeds, rows, columns, values):
    count, width = place[0].shape
    put_rows(rows, 32, partner_rows(place))
    put_rows(values, 16, value_rows(place[0:3] + speeds))

    def turn(b, _):
        block = rows[pl.ds(pl.multiple_of(b * 32, 32), 32), :]
        columns[b] = jnp.transpose(block).astype(bf16)
        return 0

    lax.fori_loop(0, count, turn, 0, unroll=4)


def list_tiles(home_ref, partner_ref, homes, partners, lower, upper, spare):
    def one(t, count):
        partner = partner_ref[t]
        homes[count] = home_ref[t]
        partners[count] = partner - lower
        return count + jnp.where((partner >= lower) & (partner < upper), 1, 0)

    count = lax.fori_loop(0, home_ref.shape[0], one, 0, unroll=4)
    for pad in range(UNROLL):
        homes[count + pad] = spare
        partners[count + pad] = 0
    return count


def add_tiles(count, homes, partners, home_side, partner_side, values, sums):
    def some(step, _):
        for k in range(UNROLL):
            home = homes[step * UNROLL + k]
            partner = partners[step * UNROLL + k]
            factors = home_side[pl.ds(pl.multiple_of(home * 32, 32), 32), :].astype(bf16)
            weight = jnp.dot(partner_side[partner], factors, preferred_element_type=f32)
            weight = jnp.maximum(weight, 0.0)
            high = weight.astype(bf16)
            low = (weight - high.astype(f32)).astype(bf16)
            value = values[pl.ds(pl.multiple_of(partner * 16, 16), 16), :].astype(bf16)
            at = pl.ds(pl.multiple_of(home * 16, 16), 16)
            sums[at, :] += jnp.dot(
                jnp.concatenate([value, value], axis=1),
                jnp.concatenate([high, low], axis=0),
                preferred_element_type=f32,
            )
        return 0

    lax.fori_loop(0, (count + UNROLL - 1) // UNROLL, some, 0)


def dot(left, right):
    return jnp.dot(left.astype(bf16), right.astype(bf16), preferred_element_type=f32)


def plan_sort(cap, cell, route, columns, depth, spots, plan, bounds):
    nblocks, width = cell.shape
    shift = depth.bit_length() - 1
    number = cell[...]
    right = (number >> shift) >= columns // 2
    deep = (number & (depth - 1)) >= depth // 2
    kind = jnp.where(right, 2, 0) + jnp.where(deep, 1, 0)
    members = [jnp.where(kind == j, 1.0, 0.0) for j in range(4)]
    before = jnp.where(iota((width, width), 0) < iota((width, width), 1), 1.0, 0.0)
    stacked = jnp.concatenate(members, axis=0)
    ranks = dot(stacked, before)
    lengths = dot(stacked, jnp.ones((width, width), f32))
    ranks = [ranks[j * nblocks : (j + 1) * nblocks] for j in range(4)]
    lengths = [lengths[j * nblocks : (j + 1) * nblocks] for j in range(4)]

    across = jnp.broadcast_to(route[...].astype(f32), (nblocks, nblocks))
    same = across == jnp.transpose(across)
    earlier = iota((nblocks, nblocks), 1) < iota((nblocks, nblocks), 0)
    side_by_side = jnp.concatenate(lengths, axis=1)
    ahead = dot(jnp.where(same & earlier, 1.0, 0.0), side_by_side)
    whole = dot(jnp.where(same, 1.0, 0.0), side_by_side)
    rows = bounds.shape[0]
    of_code = jnp.broadcast_to(route[...], (rows, nblocks)) == iota((rows, nblocks), 0)
    totals = dot(jnp.where(of_code, 1.0, 0.0), side_by_side)

    lane = iota((nblocks, width), 1)
    bound_lane = iota((rows, width), 1)
    spot = jnp.zeros((nblocks, width), f32)
    first, chunk_first = jnp.zeros((nblocks, width), f32), jnp.zeros((nblocks, width), f32)
    bound, line = jnp.zeros((rows, width), f32), jnp.zeros((rows, width), f32)
    table = jnp.zeros((nblocks, width), jnp.int32)
    own_code = jnp.transpose(across).astype(jnp.int32)
    own_code = jnp.concatenate([own_code] * (width // nblocks), axis=1)
    for j in range(4):
        at = slice(j * width, (j + 1) * width)
        spot = spot + members[j] * (first + ranks[j])
        where = (chunk_first + ahead[:, at]).astype(jnp.int32)
        start, there = first.astype(jnp.int32), where & (width - 1)
        parts = [
            own_code * (cap + 2) + (where >> (width.bit_length() - 1)),
            there,
            start,
            lengths[j].astype(jnp.int32),
            (there - start) & (width - 1),
            (start - there) & (width - 1),
        ]
        for k, part in enumerate(parts):
            table = jnp.where(lane == 4 * k + j, part, table)
        first = first + lengths[j]
        chunk_first = chunk_first + whole[:, at]
        bound = bound + totals[:, at]
        line = jnp.where(bound_lane == j, bound, line)
    spots[...] = spot
    plan[...] = table
    bounds[...] = line


def block_order(spots, b):
    width = spots.shape[1]
    row = jnp.broadcast_to(spots[pl.ds(b, 1), :].astype(bf16), (width, width))
    hit = iota((width, width), 0).astype(f32).astype(bf16) == row
    return jnp.where(hit, jnp.ones((), bf16), jnp.zeros((), bf16))


def sort_blocks(plan, spots, data, sorted_rows, tiles):
    nblocks, width = spots.shape
    lane = iota((8, width), 1)

    def order(b, _):
        rows = data[pl.ds(pl.multiple_of(b * 16, 16), 16), :].astype(bf16)
        both = lax.dot_general(
            rows, block_order(spots, b), (((1,), (1,)), ((), ())), preferred_element_type=f32
        )
        sorted_rows[b] = both[0:8] + both[8:16]
        return 0

    def spread(b, _):
        block = sorted_rows[b]
        for j in range(4):
            tile, at, length = plan[b, j], plan[b, 4 + j], plan[b, 12 + j]
            moved = pltpu.roll(block, plan[b, 16 + j], 1)
            here = (lane >= at) & (lane < at + length)
            pltpu.store(tiles.at[tile], moved, mask=here)
            pltpu.store(tiles.at[tile + 1], moved, mask=lane < at + length - width)
        return 0

    lax.fori_loop(0, nblocks, order, 0, unroll=8)
    lax.fori_loop(0, nblocks, spread, 0, unroll=8)


def own_contacts(cap, columns, depth, home_list, partner_list, state, cell, route,
                 home_side, sums, spots, plan, bounds,
                 rows, partner_side, values, homes, partners, home_ref, partner_ref, sems):
    nblocks, width = state.shape[1:]
    copies = copy_all([(home_list, home_ref), (partner_list, partner_ref)], sems)
    plan_sort(cap, cell, route, columns, depth, spots, plan, bounds)
    place = [state[c] for c in range(4)]
    put_rows(home_side, 32, home_rows(place))
    prepare_partners(place, [state[c] for c in (4, 5, 6)], rows, partner_side, values)
    home_side[nblocks * 32 :, :] = jnp.zeros((32, width), f32)
    sums[...] = jnp.zeros(sums.shape, f32)
    wait_all(copies)
    count = list_tiles(home_ref, partner_ref, homes, partners, 0, nblocks, nblocks)
    add_tiles(count, homes, partners, home_side, partner_side, values, sums)


def diffuse(fluid, below, above, before, after, skip, diffused):
    nx, ny, nz = fluid.shape[1:]
    width = before.shape[1]
    deep = iota((ny, nz), 1)

    def face(ref, c, x):
        at = skip + (c * nx + x) * (nz // width)
        return jnp.concatenate(
            [ref[at + k : at + k + 1, :] for k in range(nz // width)], axis=1
        )

    def layer(ref, c):
        at = [skip + (c * (nz // width) + k) * ny for k in range(nz // width)]
        return jnp.concatenate([ref[start : start + ny, :] for start in at], axis=1)

    for x in range(nx):
        for c in range(3):
            here = fluid[c, x]
            near = (layer(below, c) if x == 0 else fluid[c, x - 1]) + (
                layer(above, c) if x == nx - 1 else fluid[c, x + 1]
            )
            near = near + jnp.concatenate([face(before, c, x), here[:-1]], axis=0)
            near = near + jnp.concatenate([here[1:], face(after, c, x)], axis=0)
            near = near + jnp.where(deep == 0, 0.0, pltpu.roll(here, 1, 1))
            near = near + jnp.where(deep == nz - 1, 0.0, pltpu.roll(here, nz - 1, 1))
            diffused[c, x] = here + viscosity * (near - 6.0 * here)


def brick_ahead(ahead, nbrick):
    return lax.rem(lax.axis_index("brick") + ahead, nbrick)


def ghost_contacts(nbrick, cap, partner_blocks, home_list, partner_list, plan, below,
                   above, before, after, home_side, own_sums, state, cell, spots, bounds,
                   updated, down, *rest):
    outgoings = rest[:nbrick]
    (rows, columns, values, sums, data, sorted_rows, tiles, homes, partners,
     home_ref, partner_ref, plan_ref, sems) = rest[nbrick:]
    nblocks, width = state.shape[1:]
    per = partner_blocks // 4
    copies = copy_all(
        [
            (home_list, home_ref),
            (partner_list, partner_ref),
            (plan, plan_ref),
        ],
        sems,
    )
    stacked = [
        jnp.concatenate(
            [ref[c * per : (c + 1) * per, :] for ref in (below, above, before, after)], axis=0
        )
        for c in range(planes)
    ]
    prepare_partners(stacked[0:4], stacked[4:7], rows, columns, values)
    sums[...] = own_sums[...]
    wait_all(copies)
    count = list_tiles(home_ref, partner_ref, homes, partners, nblocks, nblocks + 4 * per, nblocks)
    add_tiles(count, homes, partners, home_side, columns, values, sums)

    def total(k):
        high = sums[pl.ds(k, nblocks, stride=16), :]
        return high + sums[pl.ds(k + 8, nblocks, stride=16), :]

    weights = total(6)
    radius = state[3]
    inverse = 1.0 / (radius * radius * radius)
    fresh = []
    for c in range(3):
        speed = state[c + 4]
        spring = state[c] * weights - total(c)
        friction = total(c + 3) - speed * weights
        fresh.append(speed + (stiffness * spring + damping * friction) * inverse)
        updated[c] = fresh[c]

    number = cell[...]
    zeros = jnp.zeros_like(radius)
    highs = [rounded(plane) for plane in [radius] + fresh]
    lows = [plane - high for plane, high in zip([radius] + fresh, highs)]
    highs.append(((number >> 8) * 256).astype(f32))
    lows.append((number & 255).astype(f32))
    put_rows(data, 16, highs + [zeros] * 3 + lows + [zeros] * 3)
    sort_blocks(plan_ref, spots, data, sorted_rows, tiles)

    chunk = rows_up(5 * cap + 1)
    flat = tiles.reshape(tiles.shape[0] * 8, width)
    for ahead in range(nbrick):
        target = brick_ahead(ahead, nbrick)
        for side, (outgoing, row) in enumerate(
            ((down, ahead * chunk), (outgoings[ahead], 0), (outgoings[ahead], chunk))
        ):
            code = side * nbrick + target
            for c in range(5):
                outgoing[row + c * cap : row + (c + 1) * cap, :] = flat[
                    pl.ds(code * (cap + 2) * 8 + c, cap, stride=8), :
                ]
            outgoing[row + 5 * cap : row + 5 * cap + 1, :] = bounds[pl.ds(code, 1), :]


def list_stride(segments, cap):
    return (segments + 1) * cap


def list_arrived(arrived, starts, ends, cap, places, counts):
    base, goal = places
    width = arrived.shape[1]
    stride = list_stride(len(starts), cap)
    shift = width.bit_length() - 1
    lane = iota((1, width), 1)
    filled = [jnp.int32(0)] * 4
    for start, end in zip(starts, ends):
        row = arrived[start + 5 * cap : start + 5 * cap + 1, :]
        edge = jnp.int32(0)
        for j in range(4):
            next_edge = jnp.sum(jnp.where(lane == j, row, 0.0)).astype(jnp.int32)
            first = edge >> shift
            last = jnp.where(next_edge > edge, (next_edge + width - 1) >> shift, first)
            for i in range(cap):
                base[j * stride + filled[j] + i] = start + first + i
                goal[j * stride + filled[j] + i] = end + first + i
            filled[j] = filled[j] + last - first
            edge = next_edge
    for j in range(4):
        counts[j] = filled[j]


def cell_parts(arrived, row, cap, columns, depth, bucket):
    cell = arrived[pl.ds(row + 4 * cap, 1), :].astype(jnp.int32)
    shift = (2 * depth).bit_length() - 1
    column = (cell >> shift) - (bucket // 2) * columns
    level = (cell & (2 * depth - 1)) - (bucket % 2) * depth - depth // 2
    return column.astype(f32), level.astype(f32)


def all_levels(depth, width):
    return (iota((depth, width), 0) - depth // 2).astype(f32).astype(bf16)


def level_hot(level, levels):
    hit = levels == jnp.broadcast_to(level.astype(bf16), levels.shape)
    return jnp.where(hit, jnp.ones((), bf16), jnp.zeros((), bf16))


def steps_of(counts):
    longest = jnp.maximum(
        jnp.maximum(counts[0], counts[1]), jnp.maximum(counts[2], counts[3])
    )
    return lax.shift_right_logical(longest + GROUP - 1, GROUP.bit_length() - 1)


def tile_of(counts, bucket, index, width):
    count = counts[bucket]
    real = jnp.full((1, width), jnp.where(index < count, 1, 0), jnp.int32) > 0
    return jnp.minimum(index, jnp.maximum(count - 1, 0)), real


def deposit(segments, counts, arrived, base, cap, total):
    columns, depth = total.shape[0] // 16, total.shape[1]
    width = arrived.shape[1]
    stride = list_stride(segments, cap)
    numbers = iota((columns, width), 0).astype(f32).astype(bf16)
    levels = all_levels(depth, width)

    def some(step, _):
        sums = []
        for bucket in range(4):
            high_of, low_of, level_of = [], [], []
            for k in range(GROUP):
                index, real = tile_of(counts, bucket, step * GROUP + k, width)
                row = base[bucket * stride + index]
                column, level = cell_parts(arrived, row, cap, columns, depth, bucket)
                radius = arrived[pl.ds(row, 1), :]
                mass = radius * radius * radius
                loads = [mass] + [mass * arrived[pl.ds(row + c * cap, 1), :] for c in (1, 2, 3)]
                hit = numbers == jnp.broadcast_to(column.astype(bf16), (columns, width))
                highs, lows = [], []
                for load in loads:
                    load = jnp.where(real, load, 0.0)
                    high = load.astype(bf16)
                    low = (load - high.astype(f32)).astype(bf16)
                    for parts, part in ((highs, high), (lows, low)):
                        part = jnp.broadcast_to(part, (columns, width))
                        parts.append(jnp.where(hit, part, jnp.zeros((), bf16)))
                high_of.append(jnp.concatenate(highs, axis=0))
                low_of.append(jnp.concatenate(lows, axis=0))
                level_of.append(level_hot(level, levels))
            both = lax.dot_general(
                jnp.concatenate(
                    [jnp.concatenate(high_of, axis=1), jnp.concatenate(low_of, axis=1)], axis=0
                ),
                jnp.concatenate(level_of, axis=1),
                (((1,), (1,)), ((), ())),
                preferred_element_type=f32,
            )
            sums.append(both[0 : 4 * columns] + both[4 * columns :])
        for bucket in range(4):
            total[bucket * 4 * columns : (bucket + 1) * 4 * columns, :] += sums[bucket]
        return 0

    lax.fori_loop(0, steps_of(counts), some, 0)


def sample(segments, counts, arrived, places, cap, table, answers):
    columns, depth = table.shape[0] // 24, table.shape[1]
    width = arrived.shape[1]
    stride = list_stride(segments, cap)
    levels = all_levels(depth, width)
    numbers = iota((columns, width), 0).astype(f32)
    answers[...] = jnp.zeros(answers.shape, f32)

    def some(step, _):
        found = []
        for bucket in range(4):
            hots, hits = [], []
            for k in range(GROUP):
                index, real = tile_of(counts, bucket, step * GROUP + k, width)
                row = places[0][bucket * stride + index]
                column, level = cell_parts(arrived, row, cap, columns, depth, bucket)
                hots.append(level_hot(level, levels))
                hits.append((numbers == column, real, places[1][bucket * stride + index]))
            along = jnp.dot(
                table[bucket * 6 * columns : (bucket + 1) * 6 * columns, :],
                jnp.concatenate(hots, axis=1),
                preferred_element_type=f32,
            )
            for k, (hit, real, goal) in enumerate(hits):
                part = along[:, k * width : (k + 1) * width]
                for c in range(3):
                    value = part[c * columns : (c + 1) * columns]
                    value = value + part[(c + 3) * columns : (c + 4) * columns]
                    value = jnp.sum(jnp.where(hit, value, 0.0), axis=0, keepdims=True)
                    found.append((goal + c * cap, jnp.where(real, value, 0.0)))
        for goal, value in found:
            answers[pl.ds(goal, 1), :] += value
        return 0

    lax.fori_loop(0, steps_of(counts), some, 0)


def first_deposit(nbrick, cap, skip, crossed, below, above, before, after, fluid, total, diffused,
                  flow, base, goal, counts, sems):
    reading = copy_all([(fluid, flow)], sems)
    chunk = rows_up(5 * cap + 1)
    total[...] = jnp.zeros(total.shape, f32)
    starts = [b * chunk for b in range(nbrick)]
    list_arrived(crossed, starts, starts, cap, (base, goal), counts)
    deposit(nbrick, counts, crossed, base, cap, total)
    wait_all(reading)
    diffuse(flow, below, above, before, after, skip, diffused)


def advance(nbrick, cap, start, fluid, diffused, below, *rest):
    above, rest = rest[:nbrick], rest[nbrick:]
    fluid_next, table, answers_below = rest[:3]
    answers_above, rest = rest[3 : 3 + nbrick], rest[3 + nbrick :]
    arrived, answers, total, flow, fresh_flow, base, goal, counts, sems = rest
    reading = pltpu.make_async_copy(fluid, flow, sems.at[0])
    reading.start()
    chunk = rows_up(5 * cap + 1)
    back = rows_up(3 * cap)
    rows = nbrick * chunk
    for b, part in enumerate(above):
        arrived[b * chunk : (b + 1) * chunk, :] = part[...]
    arrived[rows:, :] = below[...]
    starts = [i * chunk for i in range(2 * nbrick)]
    ends = [i * back for i in range(2 * nbrick)]
    total[...] = start[...]
    list_arrived(arrived, starts, ends, cap, (base, goal), counts)
    deposit(2 * nbrick, counts, arrived, base, cap, total)
    reading.wait()

    nx, ny, nz = flow.shape[1:]
    columns, depth = nx * ny // 2, nz // 2
    for x in range(nx):
        buckets = [2 * (x * ny // columns) + deep for deep in range(2)]
        at = x * ny % columns

        def load(c):
            spots = [4 * columns * bucket + c * columns + at for bucket in buckets]
            return jnp.concatenate([total[spot : spot + ny, :] for spot in spots], axis=1)

        volume = load(0)
        for c in range(3):
            moved = load(c + 1) - volume * flow[c, x]
            fresh = diffused[c, x] + coupling * moved
            fresh_flow[c, x] = fresh
            high = fresh.astype(bf16)
            low = (fresh - high.astype(f32)).astype(bf16)
            for deep, bucket in enumerate(buckets):
                spot = 6 * columns * bucket + c * columns + at
                half = slice(deep * depth, (deep + 1) * depth)
                table[spot : spot + ny, :] = high[:, half]
                table[spot + 3 * columns : spot + 3 * columns + ny, :] = low[:, half]
    writing = pltpu.make_async_copy(fresh_flow, fluid_next, sems.at[1])
    writing.start()
    sample(2 * nbrick, counts, arrived, (base, goal), cap, table, answers)
    for b, part in enumerate(answers_above):
        part[...] = answers[b * back : (b + 1) * back, :]
    answers_below[...] = answers[nbrick * back :, :]
    writing.wait()


def last_sample(nbrick, cap, crossed, table, *rest):
    answers, base, goal, counts = rest[nbrick:]
    chunk = rows_up(5 * cap + 1)
    back = rows_up(3 * cap)
    starts = [b * chunk for b in range(nbrick)]
    ends = [b * back for b in range(nbrick)]
    list_arrived(crossed, starts, ends, cap, (base, goal), counts)
    sample(nbrick, counts, crossed, (base, goal), cap, table, answers)
    for b, part in enumerate(rest[:nbrick]):
        part[...] = answers[b * back : (b + 1) * back, :]


def relax(nbrick, cap, plan, updated, spots, down, *rest):
    returneds = rest[:nbrick]
    velocity_next, picked, sorted_rows, tiles, plan_ref, sems = rest[nbrick:]
    copies = copy_all([(plan, plan_ref)], sems)
    nblocks, width = spots.shape
    back = rows_up(3 * cap)
    flat = tiles.reshape(tiles.shape[0] * 8, width)
    for ahead in range(nbrick):
        target = brick_ahead(ahead, nbrick)
        for side, (returned, row) in enumerate(
            ((down, ahead * back), (returneds[ahead], 0), (returneds[ahead], back))
        ):
            code = side * nbrick + target
            for c in range(3):
                flat[pl.ds(code * (cap + 2) * 8 + c, cap, stride=8), :] = returned[
                    row + c * cap : row + (c + 1) * cap, :
                ]
    lane = iota((8, width), 1)
    wait_all(copies)

    def gather(b, _):
        block = jnp.zeros((8, width), f32)
        for j in range(4):
            tile, at = plan_ref[b, j], plan_ref[b, 4 + j]
            first, length = plan_ref[b, 8 + j], plan_ref[b, 12 + j]
            run = jnp.where(lane >= at, tiles[tile], tiles[tile + 1])
            run = pltpu.roll(run, plan_ref[b, 20 + j], 1)
            block = jnp.where((lane >= first) & (lane < first + length), run, block)
        sorted_rows[b] = block
        return 0

    def order(b, _):
        block = sorted_rows[b]
        high = rounded(block)
        both = jnp.dot(
            jnp.concatenate([high, block - high], axis=0).astype(bf16),
            block_order(spots, b),
            preferred_element_type=f32,
        )
        picked[b] = both[0:8] + both[8:16]
        return 0

    lax.fori_loop(0, nblocks, gather, 0, unroll=8)
    lax.fori_loop(0, nblocks, order, 0, unroll=8)
    flat = picked.reshape(nblocks * 8, width)
    for c in range(3):
        now = updated[c]
        velocity_next[c] = now + relaxation * (flat[pl.ds(c, nblocks, stride=8), :] - now)


def on_device(
    positions, velocities, radii, cell_of, block_route, ghost_list, tile_home, tile_partner, fluid
):
    nblocks, _, width = positions.shape
    nbrick = lax.axis_size("brick")
    _, nx, ny, nz = fluid.shape
    columns = nx * ny
    codes = 3 * nbrick
    cap = max(2, (2 * nblocks + codes - 1) // codes)
    chunk, back = rows_up(5 * cap + 1), rows_up(3 * cap)
    per = ghost_list.shape[0] // 2
    tiles = tile_home.shape[0]
    routes = block_route.reshape(-1)
    positions = jnp.transpose(positions, (1, 0, 2))
    velocities = jnp.transpose(velocities, (1, 0, 2))

    def struct(*shape, dtype=f32):
        return jax.ShapeDtypeStruct(shape, dtype)

    def shifted(x, axis, step):
        if step == 0:
            return x
        count = lax.axis_size(axis)
        return lax.ppermute(x, axis, [(i, (i + step) % count) for i in range(count)])

    def ints(count):
        return pltpu.SMEM((count,), jnp.int32)

    state = jnp.concatenate([positions, radii[None], velocities], axis=0)
    ghost_rows, chunks = planes * per, 3 * (nz // width)
    up, low, right, left = call(
        pack_kernel,
        [struct(ghost_rows + chunks * ny, width)] * 2 + [struct(ghost_rows + chunks * nx, width)] * 2,
        [SMEM] + [VMEM] * 2,
        [],
        "pack",
    )(ghost_list, state, fluid)
    below = shifted(up, "slab", 1)
    above = shifted(low, "slab", -1)
    before = shifted(right, "brick", 1)
    after = shifted(left, "brick", -1)

    def sides(count):
        return [
            pltpu.VMEM((count * 32, width), f32),
            pltpu.VMEM((count, width, 32), bf16),
            pltpu.VMEM((count * 16, width), f32),
        ]

    lists = [ints(tiles + UNROLL)] * 2
    contact_flops = tiles * width * width * 200
    chunk_tiles = pltpu.VMEM((codes * (cap + 2), 8, width), f32)
    block_tiles = pltpu.VMEM((nblocks, 8, width), f32)
    plan_copy = pltpu.SMEM((nblocks, width), jnp.int32)
    home_side, sums, spots, plan, bounds = call(
        functools.partial(own_contacts, cap, columns, nz),
        [
            struct((nblocks + 1) * 32, width),
            struct((nblocks + 1) * 16, width),
            struct(nblocks, width),
            struct(nblocks, width, dtype=jnp.int32),
            struct(rows_up(codes), width),
        ],
        [HBM] * 2 + [VMEM] * 3,
        sides(nblocks) + lists + [ints(tiles)] * 2 + [pltpu.SemaphoreType.DMA((2,))],
        "own_contacts",
        contact_flops,
    )(tile_home, tile_partner, state, cell_of, routes.reshape(1, nblocks))
    updated, down, *outgoing = call(
        functools.partial(ghost_contacts, nbrick, cap, 4 * per),
        [struct(3, nblocks, width), struct(nbrick * chunk, width)]
        + [struct(2 * chunk, width)] * nbrick,
        [HBM] * 2 + [ANY] + [VMEM] * 10,
        sides(4 * per)
        + [pltpu.VMEM(((nblocks + 1) * 16, width), f32)]
        + [pltpu.VMEM((nblocks * 16, width), f32), block_tiles, chunk_tiles]
        + lists
        + [ints(tiles), ints(tiles), plan_copy, pltpu.SemaphoreType.DMA((3,))],
        "ghost_contacts",
        contact_flops // 2,
    )(tile_home, tile_partner, plan, below, above, before, after,
      home_side, sums, state, cell_of, spots, bounds)

    down = shifted(down, "slab", -1)
    near = [shifted(part, "brick", ahead) for ahead, part in enumerate(outgoing)]
    from_below = shifted(jnp.concatenate([part[chunk:] for part in near], axis=0), "slab", 1)
    from_above = [
        shifted(down[ahead * chunk : (ahead + 1) * chunk], "brick", ahead)
        for ahead in range(nbrick)
    ]
    crossed = jnp.concatenate([part[:chunk] for part in near], axis=0)

    def places(count):
        return [ints(4 * list_stride(count, cap))] * 2 + [ints(4)]

    block_flops = 8 * columns * nz * width
    started, diffused = call(
        functools.partial(first_deposit, nbrick, cap, ghost_rows),
        [struct(8 * columns, nz // 2), struct(3, nx, ny, nz)],
        [VMEM] * 5 + [HBM],
        [pltpu.VMEM((3, nx, ny, nz), f32)]
        + places(nbrick)
        + [pltpu.SemaphoreType.DMA((1,))],
        "first_deposit",
        block_flops * nblocks // 3,
    )(crossed, below, above, before, after, fluid)
    fluid_next, table, answers_below, *answers_above = call(
        functools.partial(advance, nbrick, cap),
        [
            struct(3, nx, ny, nz),
            struct(12 * columns, nz // 2, dtype=bf16),
            struct(nbrick * back, width),
        ]
        + [struct(back, width)] * nbrick,
        [VMEM, HBM] + [VMEM] * (2 + nbrick),
        [
            pltpu.VMEM((2 * nbrick * chunk, width), f32),
            pltpu.VMEM((2 * nbrick * back, width), f32),
            pltpu.VMEM((8 * columns, nz // 2), f32),
        ]
        + [pltpu.VMEM((3, nx, ny, nz), f32)] * 2
        + places(2 * nbrick)
        + [pltpu.SemaphoreType.DMA((2,))],
        "advance",
        block_flops * nblocks,
        places=[HBM] + [VMEM] * (2 + nbrick),
    )(started, fluid, diffused, from_below, *from_above)
    answers_below = shifted(answers_below, "slab", -1)
    answers_above = [
        shifted(part, "brick", -behind) for behind, part in enumerate(answers_above)
    ]
    returned_down = shifted(jnp.concatenate(answers_above, axis=0), "slab", 1)
    answers = call(
        functools.partial(last_sample, nbrick, cap),
        [struct(back, width)] * nbrick,
        [VMEM] * 2,
        [pltpu.VMEM((nbrick * back, width), f32)] + places(nbrick),
        "last_sample",
        block_flops * nblocks // 64,
    )(crossed, table)
    returned = []
    for behind in range(nbrick):
        at = slice(behind * back, (behind + 1) * back)
        part = jnp.concatenate([answers[behind], answers_below[at]], axis=0)
        returned.append(shifted(part, "brick", -behind))
    (velocity_next,) = call(
        functools.partial(relax, nbrick, cap),
        [struct(3, nblocks, width)],
        [ANY] + [VMEM] * (3 + nbrick),
        [block_tiles, block_tiles, chunk_tiles, plan_copy]
        + [pltpu.SemaphoreType.DMA((1,))],
        "relax",
    )(plan, updated, spots, returned_down, *returned)
    return (jnp.transpose(velocity_next, (1, 0, 2)), fluid_next)


def solution(mesh):
    placed = (
        P(("slab", "brick"), None, None),
        P(("slab", "brick"), None, None),
        P(("slab", "brick"), None),
        P(("slab", "brick"), None),
        P(("slab", "brick"), None),
        P(("slab", "brick")),
        P(("slab", "brick")),
        P(("slab", "brick")),
        P(None, "slab", "brick", None),
    )
    return jax.shard_map(
        on_device,
        mesh=mesh,
        in_specs=placed,
        out_specs=(P(("slab", "brick"), None, None), P(None, "slab", "brick", None)),
        check_vma=False,
    )
```

```python
import functools
import math

import jax
import jax.numpy as jnp
from jax import lax
from jax.experimental import pallas as pl
from jax.experimental.pallas import tpu as pltpu
from jax.sharding import PartitionSpec as P

stiffness = 0.01
damping = 0.005
viscosity = 0.1
coupling = 0.5
relaxation = 0.5

f32 = jnp.float32
bf16 = jnp.bfloat16
VMEM = pl.BlockSpec(memory_space=pltpu.VMEM)
SMEM = pl.BlockSpec(memory_space=pltpu.SMEM)
ANY = pl.BlockSpec(memory_space=pl.ANY)
HBM = pl.BlockSpec(memory_space=pltpu.HBM)
UNROLL = 16
GROUP = 2


def rows_up(count):
    return -(-count // 8) * 8


def call(body, outs, ins, scratch, name, flops=0, nbytes=1 << 20, places=None, vmem=40 << 20):
    return pl.pallas_call(
        body,
        out_shape=outs,
        in_specs=ins,
        out_specs=places or [VMEM] * len(outs),
        scratch_shapes=scratch,
        name=name,
        compiler_params=pltpu.CompilerParams(vmem_limit_bytes=vmem),
        cost_estimate=pl.CostEstimate(flops=flops, bytes_accessed=nbytes, transcendentals=0),
    )


def rounded(x):
    return x.astype(bf16).astype(f32)


def iota(shape, dim):
    return lax.broadcasted_iota(jnp.int32, shape, dim)


planes = 7


def copy_all(pairs, sems):
    copies = [pltpu.make_async_copy(*pair, sems.at[i]) for i, pair in enumerate(pairs)]
    for copy in copies:
        copy.start()
    return copies


def wait_all(copies):
    for copy in copies:
        copy.wait()


def pack_kernel(ghost_ref, state, fluid, up, down, right, left):
    count = ghost_ref.shape[0] // 4
    width = state.shape[2]
    nx, ny, nz = fluid.shape[1:]
    for group in range(4):
        i, j = group // 2, group % 2
        slab_to, brick_to = (up if i else down), (right if j else left)
        for g in range(count):
            block = pl.ds(ghost_ref[group * count + g], 1)
            for c in range(planes):
                row = state[c, block, :]
                at = c * 2 * count + j * count + g
                slab_to[at : at + 1, :] = row
                at = c * 2 * count + i * count + g
                brick_to[at : at + 1, :] = row
    for slab_to, x in ((up, nx - 1), (down, 0)):
        for c in range(3):
            for k in range(nz // width):
                at = planes * 2 * count + (c * (nz // width) + k) * ny
                slab_to[at : at + ny, :] = fluid[c, x, :, k * width : (k + 1) * width]
    for brick_to, y in ((right, ny - 1), (left, 0)):
        for c in range(3):
            for x in range(nx):
                for k in range(nz // width):
                    at = planes * 2 * count + (c * nx + x) * (nz // width) + k
                    brick_to[at : at + 1, :] = fluid[
                        c, x, y : y + 1, k * width : (k + 1) * width
                    ]


def three_parts(x):
    one = rounded(x)
    rest = x - one
    two = rounded(rest)
    return one, two, rest - two


def put_rows(ref, stride, rows):
    count = rows[0].shape[0]
    for k, row in enumerate(rows):
        ref[pl.ds(k, count, stride=stride), :] = row


def pair_factors(place):
    parts = [three_parts(plane) for plane in place]
    own = three_parts(
        place[3] * place[3] - place[0] * place[0] - place[1] * place[1] - place[2] * place[2]
    )
    return [[part[k] for part in parts] for k in range(3)], list(own)


def home_rows(place):
    (one, two, three), own = pair_factors(place)
    ones, zeros = jnp.ones_like(place[0]), jnp.zeros_like(place[0])
    rows = one + one + two + two + one + three
    return [2.0 * row for row in rows] + own + [ones] * 3 + [zeros] * 2


def partner_rows(place):
    (one, two, three), own = pair_factors(place)
    ones, zeros = jnp.ones_like(place[0]), jnp.zeros_like(place[0])
    return one + two + one + two + three + one + [ones] * 3 + own + [zeros] * 2


def value_rows(values):
    highs = [rounded(plane) for plane in values]
    ones, zeros = jnp.ones_like(values[0]), jnp.zeros_like(values[0])
    lows = [plane - high for plane, high in zip(values, highs)]
    return highs + [ones, zeros] + lows + [zeros, zeros]


def prepare_partners(place, speeds, rows, columns, values):
    count, width = place[0].shape
    put_rows(rows, 32, partner_rows(place))
    put_rows(values, 16, value_rows(place[0:3] + speeds))

    def turn(b, _):
        block = rows[pl.ds(pl.multiple_of(b * 32, 32), 32), :]
        columns[b] = jnp.transpose(block).astype(bf16)
        return 0

    lax.fori_loop(0, count, turn, 0, unroll=8)


def list_tiles(home_ref, partner_ref, homes, partners, lower, upper, spare):
    def one(t, count):
        partner = partner_ref[t]
        homes[count] = home_ref[t]
        partners[count] = partner - lower
        return count + jnp.where((partner >= lower) & (partner < upper), 1, 0)

    count = lax.fori_loop(0, home_ref.shape[0], one, 0, unroll=4)
    for pad in range(UNROLL):
        homes[count + pad] = spare
        partners[count + pad] = 0
    return count


def add_tiles(count, homes, partners, home_side, partner_side, values, sums):
    def some(step, _):
        for k in range(UNROLL):
            home = homes[step * UNROLL + k]
            partner = partners[step * UNROLL + k]
            factors = home_side[pl.ds(pl.multiple_of(home * 32, 32), 32), :].astype(bf16)
            weight = jnp.dot(partner_side[partner], factors, preferred_element_type=f32)
            weight = jnp.maximum(weight, 0.0)
            high = weight.astype(bf16)
            low = (weight - high.astype(f32)).astype(bf16)
            value = values[pl.ds(pl.multiple_of(partner * 16, 16), 16), :].astype(bf16)
            at = pl.ds(pl.multiple_of(home * 16, 16), 16)
            sums[at, :] += jnp.dot(
                jnp.concatenate([value, value], axis=1),
                jnp.concatenate([high, low], axis=0),
                preferred_element_type=f32,
            )
        return 0

    lax.fori_loop(0, (count + UNROLL - 1) // UNROLL, some, 0)


def dot(left, right):
    return jnp.dot(left.astype(bf16), right.astype(bf16), preferred_element_type=f32)


def plan_sort(cap, cell, route, columns, depth, spots, plan, bounds):
    nblocks, width = cell.shape
    shift = depth.bit_length() - 1
    number = cell[...]
    right = (number >> shift) >= columns // 2
    deep = (number & (depth - 1)) >= depth // 2
    kind = jnp.where(right, 2, 0) + jnp.where(deep, 1, 0)
    members = [jnp.where(kind == j, 1.0, 0.0) for j in range(4)]
    before = jnp.where(iota((width, width), 0) < iota((width, width), 1), 1.0, 0.0)
    stacked = jnp.concatenate(members, axis=0)
    ranks = dot(stacked, before)
    lengths = dot(stacked, jnp.ones((width, width), f32))
    ranks = [ranks[j * nblocks : (j + 1) * nblocks] for j in range(4)]
    lengths = [lengths[j * nblocks : (j + 1) * nblocks] for j in range(4)]

    across = jnp.broadcast_to(route[...].astype(f32), (nblocks, nblocks))
    same = across == jnp.transpose(across)
    earlier = iota((nblocks, nblocks), 1) < iota((nblocks, nblocks), 0)
    side_by_side = jnp.concatenate(lengths, axis=1)
    ahead = dot(jnp.where(same & earlier, 1.0, 0.0), side_by_side)
    whole = dot(jnp.where(same, 1.0, 0.0), side_by_side)
    rows = bounds.shape[0]
    of_code = jnp.broadcast_to(route[...], (rows, nblocks)) == iota((rows, nblocks), 0)
    totals = dot(jnp.where(of_code, 1.0, 0.0), side_by_side)

    lane = iota((nblocks, width), 1)
    bound_lane = iota((rows, width), 1)
    spot = jnp.zeros((nblocks, width), f32)
    first, chunk_first = jnp.zeros((nblocks, width), f32), jnp.zeros((nblocks, width), f32)
    bound, line = jnp.zeros((rows, width), f32), jnp.zeros((rows, width), f32)
    table = jnp.zeros((nblocks, width), jnp.int32)
    own_code = jnp.transpose(across).astype(jnp.int32)
    own_code = jnp.concatenate([own_code] * (width // nblocks), axis=1)
    for j in range(4):
        at = slice(j * width, (j + 1) * width)
        spot = spot + members[j] * (first + ranks[j])
        where = (chunk_first + ahead[:, at]).astype(jnp.int32)
        start, there = first.astype(jnp.int32), where & (width - 1)
        parts = [
            own_code * (cap + 2) + (where >> (width.bit_length() - 1)),
            there,
            start,
            lengths[j].astype(jnp.int32),
            (there - start) & (width - 1),
            (start - there) & (width - 1),
        ]
        for k, part in enumerate(parts):
            table = jnp.where(lane == 4 * k + j, part, table)
        first = first + lengths[j]
        chunk_first = chunk_first + whole[:, at]
        bound = bound + totals[:, at]
        line = jnp.where(bound_lane == j, bound, line)
    spots[...] = spot
    plan[...] = table
    bounds[...] = line


def block_order(spots, b):
    width = spots.shape[1]
    row = jnp.broadcast_to(spots[pl.ds(b, 1), :].astype(bf16), (width, width))
    hit = iota((width, width), 0).astype(f32).astype(bf16) == row
    return jnp.where(hit, jnp.ones((), bf16), jnp.zeros((), bf16))


def sort_blocks(plan, spots, data, sorted_rows, tiles):
    nblocks, width = spots.shape
    lane = iota((8, width), 1)

    def order(b, _):
        rows = data[pl.ds(pl.multiple_of(b * 16, 16), 16), :].astype(bf16)
        both = lax.dot_general(
            rows, block_order(spots, b), (((1,), (1,)), ((), ())), preferred_element_type=f32
        )
        sorted_rows[b] = both[0:8] + both[8:16]
        return 0

    def spread(b, _):
        block = sorted_rows[b]
        for j in range(4):
            tile, at, length = plan[b, j], plan[b, 4 + j], plan[b, 12 + j]
            moved = pltpu.roll(block, plan[b, 16 + j], 1)
            here = (lane >= at) & (lane < at + length)
            pltpu.store(tiles.at[tile], moved, mask=here)
            pltpu.store(tiles.at[tile + 1], moved, mask=lane < at + length - width)
        return 0

    lax.fori_loop(0, nblocks, order, 0, unroll=16)
    lax.fori_loop(0, nblocks, spread, 0, unroll=16)


def own_contacts(cap, columns, depth, home_list, partner_list, state, cell, route,
                 home_side, sums, spots, plan, bounds,
                 rows, partner_side, values, homes, partners, home_ref, partner_ref, sems):
    nblocks, width = state.shape[1:]
    copies = copy_all([(home_list, home_ref), (partner_list, partner_ref)], sems)
    plan_sort(cap, cell, route, columns, depth, spots, plan, bounds)
    place = [state[c] for c in range(4)]
    put_rows(home_side, 32, home_rows(place))
    prepare_partners(place, [state[c] for c in (4, 5, 6)], rows, partner_side, values)
    home_side[nblocks * 32 :, :] = jnp.zeros((32, width), f32)
    sums[...] = jnp.zeros(sums.shape, f32)
    wait_all(copies)
    count = list_tiles(home_ref, partner_ref, homes, partners, 0, nblocks, nblocks)
    add_tiles(count, homes, partners, home_side, partner_side, values, sums)


def diffuse(fluid, below, above, before, after, skip, diffused):
    nx, ny, nz = fluid.shape[1:]
    width = before.shape[1]
    deep = iota((ny, nz), 1)

    def face(ref, c, x):
        at = skip + (c * nx + x) * (nz // width)
        return jnp.concatenate(
            [ref[at + k : at + k + 1, :] for k in range(nz // width)], axis=1
        )

    def layer(ref, c):
        at = [skip + (c * (nz // width) + k) * ny for k in range(nz // width)]
        return jnp.concatenate([ref[start : start + ny, :] for start in at], axis=1)

    for x in range(nx):
        for c in range(3):
            here = fluid[c, x]
            near = (layer(below, c) if x == 0 else fluid[c, x - 1]) + (
                layer(above, c) if x == nx - 1 else fluid[c, x + 1]
            )
            near = near + jnp.concatenate([face(before, c, x), here[:-1]], axis=0)
            near = near + jnp.concatenate([here[1:], face(after, c, x)], axis=0)
            near = near + jnp.where(deep == 0, 0.0, pltpu.roll(here, 1, 1))
            near = near + jnp.where(deep == nz - 1, 0.0, pltpu.roll(here, nz - 1, 1))
            diffused[c, x] = here + viscosity * (near - 6.0 * here)


def brick_ahead(ahead, nbrick):
    return lax.rem(lax.axis_index("brick") + ahead, nbrick)


def ghost_contacts(nbrick, cap, partner_blocks, home_list, partner_list, plan, below,
                   above, before, after, home_side, own_sums, state, cell, spots, bounds,
                   updated, down, *rest):
    outgoings = rest[:nbrick]
    (rows, columns, values, sums, data, sorted_rows, tiles, homes, partners,
     home_ref, partner_ref, plan_ref, sems) = rest[nbrick:]
    nblocks, width = state.shape[1:]
    per = partner_blocks // 4
    copies = copy_all(
        [
            (home_list, home_ref),
            (partner_list, partner_ref),
            (plan, plan_ref),
        ],
        sems,
    )
    stacked = [
        jnp.concatenate(
            [ref[c * per : (c + 1) * per, :] for ref in (below, above, before, after)], axis=0
        )
        for c in range(planes)
    ]
    prepare_partners(stacked[0:4], stacked[4:7], rows, columns, values)
    sums[...] = own_sums[...]
    wait_all(copies)
    count = list_tiles(home_ref, partner_ref, homes, partners, nblocks, nblocks + 4 * per, nblocks)
    add_tiles(count, homes, partners, home_side, columns, values, sums)

    def total(k):
        high = sums[pl.ds(k, nblocks, stride=16), :]
        return high + sums[pl.ds(k + 8, nblocks, stride=16), :]

    weights = total(6)
    radius = state[3]
    inverse = 1.0 / (radius * radius * radius)
    fresh = []
    for c in range(3):
        speed = state[c + 4]
        spring = state[c] * weights - total(c)
        friction = total(c + 3) - speed * weights
        fresh.append(speed + (stiffness * spring + damping * friction) * inverse)
        updated[c] = fresh[c]

    number = cell[...]
    zeros = jnp.zeros_like(radius)
    highs = [rounded(plane) for plane in [radius] + fresh]
    lows = [plane - high for plane, high in zip([radius] + fresh, highs)]
    highs.append(((number >> 8) * 256).astype(f32))
    lows.append((number & 255).astype(f32))
    put_rows(data, 16, highs + [zeros] * 3 + lows + [zeros] * 3)
    sort_blocks(plan_ref, spots, data, sorted_rows, tiles)

    chunk = rows_up(5 * cap + 1)
    flat = tiles.reshape(tiles.shape[0] * 8, width)
    for ahead in range(nbrick):
        target = brick_ahead(ahead, nbrick)
        for side, (outgoing, row) in enumerate(
            ((down, ahead * chunk), (outgoings[ahead], 0), (outgoings[ahead], chunk))
        ):
            code = side * nbrick + target
            for c in range(5):
                outgoing[row + c * cap : row + (c + 1) * cap, :] = flat[
                    pl.ds(code * (cap + 2) * 8 + c, cap, stride=8), :
                ]
            outgoing[row + 5 * cap : row + 5 * cap + 1, :] = bounds[pl.ds(code, 1), :]


def list_stride(segments, cap):
    return (segments + 1) * cap


def list_arrived(arrived, starts, ends, cap, places, counts):
    base, goal = places
    width = arrived.shape[1]
    stride = list_stride(len(starts), cap)
    shift = width.bit_length() - 1
    lane = iota((1, width), 1)
    filled = [jnp.int32(0)] * 4
    for start, end in zip(starts, ends):
        row = arrived[start + 5 * cap : start + 5 * cap + 1, :]
        edge = jnp.int32(0)
        for j in range(4):
            next_edge = jnp.sum(jnp.where(lane == j, row, 0.0)).astype(jnp.int32)
            first = edge >> shift
            last = jnp.where(next_edge > edge, (next_edge + width - 1) >> shift, first)
            at = j * stride + filled[j]

            def put(some, at=at, first=first, start=start, end=end):
                for i in some:
                    base[at + i] = start + first + i
                    goal[at + i] = end + first + i

            few = min(4, cap)
            put(range(few))
            pl.when(last - first > few)(functools.partial(put, range(few, cap)))
            filled[j] = filled[j] + last - first
            edge = next_edge
    for j in range(4):
        counts[j] = filled[j]


def cell_parts(arrived, row, cap, columns, depth, bucket):
    cell = arrived[pl.ds(row + 4 * cap, 1), :].astype(jnp.int32)
    shift = (2 * depth).bit_length() - 1
    column = (cell >> shift) - (bucket // 2) * columns
    level = (cell & (2 * depth - 1)) - (bucket % 2) * depth - depth // 2
    return column.astype(f32), level.astype(f32)


def all_levels(depth, width):
    return (iota((depth, width), 0) - depth // 2).astype(f32).astype(bf16)


def level_hot(level, levels):
    hit = levels == jnp.broadcast_to(level.astype(bf16), levels.shape)
    return jnp.where(hit, jnp.ones((), bf16), jnp.zeros((), bf16))


def steps_of(counts):
    longest = jnp.maximum(
        jnp.maximum(counts[0], counts[1]), jnp.maximum(counts[2], counts[3])
    )
    return lax.shift_right_logical(longest + GROUP - 1, GROUP.bit_length() - 1)


def tile_of(counts, bucket, index, width):
    count = counts[bucket]
    real = jnp.full((1, width), jnp.where(index < count, 1, 0), jnp.int32) > 0
    return jnp.minimum(index, jnp.maximum(count - 1, 0)), real


def deposit(segments, counts, arrived, base, cap, total):
    columns, depth = total.shape[0] // 16, total.shape[1]
    width = arrived.shape[1]
    stride = list_stride(segments, cap)
    numbers = iota((columns, width), 0).astype(f32).astype(bf16)
    levels = all_levels(depth, width)

    def some(step, _):
        sums = []
        for bucket in range(4):
            high_of, low_of, level_of = [], [], []
            for k in range(GROUP):
                index, real = tile_of(counts, bucket, step * GROUP + k, width)
                row = base[bucket * stride + index]
                column, level = cell_parts(arrived, row, cap, columns, depth, bucket)
                radius = arrived[pl.ds(row, 1), :]
                mass = radius * radius * radius
                loads = [mass] + [mass * arrived[pl.ds(row + c * cap, 1), :] for c in (1, 2, 3)]
                hit = numbers == jnp.broadcast_to(column.astype(bf16), (columns, width))
                highs, lows = [], []
                for load in loads:
                    load = jnp.where(real, load, 0.0)
                    high = load.astype(bf16)
                    low = (load - high.astype(f32)).astype(bf16)
                    for parts, part in ((highs, high), (lows, low)):
                        part = jnp.broadcast_to(part, (columns, width))
                        parts.append(jnp.where(hit, part, jnp.zeros((), bf16)))
                high_of.append(jnp.concatenate(highs, axis=0))
                low_of.append(jnp.concatenate(lows, axis=0))
                level_of.append(level_hot(level, levels))
            both = lax.dot_general(
                jnp.concatenate(
                    [jnp.concatenate(high_of, axis=1), jnp.concatenate(low_of, axis=1)], axis=0
                ),
                jnp.concatenate(level_of, axis=1),
                (((1,), (1,)), ((), ())),
                preferred_element_type=f32,
            )
            sums.append(both[0 : 4 * columns] + both[4 * columns :])
        for bucket in range(4):
            total[bucket * 4 * columns : (bucket + 1) * 4 * columns, :] += sums[bucket]
        return 0

    lax.fori_loop(0, steps_of(counts), some, 0)


def sample(segments, counts, arrived, places, cap, table, answers):
    columns, depth = table.shape[0] // 24, table.shape[1]
    width = arrived.shape[1]
    stride = list_stride(segments, cap)
    levels = all_levels(depth, width)
    numbers = iota((columns, width), 0).astype(f32)
    answers[...] = jnp.zeros(answers.shape, f32)

    def some(step, _):
        found = []
        for bucket in range(4):
            hots, hits = [], []
            for k in range(GROUP):
                index, real = tile_of(counts, bucket, step * GROUP + k, width)
                row = places[0][bucket * stride + index]
                column, level = cell_parts(arrived, row, cap, columns, depth, bucket)
                hots.append(level_hot(level, levels))
                hits.append((numbers == column, real, places[1][bucket * stride + index]))
            along = jnp.dot(
                table[bucket * 6 * columns : (bucket + 1) * 6 * columns, :],
                jnp.concatenate(hots, axis=1),
                preferred_element_type=f32,
            )
            for k, (hit, real, goal) in enumerate(hits):
                part = along[:, k * width : (k + 1) * width]
                for c in range(3):
                    value = part[c * columns : (c + 1) * columns]
                    value = value + part[(c + 3) * columns : (c + 4) * columns]
                    value = jnp.sum(jnp.where(hit, value, 0.0), axis=0, keepdims=True)
                    found.append((goal + c * cap, jnp.where(real, value, 0.0)))
        for goal, value in found:
            answers[pl.ds(goal, 1), :] += value
        return 0

    lax.fori_loop(0, steps_of(counts), some, 0)


def first_deposit(nbrick, cap, skip, crossed, below, above, before, after, fluid, total, diffused,
                  flow, base, goal, counts, sems):
    reading = copy_all([(fluid, flow)], sems)
    chunk = rows_up(5 * cap + 1)
    total[...] = jnp.zeros(total.shape, f32)
    starts = [b * chunk for b in range(nbrick)]
    list_arrived(crossed, starts, starts, cap, (base, goal), counts)
    deposit(nbrick, counts, crossed, base, cap, total)
    wait_all(reading)
    diffuse(flow, below, above, before, after, skip, diffused)


def advance(nbrick, cap, start, fluid, diffused, below, *rest):
    above, rest = rest[:nbrick], rest[nbrick:]
    fluid_next, table, answers_below = rest[:3]
    answers_above, rest = rest[3 : 3 + nbrick], rest[3 + nbrick :]
    arrived, answers, total, flow, fresh_flow, base, goal, counts, sems = rest
    reading = pltpu.make_async_copy(fluid, flow, sems.at[0])
    reading.start()
    chunk = rows_up(5 * cap + 1)
    back = rows_up(3 * cap)
    rows = nbrick * chunk
    for b, part in enumerate(above):
        arrived[b * chunk : (b + 1) * chunk, :] = part[...]
    arrived[rows:, :] = below[...]
    starts = [i * chunk for i in range(2 * nbrick)]
    ends = [i * back for i in range(2 * nbrick)]
    total[...] = start[...]
    list_arrived(arrived, starts, ends, cap, (base, goal), counts)
    deposit(2 * nbrick, counts, arrived, base, cap, total)
    reading.wait()

    nx, ny, nz = flow.shape[1:]
    columns, depth = nx * ny // 2, nz // 2
    for x in range(nx):
        buckets = [2 * (x * ny // columns) + deep for deep in range(2)]
        at = x * ny % columns

        def load(c):
            spots = [4 * columns * bucket + c * columns + at for bucket in buckets]
            return jnp.concatenate([total[spot : spot + ny, :] for spot in spots], axis=1)

        volume = load(0)
        for c in range(3):
            moved = load(c + 1) - volume * flow[c, x]
            fresh = diffused[c, x] + coupling * moved
            fresh_flow[c, x] = fresh
            high = fresh.astype(bf16)
            low = (fresh - high.astype(f32)).astype(bf16)
            for deep, bucket in enumerate(buckets):
                spot = 6 * columns * bucket + c * columns + at
                half = slice(deep * depth, (deep + 1) * depth)
                table[spot : spot + ny, :] = high[:, half]
                table[spot + 3 * columns : spot + 3 * columns + ny, :] = low[:, half]
    writing = pltpu.make_async_copy(fresh_flow, fluid_next, sems.at[1])
    writing.start()
    sample(2 * nbrick, counts, arrived, (base, goal), cap, table, answers)
    for b, part in enumerate(answers_above):
        part[...] = answers[b * back : (b + 1) * back, :]
    answers_below[...] = answers[nbrick * back :, :]
    writing.wait()


def last_sample(nbrick, cap, crossed, table, *rest):
    answers, base, goal, counts = rest[nbrick:]
    chunk = rows_up(5 * cap + 1)
    back = rows_up(3 * cap)
    starts = [b * chunk for b in range(nbrick)]
    ends = [b * back for b in range(nbrick)]
    list_arrived(crossed, starts, ends, cap, (base, goal), counts)
    sample(nbrick, counts, crossed, (base, goal), cap, table, answers)
    for b, part in enumerate(rest[:nbrick]):
        part[...] = answers[b * back : (b + 1) * back, :]


def relax(nbrick, cap, plan, updated, spots, down, *rest):
    returneds = rest[:nbrick]
    velocity_next, picked, sorted_rows, tiles, plan_ref, sems = rest[nbrick:]
    copies = copy_all([(plan, plan_ref)], sems)
    nblocks, width = spots.shape
    back = rows_up(3 * cap)
    flat = tiles.reshape(tiles.shape[0] * 8, width)
    for ahead in range(nbrick):
        target = brick_ahead(ahead, nbrick)
        for side, (returned, row) in enumerate(
            ((down, ahead * back), (returneds[ahead], 0), (returneds[ahead], back))
        ):
            code = side * nbrick + target
            for c in range(3):
                flat[pl.ds(code * (cap + 2) * 8 + c, cap, stride=8), :] = returned[
                    row + c * cap : row + (c + 1) * cap, :
                ]
    lane = iota((8, width), 1)
    wait_all(copies)

    def gather(b, _):
        block = jnp.zeros((8, width), f32)
        for j in range(4):
            tile, at = plan_ref[b, j], plan_ref[b, 4 + j]
            first, length = plan_ref[b, 8 + j], plan_ref[b, 12 + j]
            run = jnp.where(lane >= at, tiles[tile], tiles[tile + 1])
            run = pltpu.roll(run, plan_ref[b, 20 + j], 1)
            block = jnp.where((lane >= first) & (lane < first + length), run, block)
        sorted_rows[b] = block
        return 0

    def order(b, _):
        block = sorted_rows[b]
        high = rounded(block)
        both = jnp.dot(
            jnp.concatenate([high, block - high], axis=0).astype(bf16),
            block_order(spots, b),
            preferred_element_type=f32,
        )
        picked[b] = both[0:8] + both[8:16]
        return 0

    lax.fori_loop(0, nblocks, gather, 0, unroll=16)
    lax.fori_loop(0, nblocks, order, 0, unroll=16)
    flat = picked.reshape(nblocks * 8, width)
    for c in range(3):
        now = updated[c]
        velocity_next[c] = now + relaxation * (flat[pl.ds(c, nblocks, stride=8), :] - now)


def on_device(
    positions, velocities, radii, cell_of, block_route, ghost_list, tile_home, tile_partner, fluid
):
    nblocks, _, width = positions.shape
    nbrick = lax.axis_size("brick")
    _, nx, ny, nz = fluid.shape
    columns = nx * ny
    codes = 3 * nbrick
    cap = max(2, (2 * nblocks + codes - 1) // codes)
    chunk, back = rows_up(5 * cap + 1), rows_up(3 * cap)
    per = ghost_list.shape[0] // 2
    tiles = tile_home.shape[0]
    routes = block_route.reshape(-1)
    positions = jnp.transpose(positions, (1, 0, 2))
    velocities = jnp.transpose(velocities, (1, 0, 2))

    def struct(*shape, dtype=f32):
        return jax.ShapeDtypeStruct(shape, dtype)

    def shifted(x, axis, step):
        if step == 0:
            return x
        count = lax.axis_size(axis)
        return lax.ppermute(x, axis, [(i, (i + step) % count) for i in range(count)])

    def ints(count):
        return pltpu.SMEM((count,), jnp.int32)

    state = jnp.concatenate([positions, radii[None], velocities], axis=0)
    ghost_rows, chunks = planes * per, 3 * (nz // width)
    up, low, right, left = call(
        pack_kernel,
        [struct(ghost_rows + chunks * ny, width)] * 2 + [struct(ghost_rows + chunks * nx, width)] * 2,
        [SMEM] + [VMEM] * 2,
        [],
        "pack",
    )(ghost_list, state, fluid)
    below = shifted(up, "slab", 1)
    above = shifted(low, "slab", -1)
    before = shifted(right, "brick", 1)
    after = shifted(left, "brick", -1)

    def sides(count):
        return [
            pltpu.VMEM((count * 32, width), f32),
            pltpu.VMEM((count, width, 32), bf16),
            pltpu.VMEM((count * 16, width), f32),
        ]

    lists = [ints(tiles + UNROLL)] * 2
    contact_flops = tiles * width * width * 200
    chunk_tiles = pltpu.VMEM((codes * (cap + 2), 8, width), f32)
    block_tiles = pltpu.VMEM((nblocks, 8, width), f32)
    plan_copy = pltpu.SMEM((nblocks, width), jnp.int32)
    home_side, sums, spots, plan, bounds = call(
        functools.partial(own_contacts, cap, columns, nz),
        [
            struct((nblocks + 1) * 32, width),
            struct((nblocks + 1) * 16, width),
            struct(nblocks, width),
            struct(nblocks, width, dtype=jnp.int32),
            struct(rows_up(codes), width),
        ],
        [HBM] * 2 + [VMEM] * 3,
        sides(nblocks) + lists + [ints(tiles)] * 2 + [pltpu.SemaphoreType.DMA((2,))],
        "own_contacts",
        contact_flops,
    )(tile_home, tile_partner, state, cell_of, routes.reshape(1, nblocks))
    updated, down, *outgoing = call(
        functools.partial(ghost_contacts, nbrick, cap, 4 * per),
        [struct(3, nblocks, width), struct(nbrick * chunk, width)]
        + [struct(2 * chunk, width)] * nbrick,
        [HBM] * 2 + [ANY] + [VMEM] * 10,
        sides(4 * per)
        + [pltpu.VMEM(((nblocks + 1) * 16, width), f32)]
        + [pltpu.VMEM((nblocks * 16, width), f32), block_tiles, chunk_tiles]
        + lists
        + [ints(tiles), ints(tiles), plan_copy, pltpu.SemaphoreType.DMA((3,))],
        "ghost_contacts",
        contact_flops // 2,
    )(tile_home, tile_partner, plan, below, above, before, after,
      home_side, sums, state, cell_of, spots, bounds)

    down = shifted(down, "slab", -1)
    near = [shifted(part, "brick", ahead) for ahead, part in enumerate(outgoing)]
    from_below = shifted(jnp.concatenate([part[chunk:] for part in near], axis=0), "slab", 1)
    from_above = [
        shifted(down[ahead * chunk : (ahead + 1) * chunk], "brick", ahead)
        for ahead in range(nbrick)
    ]
    crossed = jnp.concatenate([part[:chunk] for part in near], axis=0)

    def places(count):
        return [ints(4 * list_stride(count, cap))] * 2 + [ints(4)]

    block_flops = 8 * columns * nz * width
    started, diffused = call(
        functools.partial(first_deposit, nbrick, cap, ghost_rows),
        [struct(8 * columns, nz // 2), struct(3, nx, ny, nz)],
        [VMEM] * 5 + [HBM],
        [pltpu.VMEM((3, nx, ny, nz), f32)]
        + places(nbrick)
        + [pltpu.SemaphoreType.DMA((1,))],
        "first_deposit",
        block_flops * nblocks // 3,
    )(crossed, below, above, before, after, fluid)
    fluid_next, table, answers_below, *answers_above = call(
        functools.partial(advance, nbrick, cap),
        [
            struct(3, nx, ny, nz),
            struct(12 * columns, nz // 2, dtype=bf16),
            struct(nbrick * back, width),
        ]
        + [struct(back, width)] * nbrick,
        [VMEM, HBM] + [VMEM] * (2 + nbrick),
        [
            pltpu.VMEM((2 * nbrick * chunk, width), f32),
            pltpu.VMEM((2 * nbrick * back, width), f32),
            pltpu.VMEM((8 * columns, nz // 2), f32),
        ]
        + [pltpu.VMEM((3, nx, ny, nz), f32)] * 2
        + places(2 * nbrick)
        + [pltpu.SemaphoreType.DMA((2,))],
        "advance",
        block_flops * nblocks,
        places=[HBM] + [VMEM] * (2 + nbrick),
    )(started, fluid, diffused, from_below, *from_above)
    answers_below = shifted(answers_below, "slab", -1)
    answers_above = [
        shifted(part, "brick", -behind) for behind, part in enumerate(answers_above)
    ]
    returned_down = shifted(jnp.concatenate(answers_above, axis=0), "slab", 1)
    answers = call(
        functools.partial(last_sample, nbrick, cap),
        [struct(back, width)] * nbrick,
        [VMEM] * 2,
        [pltpu.VMEM((nbrick * back, width), f32)] + places(nbrick),
        "last_sample",
        block_flops * nblocks // 64,
    )(crossed, table)
    returned = []
    for behind in range(nbrick):
        at = slice(behind * back, (behind + 1) * back)
        part = jnp.concatenate([answers[behind], answers_below[at]], axis=0)
        returned.append(shifted(part, "brick", -behind))
    (velocity_next,) = call(
        functools.partial(relax, nbrick, cap),
        [struct(3, nblocks, width)],
        [ANY] + [VMEM] * (3 + nbrick),
        [block_tiles, block_tiles, chunk_tiles, plan_copy]
        + [pltpu.SemaphoreType.DMA((1,))],
        "relax",
    )(plan, updated, spots, returned_down, *returned)
    return (jnp.transpose(velocity_next, (1, 0, 2)), fluid_next)


def solution(mesh):
    placed = (
        P(("slab", "brick"), None, None),
        P(("slab", "brick"), None, None),
        P(("slab", "brick"), None),
        P(("slab", "brick"), None),
        P(("slab", "brick"), None),
        P(("slab", "brick")),
        P(("slab", "brick")),
        P(("slab", "brick")),
        P(None, "slab", "brick", None),
    )
    return jax.shard_map(
        on_device,
        mesh=mesh,
        in_specs=placed,
        out_specs=(P(("slab", "brick"), None, None), P(None, "slab", "brick", None)),
        check_vma=False,
    )
```

```python
import functools
import math

import jax
import jax.numpy as jnp
from jax import lax
from jax.experimental import pallas as pl
from jax.experimental.pallas import tpu as pltpu
from jax.sharding import PartitionSpec as P

stiffness = 0.01
damping = 0.005
viscosity = 0.1
coupling = 0.5
relaxation = 0.5

f32 = jnp.float32
bf16 = jnp.bfloat16
VMEM = pl.BlockSpec(memory_space=pltpu.VMEM)
SMEM = pl.BlockSpec(memory_space=pltpu.SMEM)
ANY = pl.BlockSpec(memory_space=pl.ANY)
HBM = pl.BlockSpec(memory_space=pltpu.HBM)
UNROLL = 32
TAIL = 8
GROUP = 4
REST = 2


def rows_up(count):
    return -(-count // 8) * 8


def call(body, outs, ins, scratch, name, flops=0, nbytes=1 << 20, places=None, vmem=40 << 20):
    return pl.pallas_call(
        body,
        out_shape=outs,
        in_specs=ins,
        out_specs=places or [VMEM] * len(outs),
        scratch_shapes=scratch,
        name=name,
        compiler_params=pltpu.CompilerParams(vmem_limit_bytes=vmem),
        cost_estimate=pl.CostEstimate(flops=flops, bytes_accessed=nbytes, transcendentals=0),
    )


def rounded(x):
    return x.astype(bf16).astype(f32)


def iota(shape, dim):
    return lax.broadcasted_iota(jnp.int32, shape, dim)


planes = 7


def copy_all(pairs, sems):
    copies = [pltpu.make_async_copy(*pair, sems.at[i]) for i, pair in enumerate(pairs)]
    for copy in copies:
        copy.start()
    return copies


def wait_all(copies):
    for copy in copies:
        copy.wait()


def pack_kernel(ghost_ref, state, fluid, up, down, right, left):
    count = ghost_ref.shape[0] // 4
    width = state.shape[2]
    nx, ny, nz = fluid.shape[1:]
    for group in range(4):
        i, j = group // 2, group % 2
        slab_to, brick_to = (up if i else down), (right if j else left)
        for g in range(count):
            block = pl.ds(ghost_ref[group * count + g], 1)
            for c in range(planes):
                row = state[c, block, :]
                at = c * 2 * count + j * count + g
                slab_to[at : at + 1, :] = row
                at = c * 2 * count + i * count + g
                brick_to[at : at + 1, :] = row
    for slab_to, x in ((up, nx - 1), (down, 0)):
        for c in range(3):
            for k in range(nz // width):
                at = planes * 2 * count + (c * (nz // width) + k) * ny
                slab_to[at : at + ny, :] = fluid[c, x, :, k * width : (k + 1) * width]
    for brick_to, y in ((right, ny - 1), (left, 0)):
        for c in range(3):
            for x in range(nx):
                for k in range(nz // width):
                    at = planes * 2 * count + (c * nx + x) * (nz // width) + k
                    brick_to[at : at + 1, :] = fluid[
                        c, x, y : y + 1, k * width : (k + 1) * width
                    ]


def three_parts(x):
    one = rounded(x)
    rest = x - one
    two = rounded(rest)
    return one, two, rest - two


def put_rows(ref, stride, rows):
    count = rows[0].shape[0]
    for k, row in enumerate(rows):
        ref[pl.ds(k, count, stride=stride), :] = row


def pair_factors(place):
    parts = [three_parts(plane) for plane in place]
    own = three_parts(
        place[3] * place[3] - place[0] * place[0] - place[1] * place[1] - place[2] * place[2]
    )
    return [[part[k] for part in parts] for k in range(3)], list(own)


def home_rows(place):
    (one, two, three), own = pair_factors(place)
    ones, zeros = jnp.ones_like(place[0]), jnp.zeros_like(place[0])
    rows = one + one + two + two + one + three
    return [2.0 * row for row in rows] + own + [ones] * 3 + [zeros] * 2


def partner_rows(place):
    (one, two, three), own = pair_factors(place)
    ones, zeros = jnp.ones_like(place[0]), jnp.zeros_like(place[0])
    return one + two + one + two + three + one + [ones] * 3 + own + [zeros] * 2


def value_rows(values):
    highs = [rounded(plane) for plane in values]
    ones, zeros = jnp.ones_like(values[0]), jnp.zeros_like(values[0])
    lows = [plane - high for plane, high in zip(values, highs)]
    return highs + [ones, zeros] + lows + [zeros, zeros]


def prepare_partners(place, speeds, rows, columns, values):
    count, width = place[0].shape
    put_rows(rows, 32, partner_rows(place))
    put_rows(values, 16, value_rows(place[0:3] + speeds))

    def turn(b, _):
        block = rows[pl.ds(pl.multiple_of(b * 32, 32), 32), :]
        columns[b] = jnp.transpose(block).astype(bf16)
        return 0

    lax.fori_loop(0, count, turn, 0, unroll=8)


def list_tiles(home_ref, partner_ref, homes, partners, lower, upper, spare):
    def one(t, count):
        partner = partner_ref[t]
        homes[count] = home_ref[t]
        partners[count] = partner - lower
        return count + jnp.where((partner >= lower) & (partner < upper), 1, 0)

    count = lax.fori_loop(0, home_ref.shape[0], one, 0, unroll=4)
    for pad in range(TAIL):
        homes[count + pad] = spare
        partners[count + pad] = 0
    return count


def in_groups(count, large, small, work):
    steps = count // large
    left = (count - steps * large + small - 1) // small

    def one(size, first, step, _):
        work(size, first + step * size)
        return 0

    lax.fori_loop(0, steps, functools.partial(one, large, 0), 0)
    lax.fori_loop(0, left, functools.partial(one, small, steps * large), 0)


def add_tiles(count, homes, partners, home_side, partner_side, values, sums):
    def some(tiles, start):
        added = []
        for k in range(tiles):
            home = homes[start + k]
            partner = partners[start + k]
            factors = home_side[pl.ds(pl.multiple_of(home * 32, 32), 32), :].astype(bf16)
            weight = jnp.dot(partner_side[partner], factors, preferred_element_type=f32)
            weight = jnp.maximum(weight, 0.0)
            high = weight.astype(bf16)
            low = (weight - high.astype(f32)).astype(bf16)
            value = values[pl.ds(pl.multiple_of(partner * 16, 16), 16), :].astype(bf16)
            at = pl.ds(pl.multiple_of(home * 16, 16), 16)
            term = jnp.dot(
                jnp.concatenate([value, value], axis=1),
                jnp.concatenate([high, low], axis=0),
                preferred_element_type=f32,
            )
            added.append((at, term))
        for at, term in added:
            sums[at, :] += term

    in_groups(count, UNROLL, TAIL, some)


def dot(left, right):
    return jnp.dot(left.astype(bf16), right.astype(bf16), preferred_element_type=f32)


def plan_sort(cap, cell, route, columns, depth, spots, plan, bounds):
    nblocks, width = cell.shape
    shift = depth.bit_length() - 1
    number = cell[...]
    right = (number >> shift) >= columns // 2
    deep = (number & (depth - 1)) >= depth // 2
    kind = jnp.where(right, 2, 0) + jnp.where(deep, 1, 0)
    members = [jnp.where(kind == j, 1.0, 0.0) for j in range(4)]
    before = jnp.where(iota((width, width), 0) < iota((width, width), 1), 1.0, 0.0)
    stacked = jnp.concatenate(members, axis=0)
    ranks = dot(stacked, before)
    lengths = dot(stacked, jnp.ones((width, width), f32))
    ranks = [ranks[j * nblocks : (j + 1) * nblocks] for j in range(4)]
    lengths = [lengths[j * nblocks : (j + 1) * nblocks] for j in range(4)]

    across = jnp.broadcast_to(route[...].astype(f32), (nblocks, nblocks))
    same = across == jnp.transpose(across)
    earlier = iota((nblocks, nblocks), 1) < iota((nblocks, nblocks), 0)
    side_by_side = jnp.concatenate(lengths, axis=1)
    ahead = dot(jnp.where(same & earlier, 1.0, 0.0), side_by_side)
    whole = dot(jnp.where(same, 1.0, 0.0), side_by_side)
    rows = bounds.shape[0]
    of_code = jnp.broadcast_to(route[...], (rows, nblocks)) == iota((rows, nblocks), 0)
    totals = dot(jnp.where(of_code, 1.0, 0.0), side_by_side)

    lane = iota((nblocks, width), 1)
    bound_lane = iota((rows, width), 1)
    spot = jnp.zeros((nblocks, width), f32)
    first, chunk_first = jnp.zeros((nblocks, width), f32), jnp.zeros((nblocks, width), f32)
    bound, line = jnp.zeros((rows, width), f32), jnp.zeros((rows, width), f32)
    table = jnp.zeros((nblocks, width), jnp.int32)
    own_code = jnp.transpose(across).astype(jnp.int32)
    own_code = jnp.concatenate([own_code] * (width // nblocks), axis=1)
    for j in range(4):
        at = slice(j * width, (j + 1) * width)
        spot = spot + members[j] * (first + ranks[j])
        where = (chunk_first + ahead[:, at]).astype(jnp.int32)
        start, there = first.astype(jnp.int32), where & (width - 1)
        parts = [
            own_code * (cap + 2) + (where >> (width.bit_length() - 1)),
            there,
            start,
            lengths[j].astype(jnp.int32),
            (there - start) & (width - 1),
            (start - there) & (width - 1),
        ]
        for k, part in enumerate(parts):
            table = jnp.where(lane == 4 * k + j, part, table)
        first = first + lengths[j]
        chunk_first = chunk_first + whole[:, at]
        bound = bound + totals[:, at]
        line = jnp.where(bound_lane == j, bound, line)
    spots[...] = spot
    plan[...] = table
    bounds[...] = line


def block_order(spots, b):
    width = spots.shape[1]
    row = jnp.broadcast_to(spots[pl.ds(b, 1), :].astype(bf16), (width, width))
    hit = iota((width, width), 0).astype(f32).astype(bf16) == row
    return jnp.where(hit, jnp.ones((), bf16), jnp.zeros((), bf16))


def sort_blocks(plan, spots, data, sorted_rows, tiles):
    nblocks, width = spots.shape
    lane = iota((8, width), 1)

    def order(b, _):
        rows = data[pl.ds(pl.multiple_of(b * 16, 16), 16), :].astype(bf16)
        both = lax.dot_general(
            rows, block_order(spots, b), (((1,), (1,)), ((), ())), preferred_element_type=f32
        )
        sorted_rows[b] = both[0:8] + both[8:16]
        return 0

    def spread(b, _):
        block = sorted_rows[b]
        for j in range(4):
            tile, at, length = plan[b, j], plan[b, 4 + j], plan[b, 12 + j]
            moved = pltpu.roll(block, plan[b, 16 + j], 1)
            here = (lane >= at) & (lane < at + length)
            pltpu.store(tiles.at[tile], moved, mask=here)
            pltpu.store(tiles.at[tile + 1], moved, mask=lane < at + length - width)
        return 0

    lax.fori_loop(0, nblocks, order, 0, unroll=32)
    lax.fori_loop(0, nblocks, spread, 0, unroll=32)


def own_contacts(cap, columns, depth, home_list, partner_list, state, cell, route,
                 home_side, sums, spots, plan, bounds,
                 rows, partner_side, values, homes, partners, home_ref, partner_ref, sems):
    nblocks, width = state.shape[1:]
    copies = copy_all([(home_list, home_ref), (partner_list, partner_ref)], sems)
    plan_sort(cap, cell, route, columns, depth, spots, plan, bounds)
    place = [state[c] for c in range(4)]
    put_rows(home_side, 32, home_rows(place))
    prepare_partners(place, [state[c] for c in (4, 5, 6)], rows, partner_side, values)
    home_side[nblocks * 32 :, :] = jnp.zeros((32, width), f32)
    sums[...] = jnp.zeros(sums.shape, f32)
    wait_all(copies)
    count = list_tiles(home_ref, partner_ref, homes, partners, 0, nblocks, nblocks)
    add_tiles(count, homes, partners, home_side, partner_side, values, sums)


def diffuse(fluid, below, above, before, after, skip, diffused):
    nx, ny, nz = fluid.shape[1:]
    width = before.shape[1]
    deep = iota((ny, nz), 1)

    def face(ref, c, x):
        at = skip + (c * nx + x) * (nz // width)
        return jnp.concatenate(
            [ref[at + k : at + k + 1, :] for k in range(nz // width)], axis=1
        )

    def layer(ref, c):
        at = [skip + (c * (nz // width) + k) * ny for k in range(nz // width)]
        return jnp.concatenate([ref[start : start + ny, :] for start in at], axis=1)

    for x in range(nx):
        for c in range(3):
            here = fluid[c, x]
            near = (layer(below, c) if x == 0 else fluid[c, x - 1]) + (
                layer(above, c) if x == nx - 1 else fluid[c, x + 1]
            )
            near = near + jnp.concatenate([face(before, c, x), here[:-1]], axis=0)
            near = near + jnp.concatenate([here[1:], face(after, c, x)], axis=0)
            near = near + jnp.where(deep == 0, 0.0, pltpu.roll(here, 1, 1))
            near = near + jnp.where(deep == nz - 1, 0.0, pltpu.roll(here, nz - 1, 1))
            diffused[c, x] = here + viscosity * (near - 6.0 * here)


def brick_ahead(ahead, nbrick):
    return lax.rem(lax.axis_index("brick") + ahead, nbrick)


def ghost_contacts(nbrick, cap, partner_blocks, home_list, partner_list, plan, below,
                   above, before, after, home_side, own_sums, state, cell, spots, bounds,
                   updated, down, *rest):
    outgoings = rest[:nbrick]
    (rows, columns, values, sums, data, sorted_rows, tiles, homes, partners,
     home_ref, partner_ref, plan_ref, sems) = rest[nbrick:]
    nblocks, width = state.shape[1:]
    per = partner_blocks // 4
    copies = copy_all(
        [
            (home_list, home_ref),
            (partner_list, partner_ref),
            (plan, plan_ref),
        ],
        sems,
    )
    stacked = [
        jnp.concatenate(
            [ref[c * per : (c + 1) * per, :] for ref in (below, above, before, after)], axis=0
        )
        for c in range(planes)
    ]
    prepare_partners(stacked[0:4], stacked[4:7], rows, columns, values)
    sums[...] = own_sums[...]
    wait_all(copies)
    count = list_tiles(home_ref, partner_ref, homes, partners, nblocks, nblocks + 4 * per, nblocks)
    add_tiles(count, homes, partners, home_side, columns, values, sums)

    def total(k):
        high = sums[pl.ds(k, nblocks, stride=16), :]
        return high + sums[pl.ds(k + 8, nblocks, stride=16), :]

    weights = total(6)
    radius = state[3]
    inverse = 1.0 / (radius * radius * radius)
    fresh = []
    for c in range(3):
        speed = state[c + 4]
        spring = state[c] * weights - total(c)
        friction = total(c + 3) - speed * weights
        fresh.append(speed + (stiffness * spring + damping * friction) * inverse)
        updated[c] = fresh[c]

    number = cell[...]
    zeros = jnp.zeros_like(radius)
    highs = [rounded(plane) for plane in [radius] + fresh]
    lows = [plane - high for plane, high in zip([radius] + fresh, highs)]
    highs.append(((number >> 8) * 256).astype(f32))
    lows.append((number & 255).astype(f32))
    put_rows(data, 16, highs + [zeros] * 3 + lows + [zeros] * 3)
    sort_blocks(plan_ref, spots, data, sorted_rows, tiles)

    chunk = rows_up(5 * cap + 1)
    flat = tiles.reshape(tiles.shape[0] * 8, width)
    for ahead in range(nbrick):
        target = brick_ahead(ahead, nbrick)
        for side, (outgoing, row) in enumerate(
            ((down, ahead * chunk), (outgoings[ahead], 0), (outgoings[ahead], chunk))
        ):
            code = side * nbrick + target
            for c in range(5):
                outgoing[row + c * cap : row + (c + 1) * cap, :] = flat[
                    pl.ds(code * (cap + 2) * 8 + c, cap, stride=8), :
                ]
            outgoing[row + 5 * cap : row + 5 * cap + 1, :] = bounds[pl.ds(code, 1), :]


def list_stride(segments, cap):
    return (segments + 1) * cap


def list_arrived(arrived, starts, ends, cap, places, counts):
    base, goal = places
    width = arrived.shape[1]
    stride = list_stride(len(starts), cap)
    shift = width.bit_length() - 1
    lane = iota((1, width), 1)
    filled = [jnp.int32(0)] * 4
    for start, end in zip(starts, ends):
        row = arrived[start + 5 * cap : start + 5 * cap + 1, :]
        edge = jnp.int32(0)
        for j in range(4):
            next_edge = jnp.sum(jnp.where(lane == j, row, 0.0)).astype(jnp.int32)
            first = edge >> shift
            last = jnp.where(next_edge > edge, (next_edge + width - 1) >> shift, first)
            at = j * stride + filled[j]

            def put(some, at=at, first=first, start=start, end=end):
                for i in some:
                    base[at + i] = start + first + i
                    goal[at + i] = end + first + i

            few = min(4, cap)
            put(range(few))
            pl.when(last - first > few)(functools.partial(put, range(few, cap)))
            filled[j] = filled[j] + last - first
            edge = next_edge
    for j in range(4):
        counts[j] = filled[j]


def cell_parts(arrived, row, cap, columns, depth, bucket):
    cell = arrived[pl.ds(row + 4 * cap, 1), :].astype(jnp.int32)
    shift = (2 * depth).bit_length() - 1
    column = (cell >> shift) - (bucket // 2) * columns
    level = (cell & (2 * depth - 1)) - (bucket % 2) * depth - depth // 2
    return column.astype(f32), level.astype(f32)


def all_levels(depth, width):
    return (iota((depth, width), 0) - depth // 2).astype(f32).astype(bf16)


def level_hot(level, levels):
    hit = levels == jnp.broadcast_to(level.astype(bf16), levels.shape)
    return jnp.where(hit, jnp.ones((), bf16), jnp.zeros((), bf16))


def longest(counts):
    return jnp.maximum(jnp.maximum(counts[0], counts[1]), jnp.maximum(counts[2], counts[3]))


def tile_of(counts, bucket, index, width):
    count = counts[bucket]
    real = jnp.full((1, width), jnp.where(index < count, 1, 0), jnp.int32) > 0
    return jnp.minimum(index, jnp.maximum(count - 1, 0)), real


def deposit(segments, counts, arrived, base, cap, total):
    columns, depth = total.shape[0] // 16, total.shape[1]
    width = arrived.shape[1]
    stride = list_stride(segments, cap)
    numbers = iota((columns, width), 0).astype(f32).astype(bf16)
    levels = all_levels(depth, width)

    def some(size, first):
        sums = []
        for bucket in range(4):
            high_of, low_of, level_of = [], [], []
            for k in range(size):
                index, real = tile_of(counts, bucket, first + k, width)
                row = base[bucket * stride + index]
                column, level = cell_parts(arrived, row, cap, columns, depth, bucket)
                radius = arrived[pl.ds(row, 1), :]
                mass = radius * radius * radius
                loads = [mass] + [mass * arrived[pl.ds(row + c * cap, 1), :] for c in (1, 2, 3)]
                hit = numbers == jnp.broadcast_to(column.astype(bf16), (columns, width))
                highs, lows = [], []
                for load in loads:
                    load = jnp.where(real, load, 0.0)
                    high = load.astype(bf16)
                    low = (load - high.astype(f32)).astype(bf16)
                    for parts, part in ((highs, high), (lows, low)):
                        part = jnp.broadcast_to(part, (columns, width))
                        parts.append(jnp.where(hit, part, jnp.zeros((), bf16)))
                high_of.append(jnp.concatenate(highs, axis=0))
                low_of.append(jnp.concatenate(lows, axis=0))
                level_of.append(level_hot(level, levels))
            both = lax.dot_general(
                jnp.concatenate(
                    [jnp.concatenate(high_of, axis=1), jnp.concatenate(low_of, axis=1)], axis=0
                ),
                jnp.concatenate(level_of, axis=1),
                (((1,), (1,)), ((), ())),
                preferred_element_type=f32,
            )
            sums.append(both[0 : 4 * columns] + both[4 * columns :])
        for bucket in range(4):
            total[bucket * 4 * columns : (bucket + 1) * 4 * columns, :] += sums[bucket]

    in_groups(longest(counts), GROUP, REST, some)


def sample(segments, counts, arrived, places, cap, table, answers):
    columns, depth = table.shape[0] // 24, table.shape[1]
    width = arrived.shape[1]
    stride = list_stride(segments, cap)
    levels = all_levels(depth, width)
    numbers = iota((columns, width), 0).astype(f32)
    answers[...] = jnp.zeros(answers.shape, f32)

    def some(size, first):
        found = []
        for bucket in range(4):
            hots, hits = [], []
            for k in range(size):
                index, real = tile_of(counts, bucket, first + k, width)
                row = places[0][bucket * stride + index]
                column, level = cell_parts(arrived, row, cap, columns, depth, bucket)
                hots.append(level_hot(level, levels))
                hits.append((numbers == column, real, places[1][bucket * stride + index]))
            along = jnp.dot(
                table[bucket * 6 * columns : (bucket + 1) * 6 * columns, :],
                jnp.concatenate(hots, axis=1),
                preferred_element_type=f32,
            )
            for k, (hit, real, goal) in enumerate(hits):
                part = along[:, k * width : (k + 1) * width]
                for c in range(3):
                    value = part[c * columns : (c + 1) * columns]
                    value = value + part[(c + 3) * columns : (c + 4) * columns]
                    value = jnp.sum(jnp.where(hit, value, 0.0), axis=0, keepdims=True)
                    found.append((goal + c * cap, jnp.where(real, value, 0.0)))
        for goal, value in found:
            answers[pl.ds(goal, 1), :] += value

    in_groups(longest(counts), GROUP, REST, some)


def first_deposit(nbrick, cap, skip, crossed, below, above, before, after, fluid, total, diffused,
                  flow, base, goal, counts, sems):
    reading = copy_all([(fluid, flow)], sems)
    chunk = rows_up(5 * cap + 1)
    total[...] = jnp.zeros(total.shape, f32)
    starts = [b * chunk for b in range(nbrick)]
    list_arrived(crossed, starts, starts, cap, (base, goal), counts)
    deposit(nbrick, counts, crossed, base, cap, total)
    wait_all(reading)
    diffuse(flow, below, above, before, after, skip, diffused)


def advance(nbrick, cap, start, fluid, diffused, below, *rest):
    above, rest = rest[:nbrick], rest[nbrick:]
    fluid_next, table, answers_below = rest[:3]
    answers_above, rest = rest[3 : 3 + nbrick], rest[3 + nbrick :]
    arrived, answers, total, flow, fresh_flow, base, goal, counts, sems = rest
    reading = pltpu.make_async_copy(fluid, flow, sems.at[0])
    reading.start()
    chunk = rows_up(5 * cap + 1)
    back = rows_up(3 * cap)
    rows = nbrick * chunk
    for b, part in enumerate(above):
        arrived[b * chunk : (b + 1) * chunk, :] = part[...]
    arrived[rows:, :] = below[...]
    starts = [i * chunk for i in range(2 * nbrick)]
    ends = [i * back for i in range(2 * nbrick)]
    total[...] = start[...]
    list_arrived(arrived, starts, ends, cap, (base, goal), counts)
    deposit(2 * nbrick, counts, arrived, base, cap, total)
    reading.wait()

    nx, ny, nz = flow.shape[1:]
    columns, depth = nx * ny // 2, nz // 2
    for x in range(nx):
        buckets = [2 * (x * ny // columns) + deep for deep in range(2)]
        at = x * ny % columns

        def load(c):
            spots = [4 * columns * bucket + c * columns + at for bucket in buckets]
            return jnp.concatenate([total[spot : spot + ny, :] for spot in spots], axis=1)

        volume = load(0)
        for c in range(3):
            moved = load(c + 1) - volume * flow[c, x]
            fresh = diffused[c, x] + coupling * moved
            fresh_flow[c, x] = fresh
            high = fresh.astype(bf16)
            low = (fresh - high.astype(f32)).astype(bf16)
            for deep, bucket in enumerate(buckets):
                spot = 6 * columns * bucket + c * columns + at
                half = slice(deep * depth, (deep + 1) * depth)
                table[spot : spot + ny, :] = high[:, half]
                table[spot + 3 * columns : spot + 3 * columns + ny, :] = low[:, half]
    writing = pltpu.make_async_copy(fresh_flow, fluid_next, sems.at[1])
    writing.start()
    sample(2 * nbrick, counts, arrived, (base, goal), cap, table, answers)
    for b, part in enumerate(answers_above):
        part[...] = answers[b * back : (b + 1) * back, :]
    answers_below[...] = answers[nbrick * back :, :]
    writing.wait()


def last_sample(nbrick, cap, crossed, table, *rest):
    answers, base, goal, counts = rest[nbrick:]
    chunk = rows_up(5 * cap + 1)
    back = rows_up(3 * cap)
    starts = [b * chunk for b in range(nbrick)]
    ends = [b * back for b in range(nbrick)]
    list_arrived(crossed, starts, ends, cap, (base, goal), counts)
    sample(nbrick, counts, crossed, (base, goal), cap, table, answers)
    for b, part in enumerate(rest[:nbrick]):
        part[...] = answers[b * back : (b + 1) * back, :]


def relax(nbrick, cap, plan, updated, spots, down, *rest):
    returneds = rest[:nbrick]
    velocity_next, picked, sorted_rows, tiles, plan_ref, sems = rest[nbrick:]
    copies = copy_all([(plan, plan_ref)], sems)
    nblocks, width = spots.shape
    back = rows_up(3 * cap)
    flat = tiles.reshape(tiles.shape[0] * 8, width)
    for ahead in range(nbrick):
        target = brick_ahead(ahead, nbrick)
        for side, (returned, row) in enumerate(
            ((down, ahead * back), (returneds[ahead], 0), (returneds[ahead], back))
        ):
            code = side * nbrick + target
            for c in range(3):
                flat[pl.ds(code * (cap + 2) * 8 + c, cap, stride=8), :] = returned[
                    row + c * cap : row + (c + 1) * cap, :
                ]
    lane = iota((8, width), 1)
    wait_all(copies)

    def gather(b, _):
        block = jnp.zeros((8, width), f32)
        for j in range(4):
            tile, at = plan_ref[b, j], plan_ref[b, 4 + j]
            first, length = plan_ref[b, 8 + j], plan_ref[b, 12 + j]
            run = jnp.where(lane >= at, tiles[tile], tiles[tile + 1])
            run = pltpu.roll(run, plan_ref[b, 20 + j], 1)
            block = jnp.where((lane >= first) & (lane < first + length), run, block)
        sorted_rows[b] = block
        return 0

    def order(b, _):
        block = sorted_rows[b]
        high = rounded(block)
        both = jnp.dot(
            jnp.concatenate([high, block - high], axis=0).astype(bf16),
            block_order(spots, b),
            preferred_element_type=f32,
        )
        picked[b] = both[0:8] + both[8:16]
        return 0

    lax.fori_loop(0, nblocks, gather, 0, unroll=32)
    lax.fori_loop(0, nblocks, order, 0, unroll=32)
    flat = picked.reshape(nblocks * 8, width)
    for c in range(3):
        now = updated[c]
        velocity_next[c] = now + relaxation * (flat[pl.ds(c, nblocks, stride=8), :] - now)


def on_device(
    positions, velocities, radii, cell_of, block_route, ghost_list, tile_home, tile_partner, fluid
):
    nblocks, _, width = positions.shape
    nbrick = lax.axis_size("brick")
    _, nx, ny, nz = fluid.shape
    columns = nx * ny
    codes = 3 * nbrick
    cap = max(2, (2 * nblocks + codes - 1) // codes)
    chunk, back = rows_up(5 * cap + 1), rows_up(3 * cap)
    per = ghost_list.shape[0] // 2
    tiles = tile_home.shape[0]
    routes = block_route.reshape(-1)
    positions = jnp.transpose(positions, (1, 0, 2))
    velocities = jnp.transpose(velocities, (1, 0, 2))

    def struct(*shape, dtype=f32):
        return jax.ShapeDtypeStruct(shape, dtype)

    def shifted(x, axis, step):
        if step == 0:
            return x
        count = lax.axis_size(axis)
        return lax.ppermute(x, axis, [(i, (i + step) % count) for i in range(count)])

    def ints(count):
        return pltpu.SMEM((count,), jnp.int32)

    state = jnp.concatenate([positions, radii[None], velocities], axis=0)
    ghost_rows, chunks = planes * per, 3 * (nz // width)
    up, low, right, left = call(
        pack_kernel,
        [struct(ghost_rows + chunks * ny, width)] * 2 + [struct(ghost_rows + chunks * nx, width)] * 2,
        [SMEM] + [VMEM] * 2,
        [],
        "pack",
    )(ghost_list, state, fluid)
    below = shifted(up, "slab", 1)
    above = shifted(low, "slab", -1)
    before = shifted(right, "brick", 1)
    after = shifted(left, "brick", -1)

    def sides(count):
        return [
            pltpu.VMEM((count * 32, width), f32),
            pltpu.VMEM((count, width, 32), bf16),
            pltpu.VMEM((count * 16, width), f32),
        ]

    lists = [ints(tiles + TAIL)] * 2
    contact_flops = tiles * width * width * 200
    chunk_tiles = pltpu.VMEM((codes * (cap + 2), 8, width), f32)
    block_tiles = pltpu.VMEM((nblocks, 8, width), f32)
    plan_copy = pltpu.SMEM((nblocks, width), jnp.int32)
    home_side, sums, spots, plan, bounds = call(
        functools.partial(own_contacts, cap, columns, nz),
        [
            struct((nblocks + 1) * 32, width),
            struct((nblocks + 1) * 16, width),
            struct(nblocks, width),
            struct(nblocks, width, dtype=jnp.int32),
            struct(rows_up(codes), width),
        ],
        [HBM] * 2 + [VMEM] * 3,
        sides(nblocks) + lists + [ints(tiles)] * 2 + [pltpu.SemaphoreType.DMA((2,))],
        "own_contacts",
        contact_flops,
    )(tile_home, tile_partner, state, cell_of, routes.reshape(1, nblocks))
    updated, down, *outgoing = call(
        functools.partial(ghost_contacts, nbrick, cap, 4 * per),
        [struct(3, nblocks, width), struct(nbrick * chunk, width)]
        + [struct(2 * chunk, width)] * nbrick,
        [HBM] * 2 + [ANY] + [VMEM] * 10,
        sides(4 * per)
        + [pltpu.VMEM(((nblocks + 1) * 16, width), f32)]
        + [pltpu.VMEM((nblocks * 16, width), f32), block_tiles, chunk_tiles]
        + lists
        + [ints(tiles), ints(tiles), plan_copy, pltpu.SemaphoreType.DMA((3,))],
        "ghost_contacts",
        contact_flops // 2,
    )(tile_home, tile_partner, plan, below, above, before, after,
      home_side, sums, state, cell_of, spots, bounds)

    down = shifted(down, "slab", -1)
    near = [shifted(part, "brick", ahead) for ahead, part in enumerate(outgoing)]
    from_below = shifted(jnp.concatenate([part[chunk:] for part in near], axis=0), "slab", 1)
    from_above = [
        shifted(down[ahead * chunk : (ahead + 1) * chunk], "brick", ahead)
        for ahead in range(nbrick)
    ]
    crossed = jnp.concatenate([part[:chunk] for part in near], axis=0)

    def places(count):
        return [ints(4 * list_stride(count, cap))] * 2 + [ints(4)]

    block_flops = 8 * columns * nz * width
    started, diffused = call(
        functools.partial(first_deposit, nbrick, cap, ghost_rows),
        [struct(8 * columns, nz // 2), struct(3, nx, ny, nz)],
        [VMEM] * 5 + [HBM],
        [pltpu.VMEM((3, nx, ny, nz), f32)]
        + places(nbrick)
        + [pltpu.SemaphoreType.DMA((1,))],
        "first_deposit",
        block_flops * nblocks // 3,
    )(crossed, below, above, before, after, fluid)
    fluid_next, table, answers_below, *answers_above = call(
        functools.partial(advance, nbrick, cap),
        [
            struct(3, nx, ny, nz),
            struct(12 * columns, nz // 2, dtype=bf16),
            struct(nbrick * back, width),
        ]
        + [struct(back, width)] * nbrick,
        [VMEM, HBM] + [VMEM] * (2 + nbrick),
        [
            pltpu.VMEM((2 * nbrick * chunk, width), f32),
            pltpu.VMEM((2 * nbrick * back, width), f32),
            pltpu.VMEM((8 * columns, nz // 2), f32),
        ]
        + [pltpu.VMEM((3, nx, ny, nz), f32)] * 2
        + places(2 * nbrick)
        + [pltpu.SemaphoreType.DMA((2,))],
        "advance",
        block_flops * nblocks,
        places=[HBM] + [VMEM] * (2 + nbrick),
    )(started, fluid, diffused, from_below, *from_above)
    answers_below = shifted(answers_below, "slab", -1)
    answers_above = [
        shifted(part, "brick", -behind) for behind, part in enumerate(answers_above)
    ]
    returned_down = shifted(jnp.concatenate(answers_above, axis=0), "slab", 1)
    answers = call(
        functools.partial(last_sample, nbrick, cap),
        [struct(back, width)] * nbrick,
        [VMEM] * 2,
        [pltpu.VMEM((nbrick * back, width), f32)] + places(nbrick),
        "last_sample",
        block_flops * nblocks // 64,
    )(crossed, table)
    returned = []
    for behind in range(nbrick):
        at = slice(behind * back, (behind + 1) * back)
        part = jnp.concatenate([answers[behind], answers_below[at]], axis=0)
        returned.append(shifted(part, "brick", -behind))
    (velocity_next,) = call(
        functools.partial(relax, nbrick, cap),
        [struct(3, nblocks, width)],
        [ANY] + [VMEM] * (3 + nbrick),
        [block_tiles, block_tiles, chunk_tiles, plan_copy]
        + [pltpu.SemaphoreType.DMA((1,))],
        "relax",
    )(plan, updated, spots, returned_down, *returned)
    return (jnp.transpose(velocity_next, (1, 0, 2)), fluid_next)


def solution(mesh):
    placed = (
        P(("slab", "brick"), None, None),
        P(("slab", "brick"), None, None),
        P(("slab", "brick"), None),
        P(("slab", "brick"), None),
        P(("slab", "brick"), None),
        P(("slab", "brick")),
        P(("slab", "brick")),
        P(("slab", "brick")),
        P(None, "slab", "brick", None),
    )
    return jax.shard_map(
        on_device,
        mesh=mesh,
        in_specs=placed,
        out_specs=(P(("slab", "brick"), None, None), P(None, "slab", "brick", None)),
        check_vma=False,
    )
```

```python
import functools
import math

import jax
import jax.numpy as jnp
from jax import lax
from jax.experimental import pallas as pl
from jax.experimental.pallas import tpu as pltpu
from jax.sharding import PartitionSpec as P

stiffness = 0.01
damping = 0.005
viscosity = 0.1
coupling = 0.5
relaxation = 0.5

f32 = jnp.float32
bf16 = jnp.bfloat16
VMEM = pl.BlockSpec(memory_space=pltpu.VMEM)
SMEM = pl.BlockSpec(memory_space=pltpu.SMEM)
ANY = pl.BlockSpec(memory_space=pl.ANY)
HBM = pl.BlockSpec(memory_space=pltpu.HBM)
UNROLL = 32
TAIL = 8
GROUP = 4
REST = 2


def rows_up(count):
    return -(-count // 8) * 8


def call(body, outs, ins, scratch, name, flops=0, nbytes=1 << 20, places=None, vmem=40 << 20):
    return pl.pallas_call(
        body,
        out_shape=outs,
        in_specs=ins,
        out_specs=places or [VMEM] * len(outs),
        scratch_shapes=scratch,
        name=name,
        compiler_params=pltpu.CompilerParams(vmem_limit_bytes=vmem),
        cost_estimate=pl.CostEstimate(flops=flops, bytes_accessed=nbytes, transcendentals=0),
    )


def rounded(x):
    return x.astype(bf16).astype(f32)


def iota(shape, dim):
    return lax.broadcasted_iota(jnp.int32, shape, dim)


planes = 7


def copy_all(pairs, sems):
    copies = [pltpu.make_async_copy(*pair, sems.at[i]) for i, pair in enumerate(pairs)]
    for copy in copies:
        copy.start()
    return copies


def wait_all(copies):
    for copy in copies:
        copy.wait()


def pack_kernel(ghost_ref, state, fluid, up, down, right, left):
    count = ghost_ref.shape[0] // 4
    width = state.shape[2]
    nx, ny, nz = fluid.shape[1:]
    for group in range(4):
        i, j = group // 2, group % 2
        slab_to, brick_to = (up if i else down), (right if j else left)
        for g in range(count):
            block = pl.ds(ghost_ref[group * count + g], 1)
            for c in range(planes):
                row = state[c, block, :]
                at = c * 2 * count + j * count + g
                slab_to[at : at + 1, :] = row
                at = c * 2 * count + i * count + g
                brick_to[at : at + 1, :] = row
    for slab_to, x in ((up, nx - 1), (down, 0)):
        for c in range(3):
            for k in range(nz // width):
                at = planes * 2 * count + (c * (nz // width) + k) * ny
                slab_to[at : at + ny, :] = fluid[c, x, :, k * width : (k + 1) * width]
    for brick_to, y in ((right, ny - 1), (left, 0)):
        for c in range(3):
            for x in range(nx):
                for k in range(nz // width):
                    at = planes * 2 * count + (c * nx + x) * (nz // width) + k
                    brick_to[at : at + 1, :] = fluid[
                        c, x, y : y + 1, k * width : (k + 1) * width
                    ]


def three_parts(x):
    one = rounded(x)
    rest = x - one
    two = rounded(rest)
    return one, two, rest - two


def put_rows(ref, stride, rows):
    count = rows[0].shape[0]
    for k, row in enumerate(rows):
        ref[pl.ds(k, count, stride=stride), :] = row


def pair_factors(place):
    parts = [three_parts(plane) for plane in place]
    own = three_parts(
        place[3] * place[3] - place[0] * place[0] - place[1] * place[1] - place[2] * place[2]
    )
    return [[part[k] for part in parts] for k in range(3)], list(own)


def home_rows(place):
    (one, two, three), own = pair_factors(place)
    ones, zeros = jnp.ones_like(place[0]), jnp.zeros_like(place[0])
    rows = one + one + two + two + one + three
    return [2.0 * row for row in rows] + own + [ones] * 3 + [zeros] * 2


def partner_rows(place):
    (one, two, three), own = pair_factors(place)
    ones, zeros = jnp.ones_like(place[0]), jnp.zeros_like(place[0])
    return one + two + one + two + three + one + [ones] * 3 + own + [zeros] * 2


def value_rows(values):
    highs = [rounded(plane) for plane in values]
    ones, zeros = jnp.ones_like(values[0]), jnp.zeros_like(values[0])
    lows = [plane - high for plane, high in zip(values, highs)]
    return highs + [ones, zeros] + lows + [zeros, zeros]


def prepare_partners(place, speeds, rows, columns, values):
    count, width = place[0].shape
    put_rows(rows, 32, partner_rows(place))
    put_rows(values, 16, value_rows(place[0:3] + speeds))

    def turn(b, _):
        block = rows[pl.ds(pl.multiple_of(b * 32, 32), 32), :]
        columns[b] = jnp.transpose(block).astype(bf16)
        return 0

    lax.fori_loop(0, count, turn, 0, unroll=8)


def list_tiles(home_ref, partner_ref, homes, partners, lower, upper, spare):
    def one(t, count):
        partner = partner_ref[t]
        homes[count] = home_ref[t]
        partners[count] = partner - lower
        return count + jnp.where((partner >= lower) & (partner < upper), 1, 0)

    count = lax.fori_loop(0, home_ref.shape[0], one, 0, unroll=4)
    for pad in range(TAIL):
        homes[count + pad] = spare
        partners[count + pad] = 0
    return count


def in_groups(count, large, small, work):
    steps = count // large
    left = (count - steps * large + small - 1) // small

    def one(size, first, step, _):
        work(size, first + step * size)
        return 0

    lax.fori_loop(0, steps, functools.partial(one, large, 0), 0)
    lax.fori_loop(0, left, functools.partial(one, small, steps * large), 0)


def add_tiles(count, homes, partners, home_side, partner_side, values, sums):
    def some(tiles, start):
        added = []
        for k in range(tiles):
            home = homes[start + k]
            partner = partners[start + k]
            factors = home_side[pl.ds(pl.multiple_of(home * 32, 32), 32), :].astype(bf16)
            weight = jnp.dot(partner_side[partner], factors, preferred_element_type=f32)
            weight = jnp.maximum(weight, 0.0)
            high = weight.astype(bf16)
            low = (weight - high.astype(f32)).astype(bf16)
            value = values[pl.ds(pl.multiple_of(partner * 16, 16), 16), :].astype(bf16)
            at = pl.ds(pl.multiple_of(home * 16, 16), 16)
            term = jnp.dot(
                jnp.concatenate([value, value], axis=1),
                jnp.concatenate([high, low], axis=0),
                preferred_element_type=f32,
            )
            added.append((at, term))
        for at, term in added:
            sums[at, :] += term

    in_groups(count, UNROLL, TAIL, some)


def dot(left, right):
    return jnp.dot(left.astype(bf16), right.astype(bf16), preferred_element_type=f32)


def plan_sort(cap, cell, route, columns, depth, spots, plan, bounds):
    nblocks, width = cell.shape
    shift = depth.bit_length() - 1
    number = cell[...]
    right = (number >> shift) >= columns // 2
    deep = (number & (depth - 1)) >= depth // 2
    kind = jnp.where(right, 2, 0) + jnp.where(deep, 1, 0)
    members = [jnp.where(kind == j, 1.0, 0.0) for j in range(4)]
    before = jnp.where(iota((width, width), 0) < iota((width, width), 1), 1.0, 0.0)
    stacked = jnp.concatenate(members, axis=0)
    ranks = dot(stacked, before)
    lengths = dot(stacked, jnp.ones((width, width), f32))
    ranks = [ranks[j * nblocks : (j + 1) * nblocks] for j in range(4)]
    lengths = [lengths[j * nblocks : (j + 1) * nblocks] for j in range(4)]

    across = jnp.broadcast_to(route[...].astype(f32), (nblocks, nblocks))
    same = across == jnp.transpose(across)
    earlier = iota((nblocks, nblocks), 1) < iota((nblocks, nblocks), 0)
    side_by_side = jnp.concatenate(lengths, axis=1)
    ahead = dot(jnp.where(same & earlier, 1.0, 0.0), side_by_side)
    whole = dot(jnp.where(same, 1.0, 0.0), side_by_side)
    rows = bounds.shape[0]
    of_code = jnp.broadcast_to(route[...], (rows, nblocks)) == iota((rows, nblocks), 0)
    totals = dot(jnp.where(of_code, 1.0, 0.0), side_by_side)

    lane = iota((nblocks, width), 1)
    bound_lane = iota((rows, width), 1)
    spot = jnp.zeros((nblocks, width), f32)
    first, chunk_first = jnp.zeros((nblocks, width), f32), jnp.zeros((nblocks, width), f32)
    bound, line = jnp.zeros((rows, width), f32), jnp.zeros((rows, width), f32)
    table = jnp.zeros((nblocks, width), jnp.int32)
    own_code = jnp.transpose(across).astype(jnp.int32)
    own_code = jnp.concatenate([own_code] * (width // nblocks), axis=1)
    for j in range(4):
        at = slice(j * width, (j + 1) * width)
        spot = spot + members[j] * (first + ranks[j])
        where = (chunk_first + ahead[:, at]).astype(jnp.int32)
        start, there = first.astype(jnp.int32), where & (width - 1)
        parts = [
            own_code * (cap + 2) + (where >> (width.bit_length() - 1)),
            there,
            start,
            lengths[j].astype(jnp.int32),
            (there - start) & (width - 1),
            (start - there) & (width - 1),
        ]
        for k, part in enumerate(parts):
            table = jnp.where(lane == 4 * k + j, part, table)
        first = first + lengths[j]
        chunk_first = chunk_first + whole[:, at]
        bound = bound + totals[:, at]
        line = jnp.where(bound_lane == j, bound, line)
    spots[...] = spot
    plan[...] = table
    bounds[...] = line


def block_order(spots, b):
    width = spots.shape[1]
    row = jnp.broadcast_to(spots[pl.ds(b, 1), :].astype(bf16), (width, width))
    hit = iota((width, width), 0).astype(f32).astype(bf16) == row
    return jnp.where(hit, jnp.ones((), bf16), jnp.zeros((), bf16))


def sort_blocks(plan, spots, data, sorted_rows, tiles):
    nblocks, width = spots.shape
    lane = iota((8, width), 1)

    def order(b, _):
        rows = data[pl.ds(pl.multiple_of(b * 16, 16), 16), :].astype(bf16)
        both = lax.dot_general(
            rows, block_order(spots, b), (((1,), (1,)), ((), ())), preferred_element_type=f32
        )
        sorted_rows[b] = both[0:8] + both[8:16]
        return 0

    def spread(b, _):
        block = sorted_rows[b]
        for j in range(4):
            tile, at, length = plan[b, j], plan[b, 4 + j], plan[b, 12 + j]
            moved = pltpu.roll(block, plan[b, 16 + j], 1)
            here = (lane >= at) & (lane < at + length)
            pltpu.store(tiles.at[tile], moved, mask=here)
            pltpu.store(tiles.at[tile + 1], moved, mask=lane < at + length - width)
        return 0

    lax.fori_loop(0, nblocks, order, 0, unroll=32)
    lax.fori_loop(0, nblocks, spread, 0, unroll=32)


def own_contacts(cap, columns, depth, home_list, partner_list, state, cell, route,
                 home_side, sums, spots, plan, bounds,
                 rows, partner_side, values, homes, partners, home_ref, partner_ref, sems):
    nblocks, width = state.shape[1:]
    copies = copy_all([(home_list, home_ref), (partner_list, partner_ref)], sems)
    plan_sort(cap, cell, route, columns, depth, spots, plan, bounds)
    place = [state[c] for c in range(4)]
    put_rows(home_side, 32, home_rows(place))
    prepare_partners(place, [state[c] for c in (4, 5, 6)], rows, partner_side, values)
    home_side[nblocks * 32 :, :] = jnp.zeros((32, width), f32)
    sums[...] = jnp.zeros(sums.shape, f32)
    wait_all(copies)
    count = list_tiles(home_ref, partner_ref, homes, partners, 0, nblocks, nblocks)
    add_tiles(count, homes, partners, home_side, partner_side, values, sums)


def diffuse(fluid, below, above, before, after, skip, diffused):
    nx, ny, nz = fluid.shape[1:]
    width = before.shape[1]
    deep = iota((ny, nz), 1)

    def face(ref, c, x):
        at = skip + (c * nx + x) * (nz // width)
        return jnp.concatenate(
            [ref[at + k : at + k + 1, :] for k in range(nz // width)], axis=1
        )

    def layer(ref, c):
        at = [skip + (c * (nz // width) + k) * ny for k in range(nz // width)]
        return jnp.concatenate([ref[start : start + ny, :] for start in at], axis=1)

    for x in range(nx):
        for c in range(3):
            here = fluid[c, x]
            near = (layer(below, c) if x == 0 else fluid[c, x - 1]) + (
                layer(above, c) if x == nx - 1 else fluid[c, x + 1]
            )
            near = near + jnp.concatenate([face(before, c, x), here[:-1]], axis=0)
            near = near + jnp.concatenate([here[1:], face(after, c, x)], axis=0)
            near = near + jnp.where(deep == 0, 0.0, pltpu.roll(here, 1, 1))
            near = near + jnp.where(deep == nz - 1, 0.0, pltpu.roll(here, nz - 1, 1))
            diffused[c, x] = here + viscosity * (near - 6.0 * here)


def brick_ahead(ahead, nbrick):
    return lax.rem(lax.axis_index("brick") + ahead, nbrick)


def ghost_contacts(nbrick, cap, partner_blocks, home_list, partner_list, plan, below,
                   above, before, after, home_side, own_sums, state, cell, spots, bounds,
                   updated, down, *rest):
    outgoings = rest[:nbrick]
    (rows, columns, values, sums, data, sorted_rows, tiles, homes, partners,
     home_ref, partner_ref, plan_ref, sems) = rest[nbrick:]
    nblocks, width = state.shape[1:]
    per = partner_blocks // 4
    copies = copy_all(
        [
            (home_list, home_ref),
            (partner_list, partner_ref),
            (plan, plan_ref),
        ],
        sems,
    )
    stacked = [
        jnp.concatenate(
            [ref[c * per : (c + 1) * per, :] for ref in (below, above, before, after)], axis=0
        )
        for c in range(planes)
    ]
    prepare_partners(stacked[0:4], stacked[4:7], rows, columns, values)
    sums[...] = own_sums[...]
    wait_all(copies)
    count = list_tiles(home_ref, partner_ref, homes, partners, nblocks, nblocks + 4 * per, nblocks)
    add_tiles(count, homes, partners, home_side, columns, values, sums)

    def total(k):
        high = sums[pl.ds(k, nblocks, stride=16), :]
        return high + sums[pl.ds(k + 8, nblocks, stride=16), :]

    weights = total(6)
    radius = state[3]
    inverse = 1.0 / (radius * radius * radius)
    fresh = []
    for c in range(3):
        speed = state[c + 4]
        spring = state[c] * weights - total(c)
        friction = total(c + 3) - speed * weights
        fresh.append(speed + (stiffness * spring + damping * friction) * inverse)
        updated[c] = fresh[c]

    number = cell[...]
    zeros = jnp.zeros_like(radius)
    highs = [rounded(plane) for plane in [radius] + fresh]
    lows = [plane - high for plane, high in zip([radius] + fresh, highs)]
    highs.append(((number >> 8) * 256).astype(f32))
    lows.append((number & 255).astype(f32))
    put_rows(data, 16, highs + [zeros] * 3 + lows + [zeros] * 3)
    sort_blocks(plan_ref, spots, data, sorted_rows, tiles)

    chunk = rows_up(5 * cap + 1)
    flat = tiles.reshape(tiles.shape[0] * 8, width)
    for ahead in range(nbrick):
        target = brick_ahead(ahead, nbrick)
        for side, (outgoing, row) in enumerate(
            ((down, ahead * chunk), (outgoings[ahead], 0), (outgoings[ahead], chunk))
        ):
            code = side * nbrick + target
            for c in range(5):
                outgoing[row + c * cap : row + (c + 1) * cap, :] = flat[
                    pl.ds(code * (cap + 2) * 8 + c, cap, stride=8), :
                ]
            outgoing[row + 5 * cap : row + 5 * cap + 1, :] = bounds[pl.ds(code, 1), :]


def list_stride(segments, cap):
    return (segments + 1) * cap


def list_arrived(arrived, starts, ends, cap, places, counts, early=None):
    base, goal = places
    width = arrived.shape[1]
    stride = list_stride(len(starts), cap)
    shift = width.bit_length() - 1
    lane = iota((1, width), 1)
    filled = [jnp.int32(0)] * 4
    for segment, (start, end) in enumerate(zip(starts, ends)):
        if early is not None and 2 * segment == len(starts):
            for j in range(4):
                early[j] = filled[j]
        row = arrived[start + 5 * cap : start + 5 * cap + 1, :]
        edge = jnp.int32(0)
        for j in range(4):
            next_edge = jnp.sum(jnp.where(lane == j, row, 0.0)).astype(jnp.int32)
            first = edge >> shift
            last = jnp.where(next_edge > edge, (next_edge + width - 1) >> shift, first)
            at = j * stride + filled[j]

            def put(some, at=at, first=first, start=start, end=end):
                for i in some:
                    base[at + i] = start + first + i
                    goal[at + i] = end + first + i

            few = min(4, cap)
            put(range(few))
            pl.when(last - first > few)(functools.partial(put, range(few, cap)))
            filled[j] = filled[j] + last - first
            edge = next_edge
    for j in range(4):
        counts[j] = filled[j]


def cell_parts(arrived, row, cap, columns, depth, bucket):
    cell = arrived[pl.ds(row + 4 * cap, 1), :].astype(jnp.int32)
    shift = (2 * depth).bit_length() - 1
    column = (cell >> shift) - (bucket // 2) * columns
    level = (cell & (2 * depth - 1)) - (bucket % 2) * depth - depth // 2
    return column.astype(f32), level.astype(f32)


def all_levels(depth, width):
    return (iota((depth, width), 0) - depth // 2).astype(f32).astype(bf16)


def level_hot(level, levels):
    hit = levels == jnp.broadcast_to(level.astype(bf16), levels.shape)
    return jnp.where(hit, jnp.ones((), bf16), jnp.zeros((), bf16))


def longest(counts):
    return jnp.maximum(jnp.maximum(counts[0], counts[1]), jnp.maximum(counts[2], counts[3]))


def tile_of(counts, bucket, index, width):
    count = counts[bucket]
    real = jnp.full((1, width), jnp.where(index < count, 1, 0), jnp.int32) > 0
    return jnp.minimum(index, jnp.maximum(count - 1, 0)), real


def deposit(segments, counts, arrived, base, cap, total):
    columns, depth = total.shape[0] // 16, total.shape[1]
    width = arrived.shape[1]
    stride = list_stride(segments, cap)
    numbers = iota((columns, width), 0).astype(f32).astype(bf16)
    levels = all_levels(depth, width)

    def some(size, first):
        sums = []
        for bucket in range(4):
            high_of, low_of, level_of = [], [], []
            for k in range(size):
                index, real = tile_of(counts, bucket, first + k, width)
                row = base[bucket * stride + index]
                column, level = cell_parts(arrived, row, cap, columns, depth, bucket)
                radius = arrived[pl.ds(row, 1), :]
                mass = radius * radius * radius
                loads = [mass] + [mass * arrived[pl.ds(row + c * cap, 1), :] for c in (1, 2, 3)]
                hit = numbers == jnp.broadcast_to(column.astype(bf16), (columns, width))
                highs, lows = [], []
                for load in loads:
                    load = jnp.where(real, load, 0.0)
                    high = load.astype(bf16)
                    low = (load - high.astype(f32)).astype(bf16)
                    for parts, part in ((highs, high), (lows, low)):
                        part = jnp.broadcast_to(part, (columns, width))
                        parts.append(jnp.where(hit, part, jnp.zeros((), bf16)))
                high_of.append(jnp.concatenate(highs, axis=0))
                low_of.append(jnp.concatenate(lows, axis=0))
                level_of.append(level_hot(level, levels))
            both = lax.dot_general(
                jnp.concatenate(
                    [jnp.concatenate(high_of, axis=1), jnp.concatenate(low_of, axis=1)], axis=0
                ),
                jnp.concatenate(level_of, axis=1),
                (((1,), (1,)), ((), ())),
                preferred_element_type=f32,
            )
            sums.append(both[0 : 4 * columns] + both[4 * columns :])
        for bucket in range(4):
            total[bucket * 4 * columns : (bucket + 1) * 4 * columns, :] += sums[bucket]

    in_groups(longest(counts), GROUP, REST, some)


def sample(segments, counts, arrived, places, cap, table, answers):
    columns, depth = table.shape[0] // 24, table.shape[1]
    width = arrived.shape[1]
    stride = list_stride(segments, cap)
    levels = all_levels(depth, width)
    numbers = iota((columns, width), 0).astype(f32)
    answers[...] = jnp.zeros(answers.shape, f32)

    def some(size, first):
        found = []
        for bucket in range(4):
            hots, hits = [], []
            for k in range(size):
                index, real = tile_of(counts, bucket, first + k, width)
                row = places[0][bucket * stride + index]
                column, level = cell_parts(arrived, row, cap, columns, depth, bucket)
                hots.append(level_hot(level, levels))
                hits.append((numbers == column, real, places[1][bucket * stride + index]))
            along = jnp.dot(
                table[bucket * 6 * columns : (bucket + 1) * 6 * columns, :],
                jnp.concatenate(hots, axis=1),
                preferred_element_type=f32,
            )
            for k, (hit, real, goal) in enumerate(hits):
                part = along[:, k * width : (k + 1) * width]
                for c in range(3):
                    value = part[c * columns : (c + 1) * columns]
                    value = value + part[(c + 3) * columns : (c + 4) * columns]
                    value = jnp.sum(jnp.where(hit, value, 0.0), axis=0, keepdims=True)
                    found.append((goal + c * cap, jnp.where(real, value, 0.0)))
        for goal, value in found:
            answers[pl.ds(goal, 1), :] += value

    in_groups(longest(counts), GROUP, REST, some)


def first_deposit(nbrick, cap, skip, crossed, below, above, before, after, fluid, total, diffused,
                  flow, base, goal, counts, sems):
    reading = copy_all([(fluid, flow)], sems)
    chunk = rows_up(5 * cap + 1)
    total[...] = jnp.zeros(total.shape, f32)
    starts = [b * chunk for b in range(nbrick)]
    list_arrived(crossed, starts, starts, cap, (base, goal), counts)
    deposit(nbrick, counts, crossed, base, cap, total)
    wait_all(reading)
    diffuse(flow, below, above, before, after, skip, diffused)


def advance(nbrick, cap, start, fluid, diffused, below, *rest):
    above, rest = rest[:nbrick], rest[nbrick:]
    fluid_next, table = rest[:2]
    answers_above, rest = rest[2 : 2 + nbrick], rest[2 + nbrick :]
    arrived, answers, total, flow, fresh_flow, base, goal, counts, early, sems = rest
    reading = pltpu.make_async_copy(fluid, flow, sems.at[0])
    reading.start()
    chunk = rows_up(5 * cap + 1)
    back = rows_up(3 * cap)
    rows = nbrick * chunk
    for b, part in enumerate(above):
        arrived[b * chunk : (b + 1) * chunk, :] = part[...]
    arrived[rows:, :] = below[...]
    starts = [i * chunk for i in range(2 * nbrick)]
    ends = [i * back for i in range(2 * nbrick)]
    total[...] = start[...]
    list_arrived(arrived, starts, ends, cap, (base, goal), counts, early)
    deposit(2 * nbrick, counts, arrived, base, cap, total)
    reading.wait()

    nx, ny, nz = flow.shape[1:]
    columns, depth = nx * ny // 2, nz // 2
    for x in range(nx):
        buckets = [2 * (x * ny // columns) + deep for deep in range(2)]
        at = x * ny % columns

        def load(c):
            spots = [4 * columns * bucket + c * columns + at for bucket in buckets]
            return jnp.concatenate([total[spot : spot + ny, :] for spot in spots], axis=1)

        volume = load(0)
        for c in range(3):
            moved = load(c + 1) - volume * flow[c, x]
            fresh = diffused[c, x] + coupling * moved
            fresh_flow[c, x] = fresh
            high = fresh.astype(bf16)
            low = (fresh - high.astype(f32)).astype(bf16)
            for deep, bucket in enumerate(buckets):
                spot = 6 * columns * bucket + c * columns + at
                half = slice(deep * depth, (deep + 1) * depth)
                table[spot : spot + ny, :] = high[:, half]
                table[spot + 3 * columns : spot + 3 * columns + ny, :] = low[:, half]
    writing = pltpu.make_async_copy(fresh_flow, fluid_next, sems.at[1])
    writing.start()
    sample(2 * nbrick, early, arrived, (base, goal), cap, table, answers)
    for b, part in enumerate(answers_above):
        part[...] = answers[b * back : (b + 1) * back, :]
    writing.wait()


def below_sample(nbrick, cap, below, table, answers, base, goal, counts):
    chunk = rows_up(5 * cap + 1)
    back = rows_up(3 * cap)
    starts = [b * chunk for b in range(nbrick)]
    ends = [b * back for b in range(nbrick)]
    list_arrived(below, starts, ends, cap, (base, goal), counts)
    sample(nbrick, counts, below, (base, goal), cap, table, answers)


def last_sample(nbrick, cap, crossed, table, *rest):
    answers, base, goal, counts = rest[nbrick:]
    chunk = rows_up(5 * cap + 1)
    back = rows_up(3 * cap)
    starts = [b * chunk for b in range(nbrick)]
    ends = [b * back for b in range(nbrick)]
    list_arrived(crossed, starts, ends, cap, (base, goal), counts)
    sample(nbrick, counts, crossed, (base, goal), cap, table, answers)
    for b, part in enumerate(rest[:nbrick]):
        part[...] = answers[b * back : (b + 1) * back, :]


def relax(nbrick, cap, plan, updated, spots, down, *rest):
    returneds = rest[:nbrick]
    velocity_next, picked, sorted_rows, tiles, plan_ref, sems = rest[nbrick:]
    copies = copy_all([(plan, plan_ref)], sems)
    nblocks, width = spots.shape
    back = rows_up(3 * cap)
    flat = tiles.reshape(tiles.shape[0] * 8, width)
    for ahead in range(nbrick):
        target = brick_ahead(ahead, nbrick)
        for side, (returned, row) in enumerate(
            ((down, ahead * back), (returneds[ahead], 0), (returneds[ahead], back))
        ):
            code = side * nbrick + target
            for c in range(3):
                flat[pl.ds(code * (cap + 2) * 8 + c, cap, stride=8), :] = returned[
                    row + c * cap : row + (c + 1) * cap, :
                ]
    lane = iota((8, width), 1)
    wait_all(copies)

    def gather(b, _):
        block = jnp.zeros((8, width), f32)
        for j in range(4):
            tile, at = plan_ref[b, j], plan_ref[b, 4 + j]
            first, length = plan_ref[b, 8 + j], plan_ref[b, 12 + j]
            run = jnp.where(lane >= at, tiles[tile], tiles[tile + 1])
            run = pltpu.roll(run, plan_ref[b, 20 + j], 1)
            block = jnp.where((lane >= first) & (lane < first + length), run, block)
        sorted_rows[b] = block
        return 0

    def order(b, _):
        block = sorted_rows[b]
        high = rounded(block)
        both = jnp.dot(
            jnp.concatenate([high, block - high], axis=0).astype(bf16),
            block_order(spots, b),
            preferred_element_type=f32,
        )
        picked[b] = both[0:8] + both[8:16]
        return 0

    lax.fori_loop(0, nblocks, gather, 0, unroll=32)
    lax.fori_loop(0, nblocks, order, 0, unroll=32)
    flat = picked.reshape(nblocks * 8, width)
    for c in range(3):
        now = updated[c]
        velocity_next[c] = now + relaxation * (flat[pl.ds(c, nblocks, stride=8), :] - now)


def on_device(
    positions, velocities, radii, cell_of, block_route, ghost_list, tile_home, tile_partner, fluid
):
    nblocks, _, width = positions.shape
    nbrick = lax.axis_size("brick")
    _, nx, ny, nz = fluid.shape
    columns = nx * ny
    codes = 3 * nbrick
    cap = max(2, (2 * nblocks + codes - 1) // codes)
    chunk, back = rows_up(5 * cap + 1), rows_up(3 * cap)
    per = ghost_list.shape[0] // 2
    tiles = tile_home.shape[0]
    routes = block_route.reshape(-1)
    positions = jnp.transpose(positions, (1, 0, 2))
    velocities = jnp.transpose(velocities, (1, 0, 2))

    def struct(*shape, dtype=f32):
        return jax.ShapeDtypeStruct(shape, dtype)

    def shifted(x, axis, step):
        if step == 0:
            return x
        count = lax.axis_size(axis)
        return lax.ppermute(x, axis, [(i, (i + step) % count) for i in range(count)])

    def ints(count):
        return pltpu.SMEM((count,), jnp.int32)

    state = jnp.concatenate([positions, radii[None], velocities], axis=0)
    ghost_rows, chunks = planes * per, 3 * (nz // width)
    up, low, right, left = call(
        pack_kernel,
        [struct(ghost_rows + chunks * ny, width)] * 2 + [struct(ghost_rows + chunks * nx, width)] * 2,
        [SMEM] + [VMEM] * 2,
        [],
        "pack",
    )(ghost_list, state, fluid)
    below = shifted(up, "slab", 1)
    above = shifted(low, "slab", -1)
    before = shifted(right, "brick", 1)
    after = shifted(left, "brick", -1)

    def sides(count):
        return [
            pltpu.VMEM((count * 32, width), f32),
            pltpu.VMEM((count, width, 32), bf16),
            pltpu.VMEM((count * 16, width), f32),
        ]

    lists = [ints(tiles + TAIL)] * 2
    contact_flops = tiles * width * width * 200
    chunk_tiles = pltpu.VMEM((codes * (cap + 2), 8, width), f32)
    block_tiles = pltpu.VMEM((nblocks, 8, width), f32)
    plan_copy = pltpu.SMEM((nblocks, width), jnp.int32)
    home_side, sums, spots, plan, bounds = call(
        functools.partial(own_contacts, cap, columns, nz),
        [
            struct((nblocks + 1) * 32, width),
            struct((nblocks + 1) * 16, width),
            struct(nblocks, width),
            struct(nblocks, width, dtype=jnp.int32),
            struct(rows_up(codes), width),
        ],
        [HBM] * 2 + [VMEM] * 3,
        sides(nblocks) + lists + [ints(tiles)] * 2 + [pltpu.SemaphoreType.DMA((2,))],
        "own_contacts",
        contact_flops,
    )(tile_home, tile_partner, state, cell_of, routes.reshape(1, nblocks))
    updated, down, *outgoing = call(
        functools.partial(ghost_contacts, nbrick, cap, 4 * per),
        [struct(3, nblocks, width), struct(nbrick * chunk, width)]
        + [struct(2 * chunk, width)] * nbrick,
        [HBM] * 2 + [ANY] + [VMEM] * 10,
        sides(4 * per)
        + [pltpu.VMEM(((nblocks + 1) * 16, width), f32)]
        + [pltpu.VMEM((nblocks * 16, width), f32), block_tiles, chunk_tiles]
        + lists
        + [ints(tiles), ints(tiles), plan_copy, pltpu.SemaphoreType.DMA((3,))],
        "ghost_contacts",
        contact_flops // 2,
    )(tile_home, tile_partner, plan, below, above, before, after,
      home_side, sums, state, cell_of, spots, bounds)

    down = shifted(down, "slab", -1)
    near = [shifted(part, "brick", ahead) for ahead, part in enumerate(outgoing)]
    from_below = shifted(jnp.concatenate([part[chunk:] for part in near], axis=0), "slab", 1)
    from_above = [
        shifted(down[ahead * chunk : (ahead + 1) * chunk], "brick", ahead)
        for ahead in range(nbrick)
    ]
    crossed = jnp.concatenate([part[:chunk] for part in near], axis=0)

    def places(count):
        return [ints(4 * list_stride(count, cap))] * 2 + [ints(4)]

    block_flops = 8 * columns * nz * width
    started, diffused = call(
        functools.partial(first_deposit, nbrick, cap, ghost_rows),
        [struct(8 * columns, nz // 2), struct(3, nx, ny, nz)],
        [VMEM] * 5 + [HBM],
        [pltpu.VMEM((3, nx, ny, nz), f32)]
        + places(nbrick)
        + [pltpu.SemaphoreType.DMA((1,))],
        "first_deposit",
        block_flops * nblocks // 3,
    )(crossed, below, above, before, after, fluid)
    fluid_next, table, *answers_above = call(
        functools.partial(advance, nbrick, cap),
        [
            struct(3, nx, ny, nz),
            struct(12 * columns, nz // 2, dtype=bf16),
        ]
        + [struct(back, width)] * nbrick,
        [VMEM, HBM] + [VMEM] * (2 + nbrick),
        [
            pltpu.VMEM((2 * nbrick * chunk, width), f32),
            pltpu.VMEM((nbrick * back, width), f32),
            pltpu.VMEM((8 * columns, nz // 2), f32),
        ]
        + [pltpu.VMEM((3, nx, ny, nz), f32)] * 2
        + places(2 * nbrick)
        + [ints(4)]
        + [pltpu.SemaphoreType.DMA((2,))],
        "advance",
        block_flops * nblocks,
        places=[HBM] + [VMEM] * (1 + nbrick),
    )(started, fluid, diffused, from_below, *from_above)
    (answers_below,) = call(
        functools.partial(below_sample, nbrick, cap),
        [struct(nbrick * back, width)],
        [VMEM] * 2,
        places(nbrick),
        "below_sample",
        block_flops * nblocks // 64,
    )(from_below, table)
    answers_below = shifted(answers_below, "slab", -1)
    answers_above = [
        shifted(part, "brick", -behind) for behind, part in enumerate(answers_above)
    ]
    returned_down = shifted(jnp.concatenate(answers_above, axis=0), "slab", 1)
    answers = call(
        functools.partial(last_sample, nbrick, cap),
        [struct(back, width)] * nbrick,
        [VMEM] * 2,
        [pltpu.VMEM((nbrick * back, width), f32)] + places(nbrick),
        "last_sample",
        block_flops * nblocks // 64,
    )(crossed, table)
    returned = []
    for behind in range(nbrick):
        at = slice(behind * back, (behind + 1) * back)
        part = jnp.concatenate([answers[behind], answers_below[at]], axis=0)
        returned.append(shifted(part, "brick", -behind))
    (velocity_next,) = call(
        functools.partial(relax, nbrick, cap),
        [struct(3, nblocks, width)],
        [ANY] + [VMEM] * (3 + nbrick),
        [block_tiles, block_tiles, chunk_tiles, plan_copy]
        + [pltpu.SemaphoreType.DMA((1,))],
        "relax",
    )(plan, updated, spots, returned_down, *returned)
    return (jnp.transpose(velocity_next, (1, 0, 2)), fluid_next)


def solution(mesh):
    placed = (
        P(("slab", "brick"), None, None),
        P(("slab", "brick"), None, None),
        P(("slab", "brick"), None),
        P(("slab", "brick"), None),
        P(("slab", "brick"), None),
        P(("slab", "brick")),
        P(("slab", "brick")),
        P(("slab", "brick")),
        P(None, "slab", "brick", None),
    )
    return jax.shard_map(
        on_device,
        mesh=mesh,
        in_specs=placed,
        out_specs=(P(("slab", "brick"), None, None), P(None, "slab", "brick", None)),
        check_vma=False,
    )
```

```python
import functools
import math

import jax
import jax.numpy as jnp
from jax import lax
from jax.experimental import pallas as pl
from jax.experimental.pallas import tpu as pltpu
from jax.sharding import PartitionSpec as P

stiffness = 0.01
damping = 0.005
viscosity = 0.1
coupling = 0.5
relaxation = 0.5

f32 = jnp.float32
bf16 = jnp.bfloat16
VMEM = pl.BlockSpec(memory_space=pltpu.VMEM)
SMEM = pl.BlockSpec(memory_space=pltpu.SMEM)
ANY = pl.BlockSpec(memory_space=pl.ANY)
HBM = pl.BlockSpec(memory_space=pltpu.HBM)
UNROLL = 32
TAIL = 8
GROUP = 4
REST = 2


def rows_up(count):
    return -(-count // 8) * 8


def call(body, outs, ins, scratch, name, flops=0, nbytes=1 << 20, places=None, vmem=40 << 20):
    return pl.pallas_call(
        body,
        out_shape=outs,
        in_specs=ins,
        out_specs=places or [VMEM] * len(outs),
        scratch_shapes=scratch,
        name=name,
        compiler_params=pltpu.CompilerParams(vmem_limit_bytes=vmem),
        cost_estimate=pl.CostEstimate(flops=flops, bytes_accessed=nbytes, transcendentals=0),
    )


def rounded(x):
    return x.astype(bf16).astype(f32)


def iota(shape, dim):
    return lax.broadcasted_iota(jnp.int32, shape, dim)


planes = 7


def copy_all(pairs, sems):
    copies = [pltpu.make_async_copy(*pair, sems.at[i]) for i, pair in enumerate(pairs)]
    for copy in copies:
        copy.start()
    return copies


def wait_all(copies):
    for copy in copies:
        copy.wait()


def pack_kernel(ghost_ref, state, fluid, up, down, right, left):
    count = ghost_ref.shape[0] // 4
    width = state.shape[2]
    nx, ny, nz = fluid.shape[1:]
    for group in range(4):
        i, j = group // 2, group % 2
        slab_to, brick_to = (up if i else down), (right if j else left)
        for g in range(count):
            block = pl.ds(ghost_ref[group * count + g], 1)
            for c in range(planes):
                row = state[c, block, :]
                at = c * 2 * count + j * count + g
                slab_to[at : at + 1, :] = row
                at = c * 2 * count + i * count + g
                brick_to[at : at + 1, :] = row
    for slab_to, x in ((up, nx - 1), (down, 0)):
        for c in range(3):
            for k in range(nz // width):
                at = planes * 2 * count + (c * (nz // width) + k) * ny
                slab_to[at : at + ny, :] = fluid[c, x, :, k * width : (k + 1) * width]
    for brick_to, y in ((right, ny - 1), (left, 0)):
        for c in range(3):
            for x in range(nx):
                for k in range(nz // width):
                    at = planes * 2 * count + (c * nx + x) * (nz // width) + k
                    brick_to[at : at + 1, :] = fluid[
                        c, x, y : y + 1, k * width : (k + 1) * width
                    ]


def three_parts(x):
    one = rounded(x)
    rest = x - one
    two = rounded(rest)
    return one, two, rest - two


def put_rows(ref, stride, rows):
    count = rows[0].shape[0]
    for k, row in enumerate(rows):
        ref[pl.ds(k, count, stride=stride), :] = row


def pair_factors(place):
    parts = [three_parts(plane) for plane in place]
    own = three_parts(
        place[3] * place[3] - place[0] * place[0] - place[1] * place[1] - place[2] * place[2]
    )
    return [[part[k] for part in parts] for k in range(3)], list(own)


def home_rows(place):
    (one, two, three), own = pair_factors(place)
    ones, zeros = jnp.ones_like(place[0]), jnp.zeros_like(place[0])
    rows = one + one + two + two + one + three
    return [2.0 * row for row in rows] + own + [ones] * 3 + [zeros] * 2


def partner_rows(place):
    (one, two, three), own = pair_factors(place)
    ones, zeros = jnp.ones_like(place[0]), jnp.zeros_like(place[0])
    return one + two + one + two + three + one + [ones] * 3 + own + [zeros] * 2


def value_rows(values):
    highs = [rounded(plane) for plane in values]
    ones, zeros = jnp.ones_like(values[0]), jnp.zeros_like(values[0])
    lows = [plane - high for plane, high in zip(values, highs)]
    return highs + [ones, zeros] + lows + [zeros, zeros]


def prepare_partners(place, speeds, rows, columns, values):
    count, width = place[0].shape
    put_rows(rows, 32, partner_rows(place))
    put_rows(values, 16, value_rows(place[0:3] + speeds))

    def turn(b, _):
        block = rows[pl.ds(pl.multiple_of(b * 32, 32), 32), :]
        columns[b] = jnp.transpose(block).astype(bf16)
        return 0

    lax.fori_loop(0, count, turn, 0, unroll=8)


def list_tiles(home_ref, partner_ref, homes, partners, lower, upper, spare):
    def one(t, count):
        partner = partner_ref[t]
        homes[count] = home_ref[t]
        partners[count] = partner - lower
        return count + jnp.where((partner >= lower) & (partner < upper), 1, 0)

    count = lax.fori_loop(0, home_ref.shape[0], one, 0, unroll=4)
    for pad in range(TAIL):
        homes[count + pad] = spare
        partners[count + pad] = 0
    return count


def in_groups(count, large, small, work):
    steps = count // large
    left = (count - steps * large + small - 1) // small

    def one(size, first, step, _):
        work(size, first + step * size)
        return 0

    lax.fori_loop(0, steps, functools.partial(one, large, 0), 0)
    lax.fori_loop(0, left, functools.partial(one, small, steps * large), 0)


def add_tiles(count, homes, partners, home_side, partner_side, values, sums):
    def some(tiles, start):
        added = []
        for k in range(tiles):
            home = homes[start + k]
            partner = partners[start + k]
            factors = home_side[pl.ds(pl.multiple_of(home * 32, 32), 32), :].astype(bf16)
            weight = jnp.dot(partner_side[partner], factors, preferred_element_type=f32)
            weight = jnp.maximum(weight, 0.0)
            high = weight.astype(bf16)
            low = (weight - high.astype(f32)).astype(bf16)
            value = values[pl.ds(pl.multiple_of(partner * 16, 16), 16), :].astype(bf16)
            at = pl.ds(pl.multiple_of(home * 16, 16), 16)
            term = jnp.dot(
                jnp.concatenate([value, value], axis=1),
                jnp.concatenate([high, low], axis=0),
                preferred_element_type=f32,
            )
            added.append((at, term))
        for at, term in added:
            sums[at, :] += term

    in_groups(count, UNROLL, TAIL, some)


def dot(left, right):
    return jnp.dot(left.astype(bf16), right.astype(bf16), preferred_element_type=f32)


def plan_sort(cap, cell, route, columns, depth, spots, plan, bounds):
    nblocks, width = cell.shape
    shift = depth.bit_length() - 1
    number = cell[...]
    right = (number >> shift) >= columns // 2
    deep = (number & (depth - 1)) >= depth // 2
    kind = jnp.where(right, 2, 0) + jnp.where(deep, 1, 0)
    members = [jnp.where(kind == j, 1.0, 0.0) for j in range(4)]
    before = jnp.where(iota((width, width), 0) < iota((width, width), 1), 1.0, 0.0)
    stacked = jnp.concatenate(members, axis=0)
    ranks = dot(stacked, before)
    lengths = dot(stacked, jnp.ones((width, width), f32))
    ranks = [ranks[j * nblocks : (j + 1) * nblocks] for j in range(4)]
    lengths = [lengths[j * nblocks : (j + 1) * nblocks] for j in range(4)]

    across = jnp.broadcast_to(route[...].astype(f32), (nblocks, nblocks))
    same = across == jnp.transpose(across)
    earlier = iota((nblocks, nblocks), 1) < iota((nblocks, nblocks), 0)
    side_by_side = jnp.concatenate(lengths, axis=1)
    ahead = dot(jnp.where(same & earlier, 1.0, 0.0), side_by_side)
    whole = dot(jnp.where(same, 1.0, 0.0), side_by_side)
    rows = bounds.shape[0]
    of_code = jnp.broadcast_to(route[...], (rows, nblocks)) == iota((rows, nblocks), 0)
    totals = dot(jnp.where(of_code, 1.0, 0.0), side_by_side)

    lane = iota((nblocks, width), 1)
    bound_lane = iota((rows, width), 1)
    spot = jnp.zeros((nblocks, width), f32)
    first, chunk_first = jnp.zeros((nblocks, width), f32), jnp.zeros((nblocks, width), f32)
    bound, line = jnp.zeros((rows, width), f32), jnp.zeros((rows, width), f32)
    table = jnp.zeros((nblocks, width), jnp.int32)
    own_code = jnp.transpose(across).astype(jnp.int32)
    own_code = jnp.concatenate([own_code] * (width // nblocks), axis=1)
    for j in range(4):
        at = slice(j * width, (j + 1) * width)
        spot = spot + members[j] * (first + ranks[j])
        where = (chunk_first + ahead[:, at]).astype(jnp.int32)
        start, there = first.astype(jnp.int32), where & (width - 1)
        parts = [
            own_code * (cap + 2) + (where >> (width.bit_length() - 1)),
            there,
            start,
            lengths[j].astype(jnp.int32),
            (there - start) & (width - 1),
            (start - there) & (width - 1),
        ]
        for k, part in enumerate(parts):
            table = jnp.where(lane == 4 * k + j, part, table)
        first = first + lengths[j]
        chunk_first = chunk_first + whole[:, at]
        bound = bound + totals[:, at]
        line = jnp.where(bound_lane == j, bound, line)
    spots[...] = spot
    plan[...] = table
    bounds[...] = line


def block_order(spots, b):
    width = spots.shape[1]
    row = jnp.broadcast_to(spots[pl.ds(b, 1), :].astype(bf16), (width, width))
    hit = iota((width, width), 0).astype(f32).astype(bf16) == row
    return jnp.where(hit, jnp.ones((), bf16), jnp.zeros((), bf16))


def sort_blocks(plan, spots, data, sorted_rows, tiles):
    nblocks, width = spots.shape
    lane = iota((8, width), 1)

    def order(b, _):
        rows = data[pl.ds(pl.multiple_of(b * 16, 16), 16), :].astype(bf16)
        both = lax.dot_general(
            rows, block_order(spots, b), (((1,), (1,)), ((), ())), preferred_element_type=f32
        )
        sorted_rows[b] = both[0:8] + both[8:16]
        return 0

    def spread(b, _):
        block = sorted_rows[b]
        for j in range(4):
            tile, at, length = plan[b, j], plan[b, 4 + j], plan[b, 12 + j]
            moved = pltpu.roll(block, plan[b, 16 + j], 1)
            here = (lane >= at) & (lane < at + length)
            pltpu.store(tiles.at[tile], moved, mask=here)
            pltpu.store(tiles.at[tile + 1], moved, mask=lane < at + length - width)
        return 0

    lax.fori_loop(0, nblocks, order, 0, unroll=32)
    lax.fori_loop(0, nblocks, spread, 0, unroll=32)


def own_contacts(cap, columns, depth, home_list, partner_list, state, cell, route,
                 home_side, sums, spots, plan, bounds,
                 rows, partner_side, values, homes, partners, home_ref, partner_ref, sems):
    nblocks, width = state.shape[1:]
    copies = copy_all([(home_list, home_ref), (partner_list, partner_ref)], sems)
    plan_sort(cap, cell, route, columns, depth, spots, plan, bounds)
    place = [state[c] for c in range(4)]
    put_rows(home_side, 32, home_rows(place))
    prepare_partners(place, [state[c] for c in (4, 5, 6)], rows, partner_side, values)
    home_side[nblocks * 32 :, :] = jnp.zeros((32, width), f32)
    sums[...] = jnp.zeros(sums.shape, f32)
    wait_all(copies)
    count = list_tiles(home_ref, partner_ref, homes, partners, 0, nblocks, nblocks)
    add_tiles(count, homes, partners, home_side, partner_side, values, sums)


def diffuse(fluid, below, above, before, after, skip, diffused):
    nx, ny, nz = fluid.shape[1:]
    width = before.shape[1]
    deep = iota((ny, nz), 1)

    def face(ref, c, x):
        at = skip + (c * nx + x) * (nz // width)
        return jnp.concatenate(
            [ref[at + k : at + k + 1, :] for k in range(nz // width)], axis=1
        )

    def layer(ref, c):
        at = [skip + (c * (nz // width) + k) * ny for k in range(nz // width)]
        return jnp.concatenate([ref[start : start + ny, :] for start in at], axis=1)

    for x in range(nx):
        for c in range(3):
            here = fluid[c, x]
            near = (layer(below, c) if x == 0 else fluid[c, x - 1]) + (
                layer(above, c) if x == nx - 1 else fluid[c, x + 1]
            )
            near = near + jnp.concatenate([face(before, c, x), here[:-1]], axis=0)
            near = near + jnp.concatenate([here[1:], face(after, c, x)], axis=0)
            near = near + jnp.where(deep == 0, 0.0, pltpu.roll(here, 1, 1))
            near = near + jnp.where(deep == nz - 1, 0.0, pltpu.roll(here, nz - 1, 1))
            diffused[c, x] = here + viscosity * (near - 6.0 * here)


def brick_ahead(ahead, nbrick):
    return lax.rem(lax.axis_index("brick") + ahead, nbrick)


def ghost_contacts(nbrick, cap, partner_blocks, home_list, partner_list, plan, below,
                   above, before, after, home_side, own_sums, state, cell, spots, bounds,
                   updated, down, *rest):
    outgoings = rest[:nbrick]
    (rows, columns, values, sums, data, sorted_rows, tiles, homes, partners,
     home_ref, partner_ref, plan_ref, sems) = rest[nbrick:]
    nblocks, width = state.shape[1:]
    per = partner_blocks // 4
    copies = copy_all(
        [
            (home_list, home_ref),
            (partner_list, partner_ref),
            (plan, plan_ref),
        ],
        sems,
    )
    stacked = [
        jnp.concatenate(
            [ref[c * per : (c + 1) * per, :] for ref in (below, above, before, after)], axis=0
        )
        for c in range(planes)
    ]
    prepare_partners(stacked[0:4], stacked[4:7], rows, columns, values)
    sums[...] = own_sums[...]
    wait_all(copies)
    count = list_tiles(home_ref, partner_ref, homes, partners, nblocks, nblocks + 4 * per, nblocks)
    add_tiles(count, homes, partners, home_side, columns, values, sums)

    def total(k):
        high = sums[pl.ds(k, nblocks, stride=16), :]
        return high + sums[pl.ds(k + 8, nblocks, stride=16), :]

    weights = total(6)
    radius = state[3]
    inverse = 1.0 / (radius * radius * radius)
    fresh = []
    for c in range(3):
        speed = state[c + 4]
        spring = state[c] * weights - total(c)
        friction = total(c + 3) - speed * weights
        fresh.append(speed + (stiffness * spring + damping * friction) * inverse)
        updated[c] = fresh[c]

    number = cell[...]
    zeros = jnp.zeros_like(radius)
    highs = [rounded(plane) for plane in [radius] + fresh]
    lows = [plane - high for plane, high in zip([radius] + fresh, highs)]
    highs.append(((number >> 8) * 256).astype(f32))
    lows.append((number & 255).astype(f32))
    put_rows(data, 16, highs + [zeros] * 3 + lows + [zeros] * 3)
    sort_blocks(plan_ref, spots, data, sorted_rows, tiles)

    chunk = rows_up(5 * cap + 1)
    flat = tiles.reshape(tiles.shape[0] * 8, width)
    for ahead in range(nbrick):
        target = brick_ahead(ahead, nbrick)
        for side, (outgoing, row) in enumerate(
            ((down, ahead * chunk), (outgoings[ahead], 0), (outgoings[ahead], chunk))
        ):
            code = side * nbrick + target
            for c in range(5):
                outgoing[row + c * cap : row + (c + 1) * cap, :] = flat[
                    pl.ds(code * (cap + 2) * 8 + c, cap, stride=8), :
                ]
            outgoing[row + 5 * cap : row + 5 * cap + 1, :] = bounds[pl.ds(code, 1), :]


def list_stride(segments, cap):
    return (segments + 1) * cap


def list_arrived(arrived, starts, ends, cap, places, counts, early=None):
    base, goal = places
    width = arrived.shape[1]
    stride = list_stride(len(starts), cap)
    shift = width.bit_length() - 1
    lane = iota((1, width), 1)
    filled = [jnp.int32(0)] * 4
    for segment, (start, end) in enumerate(zip(starts, ends)):
        if early is not None and 2 * segment == len(starts):
            for j in range(4):
                early[j] = filled[j]
        row = arrived[start + 5 * cap : start + 5 * cap + 1, :]
        edge = jnp.int32(0)
        for j in range(4):
            next_edge = jnp.sum(jnp.where(lane == j, row, 0.0)).astype(jnp.int32)
            first = edge >> shift
            last = jnp.where(next_edge > edge, (next_edge + width - 1) >> shift, first)
            at = j * stride + filled[j]

            def put(some, at=at, first=first, start=start, end=end):
                for i in some:
                    base[at + i] = start + first + i
                    goal[at + i] = end + first + i

            few = min(4, cap)
            put(range(few))
            pl.when(last - first > few)(functools.partial(put, range(few, cap)))
            filled[j] = filled[j] + last - first
            edge = next_edge
    for j in range(4):
        counts[j] = filled[j]


def cell_parts(arrived, row, cap, columns, depth, bucket):
    cell = arrived[pl.ds(row + 4 * cap, 1), :].astype(jnp.int32)
    shift = (2 * depth).bit_length() - 1
    column = (cell >> shift) - (bucket // 2) * columns
    level = (cell & (2 * depth - 1)) - (bucket % 2) * depth - depth // 2
    return column.astype(f32), level.astype(f32)


def all_levels(depth, width):
    return (iota((depth, width), 0) - depth // 2).astype(f32).astype(bf16)


def level_hot(level, levels):
    hit = levels == jnp.broadcast_to(level.astype(bf16), levels.shape)
    return jnp.where(hit, jnp.ones((), bf16), jnp.zeros((), bf16))


def longest(counts):
    return jnp.maximum(jnp.maximum(counts[0], counts[1]), jnp.maximum(counts[2], counts[3]))


def tile_of(counts, bucket, index, width):
    count = counts[bucket]
    real = jnp.full((1, width), jnp.where(index < count, 1, 0), jnp.int32) > 0
    return jnp.minimum(index, jnp.maximum(count - 1, 0)), real


def deposit(segments, counts, arrived, base, cap, total):
    columns, depth = total.shape[0] // 16, total.shape[1]
    width = arrived.shape[1]
    stride = list_stride(segments, cap)
    numbers = iota((columns, width), 0).astype(f32).astype(bf16)
    levels = all_levels(depth, width)

    def some(size, first):
        sums = []
        for bucket in range(4):
            high_of, low_of, level_of = [], [], []
            for k in range(size):
                index, real = tile_of(counts, bucket, first + k, width)
                row = base[bucket * stride + index]
                column, level = cell_parts(arrived, row, cap, columns, depth, bucket)
                radius = arrived[pl.ds(row, 1), :]
                mass = radius * radius * radius
                loads = [mass] + [mass * arrived[pl.ds(row + c * cap, 1), :] for c in (1, 2, 3)]
                hit = numbers == jnp.broadcast_to(column.astype(bf16), (columns, width))
                highs, lows = [], []
                for load in loads:
                    load = jnp.where(real, load, 0.0)
                    high = load.astype(bf16)
                    low = (load - high.astype(f32)).astype(bf16)
                    for parts, part in ((highs, high), (lows, low)):
                        part = jnp.broadcast_to(part, (columns, width))
                        parts.append(jnp.where(hit, part, jnp.zeros((), bf16)))
                high_of.append(jnp.concatenate(highs, axis=0))
                low_of.append(jnp.concatenate(lows, axis=0))
                level_of.append(level_hot(level, levels))
            both = lax.dot_general(
                jnp.concatenate(
                    [jnp.concatenate(high_of, axis=1), jnp.concatenate(low_of, axis=1)], axis=0
                ),
                jnp.concatenate(level_of, axis=1),
                (((1,), (1,)), ((), ())),
                preferred_element_type=f32,
            )
            sums.append(both[0 : 4 * columns] + both[4 * columns :])
        for bucket in range(4):
            total[bucket * 4 * columns : (bucket + 1) * 4 * columns, :] += sums[bucket]

    in_groups(longest(counts), GROUP, REST, some)


def sample(segments, counts, arrived, places, cap, table, answers):
    columns, depth = table.shape[0] // 24, table.shape[1]
    width = arrived.shape[1]
    stride = list_stride(segments, cap)
    levels = all_levels(depth, width)
    numbers = iota((columns, width), 0).astype(f32)
    answers[...] = jnp.zeros(answers.shape, f32)

    def some(size, first):
        found = []
        for bucket in range(4):
            hots, hits = [], []
            for k in range(size):
                index, real = tile_of(counts, bucket, first + k, width)
                row = places[0][bucket * stride + index]
                column, level = cell_parts(arrived, row, cap, columns, depth, bucket)
                hots.append(level_hot(level, levels))
                hits.append((numbers == column, real, places[1][bucket * stride + index]))
            along = jnp.dot(
                table[bucket * 6 * columns : (bucket + 1) * 6 * columns, :],
                jnp.concatenate(hots, axis=1),
                preferred_element_type=f32,
            )
            for k, (hit, real, goal) in enumerate(hits):
                part = along[:, k * width : (k + 1) * width]
                for c in range(3):
                    value = part[c * columns : (c + 1) * columns]
                    value = value + part[(c + 3) * columns : (c + 4) * columns]
                    value = jnp.sum(jnp.where(hit, value, 0.0), axis=0, keepdims=True)
                    found.append((goal + c * cap, jnp.where(real, value, 0.0)))
        for goal, value in found:
            answers[pl.ds(goal, 1), :] += value

    in_groups(longest(counts), GROUP, REST, some)


def first_deposit(nbrick, cap, skip, crossed, below, above, before, after, fluid, total, diffused,
                  flow, base, goal, counts, sems):
    reading = copy_all([(fluid, flow)], sems)
    chunk = rows_up(5 * cap + 1)
    total[...] = jnp.zeros(total.shape, f32)
    starts = [b * chunk for b in range(nbrick)]
    list_arrived(crossed, starts, starts, cap, (base, goal), counts)
    deposit(nbrick, counts, crossed, base, cap, total)
    wait_all(reading)
    diffuse(flow, below, above, before, after, skip, diffused)


def advance(nbrick, cap, start, fluid, diffused, below, *rest):
    above, rest = rest[:nbrick], rest[nbrick:]
    fluid_next, table = rest[:2]
    answers_above, rest = rest[2 : 2 + nbrick], rest[2 + nbrick :]
    arrived, answers, total, flow, fresh_flow, base, goal, counts, early, sems = rest
    reading = pltpu.make_async_copy(fluid, flow, sems.at[0])
    reading.start()
    chunk = rows_up(5 * cap + 1)
    back = rows_up(3 * cap)
    rows = nbrick * chunk
    for b, part in enumerate(above):
        arrived[b * chunk : (b + 1) * chunk, :] = part[...]
    arrived[rows:, :] = below[...]
    starts = [i * chunk for i in range(2 * nbrick)]
    ends = [i * back for i in range(2 * nbrick)]
    total[...] = start[...]
    list_arrived(arrived, starts, ends, cap, (base, goal), counts, early)
    deposit(2 * nbrick, counts, arrived, base, cap, total)
    reading.wait()

    nx, ny, nz = flow.shape[1:]
    columns, depth = nx * ny // 2, nz // 2
    for x in range(nx):
        buckets = [2 * (x * ny // columns) + deep for deep in range(2)]
        at = x * ny % columns

        def load(c):
            spots = [4 * columns * bucket + c * columns + at for bucket in buckets]
            return jnp.concatenate([total[spot : spot + ny, :] for spot in spots], axis=1)

        volume = load(0)
        for c in range(3):
            moved = load(c + 1) - volume * flow[c, x]
            fresh = diffused[c, x] + coupling * moved
            fresh_flow[c, x] = fresh
            high = fresh.astype(bf16)
            low = (fresh - high.astype(f32)).astype(bf16)
            for deep, bucket in enumerate(buckets):
                spot = 6 * columns * bucket + c * columns + at
                half = slice(deep * depth, (deep + 1) * depth)
                table[spot : spot + ny, :] = high[:, half]
                table[spot + 3 * columns : spot + 3 * columns + ny, :] = low[:, half]
    writing = pltpu.make_async_copy(fresh_flow, fluid_next, sems.at[1])
    writing.start()
    sample(2 * nbrick, early, arrived, (base, goal), cap, table, answers)
    for b, part in enumerate(answers_above):
        part[...] = answers[b * back : (b + 1) * back, :]
    writing.wait()


def below_sample(nbrick, cap, below, table, answers, base, goal, counts):
    chunk = rows_up(5 * cap + 1)
    back = rows_up(3 * cap)
    starts = [b * chunk for b in range(nbrick)]
    ends = [b * back for b in range(nbrick)]
    list_arrived(below, starts, ends, cap, (base, goal), counts)
    sample(nbrick, counts, below, (base, goal), cap, table, answers)


def last_sample(nbrick, cap, _, crossed, table, *rest):
    answers, base, goal, counts = rest[nbrick:]
    chunk = rows_up(5 * cap + 1)
    back = rows_up(3 * cap)
    starts = [b * chunk for b in range(nbrick)]
    ends = [b * back for b in range(nbrick)]
    list_arrived(crossed, starts, ends, cap, (base, goal), counts)
    sample(nbrick, counts, crossed, (base, goal), cap, table, answers)
    for b, part in enumerate(rest[:nbrick]):
        part[...] = answers[b * back : (b + 1) * back, :]


def relax(nbrick, cap, plan, updated, spots, down, *rest):
    returneds = rest[:nbrick]
    velocity_next, picked, sorted_rows, tiles, plan_ref, sems = rest[nbrick:]
    copies = copy_all([(plan, plan_ref)], sems)
    nblocks, width = spots.shape
    back = rows_up(3 * cap)
    flat = tiles.reshape(tiles.shape[0] * 8, width)
    for ahead in range(nbrick):
        target = brick_ahead(ahead, nbrick)
        for side, (returned, row) in enumerate(
            ((down, ahead * back), (returneds[ahead], 0), (returneds[ahead], back))
        ):
            code = side * nbrick + target
            for c in range(3):
                flat[pl.ds(code * (cap + 2) * 8 + c, cap, stride=8), :] = returned[
                    row + c * cap : row + (c + 1) * cap, :
                ]
    lane = iota((8, width), 1)
    wait_all(copies)

    def gather(b, _):
        block = jnp.zeros((8, width), f32)
        for j in range(4):
            tile, at = plan_ref[b, j], plan_ref[b, 4 + j]
            first, length = plan_ref[b, 8 + j], plan_ref[b, 12 + j]
            run = jnp.where(lane >= at, tiles[tile], tiles[tile + 1])
            run = pltpu.roll(run, plan_ref[b, 20 + j], 1)
            block = jnp.where((lane >= first) & (lane < first + length), run, block)
        sorted_rows[b] = block
        return 0

    def order(b, _):
        block = sorted_rows[b]
        high = rounded(block)
        both = jnp.dot(
            jnp.concatenate([high, block - high], axis=0).astype(bf16),
            block_order(spots, b),
            preferred_element_type=f32,
        )
        picked[b] = both[0:8] + both[8:16]
        return 0

    lax.fori_loop(0, nblocks, gather, 0, unroll=32)
    lax.fori_loop(0, nblocks, order, 0, unroll=32)
    flat = picked.reshape(nblocks * 8, width)
    for c in range(3):
        now = updated[c]
        velocity_next[c] = now + relaxation * (flat[pl.ds(c, nblocks, stride=8), :] - now)


def on_device(
    positions, velocities, radii, cell_of, block_route, ghost_list, tile_home, tile_partner, fluid
):
    nblocks, _, width = positions.shape
    nbrick = lax.axis_size("brick")
    _, nx, ny, nz = fluid.shape
    columns = nx * ny
    codes = 3 * nbrick
    cap = max(2, (2 * nblocks + codes - 1) // codes)
    chunk, back = rows_up(5 * cap + 1), rows_up(3 * cap)
    per = ghost_list.shape[0] // 2
    tiles = tile_home.shape[0]
    routes = block_route.reshape(-1)
    positions = jnp.transpose(positions, (1, 0, 2))
    velocities = jnp.transpose(velocities, (1, 0, 2))

    def struct(*shape, dtype=f32):
        return jax.ShapeDtypeStruct(shape, dtype)

    def shifted(x, axis, step):
        if step == 0:
            return x
        count = lax.axis_size(axis)
        return lax.ppermute(x, axis, [(i, (i + step) % count) for i in range(count)])

    def ints(count):
        return pltpu.SMEM((count,), jnp.int32)

    state = jnp.concatenate([positions, radii[None], velocities], axis=0)
    ghost_rows, chunks = planes * per, 3 * (nz // width)
    up, low, right, left = call(
        pack_kernel,
        [struct(ghost_rows + chunks * ny, width)] * 2 + [struct(ghost_rows + chunks * nx, width)] * 2,
        [SMEM] + [VMEM] * 2,
        [],
        "pack",
    )(ghost_list, state, fluid)
    below = shifted(up, "slab", 1)
    above = shifted(low, "slab", -1)
    before = shifted(right, "brick", 1)
    after = shifted(left, "brick", -1)

    def sides(count):
        return [
            pltpu.VMEM((count * 32, width), f32),
            pltpu.VMEM((count, width, 32), bf16),
            pltpu.VMEM((count * 16, width), f32),
        ]

    lists = [ints(tiles + TAIL)] * 2
    contact_flops = tiles * width * width * 200
    chunk_tiles = pltpu.VMEM((codes * (cap + 2), 8, width), f32)
    block_tiles = pltpu.VMEM((nblocks, 8, width), f32)
    plan_copy = pltpu.SMEM((nblocks, width), jnp.int32)
    home_side, sums, spots, plan, bounds = call(
        functools.partial(own_contacts, cap, columns, nz),
        [
            struct((nblocks + 1) * 32, width),
            struct((nblocks + 1) * 16, width),
            struct(nblocks, width),
            struct(nblocks, width, dtype=jnp.int32),
            struct(rows_up(codes), width),
        ],
        [HBM] * 2 + [VMEM] * 3,
        sides(nblocks) + lists + [ints(tiles)] * 2 + [pltpu.SemaphoreType.DMA((2,))],
        "own_contacts",
        contact_flops,
    )(tile_home, tile_partner, state, cell_of, routes.reshape(1, nblocks))
    updated, down, *outgoing = call(
        functools.partial(ghost_contacts, nbrick, cap, 4 * per),
        [struct(3, nblocks, width), struct(nbrick * chunk, width)]
        + [struct(2 * chunk, width)] * nbrick,
        [HBM] * 2 + [ANY] + [VMEM] * 10,
        sides(4 * per)
        + [pltpu.VMEM(((nblocks + 1) * 16, width), f32)]
        + [pltpu.VMEM((nblocks * 16, width), f32), block_tiles, chunk_tiles]
        + lists
        + [ints(tiles), ints(tiles), plan_copy, pltpu.SemaphoreType.DMA((3,))],
        "ghost_contacts",
        contact_flops // 2,
    )(tile_home, tile_partner, plan, below, above, before, after,
      home_side, sums, state, cell_of, spots, bounds)

    down = shifted(down, "slab", -1)
    near = [shifted(part, "brick", ahead) for ahead, part in enumerate(outgoing)]
    from_below = shifted(jnp.concatenate([part[chunk:] for part in near], axis=0), "slab", 1)
    from_above = [
        shifted(down[ahead * chunk : (ahead + 1) * chunk], "brick", ahead)
        for ahead in range(nbrick)
    ]
    crossed = jnp.concatenate([part[:chunk] for part in near], axis=0)

    def places(count):
        return [ints(4 * list_stride(count, cap))] * 2 + [ints(4)]

    block_flops = 8 * columns * nz * width
    started, diffused = call(
        functools.partial(first_deposit, nbrick, cap, ghost_rows),
        [struct(8 * columns, nz // 2), struct(3, nx, ny, nz)],
        [VMEM] * 5 + [HBM],
        [pltpu.VMEM((3, nx, ny, nz), f32)]
        + places(nbrick)
        + [pltpu.SemaphoreType.DMA((1,))],
        "first_deposit",
        block_flops * nblocks // 3,
    )(crossed, below, above, before, after, fluid)
    fluid_next, table, *answers_above = call(
        functools.partial(advance, nbrick, cap),
        [
            struct(3, nx, ny, nz),
            struct(12 * columns, nz // 2, dtype=bf16),
        ]
        + [struct(back, width)] * nbrick,
        [VMEM, HBM] + [VMEM] * (2 + nbrick),
        [
            pltpu.VMEM((2 * nbrick * chunk, width), f32),
            pltpu.VMEM((nbrick * back, width), f32),
            pltpu.VMEM((8 * columns, nz // 2), f32),
        ]
        + [pltpu.VMEM((3, nx, ny, nz), f32)] * 2
        + places(2 * nbrick)
        + [ints(4)]
        + [pltpu.SemaphoreType.DMA((2,))],
        "advance",
        block_flops * nblocks,
        places=[HBM] + [VMEM] * (1 + nbrick),
    )(started, fluid, diffused, from_below, *from_above)
    (answers_below,) = call(
        functools.partial(below_sample, nbrick, cap),
        [struct(nbrick * back, width)],
        [VMEM] * 2,
        places(nbrick),
        "below_sample",
        block_flops * nblocks // 64,
    )(from_below, table)
    answers_below = shifted(answers_below, "slab", -1)
    answers_above = [
        shifted(part, "brick", -behind) for behind, part in enumerate(answers_above)
    ]
    joined = jnp.concatenate(answers_above, axis=0)
    returned_down = shifted(joined, "slab", 1)
    answers = call(
        functools.partial(last_sample, nbrick, cap),
        [struct(back, width)] * nbrick,
        [ANY] + [VMEM] * 2,
        [pltpu.VMEM((nbrick * back, width), f32)] + places(nbrick),
        "last_sample",
        block_flops * nblocks // 64,
    )(joined, crossed, table)
    returned = []
    for behind in range(nbrick):
        at = slice(behind * back, (behind + 1) * back)
        part = jnp.concatenate([answers[behind], answers_below[at]], axis=0)
        returned.append(shifted(part, "brick", -behind))
    (velocity_next,) = call(
        functools.partial(relax, nbrick, cap),
        [struct(3, nblocks, width)],
        [ANY] + [VMEM] * (3 + nbrick),
        [block_tiles, block_tiles, chunk_tiles, plan_copy]
        + [pltpu.SemaphoreType.DMA((1,))],
        "relax",
    )(plan, updated, spots, returned_down, *returned)
    return (jnp.transpose(velocity_next, (1, 0, 2)), fluid_next)


def solution(mesh):
    placed = (
        P(("slab", "brick"), None, None),
        P(("slab", "brick"), None, None),
        P(("slab", "brick"), None),
        P(("slab", "brick"), None),
        P(("slab", "brick"), None),
        P(("slab", "brick")),
        P(("slab", "brick")),
        P(("slab", "brick")),
        P(None, "slab", "brick", None),
    )
    return jax.shard_map(
        on_device,
        mesh=mesh,
        in_specs=placed,
        out_specs=(P(("slab", "brick"), None, None), P(None, "slab", "brick", None)),
        check_vma=False,
    )
```
